32 devices in a mesh: sub: 8 (over z, y), pln: 4 (over x, core).
Axes of the slice: x: 2, y: 2, z: 4, core: 2. Of those that a mesh axis runs over, the one named last changes fastest.
Arguments:
- labels: int32 [8, 64, 1024], P('pln', None, 'sub'), may hold values from 0 to 3
- levels: float32 [4], replicated, may hold values from 0.1 to 1
- zvec: bfloat16 [64, 8, 64, 1024], P(None, 'pln', None, 'sub'), may hold values from -1 to 1
- resid: float32 [8, 64, 1024], P('pln', None, 'sub'), may hold values from -6 to 6
Outputs:
- coarse_solution: float32 [8, 64], P('sub')
- deflated: float32 [8, 64, 1024], P('pln', None, 'sub')
The draws below stay inside these ranges and needn't reach their ends.
All inputs are finite; a program needn't handle non-finite values.
Results may differ from the reference program's by a relative error of at most 0.0003.
Values may be sent and summed in bfloat16 or wider, within the bound.
No kernel may reach another device: no remote copies, remote signals or barrier semaphores. Data moves between devices by JAX's collectives and lax.ppermute only.
A program may use at most 128 MiB of HBM per device.

```python
import math
import jax
import jax.numpy as jnp
from jax import lax

K = 64
NLEV = 4
CITERS = 2
NY = 64
CZ = 128
NX = 8
NZ = 1024
SUBS = 8


def draw_zvec(key, part):
    mode_key = jax.random.fold_in(key, 11)
    rough_key = jax.random.fold_in(key, 12)
    modes = jax.random.truncated_normal(mode_key, -3.0, 3.0, (K, NX, NY), jnp.float32)
    rough = jax.random.uniform(rough_key, (K, NX, NY, NZ), jnp.float32, 0.5, 1.5)
    layer = jnp.arange(NZ) % CZ
    distance = jnp.minimum(layer, CZ - 1 - layer).astype(jnp.float32)
    profile = 0.5 + 1.5 * jnp.exp(-distance / 4.0)
    total = 0.0
    for position in range(CZ):
        total = total + (0.5 + 1.5 * math.exp(-min(position, CZ - 1 - position) / 4.0)) ** 2
    factor = 1.0 / math.sqrt(total * NX * NY)
    return (modes[..., None] * profile * rough * factor).astype(jnp.bfloat16)


def place_ends(result, rng, low, top_value):
    longest = result.shape.index(max(result.shape))
    spots = []
    for shift in (0, 1):
        where = [jax.random.randint(jax.random.fold_in(rng, axis), (), 0, length) for axis, length in enumerate(result.shape)]
        where[longest] = (where[longest] + shift) % result.shape[longest]
        spots.append(tuple(where))
    return result.at[spots[0]].set(low).at[spots[1]].set(top_value)


def level_of(rng, shape, split, smallest, top_value):
    level = 1.0
    for dim, blocks in split:
        heights = jax.random.uniform(jax.random.fold_in(jax.random.fold_in(rng, 6), dim), (blocks,), jnp.float32, smallest / len(split), top_value / len(split))
        level = level * jnp.repeat(jnp.exp(heights), shape[dim] // blocks).reshape((-1,) + (1,) * (len(shape) - 1 - dim))
    return level


def noise(stream_key, extent, spread, reach, split=(), kind=jnp.bfloat16):
    result = jax.random.normal(stream_key, extent, jnp.float32) * spread
    if len(split) > 0:
        result = level_of(stream_key, extent, split, -0.22, 0.18) * result
    return jnp.clip(result, min=-reach, max=reach).astype(kind)


def setup_inputs(seed: int = 0) -> dict:
    key_of = jax.random.split(jax.random.key(seed), 5)
    labels = place_ends(jax.random.randint(key_of[0], (NX, NY, NZ), 0, NLEV), jax.random.fold_in(key_of[0], 1), 0, NLEV - 1).astype(jnp.int32)
    levels = jnp.clip(jnp.exp(jax.random.uniform(key_of[1], (NLEV,), jnp.float32, math.log(0.1), math.log(1.0))), 0.1, 1.0)
    zvec = draw_zvec(jax.random.fold_in(key_of[4], 71), 0)
    resid = noise(key_of[3], (NX, NY, NZ), 1.0, 6.0, ((0, 4), (2, 8)), jnp.float32)
    return dict(labels=labels, levels=levels, zvec=zvec, resid=resid)


PRECISE = lax.Precision.HIGHEST


def harmonic(left_value, right_value):
    return 2.0 * left_value * right_value / (left_value + right_value)


def coefficients(labels, levels):
    weighted = jnp.zeros(labels.shape, jnp.float32)
    for level_index in range(levels.shape[0]):
        weighted = weighted + jnp.where(labels == level_index, levels[level_index], 0.0)
    return weighted


def apply_yz(fine_field, weights, z_below, z_above):
    zero_plane = jnp.zeros_like(fine_field[..., :1, :])
    below_y = jnp.concatenate([zero_plane, fine_field[..., :-1, :]], axis=-2)
    above_y = jnp.concatenate([fine_field[..., 1:, :], zero_plane], axis=-2)
    below_z = jnp.concatenate([z_below, fine_field[..., :-1]], axis=-1)
    above_z = jnp.concatenate([fine_field[..., 1:], z_above], axis=-1)
    return (weights[2] * (fine_field - below_y) + weights[3] * (fine_field - above_y)
            + weights[4] * (fine_field - below_z) + weights[5] * (fine_field - above_z))


def apply_full(fine_field, weights, x_below, x_above, z_below, z_above):
    below_x = jnp.concatenate([x_below, fine_field[..., :-1, :, :]], axis=-3)
    above_x = jnp.concatenate([fine_field[..., 1:, :, :], x_above], axis=-3)
    return (weights[0] * (fine_field - below_x) + weights[1] * (fine_field - above_x)
            + apply_yz(fine_field, weights, z_below, z_above))


def face_weights(density_coef):
    pad_x = jnp.pad(density_coef, ((1, 1), (0, 0), (0, 0)), mode="edge")
    pad_y = jnp.pad(density_coef, ((0, 0), (1, 1), (0, 0)), mode="edge")
    return (harmonic(density_coef, pad_x[:-2]), harmonic(density_coef, pad_x[2:]),
            harmonic(density_coef, pad_y[:, :-2]), harmonic(density_coef, pad_y[:, 2:]),
            harmonic(density_coef, jnp.roll(density_coef, 1, axis=2)),
            harmonic(density_coef, jnp.roll(density_coef, -1, axis=2)))


def coarse_apply(diag_blocks, upper_blocks, direction):
    ahead_term = jnp.roll(direction, -1, axis=0)
    behind_term = jnp.roll(direction, 1, axis=0)
    upper_behind = jnp.roll(upper_blocks, 1, axis=0)
    return (jnp.einsum("skl,sl->sk", diag_blocks, direction, precision=PRECISE)
            + jnp.einsum("skl,sl->sk", upper_blocks, ahead_term, precision=PRECISE)
            + jnp.einsum("slk,sl->sk", upper_behind, behind_term, precision=PRECISE))


def reference(labels, levels, zvec, resid):
    density_coef = coefficients(labels, levels)
    weights = face_weights(density_coef)

    def slab_terms(slab_index):
        start = (slab_index * CZ).astype(jnp.int32)
        next_start = (((slab_index + 1) % SUBS) * CZ).astype(jnp.int32)
        own_modes = lax.dynamic_slice_in_dim(zvec, start, CZ, axis=3).astype(jnp.float32)
        first_layer = lax.dynamic_slice_in_dim(zvec, next_start, 1, axis=3).astype(jnp.float32)
        slab_weights = tuple(lax.dynamic_slice_in_dim(weight_field, start, CZ, axis=2) for weight_field in weights)
        slab_resid = lax.dynamic_slice_in_dim(resid, start, CZ, axis=2)
        x_zero = jnp.zeros_like(own_modes[:, :1])
        z_zero = jnp.zeros_like(own_modes[..., :1])
        stencil_image = apply_full(own_modes, slab_weights, x_zero, x_zero, z_zero, z_zero)
        flat_modes = own_modes.reshape(K, -1)
        diag_block = jnp.dot(flat_modes, stencil_image.reshape(K, -1).T, precision=PRECISE)
        edge_rows = (own_modes[..., -1] * slab_weights[5][..., -1]).reshape(K, -1)
        upper_block = -jnp.dot(edge_rows, first_layer.reshape(K, -1).T, precision=PRECISE)
        slab_rhs = jnp.dot(flat_modes, slab_resid.reshape(-1), precision=PRECISE)
        return diag_block, upper_block, slab_rhs

    diag_blocks, upper_blocks, coarse_rhs = lax.map(slab_terms, jnp.arange(SUBS, dtype=jnp.int32))

    solution = jnp.zeros_like(coarse_rhs)
    remain = coarse_rhs
    direction = coarse_rhs
    norm_now = jnp.sum(remain * remain)
    for iteration in range(CITERS):
        stencil_image = coarse_apply(diag_blocks, upper_blocks, direction)
        step_size = norm_now / jnp.sum(direction * stencil_image)
        solution = solution + step_size * direction
        remain = remain - step_size * stencil_image
        norm_next = jnp.sum(remain * remain)
        direction = remain + (norm_next / norm_now) * direction
        norm_now = norm_next

    def slab_field(slab_index):
        start = (slab_index * CZ).astype(jnp.int32)
        own_modes = lax.dynamic_slice_in_dim(zvec, start, CZ, axis=3).astype(jnp.float32)
        return jnp.dot(solution[slab_index], own_modes.reshape(K, -1), precision=PRECISE).reshape(NX, NY, CZ)

    slabs = lax.map(slab_field, jnp.arange(SUBS, dtype=jnp.int32))
    fine_field = jnp.moveaxis(slabs, 0, 2).reshape(NX, NY, NZ)
    x_zero = jnp.zeros_like(fine_field[:1])
    stencil_image = apply_full(fine_field, weights, x_zero, x_zero, fine_field[..., -1:], fine_field[..., :1])
    return solution, resid - stencil_image
```

```python
import jax
import jax.numpy as jnp
from jax import lax
from jax.experimental import pallas as pl
from jax.experimental.pallas import tpu as pltpu
from jax.sharding import PartitionSpec as P

CITERS = 2
STEP = 4
F32 = jnp.float32
BF16 = jnp.bfloat16
PRECISE = lax.Precision.HIGHEST
NT = (((1,), (1,)), ((), ()))
TN = (((0,), (0,)), ((), ()))
VMEM = pl.BlockSpec(memory_space=pltpu.VMEM)
SMEM = pl.BlockSpec(memory_space=pltpu.SMEM)


def call(kernel, outs, specs, scratch=(), flops=0, moved=0, limit=32):
    return pl.pallas_call(
        kernel,
        out_shape=outs,
        in_specs=specs,
        out_specs=jax.tree.map(lambda _: VMEM, outs),
        scratch_shapes=list(scratch),
        cost_estimate=pl.CostEstimate(flops=flops, bytes_accessed=moved, transcendentals=0),
        compiler_params=pltpu.CompilerParams(vmem_limit_bytes=limit << 20),
    )


def harmonic(left_value, right_value):
    return 2.0 * left_value * right_value / (left_value + right_value)


def coefficients(labels, levels_ref):
    weighted = jnp.zeros(labels.shape, F32)
    for level in range(levels_ref.shape[0]):
        weighted = weighted + jnp.where(labels == level, levels_ref[level], 0.0)
    return weighted


def split(value):
    high = value.astype(BF16)
    return high, (value - high.astype(F32)).astype(BF16)


def lane_is(shape, lane):
    return lax.broadcasted_iota(jnp.int32, shape, len(shape) - 1) == lane


def pick_row(lane, width):
    row = lax.broadcasted_iota(jnp.int32, (16, width), 0)
    return ((row == 0) & lane_is((16, width), lane)).astype(BF16)


def prepare_kernel(labels, zvec, near_low, near_high, far_low, far_high, first, last):
    modes, planes, rows, layers = zvec.shape
    half = rows // 2
    for out, plane, start in ((near_high, 1, 0), (near_low, 0, half), (far_high, 1, half), (far_low, 0, 0)):
        for at in range(0, half, 16):
            out[at:at + 16] = jnp.swapaxes(zvec[:, plane, start + at:start + at + 16, :], 0, 1)
    row = lax.broadcasted_iota(jnp.int32, (16, layers), 0)
    both = ((row == 0) & lane_is((16, layers), 0)) | ((row == 1) & lane_is((16, layers), layers - 1))
    ends = lax.dot_general(
        both.astype(BF16), zvec[...].reshape(-1, layers), NT, preferred_element_type=F32
    )
    width = planes * rows
    first[:modes] = jnp.concatenate(
        [ends[0:1, k * width:(k + 1) * width] for k in range(modes)], axis=0
    ).astype(BF16)
    last[:modes] = jnp.concatenate(
        [ends[1:2, k * width:(k + 1) * width] for k in range(modes)], axis=0
    ).astype(BF16)
    flat = labels[...].astype(F32).astype(BF16).reshape(width, layers)
    for out, lane in ((first, 0), (last, layers - 1)):
        out[modes:] = lax.dot_general(
            pick_row(lane, layers), flat, NT, preferred_element_type=F32
        ).astype(BF16)


def block_kernel(
    place, levels, labels, labels_below, labels_above, resid, near_low, near_high, far_low, far_high,
    partial, weights, half_diag, link_y, link_z,
):
    planes, rows, layers = labels.shape
    modes = near_low.shape[1]
    half = rows // 2
    at_first, at_last = place[1] == 0, place[1] == place[2] - 1
    coef = [coefficients(labels[x], levels) for x in range(2)]
    below = jnp.where(at_first, coef[0], coefficients(labels_below[0], levels))
    above = jnp.where(at_last, coef[1], coefficients(labels_above[0], levels))
    low_x = harmonic(coef[0], below)
    high_x = harmonic(coef[1], above)
    mid_x = harmonic(coef[0], coef[1])
    weights[0] = low_x
    weights[1] = high_x
    weights[2] = mid_x
    row = lax.broadcasted_iota(jnp.int32, (rows, layers), 0)
    lane = lax.broadcasted_iota(jnp.int32, (rows, layers), 1)
    for x in range(2):
        c = coef[x]
        up_y = harmonic(c, jnp.where(row == rows - 1, c, pltpu.roll(c, rows - 1, 0)))
        up_z = harmonic(c, pltpu.roll(c, layers - 1, 1))
        down_y = jnp.where(row == 0, c, pltpu.roll(up_y, 1, 0))
        weights[3 + x] = up_y
        weights[5 + x] = up_z
        weights[7 + x] = c
        inner_z = jnp.where(lane == layers - 1, 0.0, up_z)
        total = (low_x, high_x)[x] + mid_x + up_y + down_y + inner_z + pltpu.roll(inner_z, 1, 1)
        half_diag[x] = 0.5 * total
        link_y[x] = jnp.where(row == rows - 1, 0.0, up_y)
        link_z[x] = inner_z

    def step(start, base, here, ahead, carry):
        total, rhs = carry
        left, high, low = [], [], []
        for u in range(STEP):
            y = base + start + u
            at = pl.ds(y, 1)
            node = [here[x][start + u] for x in range(2)]
            wide = [v.astype(F32) for v in node]
            up = [v.astype(F32) for v in ahead(start, u)]
            for x in range(2):
                image = (
                    half_diag[x, at, :] * wide[x]
                    - link_y[x, at, :] * up[x]
                    - link_z[x, at, :] * pltpu.roll(wide[x], layers - 1, 1)
                )
                if x == 0:
                    image = image - weights[2, at, :] * wide[1]
                rhs = rhs + resid[x, at, :] * wide[x]
                parts = split(image)
                left.append(node[x])
                high.append(parts[0])
                low.append(parts[1])
        right = jnp.concatenate([jnp.concatenate(high, axis=1), jnp.concatenate(low, axis=1)], axis=0)
        total = total + lax.dot_general(
            jnp.concatenate(left, axis=1), right, NT, preferred_element_type=F32
        )
        return total, rhs

    carry = (jnp.zeros((modes, 2 * modes), F32), jnp.zeros((modes, layers), F32))
    low_half, high_half = (far_low, near_high), (near_low, far_high)
    for here, then, base in ((low_half, high_half, 0), (high_half, None, half)):
        def inside(start, u, here=here):
            return [here[x][start + u + 1] for x in range(2)]

        def at_end(start, u, here=here, then=then):
            if u + 1 < STEP:
                return inside(start, u, here)
            return [here[x][start + u] if then is None else then[x][0] for x in range(2)]

        def body(j, c, here=here, base=base, inside=inside):
            return step(j * STEP, base, here, inside, c)

        carry = lax.fori_loop(0, half // STEP - 1, body, carry)
        carry = step(half - STEP, base, here, at_end, carry)
    total, rhs = carry
    partial[:modes, :] = total
    partial[modes:, :] = jnp.zeros((8, 2 * modes), F32)
    partial[modes:, :modes] = lax.dot_general(
        jnp.ones((8, layers), F32), rhs, NT, precision=PRECISE, preferred_element_type=F32
    )


def join_kernel(
    levels, partial, weights, far_low, far_high, below, above, first, last, next_first, prev_last, out
):
    half, modes, layers = far_low.shape

    def body(j, total):
        left, right = [], []
        for u in range(STEP):
            y = j * STEP + u
            image_low = split(weights[0, pl.ds(y, 1), :] * far_low[y].astype(F32))
            image_high = split(weights[1, pl.ds(half + y, 1), :] * far_high[y].astype(F32))
            left.append(jnp.concatenate(image_low, axis=0))
            left.append(jnp.concatenate(image_high, axis=0))
            right.append(below[y])
            right.append(above[y])
        return total + lax.dot_general(
            jnp.concatenate(left, axis=1), jnp.concatenate(right, axis=1), NT,
            preferred_element_type=F32,
        )

    cross = lax.fori_loop(0, half // STEP, body, jnp.zeros((2 * modes, modes), F32))

    def coef_row(pack):
        return coefficients(pack[modes:modes + 16, :].astype(F32)[0:1], levels)

    weight_low = harmonic(coef_row(first), coef_row(prev_last))
    weight_high = harmonic(coef_row(last), coef_row(next_first))
    first_modes = first[:modes, :].astype(F32)
    last_modes = last[:modes, :].astype(F32)

    def product(left, right):
        return lax.dot_general(left, right, NT, precision=PRECISE, preferred_element_type=F32)

    edge_rows = weight_high * last_modes
    ends = product(weight_low * first_modes, first_modes) + product(edge_rows, last_modes)
    summed = partial[:modes, :]
    square = summed[:, :modes] + summed[:, modes:] - cross[:modes] - cross[modes:] + 0.5 * ends
    out[:modes, :modes] = square + square.T
    out[:modes, modes:] = -product(edge_rows, next_first[:modes, :].astype(F32))
    out[modes:, :] = partial[modes:, :]


def finish_kernel(
    place, levels, blocks, zvec, below, below_rest, above, above_rest, next_first, prev_last, weights, resid,
    solution, deflated, direction_ref, image_ref, ahead_ref, spread, outer,
):
    subs = blocks.shape[0]
    modes, planes, rows, layers = zvec.shape
    half = rows // 2

    def each(body):
        if subs <= 8:
            for s in range(subs):
                body(s)
        else:
            pl.loop(0, subs)(body)

    def around(s):
        return (s + 1) % subs if isinstance(s, int) else lax.rem(s + 1, subs)

    def load(s):
        direction_ref[pl.ds(s, 1), :] = blocks[s, modes:modes + 1, :modes]

    each(load)

    def coarse_apply(direction):
        direction_ref[...] = direction

        def one(s):
            image_ref[pl.ds(s, 1), :] = jnp.dot(
                direction_ref[pl.ds(s, 1), :], blocks[s, :modes, :], precision=PRECISE,
                preferred_element_type=F32,
            )
            ahead_ref[pl.ds(s, 1), :] = lax.dot_general(
                direction_ref[pl.ds(around(s), 1), :], blocks[s, :modes, modes:], NT,
                precision=PRECISE, preferred_element_type=F32,
            )

        each(one)
        image = image_ref[...]
        behind = image[:, modes:]
        behind = jnp.concatenate([behind[subs - 1:], behind[:subs - 1]], axis=0)
        return image[:, :modes] + ahead_ref[...] + behind

    def inner(left, right):
        return jnp.sum(jnp.sum(left * right, axis=0, keepdims=True), axis=1, keepdims=True)

    remain = direction_ref[...]
    direction = remain
    result = jnp.zeros_like(remain)
    norm_now = inner(remain, remain)
    for iteration in range(CITERS):
        image = coarse_apply(direction)
        step_size = norm_now / inner(direction, image)
        result = result + step_size * direction
        if iteration + 1 < CITERS:
            remain = remain - step_size * image
            norm_next = inner(remain, remain)
            direction = remain + (norm_next / norm_now) * direction
            norm_now = norm_next
    direction_ref[...] = result
    me = place[0]
    own = direction_ref[pl.ds(me, 1), :]
    solution[...] = own

    square = (modes, modes)
    eye = lax.broadcasted_iota(jnp.int32, square, 0) == lax.broadcasted_iota(jnp.int32, square, 1)

    def column(row):
        return jnp.sum(jnp.where(eye, row, 0.0), axis=1, keepdims=True)

    own_column = jnp.broadcast_to(column(own), (modes, layers))
    spread[...] = own_column
    ahead_column = column(direction_ref[pl.ds(lax.rem(me + 1, subs), 1), :])
    behind_column = column(direction_ref[pl.ds(lax.rem(me + subs - 1, subs), 1), :])
    at_top = lane_is((modes, layers), layers - 1)
    at_bottom = lane_is((modes, layers), 0)

    def placed(pack, values, precision):
        return lax.dot_general(pack, values, TN, precision=precision, preferred_element_type=F32)

    ends = placed(
        next_first[:modes, :].astype(F32), jnp.where(at_top, ahead_column, 0.0), PRECISE
    ) + placed(prev_last[:modes, :].astype(F32), jnp.where(at_bottom, behind_column, 0.0), PRECISE)
    end_labels = placed(next_first[modes:, :], pick_row(layers - 1, layers), None) + placed(
        prev_last[modes:, :], pick_row(0, layers), None
    )
    end_coef = coefficients(end_labels, levels)

    def outer_rows(j, carry):
        for u in range(2):
            y = j * 2 + u
            for side, ref, at in (
                (0, below, y), (0, below_rest, half + y), (1, above_rest, y), (1, above, half + y)
            ):
                outer[side, pl.ds(at, 1), :] = jnp.sum(
                    own_column * ref[y].astype(F32), axis=0, keepdims=True
                )
        return carry

    lax.fori_loop(0, half // 2, outer_rows, 0)

    def add_mode(j, carry):
        fields = list(carry)
        for u in range(STEP):
            k = j * STEP + u
            scale = spread[pl.ds(k, 1), :]
            for x in range(2):
                fields[x] = fields[x] + scale * zvec[k, x].astype(F32)
        return tuple(fields)

    zero = jnp.zeros((rows, layers), F32)
    field = lax.fori_loop(0, modes // STEP, add_mode, (zero, zero))
    row = lax.broadcasted_iota(jnp.int32, (rows, layers), 0)
    lane = lax.broadcasted_iota(jnp.int32, (rows, layers), 1)
    for x in range(2):
        f = field[x]
        c = weights[7 + x]
        end_field = ends[x * rows:(x + 1) * rows]
        end_weight = harmonic(c, end_coef[x * rows:(x + 1) * rows])
        up_y, up_z = weights[3 + x], weights[5 + x]
        down_y = jnp.where(row == 0, c, pltpu.roll(up_y, 1, 0))
        down_z = jnp.where(lane == 0, end_weight, pltpu.roll(up_z, 1, 1))
        up_z = jnp.where(lane == layers - 1, end_weight, up_z)
        above_y = jnp.where(row == rows - 1, 0.0, pltpu.roll(f, rows - 1, 0))
        below_y = jnp.where(row == 0, 0.0, pltpu.roll(f, 1, 0))
        above_z = jnp.where(lane == layers - 1, end_field, pltpu.roll(f, layers - 1, 1))
        below_z = jnp.where(lane == 0, end_field, pltpu.roll(f, 1, 1))
        image = (
            weights[2] * (f - field[1 - x])
            + weights[x] * (f - outer[x])
            + down_y * (f - below_y)
            + up_y * (f - above_y)
            + down_z * (f - below_z)
            + up_z * (f - above_z)
        )
        deflated[x] = resid[x] - image


def shifted(value, axis, by, periodic):
    count = lax.axis_size(axis)
    pairs = [(i, (i + by) % count) for i in range(count) if periodic or 0 <= i + by < count]
    return lax.ppermute(value, axis, pairs)


def exchanged(value, axis, mask):
    return lax.ppermute(value, axis, [(i, i ^ mask) for i in range(lax.axis_size(axis))])


def summed(value, axis):
    count = lax.axis_size(axis)
    if count != 4:
        return lax.psum(value, axis)
    one, two, three = (exchanged(value, axis, mask) for mask in (1, 2, 3))
    return (value + one) + (two + three)


def body(labels, levels, zvec, resid):
    modes, planes, rows, layers = zvec.shape
    half = rows // 2
    subs = lax.axis_size("sub")
    shape = jax.ShapeDtypeStruct
    place = jnp.stack(
        [lax.axis_index("sub"), lax.axis_index("pln"), jnp.int32(lax.axis_size("pln"))]
    ).astype(jnp.int32)
    labels_below = shifted(labels[-1:], "pln", 1, False)
    labels_above = shifted(labels[:1], "pln", -1, False)
    part = shape((half, modes, layers), BF16)
    pack = shape((modes + 16, planes * rows), BF16)
    near_low, near_high, far_low, far_high, first, last = call(
        prepare_kernel, [part] * 4 + [pack] * 2, [VMEM] * 2, flops=10_000_000, moved=4 << 20
    )(labels, zvec)
    below = shifted(near_high, "pln", 1, False)
    above = shifted(near_low, "pln", -1, False)
    next_first = shifted(first, "sub", -1, True)
    prev_last = shifted(last, "sub", 1, True)
    below_rest = shifted(far_high, "pln", 1, False)
    above_rest = shifted(far_low, "pln", -1, False)
    field = (planes, rows, layers)
    partial, weights = call(
        block_kernel,
        [shape((modes + 8, 2 * modes), F32), shape((9, rows, layers), F32)],
        [SMEM, SMEM] + [VMEM] * 8,
        [pltpu.VMEM(field, F32)] * 3,
        flops=400_000_000,
        moved=3 << 20,
    )(place, levels, labels, labels_below, labels_above, resid, near_low, near_high, far_low, far_high)
    block = call(
        join_kernel,
        shape((modes + 8, 2 * modes), F32),
        [SMEM] + [VMEM] * 10,
        flops=100_000_000,
        moved=2 << 20,
    )(levels, partial, weights, far_low, far_high, below, above, first, last, next_first, prev_last)
    block = summed(block, "pln")
    blocks = lax.all_gather(block, "sub")
    return tuple(
        call(
            finish_kernel,
            [shape((1, modes), F32), shape(field, F32)],
            [SMEM, SMEM] + [VMEM] * 10,
            [
                pltpu.VMEM((subs, modes), F32),
                pltpu.VMEM((subs, 2 * modes), F32),
                pltpu.VMEM((subs, modes), F32),
                pltpu.VMEM((modes, layers), F32),
                pltpu.VMEM(field, F32),
            ],
            flops=10_000_000,
            moved=5 << 20,
        )(
            place, levels, blocks, zvec, below, below_rest, above, above_rest, next_first, prev_last,
            weights, resid,
        )
    )


def solution(mesh):
    in_specs = (P("pln", None, "sub"), P(), P(None, "pln", None, "sub"), P("pln", None, "sub"))
    out_specs = (P("sub", None), P("pln", None, "sub"))
    return jax.shard_map(body, mesh=mesh, in_specs=in_specs, out_specs=out_specs, check_vma=False)
```

```python
import jax
import jax.numpy as jnp
from jax import lax
from jax.experimental import pallas as pl
from jax.experimental.pallas import tpu as pltpu
from jax.sharding import PartitionSpec as P

CITERS = 2
STEP = 4
F32 = jnp.float32
BF16 = jnp.bfloat16
PRECISE = lax.Precision.HIGHEST
NT = (((1,), (1,)), ((), ()))
TN = (((0,), (0,)), ((), ()))
VMEM = pl.BlockSpec(memory_space=pltpu.VMEM)
SMEM = pl.BlockSpec(memory_space=pltpu.SMEM)


def call(kernel, outs, specs, scratch=(), flops=0, moved=0, limit=32):
    return pl.pallas_call(
        kernel,
        out_shape=outs,
        in_specs=specs,
        out_specs=jax.tree.map(lambda _: VMEM, outs),
        scratch_shapes=list(scratch),
        cost_estimate=pl.CostEstimate(flops=flops, bytes_accessed=moved, transcendentals=0),
        compiler_params=pltpu.CompilerParams(vmem_limit_bytes=limit << 20),
    )


def harmonic(left_value, right_value):
    return 2.0 * left_value * right_value / (left_value + right_value)


def coefficients(labels, levels_ref):
    weighted = jnp.zeros(labels.shape, F32)
    for level in range(levels_ref.shape[0]):
        weighted = weighted + jnp.where(labels == level, levels_ref[level], 0.0)
    return weighted


def split(value):
    high = value.astype(BF16)
    return high, (value - high.astype(F32)).astype(BF16)


def lane_is(shape, lane):
    return lax.broadcasted_iota(jnp.int32, shape, len(shape) - 1) == lane


def pick_row(lane, width):
    row = lax.broadcasted_iota(jnp.int32, (16, width), 0)
    return ((row == 0) & lane_is((16, width), lane)).astype(BF16)


def prepare_kernel(labels, zvec, near_low, near_high, far_low, far_high, first, last):
    modes, planes, rows, layers = zvec.shape
    half = rows // 2
    for out, plane, start in ((near_high, 1, 0), (near_low, 0, half), (far_high, 1, half), (far_low, 0, 0)):
        for at in range(0, half, 16):
            out[at:at + 16] = jnp.swapaxes(zvec[:, plane, start + at:start + at + 16, :], 0, 1)
    row = lax.broadcasted_iota(jnp.int32, (16, layers), 0)
    both = ((row == 0) & lane_is((16, layers), 0)) | ((row == 1) & lane_is((16, layers), layers - 1))
    ends = lax.dot_general(
        both.astype(BF16), zvec[...].reshape(-1, layers), NT, preferred_element_type=F32
    )
    width = planes * rows
    first[:modes] = jnp.concatenate(
        [ends[0:1, k * width:(k + 1) * width] for k in range(modes)], axis=0
    ).astype(BF16)
    last[:modes] = jnp.concatenate(
        [ends[1:2, k * width:(k + 1) * width] for k in range(modes)], axis=0
    ).astype(BF16)
    flat = labels[...].astype(F32).astype(BF16).reshape(width, layers)
    for out, lane in ((first, 0), (last, layers - 1)):
        out[modes:] = lax.dot_general(
            pick_row(lane, layers), flat, NT, preferred_element_type=F32
        ).astype(BF16)


def block_kernel(
    place, levels, labels, labels_below, labels_above, resid, near_low, near_high, far_low, far_high,
    partial, weights, half_diag, link_y, link_z,
):
    planes, rows, layers = labels.shape
    modes = near_low.shape[1]
    half = rows // 2
    at_first, at_last = place[1] == 0, place[1] == place[2] - 1
    coef = [coefficients(labels[x], levels) for x in range(2)]
    below = jnp.where(at_first, coef[0], coefficients(labels_below[0], levels))
    above = jnp.where(at_last, coef[1], coefficients(labels_above[0], levels))
    low_x = harmonic(coef[0], below)
    high_x = harmonic(coef[1], above)
    mid_x = harmonic(coef[0], coef[1])
    weights[0] = low_x
    weights[1] = high_x
    weights[2] = mid_x
    row = lax.broadcasted_iota(jnp.int32, (rows, layers), 0)
    lane = lax.broadcasted_iota(jnp.int32, (rows, layers), 1)
    for x in range(2):
        c = coef[x]
        up_y = harmonic(c, jnp.where(row == rows - 1, c, pltpu.roll(c, rows - 1, 0)))
        up_z = harmonic(c, pltpu.roll(c, layers - 1, 1))
        down_y = jnp.where(row == 0, c, pltpu.roll(up_y, 1, 0))
        weights[3 + x] = up_y
        weights[5 + x] = up_z
        weights[7 + x] = c
        inner_z = jnp.where(lane == layers - 1, 0.0, up_z)
        total = (low_x, high_x)[x] + mid_x + up_y + down_y + inner_z + pltpu.roll(inner_z, 1, 1)
        half_diag[x] = 0.5 * total
        link_y[x] = jnp.where(row == rows - 1, 0.0, up_y)
        link_z[x] = inner_z

    def step(start, base, here, ahead, carry):
        total, rhs = carry
        left, high, low = [], [], []
        for u in range(STEP):
            y = base + start + u
            at = pl.ds(y, 1)
            node = [here[x][start + u] for x in range(2)]
            wide = [v.astype(F32) for v in node]
            up = [v.astype(F32) for v in ahead(start, u)]
            for x in range(2):
                image = (
                    half_diag[x, at, :] * wide[x]
                    - link_y[x, at, :] * up[x]
                    - link_z[x, at, :] * pltpu.roll(wide[x], layers - 1, 1)
                )
                if x == 0:
                    image = image - weights[2, at, :] * wide[1]
                rhs = rhs + resid[x, at, :] * wide[x]
                parts = split(image)
                left.append(node[x])
                high.append(parts[0])
                low.append(parts[1])
        right = jnp.concatenate([jnp.concatenate(high, axis=1), jnp.concatenate(low, axis=1)], axis=0)
        total = total + lax.dot_general(
            jnp.concatenate(left, axis=1), right, NT, preferred_element_type=F32
        )
        return total, rhs

    carry = (jnp.zeros((modes, 2 * modes), F32), jnp.zeros((modes, layers), F32))
    low_half, high_half = (far_low, near_high), (near_low, far_high)
    for here, then, base in ((low_half, high_half, 0), (high_half, None, half)):
        def inside(start, u, here=here):
            return [here[x][start + u + 1] for x in range(2)]

        def at_end(start, u, here=here, then=then):
            if u + 1 < STEP:
                return inside(start, u, here)
            return [here[x][start + u] if then is None else then[x][0] for x in range(2)]

        def body(j, c, here=here, base=base, inside=inside):
            return step(j * STEP, base, here, inside, c)

        carry = lax.fori_loop(0, half // STEP - 1, body, carry)
        carry = step(half - STEP, base, here, at_end, carry)
    total, rhs = carry
    partial[:modes, :] = total
    partial[modes:, :] = jnp.zeros((8, 2 * modes), F32)
    partial[modes:, :modes] = lax.dot_general(
        jnp.ones((8, layers), F32), rhs, NT, precision=PRECISE, preferred_element_type=F32
    )


def join_kernel(
    levels, partial, weights, far_low, far_high, below, above, first, last, next_first, prev_last, out
):
    half, modes, layers = far_low.shape

    def body(j, total):
        left, right = [], []
        for u in range(STEP):
            y = j * STEP + u
            image_low = split(weights[0, pl.ds(y, 1), :] * far_low[y].astype(F32))
            image_high = split(weights[1, pl.ds(half + y, 1), :] * far_high[y].astype(F32))
            left.append(jnp.concatenate(image_low, axis=0))
            left.append(jnp.concatenate(image_high, axis=0))
            right.append(below[y])
            right.append(above[y])
        return total + lax.dot_general(
            jnp.concatenate(left, axis=1), jnp.concatenate(right, axis=1), NT,
            preferred_element_type=F32,
        )

    cross = lax.fori_loop(0, half // STEP, body, jnp.zeros((2 * modes, modes), F32))

    def coef_row(pack):
        return coefficients(pack[modes:modes + 16, :].astype(F32)[0:1], levels)

    weight_low = harmonic(coef_row(first), coef_row(prev_last))
    weight_high = harmonic(coef_row(last), coef_row(next_first))
    first_modes = first[:modes, :].astype(F32)
    last_modes = last[:modes, :].astype(F32)

    def product(left, right):
        return lax.dot_general(left, right, NT, precision=PRECISE, preferred_element_type=F32)

    edge_rows = weight_high * last_modes
    ends = product(weight_low * first_modes, first_modes) + product(edge_rows, last_modes)
    summed = partial[:modes, :]
    square = summed[:, :modes] + summed[:, modes:] - cross[:modes] - cross[modes:] + 0.5 * ends
    out[:modes, :modes] = square + square.T
    out[:modes, modes:] = -product(edge_rows, next_first[:modes, :].astype(F32))
    out[modes:, :] = partial[modes:, :]


def finish_kernel(place, levels, *refs):
    count = len(refs) - 16
    blocks, refs = refs[:count], refs[count:]
    zvec, below, below_rest, above, above_rest, next_first, prev_last, weights, resid = refs[:9]
    solution, deflated, direction_ref, image_ref, ahead_ref, spread, outer = refs[9:]
    subs = direction_ref.shape[0]
    modes, planes, rows, layers = zvec.shape
    half = rows // 2
    me = place[0]
    square = (modes, modes)
    eye = lax.broadcasted_iota(jnp.int32, square, 0) == lax.broadcasted_iota(jnp.int32, square, 1)

    def column(row):
        return jnp.sum(jnp.where(eye, row, 0.0), axis=1, keepdims=True)

    def each(body):
        if count > 1:
            for mask in range(count):
                body(blocks[mask], jnp.bitwise_xor(me, mask))
        else:
            pl.loop(0, subs)(lambda s: body(blocks[0].at[s], s))

    def load(block, s):
        direction_ref[pl.ds(s, 1), :] = block[modes:modes + 1, :]

    each(load)

    def turned(rows_of, by):
        by = by % subs
        return jnp.concatenate([rows_of[by:], rows_of[:by]], axis=0)

    def coarse_apply(direction):
        direction_ref[...] = jnp.concatenate([direction, turned(direction, 1)], axis=1)

        def one(block, s):
            values = block[:modes, :]
            pair = direction_ref[pl.ds(s, 1), :]
            ahead = jnp.sum(values * pair, axis=1, keepdims=True)
            ahead_ref[...] = jnp.where(lane_is((modes, 128), s), ahead, ahead_ref[...])
            image_ref[pl.ds(s, 1), :] = jnp.sum(
                values * column(pair[:, :modes]), axis=0, keepdims=True
            )

        each(one)
        return ahead_ref[...].T[:subs] + turned(image_ref[:, modes:], -1)

    def inner(left, right):
        return jnp.sum(jnp.sum(left * right, axis=0, keepdims=True), axis=1, keepdims=True)

    remain = direction_ref[:, :modes]
    direction = remain
    result = jnp.zeros_like(remain)
    norm_now = inner(remain, remain)
    for iteration in range(CITERS):
        image = coarse_apply(direction)
        step_size = norm_now / inner(direction, image)
        result = result + step_size * direction
        if iteration + 1 < CITERS:
            remain = remain - step_size * image
            norm_next = inner(remain, remain)
            direction = remain + (norm_next / norm_now) * direction
            norm_now = norm_next
    direction_ref[:, :modes] = result
    own = direction_ref[pl.ds(me, 1), :modes]
    solution[...] = own
    own_column = jnp.broadcast_to(column(own), (modes, layers))
    spread[...] = own_column
    ahead_column = column(direction_ref[pl.ds(lax.rem(me + 1, subs), 1), :modes])
    behind_column = column(direction_ref[pl.ds(lax.rem(me + subs - 1, subs), 1), :modes])
    at_top = lane_is((modes, layers), layers - 1)
    at_bottom = lane_is((modes, layers), 0)

    def placed(pack, values, precision):
        return lax.dot_general(pack, values, TN, precision=precision, preferred_element_type=F32)

    ends = placed(
        next_first[:modes, :].astype(F32), jnp.where(at_top, ahead_column, 0.0), PRECISE
    ) + placed(prev_last[:modes, :].astype(F32), jnp.where(at_bottom, behind_column, 0.0), PRECISE)
    end_labels = placed(next_first[modes:, :], pick_row(layers - 1, layers), None) + placed(
        prev_last[modes:, :], pick_row(0, layers), None
    )
    end_coef = coefficients(end_labels, levels)

    def outer_rows(j, carry):
        for u in range(2):
            y = j * 2 + u
            for side, ref, at in (
                (0, below, y), (0, below_rest, half + y), (1, above_rest, y), (1, above, half + y)
            ):
                outer[side, pl.ds(at, 1), :] = jnp.sum(
                    own_column * ref[y].astype(F32), axis=0, keepdims=True
                )
        return carry

    lax.fori_loop(0, half // 2, outer_rows, 0)

    def add_mode(j, carry):
        fields = list(carry)
        for u in range(STEP):
            k = j * STEP + u
            scale = spread[pl.ds(k, 1), :]
            for x in range(2):
                fields[x] = fields[x] + scale * zvec[k, x].astype(F32)
        return tuple(fields)

    zero = jnp.zeros((rows, layers), F32)
    field = lax.fori_loop(0, modes // STEP, add_mode, (zero, zero))
    row = lax.broadcasted_iota(jnp.int32, (rows, layers), 0)
    lane = lax.broadcasted_iota(jnp.int32, (rows, layers), 1)
    for x in range(2):
        f = field[x]
        c = weights[7 + x]
        end_field = ends[x * rows:(x + 1) * rows]
        end_weight = harmonic(c, end_coef[x * rows:(x + 1) * rows])
        up_y, up_z = weights[3 + x], weights[5 + x]
        down_y = jnp.where(row == 0, c, pltpu.roll(up_y, 1, 0))
        down_z = jnp.where(lane == 0, end_weight, pltpu.roll(up_z, 1, 1))
        up_z = jnp.where(lane == layers - 1, end_weight, up_z)
        above_y = jnp.where(row == rows - 1, 0.0, pltpu.roll(f, rows - 1, 0))
        below_y = jnp.where(row == 0, 0.0, pltpu.roll(f, 1, 0))
        above_z = jnp.where(lane == layers - 1, end_field, pltpu.roll(f, layers - 1, 1))
        below_z = jnp.where(lane == 0, end_field, pltpu.roll(f, 1, 1))
        image = (
            weights[2] * (f - field[1 - x])
            + weights[x] * (f - outer[x])
            + down_y * (f - below_y)
            + up_y * (f - above_y)
            + down_z * (f - below_z)
            + up_z * (f - above_z)
        )
        deflated[x] = resid[x] - image


def shifted(value, axis, by, periodic):
    count = lax.axis_size(axis)
    pairs = [(i, (i + by) % count) for i in range(count) if periodic or 0 <= i + by < count]
    return lax.ppermute(value, axis, pairs)


def exchanged(value, axis, mask):
    return lax.ppermute(value, axis, [(i, i ^ mask) for i in range(lax.axis_size(axis))])


def summed(value, axis):
    count = lax.axis_size(axis)
    if count != 4:
        return lax.psum(value, axis)
    one, two, three = (exchanged(value, axis, mask) for mask in (1, 2, 3))
    return (value + one) + (two + three)


def gathered(value, axis):
    count = lax.axis_size(axis)
    if count != 8:
        return [lax.all_gather(value, axis)]
    return [value] + [exchanged(value, axis, mask) for mask in range(1, count)]


def body(labels, levels, zvec, resid):
    modes, planes, rows, layers = zvec.shape
    half = rows // 2
    subs = lax.axis_size("sub")
    shape = jax.ShapeDtypeStruct
    place = jnp.stack(
        [lax.axis_index("sub"), lax.axis_index("pln"), jnp.int32(lax.axis_size("pln"))]
    ).astype(jnp.int32)
    labels_below = shifted(labels[-1:], "pln", 1, False)
    labels_above = shifted(labels[:1], "pln", -1, False)
    part = shape((half, modes, layers), BF16)
    pack = shape((modes + 16, planes * rows), BF16)
    near_low, near_high, far_low, far_high, first, last = call(
        prepare_kernel, [part] * 4 + [pack] * 2, [VMEM] * 2, flops=10_000_000, moved=4 << 20
    )(labels, zvec)
    below = shifted(near_high, "pln", 1, False)
    above = shifted(near_low, "pln", -1, False)
    next_first = shifted(first, "sub", -1, True)
    prev_last = shifted(last, "sub", 1, True)
    below_rest = shifted(far_high, "pln", 1, False)
    above_rest = shifted(far_low, "pln", -1, False)
    field = (planes, rows, layers)
    partial, weights = call(
        block_kernel,
        [shape((modes + 8, 2 * modes), F32), shape((9, rows, layers), F32)],
        [SMEM, SMEM] + [VMEM] * 8,
        [pltpu.VMEM(field, F32)] * 3,
        flops=400_000_000,
        moved=3 << 20,
    )(place, levels, labels, labels_below, labels_above, resid, near_low, near_high, far_low, far_high)
    block = call(
        join_kernel,
        shape((modes + 8, 2 * modes), F32),
        [SMEM] + [VMEM] * 10,
        flops=100_000_000,
        moved=2 << 20,
    )(levels, partial, weights, far_low, far_high, below, above, first, last, next_first, prev_last)
    block = summed(block, "pln")
    blocks = gathered(block, "sub")
    return tuple(
        call(
            finish_kernel,
            [shape((1, modes), F32), shape(field, F32)],
            [SMEM, SMEM] + [VMEM] * (9 + len(blocks)),
            [
                pltpu.VMEM((subs, 2 * modes), F32),
                pltpu.VMEM((subs, 2 * modes), F32),
                pltpu.VMEM((modes, 128), F32),
                pltpu.VMEM((modes, layers), F32),
                pltpu.VMEM(field, F32),
            ],
            flops=10_000_000,
            moved=5 << 20,
        )(
            place, levels, *blocks, zvec, below, below_rest, above, above_rest, next_first, prev_last,
            weights, resid,
        )
    )


def solution(mesh):
    in_specs = (P("pln", None, "sub"), P(), P(None, "pln", None, "sub"), P("pln", None, "sub"))
    out_specs = (P("sub", None), P("pln", None, "sub"))
    return jax.shard_map(body, mesh=mesh, in_specs=in_specs, out_specs=out_specs, check_vma=False)
```

```python
import jax
import jax.numpy as jnp
from jax import lax
from jax.experimental import pallas as pl
from jax.experimental.pallas import tpu as pltpu
from jax.sharding import PartitionSpec as P

CITERS = 2
STEP = 4
F32 = jnp.float32
BF16 = jnp.bfloat16
PRECISE = lax.Precision.HIGHEST
NT = (((1,), (1,)), ((), ()))
TN = (((0,), (0,)), ((), ()))
VMEM = pl.BlockSpec(memory_space=pltpu.VMEM)
SMEM = pl.BlockSpec(memory_space=pltpu.SMEM)


def call(kernel, outs, specs, scratch=(), flops=0, moved=0, limit=32):
    return pl.pallas_call(
        kernel,
        out_shape=outs,
        in_specs=specs,
        out_specs=jax.tree.map(lambda _: VMEM, outs),
        scratch_shapes=list(scratch),
        cost_estimate=pl.CostEstimate(flops=flops, bytes_accessed=moved, transcendentals=0),
        compiler_params=pltpu.CompilerParams(vmem_limit_bytes=limit << 20),
    )


def harmonic(left_value, right_value):
    return 2.0 * left_value * right_value / (left_value + right_value)


def coefficients(labels, levels_ref):
    weighted = jnp.zeros(labels.shape, F32)
    for level in range(levels_ref.shape[0]):
        weighted = weighted + jnp.where(labels == level, levels_ref[level], 0.0)
    return weighted


def split(value):
    high = value.astype(BF16)
    return high, (value - high.astype(F32)).astype(BF16)


def lane_is(shape, lane):
    return lax.broadcasted_iota(jnp.int32, shape, len(shape) - 1) == lane


def pick_row(lane, width):
    row = lax.broadcasted_iota(jnp.int32, (16, width), 0)
    return ((row == 0) & lane_is((16, width), lane)).astype(BF16)


def prepare_kernel(labels, zvec, near_low, near_high, far_low, far_high, first, last):
    modes, planes, rows, layers = zvec.shape
    half = rows // 2
    for out, plane, start in ((near_high, 1, 0), (near_low, 0, half), (far_high, 1, half), (far_low, 0, 0)):
        for at in range(0, half, 16):
            out[at:at + 16] = jnp.swapaxes(zvec[:, plane, start + at:start + at + 16, :], 0, 1)
    row = lax.broadcasted_iota(jnp.int32, (16, layers), 0)
    both = ((row == 0) & lane_is((16, layers), 0)) | ((row == 1) & lane_is((16, layers), layers - 1))
    ends = lax.dot_general(
        both.astype(BF16), zvec[...].reshape(-1, layers), NT, preferred_element_type=F32
    )
    width = planes * rows
    first[:modes] = jnp.concatenate(
        [ends[0:1, k * width:(k + 1) * width] for k in range(modes)], axis=0
    ).astype(BF16)
    last[:modes] = jnp.concatenate(
        [ends[1:2, k * width:(k + 1) * width] for k in range(modes)], axis=0
    ).astype(BF16)
    flat = labels[...].astype(F32).astype(BF16).reshape(width, layers)
    for out, lane in ((first, 0), (last, layers - 1)):
        out[modes:] = lax.dot_general(
            pick_row(lane, layers), flat, NT, preferred_element_type=F32
        ).astype(BF16)


def block_kernel(
    place, levels, labels, labels_below, labels_above, resid, near_low, near_high, far_low, far_high,
    partial, weights, half_diag, link_y, link_z,
):
    planes, rows, layers = labels.shape
    modes = near_low.shape[1]
    half = rows // 2
    at_first, at_last = place[1] == 0, place[1] == place[2] - 1
    coef = [coefficients(labels[x], levels) for x in range(2)]
    below = jnp.where(at_first, coef[0], coefficients(labels_below[0], levels))
    above = jnp.where(at_last, coef[1], coefficients(labels_above[0], levels))
    low_x = harmonic(coef[0], below)
    high_x = harmonic(coef[1], above)
    mid_x = harmonic(coef[0], coef[1])
    weights[0] = low_x
    weights[1] = high_x
    weights[2] = mid_x
    row = lax.broadcasted_iota(jnp.int32, (rows, layers), 0)
    lane = lax.broadcasted_iota(jnp.int32, (rows, layers), 1)
    for x in range(2):
        c = coef[x]
        up_y = harmonic(c, jnp.where(row == rows - 1, c, pltpu.roll(c, rows - 1, 0)))
        up_z = harmonic(c, pltpu.roll(c, layers - 1, 1))
        down_y = jnp.where(row == 0, c, pltpu.roll(up_y, 1, 0))
        weights[3 + x] = up_y
        weights[5 + x] = up_z
        weights[7 + x] = c
        inner_z = jnp.where(lane == layers - 1, 0.0, up_z)
        total = (low_x, high_x)[x] + mid_x + up_y + down_y + inner_z + pltpu.roll(inner_z, 1, 1)
        half_diag[x] = 0.5 * total
        link_y[x] = jnp.where(row == rows - 1, 0.0, up_y)
        link_z[x] = inner_z

    def step(start, base, here, ahead, carry):
        total, rhs = carry
        left, high, low = [], [], []
        for u in range(STEP):
            y = base + start + u
            at = pl.ds(y, 1)
            node = [here[x][start + u] for x in range(2)]
            wide = [v.astype(F32) for v in node]
            up = [v.astype(F32) for v in ahead(start, u)]
            for x in range(2):
                image = (
                    half_diag[x, at, :] * wide[x]
                    - link_y[x, at, :] * up[x]
                    - link_z[x, at, :] * pltpu.roll(wide[x], layers - 1, 1)
                )
                if x == 0:
                    image = image - weights[2, at, :] * wide[1]
                rhs = rhs + resid[x, at, :] * wide[x]
                parts = split(image)
                left.append(node[x])
                high.append(parts[0])
                low.append(parts[1])
        right = jnp.concatenate([jnp.concatenate(high, axis=1), jnp.concatenate(low, axis=1)], axis=0)
        total = total + lax.dot_general(
            jnp.concatenate(left, axis=1), right, NT, preferred_element_type=F32
        )
        return total, rhs

    carry = (jnp.zeros((modes, 2 * modes), F32), jnp.zeros((modes, layers), F32))
    low_half, high_half = (far_low, near_high), (near_low, far_high)
    for here, then, base in ((low_half, high_half, 0), (high_half, None, half)):
        def inside(start, u, here=here):
            return [here[x][start + u + 1] for x in range(2)]

        def at_end(start, u, here=here, then=then):
            if u + 1 < STEP:
                return inside(start, u, here)
            return [here[x][start + u] if then is None else then[x][0] for x in range(2)]

        def body(j, c, here=here, base=base, inside=inside):
            return step(j * STEP, base, here, inside, c)

        carry = lax.fori_loop(0, half // STEP - 1, body, carry)
        carry = step(half - STEP, base, here, at_end, carry)
    total, rhs = carry
    partial[:modes, :] = total
    partial[modes:, :] = jnp.zeros((8, 2 * modes), F32)
    partial[modes:, :modes] = lax.dot_general(
        jnp.ones((8, layers), F32), rhs, NT, precision=PRECISE, preferred_element_type=F32
    )


def join_kernel(
    levels, partial, weights, far_low, far_high, below, above, first, last, next_first, prev_last, out
):
    half, modes, layers = far_low.shape

    def body(j, total):
        left, right = [], []
        for u in range(STEP):
            y = j * STEP + u
            image_low = split(weights[0, pl.ds(y, 1), :] * far_low[y].astype(F32))
            image_high = split(weights[1, pl.ds(half + y, 1), :] * far_high[y].astype(F32))
            left.append(jnp.concatenate(image_low, axis=0))
            left.append(jnp.concatenate(image_high, axis=0))
            right.append(below[y])
            right.append(above[y])
        return total + lax.dot_general(
            jnp.concatenate(left, axis=1), jnp.concatenate(right, axis=1), NT,
            preferred_element_type=F32,
        )

    cross = lax.fori_loop(0, half // STEP, body, jnp.zeros((2 * modes, modes), F32))

    def coef_row(pack):
        return coefficients(pack[modes:modes + 16, :].astype(F32)[0:1], levels)

    weight_low = harmonic(coef_row(first), coef_row(prev_last))
    weight_high = harmonic(coef_row(last), coef_row(next_first))
    first_modes = first[:modes, :].astype(F32)
    last_modes = last[:modes, :].astype(F32)

    def product(left, right):
        return lax.dot_general(left, right, NT, precision=PRECISE, preferred_element_type=F32)

    edge_rows = weight_high * last_modes
    ends = product(weight_low * first_modes, first_modes) + product(edge_rows, last_modes)
    summed = partial[:modes, :]
    square = summed[:, :modes] + summed[:, modes:] - cross[:modes] - cross[modes:] + 0.5 * ends
    out[:modes, :modes] = square + square.T
    out[:modes, modes:] = -product(edge_rows, next_first[:modes, :].astype(F32))
    out[modes:, :] = partial[modes:, :]


def finish_kernel(
    place, levels, blocks, zvec, below, below_rest, above, above_rest, next_first, prev_last, weights, resid,
    solution, deflated, direction_ref, image_ref, ahead_ref, spread, outer,
):
    subs = direction_ref.shape[0]
    modes, planes, rows, layers = zvec.shape
    half = rows // 2
    me = place[0]
    square = (modes, modes)
    eye = lax.broadcasted_iota(jnp.int32, square, 0) == lax.broadcasted_iota(jnp.int32, square, 1)

    def column(row):
        return jnp.sum(jnp.where(eye, row, 0.0), axis=1, keepdims=True)

    def each(body):
        if subs <= 8:
            for s in range(subs):
                body(blocks.at[s], s)
        else:
            pl.loop(0, subs)(lambda s: body(blocks.at[s], s))

    def load(block, s):
        direction_ref[pl.ds(s, 1), :] = block[modes:modes + 1, :]

    each(load)

    def turned(rows_of, by):
        by = by % subs
        return jnp.concatenate([rows_of[by:], rows_of[:by]], axis=0)

    def coarse_apply(direction):
        direction_ref[...] = jnp.concatenate([direction, turned(direction, 1)], axis=1)

        def one(block, s):
            values = block[:modes, :]
            pair = direction_ref[pl.ds(s, 1), :]
            ahead = jnp.sum(values * pair, axis=1, keepdims=True)
            ahead_ref[...] = jnp.where(lane_is((modes, 128), s), ahead, ahead_ref[...])
            image_ref[pl.ds(s, 1), :] = jnp.sum(
                values * column(pair[:, :modes]), axis=0, keepdims=True
            )

        each(one)
        return ahead_ref[...].T[:subs] + turned(image_ref[:, modes:], -1)

    def inner(left, right):
        return jnp.sum(jnp.sum(left * right, axis=0, keepdims=True), axis=1, keepdims=True)

    remain = direction_ref[:, :modes]
    direction = remain
    result = jnp.zeros_like(remain)
    norm_now = inner(remain, remain)
    for iteration in range(CITERS):
        image = coarse_apply(direction)
        step_size = norm_now / inner(direction, image)
        result = result + step_size * direction
        if iteration + 1 < CITERS:
            remain = remain - step_size * image
            norm_next = inner(remain, remain)
            direction = remain + (norm_next / norm_now) * direction
            norm_now = norm_next
    direction_ref[:, :modes] = result
    own = direction_ref[pl.ds(me, 1), :modes]
    solution[...] = own
    own_column = jnp.broadcast_to(column(own), (modes, layers))
    spread[...] = own_column
    ahead_column = column(direction_ref[pl.ds(lax.rem(me + 1, subs), 1), :modes])
    behind_column = column(direction_ref[pl.ds(lax.rem(me + subs - 1, subs), 1), :modes])
    at_top = lane_is((modes, layers), layers - 1)
    at_bottom = lane_is((modes, layers), 0)

    def placed(pack, values, precision):
        return lax.dot_general(pack, values, TN, precision=precision, preferred_element_type=F32)

    ends = placed(
        next_first[:modes, :].astype(F32), jnp.where(at_top, ahead_column, 0.0), PRECISE
    ) + placed(prev_last[:modes, :].astype(F32), jnp.where(at_bottom, behind_column, 0.0), PRECISE)
    end_labels = placed(next_first[modes:, :], pick_row(layers - 1, layers), None) + placed(
        prev_last[modes:, :], pick_row(0, layers), None
    )
    end_coef = coefficients(end_labels, levels)

    def outer_rows(j, carry):
        for u in range(2):
            y = j * 2 + u
            for side, ref, at in (
                (0, below, y), (0, below_rest, half + y), (1, above_rest, y), (1, above, half + y)
            ):
                outer[side, pl.ds(at, 1), :] = jnp.sum(
                    own_column * ref[y].astype(F32), axis=0, keepdims=True
                )
        return carry

    lax.fori_loop(0, half // 2, outer_rows, 0)

    def add_mode(j, carry):
        fields = list(carry)
        for u in range(STEP):
            k = j * STEP + u
            scale = spread[pl.ds(k, 1), :]
            for x in range(2):
                fields[x] = fields[x] + scale * zvec[k, x].astype(F32)
        return tuple(fields)

    zero = jnp.zeros((rows, layers), F32)
    field = lax.fori_loop(0, modes // STEP, add_mode, (zero, zero))
    row = lax.broadcasted_iota(jnp.int32, (rows, layers), 0)
    lane = lax.broadcasted_iota(jnp.int32, (rows, layers), 1)
    for x in range(2):
        f = field[x]
        c = weights[7 + x]
        end_field = ends[x * rows:(x + 1) * rows]
        end_weight = harmonic(c, end_coef[x * rows:(x + 1) * rows])
        up_y, up_z = weights[3 + x], weights[5 + x]
        down_y = jnp.where(row == 0, c, pltpu.roll(up_y, 1, 0))
        down_z = jnp.where(lane == 0, end_weight, pltpu.roll(up_z, 1, 1))
        up_z = jnp.where(lane == layers - 1, end_weight, up_z)
        above_y = jnp.where(row == rows - 1, 0.0, pltpu.roll(f, rows - 1, 0))
        below_y = jnp.where(row == 0, 0.0, pltpu.roll(f, 1, 0))
        above_z = jnp.where(lane == layers - 1, end_field, pltpu.roll(f, layers - 1, 1))
        below_z = jnp.where(lane == 0, end_field, pltpu.roll(f, 1, 1))
        image = (
            weights[2] * (f - field[1 - x])
            + weights[x] * (f - outer[x])
            + down_y * (f - below_y)
            + up_y * (f - above_y)
            + down_z * (f - below_z)
            + up_z * (f - above_z)
        )
        deflated[x] = resid[x] - image


def shifted(value, axis, by, periodic):
    count = lax.axis_size(axis)
    pairs = [(i, (i + by) % count) for i in range(count) if periodic or 0 <= i + by < count]
    return lax.ppermute(value, axis, pairs)


def summed(value, axis):
    parts = gathered(value, axis)
    total = parts[0]
    for index in range(1, parts.shape[0]):
        total = total + parts[index]
    return total


def gathered(value, axis):
    copies = jnp.broadcast_to(value, (lax.axis_size(axis),) + value.shape)
    return lax.all_to_all(copies, axis, 0, 0)


def body(labels, levels, zvec, resid):
    modes, planes, rows, layers = zvec.shape
    half = rows // 2
    subs = lax.axis_size("sub")
    shape = jax.ShapeDtypeStruct
    place = jnp.stack(
        [lax.axis_index("sub"), lax.axis_index("pln"), jnp.int32(lax.axis_size("pln"))]
    ).astype(jnp.int32)
    labels_below = shifted(labels[-1:], "pln", 1, False)
    labels_above = shifted(labels[:1], "pln", -1, False)
    part = shape((half, modes, layers), BF16)
    pack = shape((modes + 16, planes * rows), BF16)
    near_low, near_high, far_low, far_high, first, last = call(
        prepare_kernel, [part] * 4 + [pack] * 2, [VMEM] * 2, flops=10_000_000, moved=4 << 20
    )(labels, zvec)
    below = shifted(near_high, "pln", 1, False)
    above = shifted(near_low, "pln", -1, False)
    next_first = shifted(first, "sub", -1, True)
    prev_last = shifted(last, "sub", 1, True)
    below_rest = shifted(far_high, "pln", 1, False)
    above_rest = shifted(far_low, "pln", -1, False)
    field = (planes, rows, layers)
    partial, weights = call(
        block_kernel,
        [shape((modes + 8, 2 * modes), F32), shape((9, rows, layers), F32)],
        [SMEM, SMEM] + [VMEM] * 8,
        [pltpu.VMEM(field, F32)] * 3,
        flops=400_000_000,
        moved=3 << 20,
    )(place, levels, labels, labels_below, labels_above, resid, near_low, near_high, far_low, far_high)
    block = call(
        join_kernel,
        shape((modes + 8, 2 * modes), F32),
        [SMEM] + [VMEM] * 10,
        flops=100_000_000,
        moved=2 << 20,
    )(levels, partial, weights, far_low, far_high, below, above, first, last, next_first, prev_last)
    block = summed(block, "pln")
    blocks = gathered(block, "sub")
    return tuple(
        call(
            finish_kernel,
            [shape((1, modes), F32), shape(field, F32)],
            [SMEM, SMEM] + [VMEM] * 10,
            [
                pltpu.VMEM((subs, 2 * modes), F32),
                pltpu.VMEM((subs, 2 * modes), F32),
                pltpu.VMEM((modes, 128), F32),
                pltpu.VMEM((modes, layers), F32),
                pltpu.VMEM(field, F32),
            ],
            flops=10_000_000,
            moved=5 << 20,
        )(
            place, levels, blocks, zvec, below, below_rest, above, above_rest, next_first, prev_last,
            weights, resid,
        )
    )


def solution(mesh):
    in_specs = (P("pln", None, "sub"), P(), P(None, "pln", None, "sub"), P("pln", None, "sub"))
    out_specs = (P("sub", None), P("pln", None, "sub"))
    return jax.shard_map(body, mesh=mesh, in_specs=in_specs, out_specs=out_specs, check_vma=False)
```

```python
import jax
import jax.numpy as jnp
from jax import lax
from jax.experimental import pallas as pl
from jax.experimental.pallas import tpu as pltpu
from jax.sharding import PartitionSpec as P

CITERS = 2
STEP = 2
CHUNK = 16
F32 = jnp.float32
BF16 = jnp.bfloat16
PRECISE = lax.Precision.HIGHEST
NT = (((1,), (1,)), ((), ()))
TN = (((0,), (0,)), ((), ()))
VMEM = pl.BlockSpec(memory_space=pltpu.VMEM)
SMEM = pl.BlockSpec(memory_space=pltpu.SMEM)
HBM = pl.BlockSpec(memory_space=pltpu.HBM)


def call(kernel, outs, specs, scratch=(), flops=0, moved=0, limit=32):
    return pl.pallas_call(
        kernel,
        out_shape=outs,
        in_specs=specs,
        out_specs=jax.tree.map(lambda _: VMEM, outs),
        scratch_shapes=list(scratch),
        cost_estimate=pl.CostEstimate(flops=flops, bytes_accessed=moved, transcendentals=0),
        compiler_params=pltpu.CompilerParams(vmem_limit_bytes=limit << 20),
    )


def harmonic(left_value, right_value):
    return 2.0 * left_value * right_value / (left_value + right_value)


def coefficients(labels, levels_ref):
    weighted = jnp.zeros(labels.shape, F32)
    for level in range(levels_ref.shape[0]):
        weighted = weighted + jnp.where(labels == level, levels_ref[level], 0.0)
    return weighted


def split(value):
    high = value.astype(BF16)
    return high, (value - high.astype(F32)).astype(BF16)


def lane_is(shape, lane):
    return lax.broadcasted_iota(jnp.int32, shape, len(shape) - 1) == lane


def pick_row(lane, width):
    row = lax.broadcasted_iota(jnp.int32, (16, width), 0)
    return ((row == 0) & lane_is((16, width), lane)).astype(BF16)


def prepare_kernel(
    place, labels, zvec, inner_send, outer_send, outer_rest, outer, one_pack, two_pack, held, sems
):
    modes, planes, rows, layers = zvec.shape
    half = rows // 2
    width = planes * rows
    side = lax.rem(place[1], 2)
    odd = lax.rem(place[0], 2) == 1
    copies = [
        pltpu.make_async_copy(zvec.at[pl.ds(k, CHUNK)], held.at[pl.ds(k, CHUNK)], sems.at[k // CHUNK])
        for k in range(0, modes, CHUNK)
    ]
    for copy in copies:
        copy.start()
    one_lane = jnp.where(odd, 0, layers - 1)
    two_lane = jnp.where(odd, layers - 1, 0)
    row = lax.broadcasted_iota(jnp.int32, (16, layers), 0)
    both = ((row == 0) & lane_is((16, layers), one_lane)) | ((row == 1) & lane_is((16, layers), two_lane))
    both = both.astype(BF16)
    flat = labels[...].astype(F32).astype(BF16).reshape(width, layers)
    for out, lane in ((one_pack, one_lane), (two_pack, two_lane)):
        out[modes:] = lax.dot_general(
            pick_row(lane, layers), flat, NT, preferred_element_type=F32
        ).astype(BF16)
    inner_send[rows, :rows] = labels[1 - side].astype(F32).astype(BF16)
    outer_send[half, :rows] = labels[side].astype(F32).astype(BF16)
    for k, copy in zip(range(0, modes, CHUNK), copies):
        copy.wait()
        at = slice(k, k + CHUNK)
        inner_send[:rows, at, :] = jnp.swapaxes(held[at, 1 - side], 0, 1)
        outer[:, at, :] = jnp.swapaxes(held[at, side], 0, 1)
        ends = lax.dot_general(
            both, held[at].reshape(-1, layers), NT, preferred_element_type=F32
        )
        for out, index in ((one_pack, 0), (two_pack, 1)):
            out[at] = jnp.concatenate(
                [ends[index:index + 1, j * width:(j + 1) * width] for j in range(CHUNK)], axis=0
            ).astype(BF16)
    outer_send[:half] = outer[pl.ds((1 - side) * half, half)]
    outer_rest[...] = outer[pl.ds(side * half, half)]


def block_kernel(
    place, levels, labels, resid, inner, outer, partial, weights, half_diag, link_y, link_z,
):
    planes, rows, layers = labels.shape
    modes = outer.shape[1]
    side = lax.rem(place[1], 2)
    at_edge = (place[1] == 0) | (place[1] == place[2] - 1)
    held = (1 - side, side)
    coef = [coefficients(labels[x], levels) for x in held]
    middle = harmonic(coef[0], coef[1])
    weights[0] = middle
    row = lax.broadcasted_iota(jnp.int32, (rows, layers), 0)
    lane = lax.broadcasted_iota(jnp.int32, (rows, layers), 1)
    for x in range(2):
        c = coef[x]
        up_y = harmonic(c, jnp.where(row == rows - 1, c, pltpu.roll(c, rows - 1, 0)))
        up_z = harmonic(c, pltpu.roll(c, layers - 1, 1))
        down_y = jnp.where(row == 0, c, pltpu.roll(up_y, 1, 0))
        weights[1 + x] = up_y
        weights[3 + x] = up_z
        weights[5 + x] = c
        inner_z = jnp.where(lane == layers - 1, 0.0, up_z)
        total = middle + up_y + down_y + inner_z + pltpu.roll(inner_z, 1, 1)
        if x == 1:
            total = total + jnp.where(at_edge, c, 0.0)
        half_diag[x] = 0.5 * total
        link_y[x] = jnp.where(row == rows - 1, 0.0, up_y)
        link_z[x] = inner_z
    here = (inner, outer)

    def step(j, carry):
        total, rhs = carry
        left, right = [], []
        for u in range(STEP):
            y = j * STEP + u
            at = pl.ds(y, 1)
            ahead = jnp.minimum(y + 1, rows - 1)
            node = [here[x][y] for x in range(2)]
            wide = [v.astype(F32) for v in node]
            for x in range(2):
                image = (
                    half_diag[x, at, :] * wide[x]
                    - link_y[x, at, :] * here[x][ahead].astype(F32)
                    - link_z[x, at, :] * pltpu.roll(wide[x], layers - 1, 1)
                )
                if x == 0:
                    image = image - weights[0, at, :] * wide[1]
                rhs = rhs + resid[held[x], at, :] * wide[x]
                left.append(jnp.concatenate(split(image), axis=0))
                right.append(node[x])
        total = total + lax.dot_general(
            jnp.concatenate(left, axis=1), jnp.concatenate(right, axis=1), NT,
            preferred_element_type=F32,
        )
        return total, rhs

    total, rhs = lax.fori_loop(
        0, rows // STEP, step, (jnp.zeros((2 * modes, modes), F32), jnp.zeros((modes, layers), F32))
    )
    partial[:modes, :] = total[:modes] + total[modes:]
    partial[modes:, :] = lax.dot_general(
        jnp.ones((8, layers), F32), rhs, NT, precision=PRECISE, preferred_element_type=F32
    )


def join_kernel(
    place, levels, partial, weights, inner, outer_rest, inner_got, outer_got, one_pack, two_pack,
    one_got, two_got, out, faces,
):
    half, modes, layers = outer_rest.shape
    parts = out.shape[0]
    share = modes // parts
    rows = 2 * half
    side = lax.rem(place[1], 2)
    odd = lax.rem(place[0], 2) == 1
    at_edge = (place[1] == 0) | (place[1] == place[2] - 1)
    base = side * half
    inner_coef = coefficients(inner_got[rows, :rows].astype(F32), levels)
    outer_coef = coefficients(outer_got[half, :rows].astype(F32), levels)
    faces[0] = harmonic(weights[5], inner_coef)
    faces[1] = jnp.where(at_edge, weights[6], harmonic(weights[6], outer_coef))

    def step(j, total):
        left, right = [], []
        for u in range(STEP):
            y = j * STEP + u
            at = pl.ds(base + y, 1)
            outer_weight = jnp.where(at_edge, 0.0, faces[1, at, :])
            for weight, own, other in (
                (faces[0, at, :], inner[base + y], inner_got[base + y]),
                (outer_weight, outer_rest[y], outer_got[y]),
            ):
                image = weight * (own.astype(F32) - other.astype(F32))
                left.append(jnp.concatenate(split(image), axis=0))
                right.append(jnp.concatenate([own, other], axis=0))
        return total + lax.dot_general(
            jnp.concatenate(left, axis=1), jnp.concatenate(right, axis=1), NT,
            preferred_element_type=F32,
        )

    cross = lax.fori_loop(0, half // STEP, step, jnp.zeros((2 * modes, 2 * modes), F32))
    cross = cross[:modes] + cross[modes:]
    cross = cross[:, :modes] - cross[:, modes:]

    def coef_row(pack):
        return coefficients(pack[modes:modes + 16].astype(F32)[0:1], levels)

    one, two = one_pack[...].astype(F32), two_pack[...].astype(F32)
    one_other, two_other = one_got[...].astype(F32), two_got[...].astype(F32)
    first, last = jnp.where(odd, one, two), jnp.where(odd, two, one)
    next_first = jnp.where(odd, two_other, one_other)
    prev_last = jnp.where(odd, one_other, two_other)
    weight_low = harmonic(coef_row(first), coef_row(prev_last))
    weight_high = harmonic(coef_row(last), coef_row(next_first))

    def product(left, right):
        return lax.dot_general(left, right, NT, precision=PRECISE, preferred_element_type=F32)

    edge_rows = weight_high * last[:modes]
    ends = product(weight_low * first[:modes], first[:modes]) + product(edge_rows, last[:modes])
    square = partial[:modes, :] + 0.5 * (cross + ends)
    square = square + square.T
    upper = -product(edge_rows, next_first[:modes])
    width = (8, modes)
    lane = lax.broadcasted_iota(jnp.int32, width, 1)
    for part in range(parts):
        at = slice(part * share, (part + 1) * share)
        out[part, :share, :modes] = square[at]
        out[part, :share, modes:] = upper[at]
        own = (lane >= part * share) & (lane < (part + 1) * share)
        out[part, share:, :modes] = jnp.where(own, partial[modes:, :], 0.0)
        out[part, share:, modes:] = jnp.zeros(width, F32)


def finish_kernel(
    place, levels, blocks, zvec, inner_got, outer_got, rest_got, one_got, two_got, weights, faces, resid,
    solution, deflated, direction_ref, image_ref, ahead_ref, spread, sides, ends_ref,
):
    parts, subs, share = blocks.shape[:3]
    share = share - 8
    modes, planes, rows, layers = zvec.shape
    half = rows // 2
    me = place[0]
    side = lax.rem(place[1], 2)
    odd = lax.rem(me, 2) == 1
    at_edge = (place[1] == 0) | (place[1] == place[2] - 1)
    order = place[3]
    held = (1 - side, side)
    square = (modes, modes)
    eye = lax.broadcasted_iota(jnp.int32, square, 0) == lax.broadcasted_iota(jnp.int32, square, 1)

    def column(row):
        return jnp.sum(jnp.where(eye, row, 0.0), axis=1, keepdims=True)

    def each(body):
        if subs <= 8:
            for entry in range(subs):
                body(entry, jnp.bitwise_xor(order, entry))
        else:
            pl.loop(0, subs)(lambda entry: body(entry, jnp.bitwise_xor(order, entry)))

    def load(entry, s):
        total = blocks[0, entry, share:share + 8, :]
        for part in range(1, parts):
            total = total + blocks[part, entry, share:share + 8, :]
        direction_ref[pl.ds(s, 1), :] = total[:1]

    each(load)

    def turned(rows_of, by):
        by = by % subs
        return jnp.concatenate([rows_of[by:], rows_of[:by]], axis=0)

    def coarse_apply(direction):
        direction_ref[...] = jnp.concatenate([direction, turned(direction, 1)], axis=1)

        def one(entry, s):
            values = jnp.concatenate([blocks[part, entry, :share, :] for part in range(parts)], axis=0)
            pair = direction_ref[pl.ds(s, 1), :]
            ahead = jnp.sum(values * pair, axis=1, keepdims=True)
            ahead_ref[...] = jnp.where(lane_is((modes, 128), s), ahead, ahead_ref[...])
            image_ref[pl.ds(s, 1), :] = jnp.sum(
                values * column(pair[:, :modes]), axis=0, keepdims=True
            )

        each(one)
        return ahead_ref[...].T[:subs] + turned(image_ref[:, modes:], -1)

    def inner(left, right):
        return jnp.sum(jnp.sum(left * right, axis=0, keepdims=True), axis=1, keepdims=True)

    remain = direction_ref[:, :modes]
    direction = remain
    result = jnp.zeros_like(remain)
    norm_now = inner(remain, remain)
    for iteration in range(CITERS):
        image = coarse_apply(direction)
        step_size = norm_now / inner(direction, image)
        result = result + step_size * direction
        if iteration + 1 < CITERS:
            remain = remain - step_size * image
            norm_next = inner(remain, remain)
            direction = remain + (norm_next / norm_now) * direction
            norm_now = norm_next
    direction_ref[:, :modes] = result
    own = direction_ref[pl.ds(me, 1), :modes]
    solution[...] = own
    own_column = jnp.broadcast_to(column(own), (modes, layers))
    spread[...] = own_column
    ahead_column = column(direction_ref[pl.ds(lax.rem(me + 1, subs), 1), :modes])
    behind_column = column(direction_ref[pl.ds(lax.rem(me + subs - 1, subs), 1), :modes])
    at_top = lane_is((modes, layers), layers - 1)
    at_bottom = lane_is((modes, layers), 0)

    def placed(pack, values, precision):
        return lax.dot_general(pack, values, TN, precision=precision, preferred_element_type=F32)

    one_other, two_other = one_got[...].astype(F32), two_got[...].astype(F32)
    next_first = jnp.where(odd, two_other, one_other)
    prev_last = jnp.where(odd, one_other, two_other)
    ends_ref[...] = (
        placed(next_first[:modes], jnp.where(at_top, ahead_column, 0.0), PRECISE)
        + placed(prev_last[:modes], jnp.where(at_bottom, behind_column, 0.0), PRECISE)
    ).reshape(planes, rows, layers)
    end_coef = coefficients(
        placed(next_first[modes:].astype(BF16), pick_row(layers - 1, layers), None)
        + placed(prev_last[modes:].astype(BF16), pick_row(0, layers), None),
        levels,
    ).reshape(planes, rows, layers)

    def outside_rows(j, carry):
        for u in range(2):
            y = j * 2 + u
            for slot, ref, at in (
                (0, inner_got, y), (0, inner_got, half + y), (1, outer_got, y), (1, rest_got, y)
            ):
                row = at if slot == 0 else (side * half + y if ref is outer_got else (1 - side) * half + y)
                sides[slot, pl.ds(row, 1), :] = jnp.sum(
                    own_column * ref[at].astype(F32), axis=0, keepdims=True
                )
        return carry

    lax.fori_loop(0, half // 2, outside_rows, 0)

    def add_mode(j, carry):
        fields = list(carry)
        for u in range(4):
            k = j * 4 + u
            scale = spread[pl.ds(k, 1), :]
            for x in range(2):
                fields[x] = fields[x] + scale * zvec[k, held[x]].astype(F32)
        return tuple(fields)

    zero = jnp.zeros((rows, layers), F32)
    field = lax.fori_loop(0, modes // 4, add_mode, (zero, zero))
    row = lax.broadcasted_iota(jnp.int32, (rows, layers), 0)
    lane = lax.broadcasted_iota(jnp.int32, (rows, layers), 1)
    outside = (sides[0], jnp.where(at_edge, 0.0, sides[1]))
    for x in range(2):
        f = field[x]
        c = weights[5 + x]
        end_field = ends_ref[held[x]]
        end_weight = harmonic(c, jnp.where(side == x, end_coef[1], end_coef[0]))
        up_y, up_z = weights[1 + x], weights[3 + x]
        down_y = jnp.where(row == 0, c, pltpu.roll(up_y, 1, 0))
        down_z = jnp.where(lane == 0, end_weight, pltpu.roll(up_z, 1, 1))
        up_z = jnp.where(lane == layers - 1, end_weight, up_z)
        above_y = jnp.where(row == rows - 1, 0.0, pltpu.roll(f, rows - 1, 0))
        below_y = jnp.where(row == 0, 0.0, pltpu.roll(f, 1, 0))
        above_z = jnp.where(lane == layers - 1, end_field, pltpu.roll(f, layers - 1, 1))
        below_z = jnp.where(lane == 0, end_field, pltpu.roll(f, 1, 1))
        image = (
            weights[0] * (f - field[1 - x])
            + faces[x] * (f - outside[x])
            + down_y * (f - below_y)
            + up_y * (f - above_y)
            + down_z * (f - below_z)
            + up_z * (f - above_z)
        )
        deflated[held[x]] = resid[held[x]] - image


def swapped(value, axis, first):
    count = lax.axis_size(axis)
    pairs = []
    for i in range(count):
        up = (i - first) % 2 == 0
        pairs.append((i, (i + 1) % count if up else (i - 1) % count))
    return lax.ppermute(value, axis, pairs)


def swapped_open(value, axis):
    count = lax.axis_size(axis)
    pairs = [(0, 0)] + [(i, i + 1 if i % 2 else i - 1) for i in range(1, count - 1)]
    return lax.ppermute(value, axis, pairs + [(count - 1, count - 1)])


def summed_share(parts, axis):
    got = lax.all_to_all(parts, axis, 0, 0)
    total = got[0]
    for index in range(1, got.shape[0]):
        total = total + got[index]
    return total


def gathered(value, axis):
    count = lax.axis_size(axis)
    if count != 8:
        return lax.all_gather(value, axis), 0
    all_of = value[None]
    for mask in (1, 2, 4):
        other = lax.ppermute(all_of, axis, [(i, i ^ mask) for i in range(count)])
        all_of = jnp.concatenate([all_of, other], axis=0)
    return all_of, lax.axis_index(axis)


def shared(value, axis):
    copies = jnp.broadcast_to(value, (lax.axis_size(axis),) + value.shape)
    return lax.all_to_all(copies, axis, 0, 0)


def body(labels, levels, zvec, resid):
    modes, planes, rows, layers = zvec.shape
    half = rows // 2
    subs, parts = lax.axis_size("sub"), lax.axis_size("pln")
    share = modes // parts
    shape = jax.ShapeDtypeStruct
    order = lax.axis_index("sub") if subs == 8 else 0
    place = jnp.stack(
        [jnp.int32(v) for v in (lax.axis_index("sub"), lax.axis_index("pln"), parts, order)]
    )
    pack = shape((modes + 16, planes * rows), BF16)
    inner_send, outer_send, outer_rest, outer, one_pack, two_pack = call(
        prepare_kernel,
        [
            shape((rows + 1, modes, layers), BF16),
            shape((half + 1, modes, layers), BF16),
            shape((half, modes, layers), BF16),
            shape((rows, modes, layers), BF16),
            pack,
            pack,
        ],
        [SMEM, VMEM, HBM],
        [pltpu.VMEM(zvec.shape, BF16), pltpu.SemaphoreType.DMA((modes // CHUNK,))],
        flops=10_000_000,
        moved=4 << 20,
    )(place, labels, zvec)
    outer_got = swapped_open(outer_send, "pln")
    inner_got = swapped(inner_send, "pln", 0)
    one_got = swapped(one_pack, "sub", 0)
    two_got = swapped(two_pack, "sub", 1)
    rest_got = swapped_open(outer_rest, "pln")
    field = (planes, rows, layers)
    partial, weights = call(
        block_kernel,
        [shape((modes + 8, modes), F32), shape((7, rows, layers), F32)],
        [SMEM, SMEM] + [VMEM] * 4,
        [pltpu.VMEM(field, F32)] * 3,
        flops=400_000_000,
        moved=3 << 20,
    )(place, levels, labels, resid, inner_send, outer)
    block, faces = call(
        join_kernel,
        [shape((parts, share + 8, 2 * modes), F32), shape((2, rows, layers), F32)],
        [SMEM, SMEM] + [VMEM] * 10,
        flops=200_000_000,
        moved=2 << 20,
    )(
        place, levels, partial, weights, inner_send, outer_rest, inner_got, outer_got, one_pack, two_pack,
        one_got, two_got,
    )
    blocks, _ = gathered(summed_share(block, "pln"), "sub")
    blocks = shared(blocks, "pln")
    return tuple(
        call(
            finish_kernel,
            [shape((1, modes), F32), shape(field, F32)],
            [SMEM, SMEM] + [VMEM] * 10,
            [
                pltpu.VMEM((subs, 2 * modes), F32),
                pltpu.VMEM((subs, 2 * modes), F32),
                pltpu.VMEM((modes, 128), F32),
                pltpu.VMEM((modes, layers), F32),
                pltpu.VMEM(field, F32),
                pltpu.VMEM(field, F32),
            ],
            flops=10_000_000,
            moved=5 << 20,
        )(
            place, levels, blocks, zvec, inner_got, outer_got, rest_got, one_got, two_got, weights, faces,
            resid,
        )
    )


def solution(mesh):
    in_specs = (P("pln", None, "sub"), P(), P(None, "pln", None, "sub"), P("pln", None, "sub"))
    out_specs = (P("sub", None), P("pln", None, "sub"))
    return jax.shard_map(body, mesh=mesh, in_specs=in_specs, out_specs=out_specs, check_vma=False)
```

```python
import jax
import jax.numpy as jnp
from jax import lax
from jax.experimental import pallas as pl
from jax.experimental.pallas import tpu as pltpu
from jax.sharding import PartitionSpec as P

CITERS = 2
STEP = 4
CHUNK = 16
F32 = jnp.float32
BF16 = jnp.bfloat16
PRECISE = lax.Precision.HIGHEST
NT = (((1,), (1,)), ((), ()))
TN = (((0,), (0,)), ((), ()))
VMEM = pl.BlockSpec(memory_space=pltpu.VMEM)
SMEM = pl.BlockSpec(memory_space=pltpu.SMEM)
HBM = pl.BlockSpec(memory_space=pltpu.HBM)


def call(kernel, outs, specs, scratch=(), flops=0, moved=0, limit=32):
    return pl.pallas_call(
        kernel,
        out_shape=outs,
        in_specs=specs,
        out_specs=jax.tree.map(lambda _: VMEM, outs),
        scratch_shapes=list(scratch),
        cost_estimate=pl.CostEstimate(flops=flops, bytes_accessed=moved, transcendentals=0),
        compiler_params=pltpu.CompilerParams(vmem_limit_bytes=limit << 20),
    )


def harmonic(left_value, right_value):
    return 2.0 * left_value * right_value / (left_value + right_value)


def coefficients(labels, levels_ref):
    weighted = jnp.zeros(labels.shape, F32)
    for level in range(levels_ref.shape[0]):
        weighted = weighted + jnp.where(labels == level, levels_ref[level], 0.0)
    return weighted


def lane_is(shape, lane):
    return lax.broadcasted_iota(jnp.int32, shape, len(shape) - 1) == lane


def pick_row(lane, width):
    row = lax.broadcasted_iota(jnp.int32, (16, width), 0)
    return ((row == 0) & lane_is((16, width), lane)).astype(BF16)


def prepare_kernel(
    place, labels_far, zvec, inner_send, outer_send, outer_rest, outer, one_pack, two_pack, labels, held,
    label_sem, sems,
):
    modes, planes, rows, layers = zvec.shape
    half = rows // 2
    width = planes * rows
    side = lax.rem(place[1], 2)
    odd = lax.rem(place[0], 2) == 1
    copies = [
        pltpu.make_async_copy(zvec.at[pl.ds(k, CHUNK)], held.at[pl.ds(k, CHUNK)], sems.at[k // CHUNK])
        for k in range(0, modes, CHUNK)
    ]
    label_copy = pltpu.make_async_copy(labels_far, labels, label_sem)
    label_copy.start()
    for copy in copies:
        copy.start()
    label_copy.wait()
    one_lane = jnp.where(odd, 0, layers - 1)
    two_lane = jnp.where(odd, layers - 1, 0)
    row = lax.broadcasted_iota(jnp.int32, (16, layers), 0)
    both = ((row == 0) & lane_is((16, layers), one_lane)) | ((row == 1) & lane_is((16, layers), two_lane))
    both = both.astype(BF16)
    flat = labels[...].astype(F32).astype(BF16).reshape(width, layers)
    for out, lane in ((one_pack, one_lane), (two_pack, two_lane)):
        out[modes:] = lax.dot_general(
            pick_row(lane, layers), flat, NT, preferred_element_type=F32
        ).astype(BF16)
    inner_send[rows, :rows] = labels[1 - side].astype(F32).astype(BF16)
    outer_send[half, :rows] = labels[side].astype(F32).astype(BF16)
    for k, copy in zip(range(0, modes, CHUNK), copies):
        copy.wait()
        at = slice(k, k + CHUNK)
        inner_send[:rows, at, :] = jnp.swapaxes(held[at, 1 - side], 0, 1)
        outer[:, at, :] = jnp.swapaxes(held[at, side], 0, 1)
        ends = lax.dot_general(
            both, held[at].reshape(-1, layers), NT, preferred_element_type=F32
        )
        for out, index in ((one_pack, 0), (two_pack, 1)):
            out[at] = jnp.concatenate(
                [ends[index:index + 1, j * width:(j + 1) * width] for j in range(CHUNK)], axis=0
            ).astype(BF16)
    outer_send[:half] = outer[pl.ds((1 - side) * half, half)]
    outer_rest[...] = outer[pl.ds(side * half, half)]


def block_kernel(
    place, levels, labels, resid, inner, outer, partial, weights, half_diag, link_y, link_z,
):
    planes, rows, layers = labels.shape
    modes = outer.shape[1]
    side = lax.rem(place[1], 2)
    at_edge = (place[1] == 0) | (place[1] == place[2] - 1)
    held = (1 - side, side)
    coef = [coefficients(labels[x], levels) for x in held]
    middle = harmonic(coef[0], coef[1])
    weights[0] = middle
    row = lax.broadcasted_iota(jnp.int32, (rows, layers), 0)
    lane = lax.broadcasted_iota(jnp.int32, (rows, layers), 1)
    for x in range(2):
        c = coef[x]
        up_y = harmonic(c, jnp.where(row == rows - 1, c, pltpu.roll(c, rows - 1, 0)))
        up_z = harmonic(c, pltpu.roll(c, layers - 1, 1))
        down_y = jnp.where(row == 0, c, pltpu.roll(up_y, 1, 0))
        weights[1 + x] = up_y
        weights[3 + x] = up_z
        weights[5 + x] = c
        inner_z = jnp.where(lane == layers - 1, 0.0, up_z)
        total = middle + up_y + down_y + inner_z + pltpu.roll(inner_z, 1, 1)
        if x == 1:
            total = total + jnp.where(at_edge, c, 0.0)
        half_diag[x] = 0.5 * total
        link_y[x] = jnp.where(row == rows - 1, 0.0, up_y)
        link_z[x] = inner_z
    here = (inner, outer)

    def step(j, carry):
        total, rhs = carry
        left, right = [], []
        for u in range(STEP):
            y = j * STEP + u
            at = pl.ds(y, 1)
            ahead = jnp.minimum(y + 1, rows - 1)
            node = [here[x][y] for x in range(2)]
            wide = [v.astype(F32) for v in node]
            for x in range(2):
                image = (
                    half_diag[x, at, :] * wide[x]
                    - link_y[x, at, :] * here[x][ahead].astype(F32)
                    - link_z[x, at, :] * pltpu.roll(wide[x], layers - 1, 1)
                )
                if x == 0:
                    image = image - weights[0, at, :] * wide[1]
                rhs = rhs + resid[held[x], at, :] * wide[x]
                left.append(node[x])
                right.append(image.astype(BF16))
        total = total + lax.dot_general(
            jnp.concatenate(left, axis=1), jnp.concatenate(right, axis=1), NT,
            preferred_element_type=F32,
        )
        return total, rhs

    total, rhs = lax.fori_loop(
        0, rows // STEP, step, (jnp.zeros((modes, modes), F32), jnp.zeros((modes, layers), F32))
    )
    partial[:modes, :] = total
    partial[modes:, :] = lax.dot_general(
        jnp.ones((8, layers), F32), rhs, NT, precision=PRECISE, preferred_element_type=F32
    )


def join_kernel(
    place, levels, partial, weights, inner, outer_rest, inner_got, outer_got, one_pack, two_pack,
    one_got, two_got, out, faces,
):
    half, modes, layers = outer_rest.shape
    rows = 2 * half
    side = lax.rem(place[1], 2)
    odd = lax.rem(place[0], 2) == 1
    at_edge = (place[1] == 0) | (place[1] == place[2] - 1)
    base = side * half
    inner_coef = coefficients(inner_got[rows, :rows].astype(F32), levels)
    outer_coef = coefficients(outer_got[half, :rows].astype(F32), levels)
    faces[0] = harmonic(weights[5], inner_coef)
    faces[1] = jnp.where(at_edge, weights[6], harmonic(weights[6], outer_coef))

    def step(j, total):
        left, right = [], []
        for u in range(STEP):
            y = j * STEP + u
            at = pl.ds(base + y, 1)
            outer_weight = jnp.where(at_edge, 0.0, faces[1, at, :])
            for weight, own, other in (
                (faces[0, at, :], inner[base + y], inner_got[base + y]),
                (outer_weight, outer_rest[y], outer_got[y]),
            ):
                image = weight * (own.astype(F32) - other.astype(F32))
                left.append(jnp.concatenate([own, other], axis=0))
                right.append(image.astype(BF16))
        return total + lax.dot_general(
            jnp.concatenate(left, axis=1), jnp.concatenate(right, axis=1), NT,
            preferred_element_type=F32,
        )

    cross = lax.fori_loop(0, half // STEP, step, jnp.zeros((2 * modes, modes), F32))
    cross = cross[:modes] - cross[modes:]

    def coef_row(pack):
        return coefficients(pack[modes:modes + 16].astype(F32)[0:1], levels)

    one, two = one_pack[...].astype(F32), two_pack[...].astype(F32)
    one_other, two_other = one_got[...].astype(F32), two_got[...].astype(F32)
    first, last = jnp.where(odd, one, two), jnp.where(odd, two, one)
    next_first = jnp.where(odd, two_other, one_other)
    prev_last = jnp.where(odd, one_other, two_other)
    weight_low = harmonic(coef_row(first), coef_row(prev_last))
    weight_high = harmonic(coef_row(last), coef_row(next_first))

    def product(left, right):
        return lax.dot_general(left, right, NT, precision=PRECISE, preferred_element_type=F32)

    edge_rows = weight_high * last[:modes]
    ends = product(weight_low * first[:modes], first[:modes]) + product(edge_rows, last[:modes])
    square = partial[:modes, :] + 0.5 * (cross + ends)
    square = square + square.T
    upper = -product(edge_rows, next_first[:modes])
    out[:modes, :modes] = square
    out[:modes, modes:] = upper
    out[modes:, :modes] = partial[modes:, :]
    out[modes:, modes:] = jnp.zeros((8, modes), F32)


def finish_kernel(place, levels, *refs):
    count = len(refs) - 17
    blocks, refs = refs[:count], refs[count:]
    zvec, inner_got, outer_got, rest_got, one_got, two_got, weights, faces, resid = refs[:9]
    solution, deflated, direction_ref, image_ref, ahead_ref, spread, sides, ends_ref = refs[9:]
    subs = direction_ref.shape[0]
    modes, planes, rows, layers = zvec.shape
    half = rows // 2
    me = place[0]
    side = lax.rem(place[1], 2)
    odd = lax.rem(me, 2) == 1
    at_edge = (place[1] == 0) | (place[1] == place[2] - 1)
    order = place[3]
    held = (1 - side, side)
    square = (modes, modes)
    eye = lax.broadcasted_iota(jnp.int32, square, 0) == lax.broadcasted_iota(jnp.int32, square, 1)

    def column(row):
        return jnp.sum(jnp.where(eye, row, 0.0), axis=1, keepdims=True)

    def each(body):
        for index, block in enumerate(blocks):
            held_here = block.shape[0]
            if held_here <= 8:
                for entry in range(held_here):
                    body(block.at[entry], jnp.bitwise_xor(order, index * held_here + entry))
            else:
                pl.loop(0, held_here)(lambda entry, block=block: body(block.at[entry], entry))

    def load(block, s):
        direction_ref[pl.ds(s, 1), :] = block[modes:modes + 1, :]

    each(load)

    def turned(rows_of, by):
        by = by % subs
        return jnp.concatenate([rows_of[by:], rows_of[:by]], axis=0)

    def coarse_apply(direction):
        direction_ref[...] = jnp.concatenate([direction, turned(direction, 1)], axis=1)

        def one(block, s):
            values = block[:modes, :]
            pair = direction_ref[pl.ds(s, 1), :]
            ahead = jnp.sum(values * pair, axis=1, keepdims=True)
            ahead_ref[...] = jnp.where(lane_is((modes, 128), s), ahead, ahead_ref[...])
            image_ref[pl.ds(s, 1), :] = jnp.sum(
                values * column(pair[:, :modes]), axis=0, keepdims=True
            )

        each(one)
        return ahead_ref[...].T[:subs] + turned(image_ref[:, modes:], -1)

    def inner(left, right):
        return jnp.sum(jnp.sum(left * right, axis=0, keepdims=True), axis=1, keepdims=True)

    remain = direction_ref[:, :modes]
    direction = remain
    result = jnp.zeros_like(remain)
    norm_now = inner(remain, remain)
    for iteration in range(CITERS):
        image = coarse_apply(direction)
        step_size = norm_now / inner(direction, image)
        result = result + step_size * direction
        if iteration + 1 < CITERS:
            remain = remain - step_size * image
            norm_next = inner(remain, remain)
            direction = remain + (norm_next / norm_now) * direction
            norm_now = norm_next
    direction_ref[:, :modes] = result
    own = direction_ref[pl.ds(me, 1), :modes]
    solution[...] = own
    own_column = jnp.broadcast_to(column(own), (modes, layers))
    spread[...] = own_column
    ahead_column = column(direction_ref[pl.ds(lax.rem(me + 1, subs), 1), :modes])
    behind_column = column(direction_ref[pl.ds(lax.rem(me + subs - 1, subs), 1), :modes])
    at_top = lane_is((modes, layers), layers - 1)
    at_bottom = lane_is((modes, layers), 0)

    def placed(pack, values, precision):
        return lax.dot_general(pack, values, TN, precision=precision, preferred_element_type=F32)

    one_other, two_other = one_got[...].astype(F32), two_got[...].astype(F32)
    next_first = jnp.where(odd, two_other, one_other)
    prev_last = jnp.where(odd, one_other, two_other)
    ends_ref[...] = (
        placed(next_first[:modes], jnp.where(at_top, ahead_column, 0.0), PRECISE)
        + placed(prev_last[:modes], jnp.where(at_bottom, behind_column, 0.0), PRECISE)
    ).reshape(planes, rows, layers)
    end_coef = coefficients(
        placed(next_first[modes:].astype(BF16), pick_row(layers - 1, layers), None)
        + placed(prev_last[modes:].astype(BF16), pick_row(0, layers), None),
        levels,
    ).reshape(planes, rows, layers)

    def outside_rows(j, carry):
        for u in range(2):
            y = j * 2 + u
            for slot, ref, at in (
                (0, inner_got, y), (0, inner_got, half + y), (1, outer_got, y), (1, rest_got, y)
            ):
                row = at if slot == 0 else (side * half + y if ref is outer_got else (1 - side) * half + y)
                sides[slot, pl.ds(row, 1), :] = jnp.sum(
                    own_column * ref[at].astype(F32), axis=0, keepdims=True
                )
        return carry

    lax.fori_loop(0, half // 2, outside_rows, 0)

    def add_mode(j, carry):
        fields = list(carry)
        for u in range(4):
            k = j * 4 + u
            scale = spread[pl.ds(k, 1), :]
            for x in range(2):
                fields[x] = fields[x] + scale * zvec[k, held[x]].astype(F32)
        return tuple(fields)

    zero = jnp.zeros((rows, layers), F32)
    field = lax.fori_loop(0, modes // 4, add_mode, (zero, zero))
    row = lax.broadcasted_iota(jnp.int32, (rows, layers), 0)
    lane = lax.broadcasted_iota(jnp.int32, (rows, layers), 1)
    outside = (sides[0], jnp.where(at_edge, 0.0, sides[1]))
    for x in range(2):
        f = field[x]
        c = weights[5 + x]
        end_field = ends_ref[held[x]]
        end_weight = harmonic(c, jnp.where(side == x, end_coef[1], end_coef[0]))
        up_y, up_z = weights[1 + x], weights[3 + x]
        down_y = jnp.where(row == 0, c, pltpu.roll(up_y, 1, 0))
        down_z = jnp.where(lane == 0, end_weight, pltpu.roll(up_z, 1, 1))
        up_z = jnp.where(lane == layers - 1, end_weight, up_z)
        above_y = jnp.where(row == rows - 1, 0.0, pltpu.roll(f, rows - 1, 0))
        below_y = jnp.where(row == 0, 0.0, pltpu.roll(f, 1, 0))
        above_z = jnp.where(lane == layers - 1, end_field, pltpu.roll(f, layers - 1, 1))
        below_z = jnp.where(lane == 0, end_field, pltpu.roll(f, 1, 1))
        image = (
            weights[0] * (f - field[1 - x])
            + faces[x] * (f - outside[x])
            + down_y * (f - below_y)
            + up_y * (f - above_y)
            + down_z * (f - below_z)
            + up_z * (f - above_z)
        )
        deflated[held[x]] = resid[held[x]] - image


def swapped(value, axis, first):
    count = lax.axis_size(axis)
    pairs = []
    for i in range(count):
        up = (i - first) % 2 == 0
        pairs.append((i, (i + 1) % count if up else (i - 1) % count))
    return lax.ppermute(value, axis, pairs)


def swapped_open(value, axis):
    count = lax.axis_size(axis)
    pairs = [(0, 0)] + [(i, i + 1 if i % 2 else i - 1) for i in range(1, count - 1)]
    return lax.ppermute(value, axis, pairs + [(count - 1, count - 1)])


def exchanged(value, axis, mask):
    return lax.ppermute(value, axis, [(i, i ^ mask) for i in range(lax.axis_size(axis))])


def summed(value, axis):
    if lax.axis_size(axis) != 4:
        return lax.psum(value, axis)
    one, two, three = (exchanged(value, axis, mask) for mask in (1, 2, 3))
    return (value + one) + (two + three)


def gathered(value, axis):
    if lax.axis_size(axis) != 8:
        return [lax.all_gather(value, axis)]
    pair = jnp.stack([value, exchanged(value, axis, 1)])
    return [pair] + [exchanged(pair, axis, mask) for mask in (2, 4, 6)]


def body(labels, levels, zvec, resid):
    modes, planes, rows, layers = zvec.shape
    half = rows // 2
    subs, parts = lax.axis_size("sub"), lax.axis_size("pln")
    shape = jax.ShapeDtypeStruct
    order = lax.axis_index("sub") if subs == 8 else 0
    place = jnp.stack(
        [jnp.int32(v) for v in (lax.axis_index("sub"), lax.axis_index("pln"), parts, order)]
    )
    pack = shape((modes + 16, planes * rows), BF16)
    inner_send, outer_send, outer_rest, outer, one_pack, two_pack = call(
        prepare_kernel,
        [
            shape((rows + 1, modes, layers), BF16),
            shape((half + 1, modes, layers), BF16),
            shape((half, modes, layers), BF16),
            shape((rows, modes, layers), BF16),
            pack,
            pack,
        ],
        [SMEM, HBM, HBM],
        [
            pltpu.VMEM(labels.shape, jnp.int32),
            pltpu.VMEM(zvec.shape, BF16),
            pltpu.SemaphoreType.DMA,
            pltpu.SemaphoreType.DMA((modes // CHUNK,)),
        ],
        flops=10_000_000,
        moved=4 << 20,
    )(place, *(pltpu.with_memory_space_constraint(v, pltpu.HBM) for v in (labels, zvec)))
    outer_got = swapped_open(outer_send, "pln")
    inner_got = swapped(inner_send, "pln", 0)
    one_got = swapped(one_pack, "sub", 0)
    two_got = swapped(two_pack, "sub", 1)
    rest_got = swapped_open(outer_rest, "pln")
    field = (planes, rows, layers)
    partial, weights = call(
        block_kernel,
        [shape((modes + 8, modes), F32), shape((7, rows, layers), F32)],
        [SMEM, SMEM] + [VMEM] * 4,
        [pltpu.VMEM(field, F32)] * 3,
        flops=400_000_000,
        moved=3 << 20,
    )(place, levels, labels, resid, inner_send, outer)
    block, faces = call(
        join_kernel,
        [shape((modes + 8, 2 * modes), F32), shape((2, rows, layers), F32)],
        [SMEM, SMEM] + [VMEM] * 10,
        flops=200_000_000,
        moved=2 << 20,
    )(
        place, levels, partial, weights, inner_send, outer_rest, inner_got, outer_got, one_pack, two_pack,
        one_got, two_got,
    )
    blocks = gathered(summed(block, "pln"), "sub")
    return tuple(
        call(
            finish_kernel,
            [shape((1, modes), F32), shape(field, F32)],
            [SMEM, SMEM] + [VMEM] * (9 + len(blocks)),
            [
                pltpu.VMEM((subs, 2 * modes), F32),
                pltpu.VMEM((subs, 2 * modes), F32),
                pltpu.VMEM((modes, 128), F32),
                pltpu.VMEM((modes, layers), F32),
                pltpu.VMEM(field, F32),
                pltpu.VMEM(field, F32),
            ],
            flops=10_000_000,
            moved=5 << 20,
        )(
            place, levels, *blocks, zvec, inner_got, outer_got, rest_got, one_got, two_got, weights, faces,
            resid,
        )
    )


def solution(mesh):
    in_specs = (P("pln", None, "sub"), P(), P(None, "pln", None, "sub"), P("pln", None, "sub"))
    out_specs = (P("sub", None), P("pln", None, "sub"))
    return jax.shard_map(body, mesh=mesh, in_specs=in_specs, out_specs=out_specs, check_vma=False)
```

```python
import jax
import jax.numpy as jnp
from jax import lax
from jax.experimental import pallas as pl
from jax.experimental.pallas import tpu as pltpu
from jax.sharding import PartitionSpec as P

CITERS = 2
STEP = 4
CHUNK = 16
F32 = jnp.float32
BF16 = jnp.bfloat16
PRECISE = lax.Precision.HIGHEST
NT = (((1,), (1,)), ((), ()))
TN = (((0,), (0,)), ((), ()))
VMEM = pl.BlockSpec(memory_space=pltpu.VMEM)
SMEM = pl.BlockSpec(memory_space=pltpu.SMEM)
HBM = pl.BlockSpec(memory_space=pltpu.HBM)
ANY = pl.BlockSpec(memory_space=pl.ANY)


def call(kernel, outs, specs, scratch=(), flops=0, moved=0, limit=32, aliases=None):
    return pl.pallas_call(
        kernel,
        out_shape=outs,
        in_specs=specs,
        out_specs=[ANY if at in (aliases or {}).values() else VMEM for at in range(len(outs))],
        input_output_aliases=aliases or {},
        scratch_shapes=list(scratch),
        cost_estimate=pl.CostEstimate(flops=flops, bytes_accessed=moved, transcendentals=0),
        compiler_params=pltpu.CompilerParams(vmem_limit_bytes=limit << 20),
    )


def harmonic(left_value, right_value):
    return 2.0 * left_value * right_value / (left_value + right_value)


def coefficients(labels, levels_ref):
    weighted = jnp.zeros(labels.shape, F32)
    for level in range(levels_ref.shape[0]):
        weighted = weighted + jnp.where(labels == level, levels_ref[level], 0.0)
    return weighted


def lane_is(shape, lane):
    return lax.broadcasted_iota(jnp.int32, shape, len(shape) - 1) == lane


def pick_row(lane, width):
    row = lax.broadcasted_iota(jnp.int32, (16, width), 0)
    return ((row == 0) & lane_is((16, width), lane)).astype(BF16)


def pack_kernel(place, labels_far, zvec, one_pack, two_pack, held, labels, label_sem, sems):
    modes, planes, rows, layers = zvec.shape
    width = planes * rows
    odd = lax.rem(place[0], 2) == 1
    copies = [
        pltpu.make_async_copy(zvec.at[pl.ds(k, CHUNK)], held.at[pl.ds(k, CHUNK)], sems.at[k // CHUNK])
        for k in range(0, modes, CHUNK)
    ]
    label_copy = pltpu.make_async_copy(labels_far, labels, label_sem)
    label_copy.start()
    for copy in copies:
        copy.start()
    label_copy.wait()
    one_lane = jnp.where(odd, 0, layers - 1)
    two_lane = jnp.where(odd, layers - 1, 0)
    row = lax.broadcasted_iota(jnp.int32, (16, layers), 0)
    both = ((row == 0) & lane_is((16, layers), one_lane)) | ((row == 1) & lane_is((16, layers), two_lane))
    both = both.astype(BF16)
    flat = labels[...].astype(F32).astype(BF16).reshape(width, layers)
    for out, lane in ((one_pack, one_lane), (two_pack, two_lane)):
        out[modes:] = lax.dot_general(
            pick_row(lane, layers), flat, NT, preferred_element_type=F32
        ).astype(BF16)
    for k, copy in zip(range(0, modes, CHUNK), copies):
        copy.wait()
        at = slice(k, k + CHUNK)
        ends = lax.dot_general(
            both, held[at].reshape(-1, layers), NT, preferred_element_type=F32
        )
        for out, index in ((one_pack, 0), (two_pack, 1)):
            out[at] = jnp.concatenate(
                [ends[index:index + 1, j * width:(j + 1) * width] for j in range(CHUNK)], axis=0
            ).astype(BF16)


def prepare_kernel(place, labels, held, inner_send, outer_send, inner_rest, outer_rest, planes_out):
    modes, planes, rows, layers = held.shape
    half = rows // 2
    side = lax.rem(place[1], 2)
    for slot, plane, send, rest in (
        (0, 1 - side, inner_send, inner_rest), (1, side, outer_send, outer_rest)
    ):
        for k in range(0, modes, CHUNK):
            at = slice(k, k + CHUNK)
            planes_out[slot, :, at, :] = jnp.swapaxes(held[at, plane], 0, 1)
        send[half, :rows] = labels[plane].astype(F32).astype(BF16)
        send[:half] = planes_out[slot, pl.ds((1 - side) * half, half)]
        rest[...] = planes_out[slot, pl.ds(side * half, half)]


def block_kernel(
    place, levels, labels, resid, here, partial, weights, half_diag, link_y, link_z,
):
    planes, rows, layers = labels.shape
    modes = here.shape[2]
    side = lax.rem(place[1], 2)
    at_edge = (place[1] == 0) | (place[1] == place[2] - 1)
    held = (1 - side, side)
    coef = [coefficients(labels[x], levels) for x in held]
    middle = harmonic(coef[0], coef[1])
    weights[0] = middle
    row = lax.broadcasted_iota(jnp.int32, (rows, layers), 0)
    lane = lax.broadcasted_iota(jnp.int32, (rows, layers), 1)
    for x in range(2):
        c = coef[x]
        up_y = harmonic(c, jnp.where(row == rows - 1, c, pltpu.roll(c, rows - 1, 0)))
        up_z = harmonic(c, pltpu.roll(c, layers - 1, 1))
        down_y = jnp.where(row == 0, c, pltpu.roll(up_y, 1, 0))
        weights[1 + x] = up_y
        weights[3 + x] = up_z
        weights[5 + x] = c
        inner_z = jnp.where(lane == layers - 1, 0.0, up_z)
        total = middle + up_y + down_y + inner_z + pltpu.roll(inner_z, 1, 1)
        if x == 1:
            total = total + jnp.where(at_edge, c, 0.0)
        half_diag[x] = 0.5 * total
        link_y[x] = jnp.where(row == rows - 1, 0.0, up_y)
        link_z[x] = inner_z

    def step(j, carry):
        total, rhs, wide = carry
        for u in range(STEP):
            y = j * STEP + u
            at = pl.ds(y, 1)
            ahead = jnp.minimum(y + 1, rows - 1)
            up = [here[x, ahead].astype(F32) for x in range(2)]
            images = []
            for x in range(2):
                image = (
                    half_diag[x, at, :] * wide[x]
                    - link_y[x, at, :] * up[x]
                    - link_z[x, at, :] * pltpu.roll(wide[x], layers - 1, 1)
                )
                if x == 0:
                    image = image - weights[0, at, :] * wide[1]
                rhs = rhs + resid[held[x], at, :] * wide[x]
                images.append(image.astype(BF16))
            total = total + lax.dot_general(
                jnp.concatenate(images, axis=1),
                jnp.concatenate([here[0, y], here[1, y]], axis=1),
                NT,
                preferred_element_type=F32,
            )
            wide = up
        return total, rhs, wide

    total, rhs, _ = lax.fori_loop(
        0,
        rows // STEP,
        step,
        (
            jnp.zeros((modes, modes), F32),
            jnp.zeros((modes, layers), F32),
            [here[x, 0].astype(F32) for x in range(2)],
        ),
    )
    partial[:modes, :] = total
    partial[modes:, :] = lax.dot_general(
        jnp.ones((8, layers), F32), rhs, NT, precision=PRECISE, preferred_element_type=F32
    )


def join_kernel(
    place, levels, partial, weights, inner_rest, outer_rest, inner_got, outer_got, one_pack, two_pack,
    one_got, two_got, out, faces,
):
    half, modes, layers = outer_rest.shape
    rows = 2 * half
    side = lax.rem(place[1], 2)
    odd = lax.rem(place[0], 2) == 1
    at_edge = (place[1] == 0) | (place[1] == place[2] - 1)
    base = side * half
    inner_coef = coefficients(inner_got[half, :rows].astype(F32), levels)
    outer_coef = coefficients(outer_got[half, :rows].astype(F32), levels)
    faces[0] = harmonic(weights[5], inner_coef)
    faces[1] = jnp.where(at_edge, weights[6], harmonic(weights[6], outer_coef))

    def step(j, total):
        left, right = [], []
        for u in range(STEP):
            y = j * STEP + u
            at = pl.ds(base + y, 1)
            outer_weight = jnp.where(at_edge, 0.0, faces[1, at, :])
            for weight, own, other in (
                (faces[0, at, :], inner_rest[y], inner_got[y]),
                (outer_weight, outer_rest[y], outer_got[y]),
            ):
                image = weight * (own.astype(F32) - other.astype(F32))
                left.append(jnp.concatenate([own, other], axis=0))
                right.append(image.astype(BF16))
        return total + lax.dot_general(
            jnp.concatenate(left, axis=1), jnp.concatenate(right, axis=1), NT,
            preferred_element_type=F32,
        )

    cross = lax.fori_loop(0, half // STEP, step, jnp.zeros((2 * modes, modes), F32))
    cross = cross[:modes] - cross[modes:]

    def coef_row(pack):
        return coefficients(pack[modes:modes + 16].astype(F32)[0:1], levels)

    one, two = one_pack[...].astype(F32), two_pack[...].astype(F32)
    one_other, two_other = one_got[...].astype(F32), two_got[...].astype(F32)
    first, last = jnp.where(odd, one, two), jnp.where(odd, two, one)
    next_first = jnp.where(odd, two_other, one_other)
    prev_last = jnp.where(odd, one_other, two_other)
    weight_low = harmonic(coef_row(first), coef_row(prev_last))
    weight_high = harmonic(coef_row(last), coef_row(next_first))

    def product(left, right):
        return lax.dot_general(left, right, NT, precision=PRECISE, preferred_element_type=F32)

    edge_rows = weight_high * last[:modes]
    ends = product(weight_low * first[:modes], first[:modes]) + product(edge_rows, last[:modes])
    square = partial[:modes, :] + 0.5 * (cross + ends)
    square = square + square.T
    upper = -product(edge_rows, next_first[:modes])
    out[:modes, :modes] = square
    out[:modes, modes:] = upper
    out[modes:, :modes] = partial[modes:, :]
    out[modes:, modes:] = jnp.zeros((8, modes), F32)


def sum_kernel(own, one, two, three, inner_rest, outer_rest, out, inner_out, outer_out):
    out[...] = (own[...] + one[...]) + (two[...] + three[...])


def finish_kernel(place, levels, *refs):
    count = len(refs) - 18
    blocks, refs = refs[:count], refs[count:]
    zvec, inner_got, outer_got, inner_last, outer_last, one_got, two_got, weights, faces, resid = refs[:10]
    solution, deflated, direction_ref, image_ref, ahead_ref, spread, sides, ends_ref = refs[10:]
    subs = direction_ref.shape[0]
    modes, planes, rows, layers = zvec.shape
    half = rows // 2
    me = place[0]
    side = lax.rem(place[1], 2)
    odd = lax.rem(me, 2) == 1
    at_edge = (place[1] == 0) | (place[1] == place[2] - 1)
    order = place[3]
    held = (1 - side, side)
    square = (modes, modes)
    eye = lax.broadcasted_iota(jnp.int32, square, 0) == lax.broadcasted_iota(jnp.int32, square, 1)

    def column(row):
        return jnp.sum(jnp.where(eye, row, 0.0), axis=1, keepdims=True)

    def each(body):
        for index, block in enumerate(blocks):
            held_here = block.shape[0]
            if held_here <= 8:
                for entry in range(held_here):
                    body(block.at[entry], jnp.bitwise_xor(order, index * held_here + entry))
            else:
                pl.loop(0, held_here)(lambda entry, block=block: body(block.at[entry], entry))

    def load(block, s):
        direction_ref[pl.ds(s, 1), :] = block[modes:modes + 1, :]

    each(load)

    def turned(rows_of, by):
        by = by % subs
        return jnp.concatenate([rows_of[by:], rows_of[:by]], axis=0)

    def coarse_apply(direction):
        direction_ref[...] = jnp.concatenate([direction, turned(direction, 1)], axis=1)

        def one(block, s):
            values = block[:modes, :]
            pair = direction_ref[pl.ds(s, 1), :]
            ahead = jnp.sum(values * pair, axis=1, keepdims=True)
            ahead_ref[...] = jnp.where(lane_is((modes, 128), s), ahead, ahead_ref[...])
            image_ref[pl.ds(s, 1), :] = jnp.sum(
                values * column(pair[:, :modes]), axis=0, keepdims=True
            )

        each(one)
        return ahead_ref[...].T[:subs] + turned(image_ref[:, modes:], -1)

    def inner(left, right):
        return jnp.sum(jnp.sum(left * right, axis=0, keepdims=True), axis=1, keepdims=True)

    remain = direction_ref[:, :modes]
    direction = remain
    result = jnp.zeros_like(remain)
    norm_now = inner(remain, remain)
    for iteration in range(CITERS):
        image = coarse_apply(direction)
        step_size = norm_now / inner(direction, image)
        result = result + step_size * direction
        if iteration + 1 < CITERS:
            remain = remain - step_size * image
            norm_next = inner(remain, remain)
            direction = remain + (norm_next / norm_now) * direction
            norm_now = norm_next
    direction_ref[:, :modes] = result
    own = direction_ref[pl.ds(me, 1), :modes]
    solution[...] = own
    own_column = jnp.broadcast_to(column(own), (modes, layers))
    spread[...] = own_column
    ahead_column = column(direction_ref[pl.ds(lax.rem(me + 1, subs), 1), :modes])
    behind_column = column(direction_ref[pl.ds(lax.rem(me + subs - 1, subs), 1), :modes])
    at_top = lane_is((modes, layers), layers - 1)
    at_bottom = lane_is((modes, layers), 0)

    def placed(pack, values, precision):
        return lax.dot_general(pack, values, TN, precision=precision, preferred_element_type=F32)

    one_other, two_other = one_got[...].astype(F32), two_got[...].astype(F32)
    next_first = jnp.where(odd, two_other, one_other)
    prev_last = jnp.where(odd, one_other, two_other)
    ends_ref[...] = (
        placed(next_first[:modes], jnp.where(at_top, ahead_column, 0.0), PRECISE)
        + placed(prev_last[:modes], jnp.where(at_bottom, behind_column, 0.0), PRECISE)
    ).reshape(planes, rows, layers)
    end_coef = coefficients(
        placed(next_first[modes:].astype(BF16), pick_row(layers - 1, layers), None)
        + placed(prev_last[modes:].astype(BF16), pick_row(0, layers), None),
        levels,
    ).reshape(planes, rows, layers)

    def outside_rows(j, carry):
        for u in range(2):
            y = j * 2 + u
            for slot, near, last in ((0, inner_got, inner_last), (1, outer_got, outer_last)):
                for ref, base in ((near, side * half), (last, (1 - side) * half)):
                    sides[slot, pl.ds(base + y, 1), :] = jnp.sum(
                        own_column * ref[y].astype(F32), axis=0, keepdims=True
                    )
        return carry

    lax.fori_loop(0, half // 2, outside_rows, 0)

    def add_mode(j, carry):
        fields = list(carry)
        for u in range(4):
            k = j * 4 + u
            scale = spread[pl.ds(k, 1), :]
            for x in range(2):
                fields[x] = fields[x] + scale * zvec[k, held[x]].astype(F32)
        return tuple(fields)

    zero = jnp.zeros((rows, layers), F32)
    field = lax.fori_loop(0, modes // 4, add_mode, (zero, zero))
    row = lax.broadcasted_iota(jnp.int32, (rows, layers), 0)
    lane = lax.broadcasted_iota(jnp.int32, (rows, layers), 1)
    outside = (sides[0], jnp.where(at_edge, 0.0, sides[1]))
    for x in range(2):
        f = field[x]
        c = weights[5 + x]
        end_field = ends_ref[held[x]]
        end_weight = harmonic(c, jnp.where(side == x, end_coef[1], end_coef[0]))
        up_y, up_z = weights[1 + x], weights[3 + x]
        down_y = jnp.where(row == 0, c, pltpu.roll(up_y, 1, 0))
        down_z = jnp.where(lane == 0, end_weight, pltpu.roll(up_z, 1, 1))
        up_z = jnp.where(lane == layers - 1, end_weight, up_z)
        above_y = jnp.where(row == rows - 1, 0.0, pltpu.roll(f, rows - 1, 0))
        below_y = jnp.where(row == 0, 0.0, pltpu.roll(f, 1, 0))
        above_z = jnp.where(lane == layers - 1, end_field, pltpu.roll(f, layers - 1, 1))
        below_z = jnp.where(lane == 0, end_field, pltpu.roll(f, 1, 1))
        image = (
            weights[0] * (f - field[1 - x])
            + faces[x] * (f - outside[x])
            + down_y * (f - below_y)
            + up_y * (f - above_y)
            + down_z * (f - below_z)
            + up_z * (f - above_z)
        )
        deflated[held[x]] = resid[held[x]] - image


def swapped(value, axis, first):
    count = lax.axis_size(axis)
    pairs = []
    for i in range(count):
        up = (i - first) % 2 == 0
        pairs.append((i, (i + 1) % count if up else (i - 1) % count))
    return lax.ppermute(value, axis, pairs)


def swapped_open(value, axis):
    count = lax.axis_size(axis)
    pairs = [(0, 0)] + [(i, i + 1 if i % 2 else i - 1) for i in range(1, count - 1)]
    return lax.ppermute(value, axis, pairs + [(count - 1, count - 1)])


def exchanged(value, axis, mask):
    return lax.ppermute(value, axis, [(i, i ^ mask) for i in range(lax.axis_size(axis))])


def gathered(value, axis):
    if lax.axis_size(axis) != 8:
        return [lax.all_gather(value, axis)]
    pair = jnp.stack([value, exchanged(value, axis, 1)])
    return [pair] + [exchanged(pair, axis, mask) for mask in (2, 4, 6)]


def body(labels, levels, zvec, resid):
    modes, planes, rows, layers = zvec.shape
    half = rows // 2
    subs, parts = lax.axis_size("sub"), lax.axis_size("pln")
    shape = jax.ShapeDtypeStruct
    order = lax.axis_index("sub") if subs == 8 else 0
    place = jnp.stack(
        [jnp.int32(v) for v in (lax.axis_index("sub"), lax.axis_index("pln"), parts, order)]
    )
    pack = shape((modes + 16, planes * rows), BF16)
    one_pack, two_pack, held = call(
        pack_kernel,
        [pack, pack, shape(zvec.shape, BF16)],
        [SMEM, HBM, HBM],
        [
            pltpu.VMEM(labels.shape, jnp.int32),
            pltpu.SemaphoreType.DMA,
            pltpu.SemaphoreType.DMA((modes // CHUNK,)),
        ],
        flops=10_000_000,
        moved=4 << 20,
    )(place, *(pltpu.with_memory_space_constraint(v, pltpu.HBM) for v in (labels, zvec)))
    one_got = swapped(one_pack, "sub", 0)
    two_got = swapped(two_pack, "sub", 1)
    send, rest = shape((half + 1, modes, layers), BF16), shape((half, modes, layers), BF16)
    inner_send, outer_send, inner_rest, outer_rest, here = call(
        prepare_kernel,
        [send, send, rest, rest, shape((planes, rows, modes, layers), BF16)],
        [SMEM, VMEM, VMEM],
        flops=1_000_000,
        moved=6 << 20,
    )(place, labels, held)
    outer_got = swapped_open(outer_send, "pln")
    inner_got = swapped(inner_send, "pln", 0)
    field = (planes, rows, layers)
    partial, weights = call(
        block_kernel,
        [shape((modes + 8, modes), F32), shape((7, rows, layers), F32)],
        [SMEM, SMEM] + [VMEM] * 3,
        [pltpu.VMEM(field, F32)] * 3,
        flops=400_000_000,
        moved=3 << 20,
    )(place, levels, labels, resid, here)
    block, faces = call(
        join_kernel,
        [shape((modes + 8, 2 * modes), F32), shape((2, rows, layers), F32)],
        [SMEM, SMEM] + [VMEM] * 10,
        flops=200_000_000,
        moved=2 << 20,
    )(
        place, levels, partial, weights, inner_rest, outer_rest, inner_got, outer_got, one_pack, two_pack,
        one_got, two_got,
    )
    if parts == 4:
        block, inner_rest, outer_rest = call(
            sum_kernel,
            [shape(block.shape, F32), rest, rest],
            [VMEM] * 4 + [ANY] * 2,
            aliases={4: 1, 5: 2},
        )(block, *(exchanged(block, "pln", mask) for mask in (1, 2, 3)), inner_rest, outer_rest)
    else:
        block = lax.psum(block, "pln")
    inner_last = swapped(inner_rest, "pln", 0)
    outer_last = swapped_open(outer_rest, "pln")
    blocks = gathered(block, "sub")
    return tuple(
        call(
            finish_kernel,
            [shape((1, modes), F32), shape(field, F32)],
            [SMEM, SMEM] + [VMEM] * (10 + len(blocks)),
            [
                pltpu.VMEM((subs, 2 * modes), F32),
                pltpu.VMEM((subs, 2 * modes), F32),
                pltpu.VMEM((modes, 128), F32),
                pltpu.VMEM((modes, layers), F32),
                pltpu.VMEM(field, F32),
                pltpu.VMEM(field, F32),
            ],
            flops=10_000_000,
            moved=5 << 20,
        )(
            place, levels, *blocks, held, inner_got, outer_got, inner_last, outer_last, one_got, two_got, weights,
            faces, resid,
        )
    )


def solution(mesh):
    in_specs = (P("pln", None, "sub"), P(), P(None, "pln", None, "sub"), P("pln", None, "sub"))
    out_specs = (P("sub", None), P("pln", None, "sub"))
    return jax.shard_map(body, mesh=mesh, in_specs=in_specs, out_specs=out_specs, check_vma=False)
```

```python
import jax
import jax.numpy as jnp
from jax import lax
from jax.experimental import pallas as pl
from jax.experimental.pallas import tpu as pltpu
from jax.sharding import PartitionSpec as P

CITERS = 2
STEP = 16
MODES = 8
CHUNK = 16
F32 = jnp.float32
BF16 = jnp.bfloat16
PRECISE = lax.Precision.HIGHEST
NT = (((1,), (1,)), ((), ()))
TN = (((0,), (0,)), ((), ()))
VMEM = pl.BlockSpec(memory_space=pltpu.VMEM)
SMEM = pl.BlockSpec(memory_space=pltpu.SMEM)
HBM = pl.BlockSpec(memory_space=pltpu.HBM)
ANY = pl.BlockSpec(memory_space=pl.ANY)


def call(kernel, outs, specs, scratch=(), flops=0, moved=0, limit=32, aliases=None):
    return pl.pallas_call(
        kernel,
        out_shape=outs,
        in_specs=specs,
        out_specs=[ANY if at in (aliases or {}).values() else VMEM for at in range(len(outs))],
        input_output_aliases=aliases or {},
        scratch_shapes=list(scratch),
        cost_estimate=pl.CostEstimate(flops=flops, bytes_accessed=moved, transcendentals=0),
        compiler_params=pltpu.CompilerParams(vmem_limit_bytes=limit << 20),
    )


def harmonic(left_value, right_value):
    return 2.0 * left_value * right_value / (left_value + right_value)


def coefficients(labels, levels_ref):
    weighted = jnp.zeros(labels.shape, F32)
    for level in range(levels_ref.shape[0]):
        weighted = weighted + jnp.where(labels == level, levels_ref[level], 0.0)
    return weighted


def lane_is(shape, lane):
    return lax.broadcasted_iota(jnp.int32, shape, len(shape) - 1) == lane


def pick_row(lane, width):
    row = lax.broadcasted_iota(jnp.int32, (16, width), 0)
    return ((row == 0) & lane_is((16, width), lane)).astype(BF16)


def stage_kernel(place, labels_far, zvec, inner_near, outer_near, labels, label_sem, sems):
    modes, planes, rows, layers = zvec.shape
    half = rows // 2
    side = lax.rem(place[1], 2)
    start = pl.multiple_of((1 - side) * half, half)
    label_copy = pltpu.make_async_copy(labels_far, labels, label_sem)
    copies = [
        pltpu.make_async_copy(
            zvec.at[:, plane, pl.ds(start, half), :], out.at[pl.ds(0, modes)], sems.at[slot]
        )
        for slot, plane, out in ((1, side, outer_near), (0, 1 - side, inner_near))
    ]
    label_copy.start()
    for copy in copies:
        copy.start()
    label_copy.wait()
    for plane, out in ((side, outer_near), (1 - side, inner_near)):
        out[modes:] = labels[plane].astype(F32).astype(BF16).reshape(rows // half, half, layers)
    for copy in copies:
        copy.wait()


def prepare_kernel(place, labels, held, planes_out, inner_rest, outer_rest, one_pack, two_pack):
    modes, planes, rows, layers = held.shape
    half = rows // 2
    width = planes * rows
    side = lax.rem(place[1], 2)
    odd = lax.rem(place[0], 2) == 1
    one_lane = jnp.where(odd, 0, layers - 1)
    two_lane = jnp.where(odd, layers - 1, 0)
    row = lax.broadcasted_iota(jnp.int32, (16, layers), 0)
    both = ((row == 0) & lane_is((16, layers), one_lane)) | ((row == 1) & lane_is((16, layers), two_lane))
    both = both.astype(BF16)
    flat = labels[...].astype(F32).astype(BF16).reshape(width, layers)
    for out, lane in ((one_pack, one_lane), (two_pack, two_lane)):
        out[modes:] = lax.dot_general(
            pick_row(lane, layers), flat, NT, preferred_element_type=F32
        ).astype(BF16)
    for k in range(0, modes, CHUNK):
        at = slice(k, k + CHUNK)
        ends = lax.dot_general(
            both, held[at].reshape(-1, layers), NT, preferred_element_type=F32
        )
        for out, index in ((one_pack, 0), (two_pack, 1)):
            out[at] = jnp.concatenate(
                [ends[index:index + 1, j * width:(j + 1) * width] for j in range(CHUNK)], axis=0
            ).astype(BF16)
        for slot, plane, rest in ((0, 1 - side, inner_rest), (1, side, outer_rest)):
            planes_out[slot, :, at, :] = jnp.swapaxes(held[at, plane], 0, 1)
            rest[at] = held[at, plane, pl.ds(pl.multiple_of(side * half, half), half), :]


def block_kernel(
    place, levels, labels, resid, here, partial, weights, half_diag, link_y, link_z,
):
    planes, rows, layers = labels.shape
    modes = here.shape[2]
    side = lax.rem(place[1], 2)
    at_edge = (place[1] == 0) | (place[1] == place[2] - 1)
    held = (1 - side, side)
    coef = [coefficients(labels[x], levels) for x in held]
    middle = harmonic(coef[0], coef[1])
    weights[0] = middle
    row = lax.broadcasted_iota(jnp.int32, (rows, layers), 0)
    lane = lax.broadcasted_iota(jnp.int32, (rows, layers), 1)
    for x in range(2):
        c = coef[x]
        up_y = harmonic(c, jnp.where(row == rows - 1, c, pltpu.roll(c, rows - 1, 0)))
        up_z = harmonic(c, pltpu.roll(c, layers - 1, 1))
        down_y = jnp.where(row == 0, c, pltpu.roll(up_y, 1, 0))
        weights[1 + x] = up_y
        weights[3 + x] = up_z
        weights[5 + x] = c
        inner_z = jnp.where(lane == layers - 1, 0.0, up_z)
        total = middle + up_y + down_y + inner_z + pltpu.roll(inner_z, 1, 1)
        if x == 1:
            total = total + jnp.where(at_edge, c, 0.0)
        half_diag[x] = 0.5 * total
        link_y[x] = jnp.where(row == rows - 1, 0.0, up_y)
        link_z[x] = inner_z

    def step(j, carry):
        total, rhs, wide = carry
        for u in range(STEP):
            y = j * STEP + u
            at = pl.ds(y, 1)
            ahead = jnp.minimum(y + 1, rows - 1)
            up = [here[x, ahead].astype(F32) for x in range(2)]
            images = []
            for x in range(2):
                image = (
                    half_diag[x, at, :] * wide[x]
                    - link_y[x, at, :] * up[x]
                    - link_z[x, at, :] * pltpu.roll(wide[x], layers - 1, 1)
                )
                if x == 0:
                    image = image - weights[0, at, :] * wide[1]
                rhs = rhs + resid[held[x], at, :] * wide[x]
                images.append(image.astype(BF16))
            total = total + lax.dot_general(
                jnp.concatenate(images, axis=1),
                jnp.concatenate([here[0, y], here[1, y]], axis=1),
                NT,
                preferred_element_type=F32,
            )
            wide = up
        return total, rhs, wide

    total, rhs, _ = lax.fori_loop(
        0,
        rows // STEP,
        step,
        (
            jnp.zeros((modes, modes), F32),
            jnp.zeros((modes, layers), F32),
            [here[x, 0].astype(F32) for x in range(2)],
        ),
    )
    partial[:modes, :] = total
    partial[modes:, :] = lax.dot_general(
        jnp.ones((8, layers), F32), rhs, NT, precision=PRECISE, preferred_element_type=F32
    )


def join_kernel(
    place, levels, partial, weights, here, inner_got, outer_got, one_pack, two_pack, one_got, two_got,
    out, faces, other_planes,
):
    planes, rows, modes, layers = here.shape
    half = rows // 2
    side = lax.rem(place[1], 2)
    odd = lax.rem(place[0], 2) == 1
    at_edge = (place[1] == 0) | (place[1] == place[2] - 1)
    base = side * half
    for slot, got in ((0, inner_got), (1, outer_got)):
        for k in range(0, modes, CHUNK):
            other_planes[slot, :, k:k + CHUNK, :] = jnp.swapaxes(got[k:k + CHUNK], 0, 1)
    inner_coef, outer_coef = (
        coefficients(got[modes:].astype(F32).reshape(rows, layers), levels)
        for got in (inner_got, outer_got)
    )
    faces[0] = harmonic(weights[5], inner_coef)
    faces[1] = jnp.where(at_edge, weights[6], harmonic(weights[6], outer_coef))

    def step(j, total):
        left, right = [], []
        for u in range(STEP):
            y = j * STEP + u
            at = pl.ds(base + y, 1)
            outer_weight = jnp.where(at_edge, 0.0, faces[1, at, :])
            for weight, own, other in (
                (faces[0, at, :], here[0, base + y], other_planes[0, y]),
                (outer_weight, here[1, base + y], other_planes[1, y]),
            ):
                image = weight * (own.astype(F32) - other.astype(F32))
                left.append(jnp.concatenate([own, other], axis=0))
                right.append(image.astype(BF16))
        return total + lax.dot_general(
            jnp.concatenate(left, axis=1), jnp.concatenate(right, axis=1), NT,
            preferred_element_type=F32,
        )

    cross = lax.fori_loop(0, half // STEP, step, jnp.zeros((2 * modes, modes), F32))
    cross = cross[:modes] - cross[modes:]

    def coef_row(pack):
        return coefficients(pack[modes:modes + 16].astype(F32)[0:1], levels)

    one, two = one_pack[...].astype(F32), two_pack[...].astype(F32)
    one_other, two_other = one_got[...].astype(F32), two_got[...].astype(F32)
    first, last = jnp.where(odd, one, two), jnp.where(odd, two, one)
    next_first = jnp.where(odd, two_other, one_other)
    prev_last = jnp.where(odd, one_other, two_other)
    weight_low = harmonic(coef_row(first), coef_row(prev_last))
    weight_high = harmonic(coef_row(last), coef_row(next_first))

    def product(left, right):
        return lax.dot_general(left, right, NT, precision=PRECISE, preferred_element_type=F32)

    edge_rows = weight_high * last[:modes]
    ends = product(weight_low * first[:modes], first[:modes]) + product(edge_rows, last[:modes])
    square = partial[:modes, :] + 0.5 * (cross + ends)
    square = square + square.T
    upper = -product(edge_rows, next_first[:modes])
    out[:modes, :modes] = square
    out[:modes, modes:] = upper
    out[modes:, :modes] = partial[modes:, :]
    out[modes:, modes:] = jnp.zeros((8, modes), F32)


def sum_kernel(own, one, two, three, inner_rest, outer_rest, out, inner_out, outer_out):
    out[...] = (own[...] + one[...]) + (two[...] + three[...])


def finish_kernel(place, levels, *refs):
    count = len(refs) - 18
    blocks, refs = refs[:count], refs[count:]
    zvec, inner_got, outer_got, inner_last, outer_last, one_got, two_got, weights, faces, resid = refs[:10]
    solution, deflated, direction_ref, image_ref, ahead_ref, spread, sides, ends_ref = refs[10:]
    subs = direction_ref.shape[0]
    modes, planes, rows, layers = zvec.shape
    half = rows // 2
    me = place[0]
    side = lax.rem(place[1], 2)
    odd = lax.rem(me, 2) == 1
    at_edge = (place[1] == 0) | (place[1] == place[2] - 1)
    order = place[3]
    held = (1 - side, side)
    square = (modes, modes)
    eye = lax.broadcasted_iota(jnp.int32, square, 0) == lax.broadcasted_iota(jnp.int32, square, 1)

    def column(row):
        return jnp.sum(jnp.where(eye, row, 0.0), axis=1, keepdims=True)

    def each(body):
        for index, block in enumerate(blocks):
            held_here = block.shape[0]
            if held_here <= 8:
                for entry in range(held_here):
                    body(block.at[entry], jnp.bitwise_xor(order, index * held_here + entry))
            else:
                pl.loop(0, held_here)(lambda entry, block=block: body(block.at[entry], entry))

    def load(block, s):
        direction_ref[pl.ds(s, 1), :] = block[modes:modes + 1, :]

    each(load)

    def turned(rows_of, by):
        by = by % subs
        return jnp.concatenate([rows_of[by:], rows_of[:by]], axis=0)

    def coarse_apply(direction):
        direction_ref[...] = jnp.concatenate([direction, turned(direction, 1)], axis=1)

        def one(block, s):
            values = block[:modes, :]
            pair = direction_ref[pl.ds(s, 1), :]
            ahead = jnp.sum(values * pair, axis=1, keepdims=True)
            ahead_ref[...] = jnp.where(lane_is((modes, 128), s), ahead, ahead_ref[...])
            image_ref[pl.ds(s, 1), :] = jnp.sum(
                values * column(pair[:, :modes]), axis=0, keepdims=True
            )

        each(one)
        return ahead_ref[...].T[:subs] + turned(image_ref[:, modes:], -1)

    def inner(left, right):
        return jnp.sum(jnp.sum(left * right, axis=0, keepdims=True), axis=1, keepdims=True)

    remain = direction_ref[:, :modes]
    direction = remain
    result = jnp.zeros_like(remain)
    norm_now = inner(remain, remain)
    for iteration in range(CITERS):
        image = coarse_apply(direction)
        step_size = norm_now / inner(direction, image)
        result = result + step_size * direction
        if iteration + 1 < CITERS:
            remain = remain - step_size * image
            norm_next = inner(remain, remain)
            direction = remain + (norm_next / norm_now) * direction
            norm_now = norm_next
    direction_ref[:, :modes] = result
    own = direction_ref[pl.ds(me, 1), :modes]
    solution[...] = own
    spread[...] = jnp.broadcast_to(column(own), (modes, layers))
    ahead_column = column(direction_ref[pl.ds(lax.rem(me + 1, subs), 1), :modes])
    behind_column = column(direction_ref[pl.ds(lax.rem(me + subs - 1, subs), 1), :modes])
    at_top = lane_is((modes, layers), layers - 1)
    at_bottom = lane_is((modes, layers), 0)

    def placed(pack, values, precision):
        return lax.dot_general(pack, values, TN, precision=precision, preferred_element_type=F32)

    one_other, two_other = one_got[...].astype(F32), two_got[...].astype(F32)
    next_first = jnp.where(odd, two_other, one_other)
    prev_last = jnp.where(odd, one_other, two_other)
    ends_ref[...] = (
        placed(next_first[:modes], jnp.where(at_top, ahead_column, 0.0), PRECISE)
        + placed(prev_last[:modes], jnp.where(at_bottom, behind_column, 0.0), PRECISE)
    ).reshape(planes, rows, layers)
    end_coef = coefficients(
        placed(next_first[modes:].astype(BF16), pick_row(layers - 1, layers), None)
        + placed(prev_last[modes:].astype(BF16), pick_row(0, layers), None),
        levels,
    ).reshape(planes, rows, layers)

    others = (inner_got, inner_last, outer_got, outer_last)

    def add_mode(j, carry):
        fields, edges = list(carry[0]), list(carry[1])
        for u in range(MODES):
            k = j * MODES + u
            scale = spread[pl.ds(k, 1), :]
            for x in range(2):
                fields[x] = fields[x] + scale * zvec[k, held[x]].astype(F32)
            for index, other in enumerate(others):
                edges[index] = edges[index] + scale * other[k].astype(F32)
        return tuple(fields), tuple(edges)

    zero, short = jnp.zeros((rows, layers), F32), jnp.zeros((half, layers), F32)
    field, edges = lax.fori_loop(0, modes // MODES, add_mode, ((zero, zero), (short,) * 4))
    for slot in range(2):
        sides[slot, pl.ds(pl.multiple_of(side * half, half), half), :] = edges[2 * slot]
        sides[slot, pl.ds(pl.multiple_of((1 - side) * half, half), half), :] = edges[2 * slot + 1]
    row = lax.broadcasted_iota(jnp.int32, (rows, layers), 0)
    lane = lax.broadcasted_iota(jnp.int32, (rows, layers), 1)
    outside = (sides[0], jnp.where(at_edge, 0.0, sides[1]))
    for x in range(2):
        f = field[x]
        c = weights[5 + x]
        end_field = ends_ref[held[x]]
        end_weight = harmonic(c, jnp.where(side == x, end_coef[1], end_coef[0]))
        up_y, up_z = weights[1 + x], weights[3 + x]
        down_y = jnp.where(row == 0, c, pltpu.roll(up_y, 1, 0))
        down_z = jnp.where(lane == 0, end_weight, pltpu.roll(up_z, 1, 1))
        up_z = jnp.where(lane == layers - 1, end_weight, up_z)
        above_y = jnp.where(row == rows - 1, 0.0, pltpu.roll(f, rows - 1, 0))
        below_y = jnp.where(row == 0, 0.0, pltpu.roll(f, 1, 0))
        above_z = jnp.where(lane == layers - 1, end_field, pltpu.roll(f, layers - 1, 1))
        below_z = jnp.where(lane == 0, end_field, pltpu.roll(f, 1, 1))
        image = (
            weights[0] * (f - field[1 - x])
            + faces[x] * (f - outside[x])
            + down_y * (f - below_y)
            + up_y * (f - above_y)
            + down_z * (f - below_z)
            + up_z * (f - above_z)
        )
        deflated[held[x]] = resid[held[x]] - image


def swapped(value, axis, first):
    count = lax.axis_size(axis)
    pairs = []
    for i in range(count):
        up = (i - first) % 2 == 0
        pairs.append((i, (i + 1) % count if up else (i - 1) % count))
    return lax.ppermute(value, axis, pairs)


def swapped_open(value):
    subs, count = lax.axis_size("sub"), lax.axis_size("pln")
    pairs = []
    for s in range(subs):
        for i in range(count):
            if 0 < i < count - 1:
                to = (s, i + 1 if i % 2 else i - 1)
            else:
                to = (s ^ 1, i)
            pairs.append((s * count + i, to[0] * count + to[1]))
    return lax.ppermute(value, ("sub", "pln"), pairs)


def exchanged(value, axis, mask):
    return lax.ppermute(value, axis, [(i, i ^ mask) for i in range(lax.axis_size(axis))])


def gathered(value, axis):
    if lax.axis_size(axis) != 8:
        return [lax.all_gather(value, axis)]
    pair = jnp.stack([value, exchanged(value, axis, 1)])
    return [pair] + [exchanged(pair, axis, mask) for mask in (2, 4, 6)]


def body(labels, levels, zvec, resid):
    modes, planes, rows, layers = zvec.shape
    half = rows // 2
    subs, parts = lax.axis_size("sub"), lax.axis_size("pln")
    shape = jax.ShapeDtypeStruct
    order = lax.axis_index("sub") if subs == 8 else 0
    place = jnp.stack(
        [jnp.int32(v) for v in (lax.axis_index("sub"), lax.axis_index("pln"), parts, order)]
    )
    pack = shape((modes + 16, planes * rows), BF16)
    near = shape((modes + rows // half, half, layers), BF16)
    inner_near, outer_near = call(
        stage_kernel,
        [near, near],
        [SMEM, HBM, HBM],
        [pltpu.VMEM(labels.shape, jnp.int32), pltpu.SemaphoreType.DMA, pltpu.SemaphoreType.DMA((2,))],
        moved=2 << 20,
    )(place, *(pltpu.with_memory_space_constraint(v, pltpu.HBM) for v in (labels, zvec)))
    outer_got = swapped_open(outer_near)
    inner_got = swapped(inner_near, "pln", 0)
    rest = shape((modes, half, layers), BF16)
    here, inner_rest, outer_rest, one_pack, two_pack = call(
        prepare_kernel,
        [shape((planes, rows, modes, layers), BF16), rest, rest, pack, pack],
        [SMEM, VMEM, VMEM],
        flops=10_000_000,
        moved=6 << 20,
    )(place, labels, zvec)
    one_got = swapped(one_pack, "sub", 0)
    two_got = swapped(two_pack, "sub", 1)
    field = (planes, rows, layers)
    partial, weights = call(
        block_kernel,
        [shape((modes + 8, modes), F32), shape((7, rows, layers), F32)],
        [SMEM, SMEM] + [VMEM] * 3,
        [pltpu.VMEM(field, F32)] * 3,
        flops=400_000_000,
        moved=3 << 20,
    )(place, levels, labels, resid, here)
    block, faces = call(
        join_kernel,
        [shape((modes + 8, 2 * modes), F32), shape((2, rows, layers), F32)],
        [SMEM, SMEM] + [VMEM] * 9,
        [pltpu.VMEM((planes, half, modes, layers), BF16)],
        flops=200_000_000,
        moved=2 << 20,
    )(
        place, levels, partial, weights, here, inner_got, outer_got, one_pack, two_pack, one_got, two_got
    )
    if parts == 4:
        block, inner_rest, outer_rest = call(
            sum_kernel,
            [shape(block.shape, F32), rest, rest],
            [VMEM] * 4 + [ANY] * 2,
            aliases={4: 1, 5: 2},
        )(block, *(exchanged(block, "pln", mask) for mask in (1, 2, 3)), inner_rest, outer_rest)
    else:
        block = lax.psum(block, "pln")
    inner_last = swapped(inner_rest, "pln", 0)
    outer_last = swapped_open(outer_rest)
    blocks = gathered(block, "sub")
    return tuple(
        call(
            finish_kernel,
            [shape((1, modes), F32), shape(field, F32)],
            [SMEM, SMEM] + [VMEM] * (10 + len(blocks)),
            [
                pltpu.VMEM((subs, 2 * modes), F32),
                pltpu.VMEM((subs, 2 * modes), F32),
                pltpu.VMEM((modes, 128), F32),
                pltpu.VMEM((modes, layers), F32),
                pltpu.VMEM(field, F32),
                pltpu.VMEM(field, F32),
            ],
            flops=10_000_000,
            moved=5 << 20,
        )(
            place, levels, *blocks, zvec, inner_got, outer_got, inner_last, outer_last, one_got, two_got, weights,
            faces, resid,
        )
    )


def solution(mesh):
    in_specs = (P("pln", None, "sub"), P(), P(None, "pln", None, "sub"), P("pln", None, "sub"))
    out_specs = (P("sub", None), P("pln", None, "sub"))
    return jax.shard_map(body, mesh=mesh, in_specs=in_specs, out_specs=out_specs, check_vma=False)
```

```python
import jax
import jax.numpy as jnp
from jax import lax
from jax.experimental import pallas as pl
from jax.experimental.pallas import tpu as pltpu
from jax.sharding import PartitionSpec as P

CITERS = 2
STEP = 16
MODES = 8
CHUNK = 16
F32 = jnp.float32
BF16 = jnp.bfloat16
PRECISE = lax.Precision.HIGHEST
NT = (((1,), (1,)), ((), ()))
TN = (((0,), (0,)), ((), ()))
VMEM = pl.BlockSpec(memory_space=pltpu.VMEM)
SMEM = pl.BlockSpec(memory_space=pltpu.SMEM)
HBM = pl.BlockSpec(memory_space=pltpu.HBM)
ANY = pl.BlockSpec(memory_space=pl.ANY)


def call(kernel, outs, specs, scratch=(), flops=0, moved=0, limit=32, aliases=None):
    return pl.pallas_call(
        kernel,
        out_shape=outs,
        in_specs=specs,
        out_specs=[ANY if at in (aliases or {}).values() else VMEM for at in range(len(outs))],
        input_output_aliases=aliases or {},
        scratch_shapes=list(scratch),
        cost_estimate=pl.CostEstimate(flops=flops, bytes_accessed=moved, transcendentals=0),
        compiler_params=pltpu.CompilerParams(vmem_limit_bytes=limit << 20),
    )


def harmonic(left_value, right_value):
    return 2.0 * left_value * right_value / (left_value + right_value)


def coefficients(labels, levels_ref):
    weighted = jnp.zeros(labels.shape, F32)
    for level in range(levels_ref.shape[0]):
        weighted = weighted + jnp.where(labels == level, levels_ref[level], 0.0)
    return weighted


def lane_is(shape, lane):
    return lax.broadcasted_iota(jnp.int32, shape, len(shape) - 1) == lane


def pick_row(lane, width):
    row = lax.broadcasted_iota(jnp.int32, (16, width), 0)
    return ((row == 0) & lane_is((16, width), lane)).astype(BF16)


def stage_kernel(place, labels_far, zvec, outer_near, labels, label_sem, sem):
    modes, planes, rows, layers = zvec.shape
    half = rows // 2
    side = lax.rem(place[1], 2)
    start = pl.multiple_of((1 - side) * half, half)
    label_copy = pltpu.make_async_copy(labels_far, labels, label_sem)
    copy = pltpu.make_async_copy(
        zvec.at[:, side, pl.ds(start, half), :], outer_near.at[pl.ds(0, modes)], sem
    )
    copy.start()
    label_copy.start()
    label_copy.wait()
    outer_near[modes:] = labels[side].astype(F32).astype(BF16).reshape(rows // half, half, layers)
    copy.wait()


def prepare_kernel(place, labels, held, staged, planes_out, inner_near, one_pack, two_pack):
    modes, planes, rows, layers = held.shape
    half = rows // 2
    width = planes * rows
    side = lax.rem(place[1], 2)
    odd = lax.rem(place[0], 2) == 1
    one_lane = jnp.where(odd, 0, layers - 1)
    two_lane = jnp.where(odd, layers - 1, 0)
    row = lax.broadcasted_iota(jnp.int32, (16, layers), 0)
    both = ((row == 0) & lane_is((16, layers), one_lane)) | ((row == 1) & lane_is((16, layers), two_lane))
    both = both.astype(BF16)
    flat = labels[...].astype(F32).astype(BF16).reshape(width, layers)
    for out, lane in ((one_pack, one_lane), (two_pack, two_lane)):
        out[modes:] = lax.dot_general(
            pick_row(lane, layers), flat, NT, preferred_element_type=F32
        ).astype(BF16)
    for k in range(0, modes, CHUNK):
        at = slice(k, k + CHUNK)
        ends = lax.dot_general(
            both, held[at].reshape(-1, layers), NT, preferred_element_type=F32
        )
        for out, index in ((one_pack, 0), (two_pack, 1)):
            out[at] = jnp.concatenate(
                [ends[index:index + 1, j * width:(j + 1) * width] for j in range(CHUNK)], axis=0
            ).astype(BF16)
        for slot, plane in ((0, 1 - side), (1, side)):
            planes_out[slot, :, at, :] = jnp.swapaxes(held[at, plane], 0, 1)
        inner_near[at] = held[at, 1 - side, pl.ds(pl.multiple_of((1 - side) * half, half), half), :]
    inner_near[modes:] = (
        labels[1 - side].astype(F32).astype(BF16).reshape(rows // half, half, layers)
    )


def block_kernel(
    place, levels, labels, resid, here, partial, weights, half_diag, link_y, link_z,
):
    planes, rows, layers = labels.shape
    modes = here.shape[2]
    side = lax.rem(place[1], 2)
    at_edge = (place[1] == 0) | (place[1] == place[2] - 1)
    held = (1 - side, side)
    coef = [coefficients(labels[x], levels) for x in held]
    middle = harmonic(coef[0], coef[1])
    weights[0] = middle
    row = lax.broadcasted_iota(jnp.int32, (rows, layers), 0)
    lane = lax.broadcasted_iota(jnp.int32, (rows, layers), 1)
    for x in range(2):
        c = coef[x]
        up_y = harmonic(c, jnp.where(row == rows - 1, c, pltpu.roll(c, rows - 1, 0)))
        up_z = harmonic(c, pltpu.roll(c, layers - 1, 1))
        down_y = jnp.where(row == 0, c, pltpu.roll(up_y, 1, 0))
        weights[1 + x] = up_y
        weights[3 + x] = up_z
        weights[5 + x] = c
        inner_z = jnp.where(lane == layers - 1, 0.0, up_z)
        total = middle + up_y + down_y + inner_z + pltpu.roll(inner_z, 1, 1)
        if x == 1:
            total = total + jnp.where(at_edge, c, 0.0)
        half_diag[x] = 0.5 * total
        link_y[x] = jnp.where(row == rows - 1, 0.0, up_y)
        link_z[x] = inner_z

    def step(j, carry):
        total, rhs, wide = carry
        for u in range(STEP):
            y = j * STEP + u
            at = pl.ds(y, 1)
            ahead = jnp.minimum(y + 1, rows - 1)
            up = [here[x, ahead].astype(F32) for x in range(2)]
            images = []
            for x in range(2):
                image = (
                    half_diag[x, at, :] * wide[x]
                    - link_y[x, at, :] * up[x]
                    - link_z[x, at, :] * pltpu.roll(wide[x], layers - 1, 1)
                )
                if x == 0:
                    image = image - weights[0, at, :] * wide[1]
                rhs = rhs + resid[held[x], at, :] * wide[x]
                images.append(image.astype(BF16))
            total = total + lax.dot_general(
                jnp.concatenate(images, axis=1),
                jnp.concatenate([here[0, y], here[1, y]], axis=1),
                NT,
                preferred_element_type=F32,
            )
            wide = up
        return total, rhs, wide

    total, rhs, _ = lax.fori_loop(
        0,
        rows // STEP,
        step,
        (
            jnp.zeros((modes, modes), F32),
            jnp.zeros((modes, layers), F32),
            [here[x, 0].astype(F32) for x in range(2)],
        ),
    )
    partial[:modes, :] = total
    partial[modes:, :] = lax.dot_general(
        jnp.ones((8, layers), F32), rhs, NT, precision=PRECISE, preferred_element_type=F32
    )


def join_kernel(
    place, levels, partial, weights, here, inner_got, outer_got, one_pack, two_pack, one_got, two_got,
    out, faces, other_planes,
):
    planes, rows, modes, layers = here.shape
    half = rows // 2
    side = lax.rem(place[1], 2)
    odd = lax.rem(place[0], 2) == 1
    at_edge = (place[1] == 0) | (place[1] == place[2] - 1)
    base = side * half
    for slot, got in ((0, inner_got), (1, outer_got)):
        for k in range(0, modes, CHUNK):
            other_planes[slot, :, k:k + CHUNK, :] = jnp.swapaxes(got[k:k + CHUNK], 0, 1)
    inner_coef, outer_coef = (
        coefficients(got[modes:].astype(F32).reshape(rows, layers), levels)
        for got in (inner_got, outer_got)
    )
    faces[0] = harmonic(weights[5], inner_coef)
    faces[1] = jnp.where(at_edge, weights[6], harmonic(weights[6], outer_coef))

    def step(j, total):
        left, right = [], []
        for u in range(STEP):
            y = j * STEP + u
            at = pl.ds(base + y, 1)
            outer_weight = jnp.where(at_edge, 0.0, faces[1, at, :])
            for weight, own, other in (
                (faces[0, at, :], here[0, base + y], other_planes[0, y]),
                (outer_weight, here[1, base + y], other_planes[1, y]),
            ):
                image = weight * (own.astype(F32) - other.astype(F32))
                left.append(jnp.concatenate([own, other], axis=0))
                right.append(image.astype(BF16))
        return total + lax.dot_general(
            jnp.concatenate(left, axis=1), jnp.concatenate(right, axis=1), NT,
            preferred_element_type=F32,
        )

    cross = lax.fori_loop(0, half // STEP, step, jnp.zeros((2 * modes, modes), F32))
    cross = cross[:modes] - cross[modes:]

    def coef_row(pack):
        return coefficients(pack[modes:modes + 16].astype(F32)[0:1], levels)

    one, two = one_pack[...].astype(F32), two_pack[...].astype(F32)
    one_other, two_other = one_got[...].astype(F32), two_got[...].astype(F32)
    first, last = jnp.where(odd, one, two), jnp.where(odd, two, one)
    next_first = jnp.where(odd, two_other, one_other)
    prev_last = jnp.where(odd, one_other, two_other)
    weight_low = harmonic(coef_row(first), coef_row(prev_last))
    weight_high = harmonic(coef_row(last), coef_row(next_first))

    def product(left, right):
        return lax.dot_general(left, right, NT, precision=PRECISE, preferred_element_type=F32)

    edge_rows = weight_high * last[:modes]
    ends = product(weight_low * first[:modes], first[:modes]) + product(edge_rows, last[:modes])
    square = partial[:modes, :] + 0.5 * (cross + ends)
    square = square + square.T
    upper = -product(edge_rows, next_first[:modes])
    out[:modes, :modes] = square
    out[:modes, modes:] = upper
    out[modes:, :modes] = partial[modes:, :]
    out[modes:, modes:] = jnp.zeros((8, modes), F32)


def solve_kernel(place, *refs):
    count = len(refs) - 9
    blocks, refs = refs[:count], refs[count:]
    zvec, solution, beside, inner_field, outer_field, direction_ref, image_ref, ahead_ref, spread = refs
    subs = direction_ref.shape[0]
    modes, planes, rows, layers = zvec.shape
    me = place[0]
    side = lax.rem(place[1], 2)
    order = place[3]
    held = (1 - side, side)
    square = (modes, modes)
    eye = lax.broadcasted_iota(jnp.int32, square, 0) == lax.broadcasted_iota(jnp.int32, square, 1)

    def column(row):
        return jnp.sum(jnp.where(eye, row, 0.0), axis=1, keepdims=True)

    def each(body):
        for index, block in enumerate(blocks):
            held_here = block.shape[0]
            if held_here <= 8:
                for entry in range(held_here):
                    body(block.at[entry], jnp.bitwise_xor(order, index * held_here + entry))
            else:
                pl.loop(0, held_here)(lambda entry, block=block: body(block.at[entry], entry))

    def load(block, s):
        direction_ref[pl.ds(s, 1), :] = block[modes:modes + 1, :]

    each(load)

    def turned(rows_of, by):
        by = by % subs
        return jnp.concatenate([rows_of[by:], rows_of[:by]], axis=0)

    def coarse_apply(direction):
        direction_ref[...] = jnp.concatenate([direction, turned(direction, 1)], axis=1)

        def one(block, s):
            values = block[:modes, :]
            pair = direction_ref[pl.ds(s, 1), :]
            ahead = jnp.sum(values * pair, axis=1, keepdims=True)
            ahead_ref[...] = jnp.where(lane_is((modes, 128), s), ahead, ahead_ref[...])
            image_ref[pl.ds(s, 1), :] = jnp.sum(
                values * column(pair[:, :modes]), axis=0, keepdims=True
            )

        each(one)
        return ahead_ref[...].T[:subs] + turned(image_ref[:, modes:], -1)

    def inner(left, right):
        return jnp.sum(jnp.sum(left * right, axis=0, keepdims=True), axis=1, keepdims=True)

    remain = direction_ref[:, :modes]
    direction = remain
    result = jnp.zeros_like(remain)
    norm_now = inner(remain, remain)
    for iteration in range(CITERS):
        image = coarse_apply(direction)
        step_size = norm_now / inner(direction, image)
        result = result + step_size * direction
        if iteration + 1 < CITERS:
            remain = remain - step_size * image
            norm_next = inner(remain, remain)
            direction = remain + (norm_next / norm_now) * direction
            norm_now = norm_next
    direction_ref[:, :modes] = result
    own = direction_ref[pl.ds(me, 1), :modes]
    solution[...] = own
    spread[...] = jnp.broadcast_to(column(own), (modes, layers))
    beside[0:1, :] = direction_ref[pl.ds(lax.rem(me + 1, subs), 1), :modes]
    beside[1:2, :] = direction_ref[pl.ds(lax.rem(me + subs - 1, subs), 1), :modes]

    def add_mode(j, carry):
        fields = list(carry)
        for u in range(MODES):
            k = j * MODES + u
            scale = spread[pl.ds(k, 1), :]
            for x in range(2):
                fields[x] = fields[x] + scale * zvec[k, held[x]].astype(F32)
        return tuple(fields)

    zero = jnp.zeros((rows, layers), F32)
    inner_field[...], outer_field[...] = lax.fori_loop(0, modes // MODES, add_mode, (zero, zero))


def stencil_kernel(
    place, levels, beside, inner_field, outer_field, one_got, two_got, weights, faces, resid, inside,
    ends_ref,
):
    rows, layers = inner_field.shape
    planes = resid.shape[0]
    modes = beside.shape[1]
    side = lax.rem(place[1], 2)
    odd = lax.rem(place[0], 2) == 1
    held = (1 - side, side)
    square = (modes, modes)
    eye = lax.broadcasted_iota(jnp.int32, square, 0) == lax.broadcasted_iota(jnp.int32, square, 1)

    def column(row):
        return jnp.sum(jnp.where(eye, row, 0.0), axis=1, keepdims=True)

    ahead_column = column(beside[0:1, :])
    behind_column = column(beside[1:2, :])
    at_top = lane_is((modes, layers), layers - 1)
    at_bottom = lane_is((modes, layers), 0)

    def placed(pack, values, precision):
        return lax.dot_general(pack, values, TN, precision=precision, preferred_element_type=F32)

    one_other, two_other = one_got[...].astype(F32), two_got[...].astype(F32)
    next_first = jnp.where(odd, two_other, one_other)
    prev_last = jnp.where(odd, one_other, two_other)
    ends_ref[...] = (
        placed(next_first[:modes], jnp.where(at_top, ahead_column, 0.0), PRECISE)
        + placed(prev_last[:modes], jnp.where(at_bottom, behind_column, 0.0), PRECISE)
    ).reshape(planes, rows, layers)
    end_coef = coefficients(
        placed(next_first[modes:].astype(BF16), pick_row(layers - 1, layers), None)
        + placed(prev_last[modes:].astype(BF16), pick_row(0, layers), None),
        levels,
    ).reshape(planes, rows, layers)
    field = (inner_field[...], outer_field[...])
    row = lax.broadcasted_iota(jnp.int32, (rows, layers), 0)
    lane = lax.broadcasted_iota(jnp.int32, (rows, layers), 1)
    for x in range(2):
        f = field[x]
        c = weights[5 + x]
        end_field = ends_ref[held[x]]
        end_weight = harmonic(c, jnp.where(side == x, end_coef[1], end_coef[0]))
        up_y, up_z = weights[1 + x], weights[3 + x]
        down_y = jnp.where(row == 0, c, pltpu.roll(up_y, 1, 0))
        down_z = jnp.where(lane == 0, end_weight, pltpu.roll(up_z, 1, 1))
        up_z = jnp.where(lane == layers - 1, end_weight, up_z)
        above_y = jnp.where(row == rows - 1, 0.0, pltpu.roll(f, rows - 1, 0))
        below_y = jnp.where(row == 0, 0.0, pltpu.roll(f, 1, 0))
        above_z = jnp.where(lane == layers - 1, end_field, pltpu.roll(f, layers - 1, 1))
        below_z = jnp.where(lane == 0, end_field, pltpu.roll(f, 1, 1))
        image = (
            weights[0] * (f - field[1 - x])
            + faces[x] * f
            + down_y * (f - below_y)
            + up_y * (f - above_y)
            + down_z * (f - below_z)
            + up_z * (f - above_z)
        )
        inside[x] = resid[held[x]] - image


def outside_kernel(place, inside, faces, inner_got, outer_got, deflated):
    side = lax.rem(place[1], 2)
    at_edge = (place[1] == 0) | (place[1] == place[2] - 1)
    deflated[1 - side] = inside[0] + faces[0] * inner_got[...]
    deflated[side] = inside[1] + jnp.where(at_edge, 0.0, faces[1] * outer_got[...])


def swapped(value, axis, first):
    count = lax.axis_size(axis)
    pairs = []
    for i in range(count):
        up = (i - first) % 2 == 0
        pairs.append((i, (i + 1) % count if up else (i - 1) % count))
    return lax.ppermute(value, axis, pairs)


def swapped_open(value):
    subs, count = lax.axis_size("sub"), lax.axis_size("pln")
    pairs = []
    for s in range(subs):
        for i in range(count):
            if 0 < i < count - 1:
                to = (s, i + 1 if i % 2 else i - 1)
            else:
                to = (s ^ 1, i)
            pairs.append((s * count + i, to[0] * count + to[1]))
    return lax.ppermute(value, ("sub", "pln"), pairs)


def exchanged(value, axis, mask):
    return lax.ppermute(value, axis, [(i, i ^ mask) for i in range(lax.axis_size(axis))])


def summed(value, axis):
    if lax.axis_size(axis) != 4:
        return lax.psum(value, axis)
    one, two, three = (exchanged(value, axis, mask) for mask in (1, 2, 3))
    return (value + one) + (two + three)


def gathered(value, axis):
    if lax.axis_size(axis) != 8:
        return [lax.all_gather(value, axis)]
    pair = jnp.stack([value, exchanged(value, axis, 1)])
    return [pair] + [exchanged(pair, axis, mask) for mask in (2, 4, 6)]


def body(labels, levels, zvec, resid):
    modes, planes, rows, layers = zvec.shape
    half = rows // 2
    subs, parts = lax.axis_size("sub"), lax.axis_size("pln")
    shape = jax.ShapeDtypeStruct
    order = lax.axis_index("sub") if subs == 8 else 0
    place = jnp.stack(
        [jnp.int32(v) for v in (lax.axis_index("sub"), lax.axis_index("pln"), parts, order)]
    )
    pack = shape((modes + 16, planes * rows), BF16)
    near = shape((modes + rows // half, half, layers), BF16)
    [outer_near] = call(
        stage_kernel,
        [near],
        [SMEM, HBM, HBM],
        [pltpu.VMEM(labels.shape, jnp.int32), pltpu.SemaphoreType.DMA, pltpu.SemaphoreType.DMA],
        moved=1 << 20,
    )(place, *(pltpu.with_memory_space_constraint(v, pltpu.HBM) for v in (labels, zvec)))
    outer_got = swapped_open(outer_near)
    here, inner_near, one_pack, two_pack = call(
        prepare_kernel,
        [shape((planes, rows, modes, layers), BF16), near, pack, pack],
        [SMEM, VMEM, VMEM, ANY],
        flops=10_000_000,
        moved=6 << 20,
    )(place, labels, zvec, outer_near)
    inner_got = swapped(inner_near, "pln", 0)
    one_got = swapped(one_pack, "sub", 0)
    two_got = swapped(two_pack, "sub", 1)
    field = (planes, rows, layers)
    partial, weights = call(
        block_kernel,
        [shape((modes + 8, modes), F32), shape((7, rows, layers), F32)],
        [SMEM, SMEM] + [VMEM] * 3,
        [pltpu.VMEM(field, F32)] * 3,
        flops=400_000_000,
        moved=3 << 20,
    )(place, levels, labels, resid, here)
    block, faces = call(
        join_kernel,
        [shape((modes + 8, 2 * modes), F32), shape((2, rows, layers), F32)],
        [SMEM, SMEM] + [VMEM] * 9,
        [pltpu.VMEM((planes, half, modes, layers), BF16)],
        flops=200_000_000,
        moved=2 << 20,
    )(
        place, levels, partial, weights, here, inner_got, outer_got, one_pack, two_pack, one_got, two_got
    )
    blocks = gathered(summed(block, "pln"), "sub")
    plane = shape((rows, layers), F32)
    solved, beside, inner_field, outer_field = call(
        solve_kernel,
        [shape((1, modes), F32), shape((2, modes), F32), plane, plane],
        [SMEM] + [VMEM] * (1 + len(blocks)),
        [
            pltpu.VMEM((subs, 2 * modes), F32),
            pltpu.VMEM((subs, 2 * modes), F32),
            pltpu.VMEM((modes, 128), F32),
            pltpu.VMEM((modes, layers), F32),
        ],
        flops=10_000_000,
        moved=5 << 20,
    )(place, *blocks, zvec)
    inner_beside = swapped(inner_field, "pln", 0)
    outer_beside = swapped(outer_field, "pln", 1)
    [inside] = call(
        stencil_kernel,
        [shape(field, F32)],
        [SMEM, SMEM] + [VMEM] * 8,
        [pltpu.VMEM(field, F32)],
        flops=10_000_000,
        moved=1 << 20,
    )(place, levels, beside, inner_field, outer_field, one_got, two_got, weights, faces, resid)
    [deflated] = call(outside_kernel, [shape(field, F32)], [SMEM] + [VMEM] * 4, moved=1 << 18)(
        place, inside, faces, inner_beside, outer_beside
    )
    return solved, deflated


def solution(mesh):
    in_specs = (P("pln", None, "sub"), P(), P(None, "pln", None, "sub"), P("pln", None, "sub"))
    out_specs = (P("sub", None), P("pln", None, "sub"))
    return jax.shard_map(body, mesh=mesh, in_specs=in_specs, out_specs=out_specs, check_vma=False)
```

```python
import jax
import jax.numpy as jnp
from jax import lax
from jax.experimental import pallas as pl
from jax.experimental.pallas import tpu as pltpu
from jax.sharding import PartitionSpec as P

CITERS = 2
STEP = 16
MODES = 8
CHUNK = 16
F32 = jnp.float32
BF16 = jnp.bfloat16
PRECISE = lax.Precision.HIGHEST
NT = (((1,), (1,)), ((), ()))
TN = (((0,), (0,)), ((), ()))
VMEM = pl.BlockSpec(memory_space=pltpu.VMEM)
SMEM = pl.BlockSpec(memory_space=pltpu.SMEM)
HBM = pl.BlockSpec(memory_space=pltpu.HBM)
ANY = pl.BlockSpec(memory_space=pl.ANY)


def call(kernel, outs, specs, scratch=(), flops=0, moved=0, limit=32, aliases=None):
    return pl.pallas_call(
        kernel,
        out_shape=outs,
        in_specs=specs,
        out_specs=[ANY if at in (aliases or {}).values() else VMEM for at in range(len(outs))],
        input_output_aliases=aliases or {},
        scratch_shapes=list(scratch),
        cost_estimate=pl.CostEstimate(flops=flops, bytes_accessed=moved, transcendentals=0),
        compiler_params=pltpu.CompilerParams(vmem_limit_bytes=limit << 20),
    )


def harmonic(left_value, right_value):
    return 2.0 * left_value * right_value / (left_value + right_value)


def coefficients(labels, levels_ref):
    weighted = jnp.zeros(labels.shape, F32)
    for level in range(levels_ref.shape[0]):
        weighted = weighted + jnp.where(labels == level, levels_ref[level], 0.0)
    return weighted


def lane_is(shape, lane):
    return lax.broadcasted_iota(jnp.int32, shape, len(shape) - 1) == lane


def pick_row(lane, width):
    row = lax.broadcasted_iota(jnp.int32, (16, width), 0)
    return ((row == 0) & lane_is((16, width), lane)).astype(BF16)


def stage_kernel(place, labels_far, zvec, inner_send, outer_near, labels, label_sem, sems):
    modes, planes, rows, layers = zvec.shape
    half = rows // 2
    side = lax.rem(place[1], 2)
    start = pl.multiple_of((1 - side) * half, half)
    label_copy = pltpu.make_async_copy(labels_far, labels, label_sem)
    copies = [
        pltpu.make_async_copy(
            zvec.at[:, side, pl.ds(start, half), :], outer_near.at[pl.ds(0, modes)], sems.at[0]
        ),
        pltpu.make_async_copy(zvec.at[:, 1 - side], inner_send.at[pl.ds(0, modes)], sems.at[1]),
    ]
    label_copy.start()
    for copy in copies:
        copy.start()
    label_copy.wait()
    outer_near[modes:] = labels[side].astype(F32).astype(BF16).reshape(rows // half, half, layers)
    inner_send[modes] = labels[1 - side].astype(F32).astype(BF16)
    for copy in copies:
        copy.wait()


def prepare_kernel(place, labels, held, planes_out, outer_rest, one_pack, two_pack):
    modes, planes, rows, layers = held.shape
    half = rows // 2
    width = planes * rows
    side = lax.rem(place[1], 2)
    odd = lax.rem(place[0], 2) == 1
    one_lane = jnp.where(odd, 0, layers - 1)
    two_lane = jnp.where(odd, layers - 1, 0)
    row = lax.broadcasted_iota(jnp.int32, (16, layers), 0)
    both = ((row == 0) & lane_is((16, layers), one_lane)) | ((row == 1) & lane_is((16, layers), two_lane))
    both = both.astype(BF16)
    flat = labels[...].astype(F32).astype(BF16).reshape(width, layers)
    for out, lane in ((one_pack, one_lane), (two_pack, two_lane)):
        out[modes:] = lax.dot_general(
            pick_row(lane, layers), flat, NT, preferred_element_type=F32
        ).astype(BF16)
    for k in range(0, modes, CHUNK):
        at = slice(k, k + CHUNK)
        ends = lax.dot_general(
            both, held[at].reshape(-1, layers), NT, preferred_element_type=F32
        )
        for out, index in ((one_pack, 0), (two_pack, 1)):
            out[at] = jnp.concatenate(
                [ends[index:index + 1, j * width:(j + 1) * width] for j in range(CHUNK)], axis=0
            ).astype(BF16)
        for slot, plane in ((0, 1 - side), (1, side)):
            planes_out[slot, :, at, :] = jnp.swapaxes(held[at, plane], 0, 1)
        outer_rest[at] = held[at, side, pl.ds(pl.multiple_of(side * half, half), half), :]


def block_kernel(
    place, levels, labels, resid, here, partial, weights, half_diag, link_y, link_z,
):
    planes, rows, layers = labels.shape
    modes = here.shape[2]
    side = lax.rem(place[1], 2)
    at_edge = (place[1] == 0) | (place[1] == place[2] - 1)
    held = (1 - side, side)
    coef = [coefficients(labels[x], levels) for x in held]
    middle = harmonic(coef[0], coef[1])
    weights[0] = middle
    row = lax.broadcasted_iota(jnp.int32, (rows, layers), 0)
    lane = lax.broadcasted_iota(jnp.int32, (rows, layers), 1)
    for x in range(2):
        c = coef[x]
        up_y = harmonic(c, jnp.where(row == rows - 1, c, pltpu.roll(c, rows - 1, 0)))
        up_z = harmonic(c, pltpu.roll(c, layers - 1, 1))
        down_y = jnp.where(row == 0, c, pltpu.roll(up_y, 1, 0))
        weights[1 + x] = up_y
        weights[3 + x] = up_z
        weights[5 + x] = c
        inner_z = jnp.where(lane == layers - 1, 0.0, up_z)
        total = middle + up_y + down_y + inner_z + pltpu.roll(inner_z, 1, 1)
        if x == 1:
            total = total + jnp.where(at_edge, c, 0.0)
        half_diag[x] = 0.5 * total
        link_y[x] = jnp.where(row == rows - 1, 0.0, up_y)
        link_z[x] = inner_z

    def step(j, carry):
        total, rhs, wide = carry
        for u in range(STEP):
            y = j * STEP + u
            at = pl.ds(y, 1)
            ahead = jnp.minimum(y + 1, rows - 1)
            up = [here[x, ahead].astype(F32) for x in range(2)]
            images = []
            for x in range(2):
                image = (
                    half_diag[x, at, :] * wide[x]
                    - link_y[x, at, :] * up[x]
                    - link_z[x, at, :] * pltpu.roll(wide[x], layers - 1, 1)
                )
                if x == 0:
                    image = image - weights[0, at, :] * wide[1]
                rhs = rhs + resid[held[x], at, :] * wide[x]
                images.append(image.astype(BF16))
            total = total + lax.dot_general(
                jnp.concatenate(images, axis=1),
                jnp.concatenate([here[0, y], here[1, y]], axis=1),
                NT,
                preferred_element_type=F32,
            )
            wide = up
        return total, rhs, wide

    total, rhs, _ = lax.fori_loop(
        0,
        rows // STEP,
        step,
        (
            jnp.zeros((modes, modes), F32),
            jnp.zeros((modes, layers), F32),
            [here[x, 0].astype(F32) for x in range(2)],
        ),
    )
    partial[:modes, :] = total
    partial[modes:, :] = lax.dot_general(
        jnp.ones((8, layers), F32), rhs, NT, precision=PRECISE, preferred_element_type=F32
    )


def turn(got, start, out):
    half, modes, layers = out.shape
    for k in range(0, modes, CHUNK):
        out[:, k:k + CHUNK, :] = jnp.swapaxes(got[k:k + CHUNK, pl.ds(start, half), :], 0, 1)


def face_product(weight_ref, base, own, other):
    half, modes, layers = other.shape

    def step(j, total):
        left, right = [], []
        for u in range(STEP):
            y = j * STEP + u
            weight = weight_ref[pl.ds(base + y, 1), :]
            image = weight * (own[base + y].astype(F32) - other[y].astype(F32))
            left.append(jnp.concatenate([own[base + y], other[y]], axis=0))
            right.append(image.astype(BF16))
        return total + lax.dot_general(
            jnp.concatenate(left, axis=1), jnp.concatenate(right, axis=1), NT,
            preferred_element_type=F32,
        )

    total = lax.fori_loop(0, half // STEP, step, jnp.zeros((2 * modes, modes), F32))
    return total[:modes] - total[modes:]


def inner_kernel(
    place, levels, partial, weights, here, inner_got, one_pack, two_pack, one_got, two_got, out, face, turned,
):
    planes, rows, modes, layers = here.shape
    half = rows // 2
    side = lax.rem(place[1], 2)
    odd = lax.rem(place[0], 2) == 1
    base = pl.multiple_of(side * half, half)
    turn(inner_got, base, turned)
    face[...] = harmonic(weights[5], coefficients(inner_got[modes].astype(F32), levels))
    cross = face_product(face, base, here.at[0], turned)

    def coef_row(pack):
        return coefficients(pack[modes:modes + 16].astype(F32)[0:1], levels)

    one, two = one_pack[...].astype(F32), two_pack[...].astype(F32)
    one_other, two_other = one_got[...].astype(F32), two_got[...].astype(F32)
    first, last = jnp.where(odd, one, two), jnp.where(odd, two, one)
    next_first = jnp.where(odd, two_other, one_other)
    prev_last = jnp.where(odd, one_other, two_other)
    weight_low = harmonic(coef_row(first), coef_row(prev_last))
    weight_high = harmonic(coef_row(last), coef_row(next_first))

    def product(left, right):
        return lax.dot_general(left, right, NT, precision=PRECISE, preferred_element_type=F32)

    edge_rows = weight_high * last[:modes]
    ends = product(weight_low * first[:modes], first[:modes]) + product(edge_rows, last[:modes])
    out[:modes, :modes] = partial[:modes, :] + 0.5 * (cross + ends)
    out[:modes, modes:] = -product(edge_rows, next_first[:modes])
    out[modes:, :modes] = partial[modes:, :]
    out[modes:, modes:] = jnp.zeros((8, modes), F32)


def outer_kernel(place, levels, block, weights, here, outer_got, out, face, turned, face_here):
    planes, rows, modes, layers = here.shape
    half = rows // 2
    side = lax.rem(place[1], 2)
    at_edge = (place[1] == 0) | (place[1] == place[2] - 1)
    base = pl.multiple_of(side * half, half)
    turn(outer_got, 0, turned)
    coef = coefficients(outer_got[modes:].astype(F32).reshape(rows, layers), levels)
    between = harmonic(weights[6], coef)
    face[...] = jnp.where(at_edge, weights[6], between)
    face_here[...] = jnp.where(at_edge, 0.0, between)
    cross = face_product(face_here, base, here.at[1], turned)
    square = block[:modes, :modes] + 0.5 * cross
    out[:modes, :modes] = square + square.T
    out[:modes, modes:] = block[:modes, modes:]
    out[modes:, :] = block[modes:, :]


def sum_kernel(own, one, two, three, outer_rest, out, outer_out):
    modes = own.shape[1] // 2
    total = (own[...] + one[...]) + (two[...] + three[...])
    encode(total, modes, out)


def encode(total, modes, out):
    row = lax.broadcasted_iota(jnp.int32, (modes, 2 * modes), 0)
    lane = lax.broadcasted_iota(jnp.int32, (modes, 2 * modes), 1)
    values = total[:modes]
    high = values.astype(BF16).astype(F32)
    low = values - high
    out[:modes] = jnp.where((lane <= row) | (lane >= modes), high, low).astype(BF16)
    diagonal = lane == row
    right = total[modes:modes + 1]
    parts = []
    for _ in range(3):
        part = right.astype(BF16).astype(F32)
        parts.append(part)
        right = right - part
    for part in (high, low):
        parts.append(jnp.sum(jnp.where(diagonal, part, 0.0), axis=0, keepdims=True))
    rows = lax.broadcasted_iota(jnp.int32, (16, 2 * modes), 0)
    extra = jnp.zeros((16, 2 * modes), F32)
    for index, part in enumerate(parts):
        extra = jnp.where(rows == index, part, extra)
    out[modes:] = extra.astype(BF16)


def finish_kernel(place, levels, *refs):
    count = len(refs) - 19
    blocks, refs = refs[:count], refs[count:]
    zvec, inner_got, outer_got, outer_last, one_got, two_got, weights, inner_face, outer_face, resid = refs[:10]
    solution, deflated, direction_ref, image_ref, ahead_ref, spread, outer_field, ends_ref, fix_ref = refs[10:]
    subs = direction_ref.shape[0]
    modes, planes, rows, layers = zvec.shape
    half = rows // 2
    me = place[0]
    side = lax.rem(place[1], 2)
    odd = lax.rem(me, 2) == 1
    at_edge = (place[1] == 0) | (place[1] == place[2] - 1)
    order = place[3]
    held = (1 - side, side)
    square = (modes, modes)
    eye = lax.broadcasted_iota(jnp.int32, square, 0) == lax.broadcasted_iota(jnp.int32, square, 1)

    def column(row):
        return jnp.sum(jnp.where(eye, row, 0.0), axis=1, keepdims=True)

    def each(body):
        for index, block in enumerate(blocks):
            held_here = block.shape[0]
            if held_here <= 8:
                for entry in range(held_here):
                    body(block.at[entry], jnp.bitwise_xor(order, index * held_here + entry))
            else:
                pl.loop(0, held_here)(lambda entry, block=block: body(block.at[entry], entry))

    def load(block, s):
        extra = block[modes:modes + 16, :].astype(F32)
        direction_ref[pl.ds(s, 1), :] = (extra[0:1] + extra[1:2]) + extra[2:3]
        fix_ref[pl.ds(s, 1), :] = extra[4:5] - extra[3:4]

    each(load)
    fix = fix_ref[:, :modes]

    def turned(rows_of, by):
        by = by % subs
        return jnp.concatenate([rows_of[by:], rows_of[:by]], axis=0)

    def coarse_apply(direction):
        direction_ref[...] = jnp.concatenate([direction, turned(direction, 1)], axis=1)

        def one(block, s):
            values = block[:modes, :].astype(F32)
            pair = direction_ref[pl.ds(s, 1), :]
            ahead = jnp.sum(values * pair, axis=1, keepdims=True)
            ahead_ref[...] = jnp.where(lane_is((modes, 128), s), ahead, ahead_ref[...])
            image_ref[pl.ds(s, 1), :] = jnp.sum(
                values * column(pair[:, :modes]), axis=0, keepdims=True
            )

        each(one)
        image = image_ref[...]
        square_part = ahead_ref[...].T[:subs] + image[:, :modes] + fix * direction
        return square_part + turned(image[:, modes:], -1)

    def inner(left, right):
        return jnp.sum(jnp.sum(left * right, axis=0, keepdims=True), axis=1, keepdims=True)

    remain = direction_ref[:, :modes]
    direction = remain
    result = jnp.zeros_like(remain)
    norm_now = inner(remain, remain)
    for iteration in range(CITERS):
        image = coarse_apply(direction)
        step_size = norm_now / inner(direction, image)
        result = result + step_size * direction
        if iteration + 1 < CITERS:
            remain = remain - step_size * image
            norm_next = inner(remain, remain)
            direction = remain + (norm_next / norm_now) * direction
            norm_now = norm_next
    direction_ref[:, :modes] = result
    own = direction_ref[pl.ds(me, 1), :modes]
    solution[...] = own
    spread[...] = jnp.broadcast_to(column(own), (modes, layers))
    ahead_column = column(direction_ref[pl.ds(lax.rem(me + 1, subs), 1), :modes])
    behind_column = column(direction_ref[pl.ds(lax.rem(me + subs - 1, subs), 1), :modes])
    at_top = lane_is((modes, layers), layers - 1)
    at_bottom = lane_is((modes, layers), 0)

    def placed(pack, values, precision):
        return lax.dot_general(pack, values, TN, precision=precision, preferred_element_type=F32)

    one_other, two_other = one_got[...].astype(F32), two_got[...].astype(F32)
    next_first = jnp.where(odd, two_other, one_other)
    prev_last = jnp.where(odd, one_other, two_other)
    ends_ref[...] = (
        placed(next_first[:modes], jnp.where(at_top, ahead_column, 0.0), PRECISE)
        + placed(prev_last[:modes], jnp.where(at_bottom, behind_column, 0.0), PRECISE)
    ).reshape(planes, rows, layers)
    end_coef = coefficients(
        placed(next_first[modes:].astype(BF16), pick_row(layers - 1, layers), None)
        + placed(prev_last[modes:].astype(BF16), pick_row(0, layers), None),
        levels,
    ).reshape(planes, rows, layers)

    def add_mode(j, carry):
        fields, near, last = list(carry[0]), carry[1], carry[2]
        for u in range(MODES):
            k = j * MODES + u
            scale = spread[pl.ds(k, 1), :]
            for x, plane in enumerate((zvec[k, held[0]], zvec[k, held[1]], inner_got[k])):
                fields[x] = fields[x] + scale * plane.astype(F32)
            near = near + scale * outer_got[k].astype(F32)
            last = last + scale * outer_last[k].astype(F32)
        return tuple(fields), near, last

    zero, short = jnp.zeros((rows, layers), F32), jnp.zeros((half, layers), F32)
    field, near, last = lax.fori_loop(0, modes // MODES, add_mode, ((zero,) * 3, short, short))
    outer_field[pl.ds(pl.multiple_of(side * half, half), half), :] = near
    outer_field[pl.ds(pl.multiple_of((1 - side) * half, half), half), :] = last
    outside = (field[2], jnp.where(at_edge, 0.0, outer_field[...]))
    faces = (inner_face[...], outer_face[...])
    row = lax.broadcasted_iota(jnp.int32, (rows, layers), 0)
    lane = lax.broadcasted_iota(jnp.int32, (rows, layers), 1)
    for x in range(2):
        f = field[x]
        c = weights[5 + x]
        end_field = ends_ref[held[x]]
        end_weight = harmonic(c, jnp.where(side == x, end_coef[1], end_coef[0]))
        up_y, up_z = weights[1 + x], weights[3 + x]
        down_y = jnp.where(row == 0, c, pltpu.roll(up_y, 1, 0))
        down_z = jnp.where(lane == 0, end_weight, pltpu.roll(up_z, 1, 1))
        up_z = jnp.where(lane == layers - 1, end_weight, up_z)
        above_y = jnp.where(row == rows - 1, 0.0, pltpu.roll(f, rows - 1, 0))
        below_y = jnp.where(row == 0, 0.0, pltpu.roll(f, 1, 0))
        above_z = jnp.where(lane == layers - 1, end_field, pltpu.roll(f, layers - 1, 1))
        below_z = jnp.where(lane == 0, end_field, pltpu.roll(f, 1, 1))
        image = (
            weights[0] * (f - field[1 - x])
            + faces[x] * (f - outside[x])
            + down_y * (f - below_y)
            + up_y * (f - above_y)
            + down_z * (f - below_z)
            + up_z * (f - above_z)
        )
        deflated[held[x]] = resid[held[x]] - image


def swapped(value, axis, first):
    count = lax.axis_size(axis)
    pairs = []
    for i in range(count):
        up = (i - first) % 2 == 0
        pairs.append((i, (i + 1) % count if up else (i - 1) % count))
    return lax.ppermute(value, axis, pairs)


def swapped_open(value, axis):
    pairs = []
    for i in range(1, lax.axis_size(axis) - 1):
        pairs.append((i, i + 1 if i % 2 else i - 1))
    return lax.ppermute(value, axis, pairs)


def exchanged(value, axis, mask):
    return lax.ppermute(value, axis, [(i, i ^ mask) for i in range(lax.axis_size(axis))])


def gathered(value, axis):
    if lax.axis_size(axis) != 8:
        return [lax.all_gather(value, axis)]
    pair = jnp.stack([value, exchanged(value, axis, 1)])
    return [pair] + [exchanged(pair, axis, mask) for mask in (2, 4, 6)]


def body(labels, levels, zvec, resid):
    modes, planes, rows, layers = zvec.shape
    half = rows // 2
    subs, parts = lax.axis_size("sub"), lax.axis_size("pln")
    shape = jax.ShapeDtypeStruct
    order = lax.axis_index("sub") if subs == 8 else 0
    place = jnp.stack(
        [jnp.int32(v) for v in (lax.axis_index("sub"), lax.axis_index("pln"), parts, order)]
    )
    pack = shape((modes + 16, planes * rows), BF16)
    inner_send, outer_near = call(
        stage_kernel,
        [shape((modes + 1, rows, layers), BF16), shape((modes + rows // half, half, layers), BF16)],
        [SMEM, HBM, HBM],
        [pltpu.VMEM(labels.shape, jnp.int32), pltpu.SemaphoreType.DMA, pltpu.SemaphoreType.DMA((2,))],
        moved=2 << 20,
    )(place, *(pltpu.with_memory_space_constraint(v, pltpu.HBM) for v in (labels, zvec)))
    outer_got = swapped_open(outer_near, "pln")
    inner_got = swapped(inner_send, "pln", 0)
    rest = shape((modes, half, layers), BF16)
    here, outer_rest, one_pack, two_pack = call(
        prepare_kernel,
        [shape((planes, rows, modes, layers), BF16), rest, pack, pack],
        [SMEM, VMEM, VMEM],
        flops=10_000_000,
        moved=6 << 20,
    )(place, labels, zvec)
    one_got = swapped(one_pack, "sub", 0)
    two_got = swapped(two_pack, "sub", 1)
    field = (planes, rows, layers)
    plane = (rows, layers)
    block_shape = shape((modes + 8, 2 * modes), F32)
    partial, weights = call(
        block_kernel,
        [shape((modes + 8, modes), F32), shape((7,) + plane, F32)],
        [SMEM, SMEM] + [VMEM] * 3,
        [pltpu.VMEM(field, F32)] * 3,
        flops=400_000_000,
        moved=3 << 20,
    )(place, levels, labels, resid, here)
    turned = pltpu.VMEM((half, modes, layers), BF16)
    block, inner_face = call(
        inner_kernel,
        [block_shape, shape(plane, F32)],
        [SMEM, SMEM] + [VMEM] * 8,
        [turned],
        flops=100_000_000,
        moved=1 << 20,
    )(place, levels, partial, weights, here, inner_got, one_pack, two_pack, one_got, two_got)
    block, outer_face = call(
        outer_kernel,
        [block_shape, shape(plane, F32)],
        [SMEM, SMEM] + [VMEM] * 4,
        [turned, pltpu.VMEM(plane, F32)],
        flops=100_000_000,
        moved=1 << 20,
    )(place, levels, block, weights, here, outer_got)
    packed = shape((modes + 16, 2 * modes), BF16)
    if parts == 4:
        others = [exchanged(block, "pln", mask) for mask in (1, 2, 3)]
    else:
        block = lax.psum(block, "pln")
        others = [jnp.zeros_like(block)] * 3
    packed, outer_rest = call(
        sum_kernel, [packed, rest], [VMEM] * 4 + [ANY], aliases={4: 1}
    )(block, *others, outer_rest)
    blocks = gathered(packed, "sub")
    outer_last = swapped_open(outer_rest, "pln")
    return tuple(
        call(
            finish_kernel,
            [shape((1, modes), F32), shape(field, F32)],
            [SMEM, SMEM] + [VMEM] * (10 + len(blocks)),
            [
                pltpu.VMEM((subs, 2 * modes), F32),
                pltpu.VMEM((subs, 2 * modes), F32),
                pltpu.VMEM((modes, 128), F32),
                pltpu.VMEM((modes, layers), F32),
                pltpu.VMEM(plane, F32),
                pltpu.VMEM(field, F32),
                pltpu.VMEM((subs, 2 * modes), F32),
            ],
            flops=10_000_000,
            moved=5 << 20,
        )(
            place, levels, *blocks, zvec, inner_got, outer_got, outer_last, one_got, two_got, weights,
            inner_face, outer_face, resid,
        )
    )


def solution(mesh):
    in_specs = (P("pln", None, "sub"), P(), P(None, "pln", None, "sub"), P("pln", None, "sub"))
    out_specs = (P("sub", None), P("pln", None, "sub"))
    return jax.shard_map(body, mesh=mesh, in_specs=in_specs, out_specs=out_specs, check_vma=False)
```

```python
import jax
import jax.numpy as jnp
from jax import lax
from jax.experimental import pallas as pl
from jax.experimental.pallas import tpu as pltpu
from jax.sharding import PartitionSpec as P

CITERS = 2
STEP = 16
MODES = 8
CHUNK = 16
F32 = jnp.float32
BF16 = jnp.bfloat16
PRECISE = lax.Precision.HIGHEST
NT = (((1,), (1,)), ((), ()))
TN = (((0,), (0,)), ((), ()))
VMEM = pl.BlockSpec(memory_space=pltpu.VMEM)
SMEM = pl.BlockSpec(memory_space=pltpu.SMEM)
HBM = pl.BlockSpec(memory_space=pltpu.HBM)
ANY = pl.BlockSpec(memory_space=pl.ANY)


def call(kernel, outs, specs, scratch=(), flops=0, moved=0, limit=32, aliases=None):
    return pl.pallas_call(
        kernel,
        out_shape=outs,
        in_specs=specs,
        out_specs=[ANY if at in (aliases or {}).values() else VMEM for at in range(len(outs))],
        input_output_aliases=aliases or {},
        scratch_shapes=list(scratch),
        cost_estimate=pl.CostEstimate(flops=flops, bytes_accessed=moved, transcendentals=0),
        compiler_params=pltpu.CompilerParams(vmem_limit_bytes=limit << 20),
    )


def harmonic(left_value, right_value):
    return 2.0 * left_value * right_value / (left_value + right_value)


def coefficients(labels, levels_ref):
    weighted = jnp.zeros(labels.shape, F32)
    for level in range(levels_ref.shape[0]):
        weighted = weighted + jnp.where(labels == level, levels_ref[level], 0.0)
    return weighted


def lane_is(shape, lane):
    return lax.broadcasted_iota(jnp.int32, shape, len(shape) - 1) == lane


def pick_row(lane, width):
    row = lax.broadcasted_iota(jnp.int32, (16, width), 0)
    return ((row == 0) & lane_is((16, width), lane)).astype(BF16)


def stage_kernel(place, labels_far, zvec, inner_send, outer_near, labels, label_sem, sems):
    modes, planes, rows, layers = zvec.shape
    half = rows // 2
    side = lax.rem(place[1], 2)
    start = pl.multiple_of((1 - side) * half, half)
    label_copy = pltpu.make_async_copy(labels_far, labels, label_sem)
    copies = [
        pltpu.make_async_copy(
            zvec.at[:, side, pl.ds(start, half), :], outer_near.at[pl.ds(0, modes)], sems.at[0]
        ),
        pltpu.make_async_copy(zvec.at[:, 1 - side], inner_send.at[pl.ds(0, modes)], sems.at[1]),
    ]
    label_copy.start()
    for copy in copies:
        copy.start()
    label_copy.wait()
    outer_near[modes:] = labels[side].astype(F32).astype(BF16).reshape(rows // half, half, layers)
    inner_send[modes] = labels[1 - side].astype(F32).astype(BF16)
    for copy in copies:
        copy.wait()


def prepare_kernel(place, labels, held, planes_out, outer_rest, one_pack, two_pack):
    modes, planes, rows, layers = held.shape
    half = rows // 2
    width = planes * rows
    side = lax.rem(place[1], 2)
    odd = lax.rem(place[0], 2) == 1
    one_lane = jnp.where(odd, 0, layers - 1)
    two_lane = jnp.where(odd, layers - 1, 0)
    row = lax.broadcasted_iota(jnp.int32, (16, layers), 0)
    both = ((row == 0) & lane_is((16, layers), one_lane)) | ((row == 1) & lane_is((16, layers), two_lane))
    both = both.astype(BF16)
    flat = labels[...].astype(F32).astype(BF16).reshape(width, layers)
    for out, lane in ((one_pack, one_lane), (two_pack, two_lane)):
        out[modes:] = lax.dot_general(
            pick_row(lane, layers), flat, NT, preferred_element_type=F32
        ).astype(BF16)
    for k in range(0, modes, CHUNK):
        at = slice(k, k + CHUNK)
        ends = lax.dot_general(
            both, held[at].reshape(-1, layers), NT, preferred_element_type=F32
        )
        for out, index in ((one_pack, 0), (two_pack, 1)):
            out[at] = jnp.concatenate(
                [ends[index:index + 1, j * width:(j + 1) * width] for j in range(CHUNK)], axis=0
            ).astype(BF16)
        for slot, plane in ((0, 1 - side), (1, side)):
            planes_out[slot, :, at, :] = jnp.swapaxes(held[at, plane], 0, 1)
        outer_rest[at] = held[at, side, pl.ds(pl.multiple_of(side * half, half), half), :]


def block_kernel(
    place, levels, labels, resid, here, partial, weights, half_diag, link_y, link_z,
):
    planes, rows, layers = labels.shape
    modes = here.shape[2]
    side = lax.rem(place[1], 2)
    at_edge = (place[1] == 0) | (place[1] == place[2] - 1)
    held = (1 - side, side)
    coef = [coefficients(labels[x], levels) for x in held]
    middle = harmonic(coef[0], coef[1])
    weights[0] = middle
    row = lax.broadcasted_iota(jnp.int32, (rows, layers), 0)
    lane = lax.broadcasted_iota(jnp.int32, (rows, layers), 1)
    for x in range(2):
        c = coef[x]
        up_y = harmonic(c, jnp.where(row == rows - 1, c, pltpu.roll(c, rows - 1, 0)))
        up_z = harmonic(c, pltpu.roll(c, layers - 1, 1))
        down_y = jnp.where(row == 0, c, pltpu.roll(up_y, 1, 0))
        weights[1 + x] = up_y
        weights[3 + x] = up_z
        weights[5 + x] = c
        inner_z = jnp.where(lane == layers - 1, 0.0, up_z)
        total = middle + up_y + down_y + inner_z + pltpu.roll(inner_z, 1, 1)
        if x == 1:
            total = total + jnp.where(at_edge, c, 0.0)
        half_diag[x] = 0.5 * total
        link_y[x] = jnp.where(row == rows - 1, 0.0, up_y)
        link_z[x] = inner_z

    def step(j, carry):
        total, rhs, wide = carry
        for u in range(STEP):
            y = j * STEP + u
            at = pl.ds(y, 1)
            ahead = jnp.minimum(y + 1, rows - 1)
            up = [here[x, ahead].astype(F32) for x in range(2)]
            images = []
            for x in range(2):
                image = (
                    half_diag[x, at, :] * wide[x]
                    - link_y[x, at, :] * up[x]
                    - link_z[x, at, :] * pltpu.roll(wide[x], layers - 1, 1)
                )
                if x == 0:
                    image = image - weights[0, at, :] * wide[1]
                rhs = rhs + resid[held[x], at, :] * wide[x]
                images.append(image.astype(BF16))
            total = total + lax.dot_general(
                jnp.concatenate(images, axis=1),
                jnp.concatenate([here[0, y], here[1, y]], axis=1),
                NT,
                preferred_element_type=F32,
            )
            wide = up
        return total, rhs, wide

    total, rhs, _ = lax.fori_loop(
        0,
        rows // STEP,
        step,
        (
            jnp.zeros((modes, modes), F32),
            jnp.zeros((modes, layers), F32),
            [here[x, 0].astype(F32) for x in range(2)],
        ),
    )
    partial[:modes, :] = total
    partial[modes:, :] = lax.dot_general(
        jnp.ones((8, layers), F32), rhs, NT, precision=PRECISE, preferred_element_type=F32
    )


def turn(got, start, out):
    half, modes, layers = out.shape
    for k in range(0, modes, CHUNK):
        out[:, k:k + CHUNK, :] = jnp.swapaxes(got[k:k + CHUNK, pl.ds(start, half), :], 0, 1)


def face_product(weight_ref, base, own, other):
    half, modes, layers = other.shape

    def step(j, total):
        left, right = [], []
        for u in range(STEP):
            y = j * STEP + u
            weight = weight_ref[pl.ds(base + y, 1), :]
            image = weight * (own[base + y].astype(F32) - other[y].astype(F32))
            left.append(jnp.concatenate([own[base + y], other[y]], axis=0))
            right.append(image.astype(BF16))
        return total + lax.dot_general(
            jnp.concatenate(left, axis=1), jnp.concatenate(right, axis=1), NT,
            preferred_element_type=F32,
        )

    total = lax.fori_loop(0, half // STEP, step, jnp.zeros((2 * modes, modes), F32))
    return total[:modes] - total[modes:]


def inner_kernel(place, levels, partial, weights, here, inner_got, out, face, turned):
    planes, rows, modes, layers = here.shape
    half = rows // 2
    side = lax.rem(place[1], 2)
    base = pl.multiple_of(side * half, half)
    turn(inner_got, base, turned)
    face[...] = harmonic(weights[5], coefficients(inner_got[modes].astype(F32), levels))
    out[:modes, :] = partial[:modes, :] + 0.5 * face_product(face, base, here.at[0], turned)
    out[modes:, :] = partial[modes:, :]


def outer_kernel(
    place, levels, partial, weights, here, outer_got, one_pack, two_pack, one_got, two_got,
    out, face, turned, face_here,
):
    planes, rows, modes, layers = here.shape
    half = rows // 2
    side = lax.rem(place[1], 2)
    odd = lax.rem(place[0], 2) == 1
    at_edge = (place[1] == 0) | (place[1] == place[2] - 1)
    base = pl.multiple_of(side * half, half)
    turn(outer_got, 0, turned)
    coef = coefficients(outer_got[modes:].astype(F32).reshape(rows, layers), levels)
    between = harmonic(weights[6], coef)
    face[...] = jnp.where(at_edge, weights[6], between)
    face_here[...] = jnp.where(at_edge, 0.0, between)
    cross = face_product(face_here, base, here.at[1], turned)

    def coef_row(pack):
        return coefficients(pack[modes:modes + 16].astype(F32)[0:1], levels)

    one, two = one_pack[...].astype(F32), two_pack[...].astype(F32)
    one_other, two_other = one_got[...].astype(F32), two_got[...].astype(F32)
    first, last = jnp.where(odd, one, two), jnp.where(odd, two, one)
    next_first = jnp.where(odd, two_other, one_other)
    prev_last = jnp.where(odd, one_other, two_other)
    weight_low = harmonic(coef_row(first), coef_row(prev_last))
    weight_high = harmonic(coef_row(last), coef_row(next_first))

    def product(left, right):
        return lax.dot_general(left, right, NT, precision=PRECISE, preferred_element_type=F32)

    edge_rows = weight_high * last[:modes]
    ends = product(weight_low * first[:modes], first[:modes]) + product(edge_rows, last[:modes])
    square = partial[:modes, :] + 0.5 * (cross + ends)
    out[:modes, :modes] = square + square.T
    out[:modes, modes:] = -product(edge_rows, next_first[:modes])
    out[modes:, :modes] = partial[modes:, :]
    out[modes:, modes:] = jnp.zeros((8, modes), F32)


def terms_kernel(
    place, levels, pair, one_got, two_got, weights, inner_face, outer_face, terms, picked, coef_ref
):
    modes, width = picked.shape[1:]
    rows, layers = inner_face.shape
    side = lax.rem(place[1], 2)
    odd = lax.rem(place[0], 2) == 1
    one_other, two_other = one_got[...].astype(F32), two_got[...].astype(F32)
    next_first = jnp.where(odd, two_other, one_other)
    prev_last = jnp.where(odd, one_other, two_other)
    picked[0] = next_first[:modes]
    picked[1] = prev_last[:modes]
    end_labels = lax.dot_general(
        next_first[modes:].astype(BF16), pick_row(layers - 1, layers), TN, preferred_element_type=F32
    ) + lax.dot_general(
        prev_last[modes:].astype(BF16), pick_row(0, layers), TN, preferred_element_type=F32
    )
    coef_ref[...] = coefficients(end_labels, levels).reshape(width // rows, rows, layers)
    row = lax.broadcasted_iota(jnp.int32, (rows, layers), 0)
    lane = lax.broadcasted_iota(jnp.int32, (rows, layers), 1)
    for x, face in enumerate((inner_face, outer_face)):
        c = weights[5 + x]
        end_weight = harmonic(c, coef_ref[1 - side if x == 0 else side])
        up_y, up_z = weights[1 + x], weights[3 + x]
        down_y = jnp.where(row == 0, c, pltpu.roll(up_y, 1, 0))
        down_z = pltpu.roll(up_z, 1, 1)
        total = face[...] + weights[0] + up_y + down_y
        total = total + jnp.where(lane == layers - 1, end_weight, up_z)
        terms[x, 0] = total + jnp.where(lane == 0, end_weight, down_z)
        terms[x, 1] = jnp.where(row == 0, 0.0, down_y)
        terms[x, 2] = jnp.where(row == rows - 1, 0.0, up_y)
        terms[x, 3] = jnp.where(lane == 0, 0.0, down_z)
        terms[x, 4] = jnp.where(lane == layers - 1, 0.0, up_z)
        terms[x, 5] = end_weight


def sum_kernel(own, one, two, three, outer_rest, out, outer_out):
    modes = own.shape[1] // 2
    total = (own[...] + one[...]) + (two[...] + three[...])
    encode(total, modes, out)


def encode(total, modes, out):
    row = lax.broadcasted_iota(jnp.int32, (modes, 2 * modes), 0)
    lane = lax.broadcasted_iota(jnp.int32, (modes, 2 * modes), 1)
    values = total[:modes]
    high = values.astype(BF16).astype(F32)
    low = values - high
    out[:modes] = jnp.where((lane <= row) | (lane >= modes), high, low).astype(BF16)
    diagonal = lane == row
    right = total[modes:modes + 1]
    parts = []
    for _ in range(3):
        part = right.astype(BF16).astype(F32)
        parts.append(part)
        right = right - part
    for part in (high, low):
        parts.append(jnp.sum(jnp.where(diagonal, part, 0.0), axis=0, keepdims=True))
    rows = lax.broadcasted_iota(jnp.int32, (16, 2 * modes), 0)
    extra = jnp.zeros((16, 2 * modes), F32)
    for index, part in enumerate(parts):
        extra = jnp.where(rows == index, part, extra)
    out[modes:] = extra.astype(BF16)


def finish_kernel(place, *refs):
    count = len(refs) - 18
    blocks, refs = refs[:count], refs[count:]
    zvec, inner_got, outer_got, outer_last, picked, terms, middle, inner_face, outer_face, resid = refs[:10]
    solution, deflated, direction_ref, image_ref, ahead_ref, spread, outer_field, fix_ref = refs[10:]
    subs = direction_ref.shape[0]
    modes, planes, rows, layers = zvec.shape
    half = rows // 2
    me = place[0]
    side = lax.rem(place[1], 2)
    odd = lax.rem(me, 2) == 1
    at_edge = (place[1] == 0) | (place[1] == place[2] - 1)
    order = place[3]
    held = (1 - side, side)
    square = (modes, modes)
    eye = lax.broadcasted_iota(jnp.int32, square, 0) == lax.broadcasted_iota(jnp.int32, square, 1)

    def column(row):
        return jnp.sum(jnp.where(eye, row, 0.0), axis=1, keepdims=True)

    def each(body):
        for index, block in enumerate(blocks):
            held_here = block.shape[0]
            if held_here <= 8:
                for entry in range(held_here):
                    body(block.at[entry], jnp.bitwise_xor(order, index * held_here + entry))
            else:
                pl.loop(0, held_here)(lambda entry, block=block: body(block.at[entry], entry))

    def load(block, s):
        extra = block[modes:modes + 16, :].astype(F32)
        direction_ref[pl.ds(s, 1), :] = (extra[0:1] + extra[1:2]) + extra[2:3]
        fix_ref[pl.ds(s, 1), :] = extra[4:5] - extra[3:4]

    each(load)
    fix = fix_ref[:, :modes]

    def turned(rows_of, by):
        by = by % subs
        return jnp.concatenate([rows_of[by:], rows_of[:by]], axis=0)

    def coarse_apply(direction):
        direction_ref[...] = jnp.concatenate([direction, turned(direction, 1)], axis=1)

        def one(block, s):
            values = block[:modes, :].astype(F32)
            pair = direction_ref[pl.ds(s, 1), :]
            ahead = jnp.sum(values * pair, axis=1, keepdims=True)
            ahead_ref[...] = jnp.where(lane_is((modes, 128), s), ahead, ahead_ref[...])
            image_ref[pl.ds(s, 1), :] = jnp.sum(
                values * column(pair[:, :modes]), axis=0, keepdims=True
            )

        each(one)
        image = image_ref[...]
        square_part = ahead_ref[...].T[:subs] + image[:, :modes] + fix * direction
        return square_part + turned(image[:, modes:], -1)

    def inner(left, right):
        return jnp.sum(jnp.sum(left * right, axis=0, keepdims=True), axis=1, keepdims=True)

    remain = direction_ref[:, :modes]
    direction = remain
    result = jnp.zeros_like(remain)
    norm_now = inner(remain, remain)
    for iteration in range(CITERS):
        image = coarse_apply(direction)
        step_size = norm_now / inner(direction, image)
        result = result + step_size * direction
        if iteration + 1 < CITERS:
            remain = remain - step_size * image
            norm_next = inner(remain, remain)
            direction = remain + (norm_next / norm_now) * direction
            norm_now = norm_next
    direction_ref[:, :modes] = result
    own = direction_ref[pl.ds(me, 1), :modes]
    solution[...] = own
    spread[...] = jnp.broadcast_to(column(own), (modes, layers))
    ahead_column = column(direction_ref[pl.ds(lax.rem(me + 1, subs), 1), :modes])
    behind_column = column(direction_ref[pl.ds(lax.rem(me + subs - 1, subs), 1), :modes])
    at_top = lane_is((modes, layers), layers - 1)
    at_bottom = lane_is((modes, layers), 0)

    def placed(pack, values):
        return lax.dot_general(
            pack, values, TN, precision=PRECISE, preferred_element_type=F32
        ).reshape(planes, rows, layers)

    ends = placed(picked[0], jnp.where(at_top, ahead_column, 0.0)) + placed(
        picked[1], jnp.where(at_bottom, behind_column, 0.0)
    )

    def add_mode(j, carry):
        fields, near, last = list(carry[0]), carry[1], carry[2]
        for u in range(MODES):
            k = j * MODES + u
            scale = spread[pl.ds(k, 1), :]
            for x, plane in enumerate((zvec[k, held[0]], zvec[k, held[1]], inner_got[k])):
                fields[x] = fields[x] + scale * plane.astype(F32)
            near = near + scale * outer_got[k].astype(F32)
            last = last + scale * outer_last[k].astype(F32)
        return tuple(fields), near, last

    zero, short = jnp.zeros((rows, layers), F32), jnp.zeros((half, layers), F32)
    field, near, last = lax.fori_loop(0, modes // MODES, add_mode, ((zero,) * 3, short, short))
    outer_field[pl.ds(pl.multiple_of(side * half, half), half), :] = near
    outer_field[pl.ds(pl.multiple_of((1 - side) * half, half), half), :] = last
    outside = (field[2], jnp.where(at_edge, 0.0, outer_field[...]))
    faces = (inner_face[...], outer_face[...])
    for x in range(2):
        f = field[x]
        end_field = jnp.where(side == x, ends[1], ends[0])
        image = (
            terms[x, 0] * f
            - middle[0] * field[1 - x]
            - faces[x] * outside[x]
            - terms[x, 1] * pltpu.roll(f, 1, 0)
            - terms[x, 2] * pltpu.roll(f, rows - 1, 0)
            - terms[x, 3] * pltpu.roll(f, 1, 1)
            - terms[x, 4] * pltpu.roll(f, layers - 1, 1)
            - terms[x, 5] * end_field
        )
        deflated[held[x]] = resid[held[x]] - image


def swapped(value, axis, first):
    count = lax.axis_size(axis)
    pairs = []
    for i in range(count):
        up = (i - first) % 2 == 0
        pairs.append((i, (i + 1) % count if up else (i - 1) % count))
    return lax.ppermute(value, axis, pairs)


def swapped_open(value):
    pairs = []
    for i in range(1, lax.axis_size("pln") - 1):
        pairs.append((i, i + 1 if i % 2 else i - 1))
    return lax.ppermute(value, "pln", pairs)


def swapped_all(value):
    subs, count = lax.axis_size("sub"), lax.axis_size("pln")
    pairs = []
    for s in range(subs):
        for i in range(count):
            if 0 < i < count - 1:
                to = (s, i + 1 if i % 2 else i - 1)
            else:
                to = (s ^ 1, i)
            pairs.append((s * count + i, to[0] * count + to[1]))
    return lax.ppermute(value, ("sub", "pln"), pairs)


def exchanged(value, axis, mask):
    return lax.ppermute(value, axis, [(i, i ^ mask) for i in range(lax.axis_size(axis))])


def gathered(value, axis):
    if lax.axis_size(axis) != 8:
        return [lax.all_gather(value, axis)]
    pair = jnp.stack([value, exchanged(value, axis, 1)])
    return [pair] + [exchanged(pair, axis, mask) for mask in (2, 4, 6)]


def body(labels, levels, zvec, resid):
    modes, planes, rows, layers = zvec.shape
    half = rows // 2
    subs, parts = lax.axis_size("sub"), lax.axis_size("pln")
    shape = jax.ShapeDtypeStruct
    order = lax.axis_index("sub") if subs == 8 else 0
    place = jnp.stack(
        [jnp.int32(v) for v in (lax.axis_index("sub"), lax.axis_index("pln"), parts, order)]
    )
    pack = shape((modes + 16, planes * rows), BF16)
    inner_send, outer_near = call(
        stage_kernel,
        [shape((modes + 1, rows, layers), BF16), shape((modes + rows // half, half, layers), BF16)],
        [SMEM, HBM, HBM],
        [pltpu.VMEM(labels.shape, jnp.int32), pltpu.SemaphoreType.DMA, pltpu.SemaphoreType.DMA((2,))],
        moved=2 << 20,
    )(place, *(pltpu.with_memory_space_constraint(v, pltpu.HBM) for v in (labels, zvec)))
    outer_got = swapped_all(outer_near)
    inner_got = swapped(inner_send, "pln", 0)
    rest = shape((modes, half, layers), BF16)
    here, outer_rest, one_pack, two_pack = call(
        prepare_kernel,
        [shape((planes, rows, modes, layers), BF16), rest, pack, pack],
        [SMEM, VMEM, VMEM],
        flops=10_000_000,
        moved=6 << 20,
    )(place, labels, zvec)
    one_got = swapped(one_pack, "sub", 0)
    two_got = swapped(two_pack, "sub", 1)
    field = (planes, rows, layers)
    plane = (rows, layers)
    partial, weights = call(
        block_kernel,
        [shape((modes + 8, modes), F32), shape((7,) + plane, F32)],
        [SMEM, SMEM] + [VMEM] * 3,
        [pltpu.VMEM(field, F32)] * 3,
        flops=400_000_000,
        moved=3 << 20,
    )(place, levels, labels, resid, here)
    turned = pltpu.VMEM((half, modes, layers), BF16)
    partial, inner_face = call(
        inner_kernel,
        [shape((modes + 8, modes), F32), shape(plane, F32)],
        [SMEM, SMEM] + [VMEM] * 4,
        [turned],
        flops=100_000_000,
        moved=1 << 20,
    )(place, levels, partial, weights, here, inner_got)
    block, outer_face = call(
        outer_kernel,
        [shape((modes + 8, 2 * modes), F32), shape(plane, F32)],
        [SMEM, SMEM] + [VMEM] * 8,
        [turned, pltpu.VMEM(plane, F32)],
        flops=100_000_000,
        moved=1 << 20,
    )(place, levels, partial, weights, here, outer_got, one_pack, two_pack, one_got, two_got)
    packed = shape((modes + 16, 2 * modes), BF16)
    if parts == 4:
        others = [exchanged(block, "pln", mask) for mask in (1, 2, 3)]
    else:
        block = lax.psum(block, "pln")
        others = [jnp.zeros_like(block)] * 3
    packed, outer_rest = call(
        sum_kernel, [packed, rest], [VMEM] * 4 + [ANY], aliases={4: 1}
    )(block, *others, outer_rest)
    blocks = gathered(packed, "sub")
    outer_last = swapped_open(outer_rest)
    terms, picked = call(
        terms_kernel,
        [shape((planes, 6) + plane, F32), shape((2, modes, planes * rows), F32)],
        [SMEM, SMEM, ANY] + [VMEM] * 5,
        [pltpu.VMEM(field, F32)],
        flops=1_000_000,
        moved=64 << 20,
    )(place, levels, blocks[0], one_got, two_got, weights, inner_face, outer_face)
    return tuple(
        call(
            finish_kernel,
            [shape((1, modes), F32), shape(field, F32)],
            [SMEM] + [VMEM] * (10 + len(blocks)),
            [
                pltpu.VMEM((subs, 2 * modes), F32),
                pltpu.VMEM((subs, 2 * modes), F32),
                pltpu.VMEM((modes, 128), F32),
                pltpu.VMEM((modes, layers), F32),
                pltpu.VMEM(plane, F32),
                pltpu.VMEM((subs, 2 * modes), F32),
            ],
            flops=10_000_000,
            moved=5 << 20,
        )(
            place, *blocks, zvec, inner_got, outer_got, outer_last, picked, terms, weights, inner_face,
            outer_face, resid,
        )
    )


def solution(mesh):
    in_specs = (P("pln", None, "sub"), P(), P(None, "pln", None, "sub"), P("pln", None, "sub"))
    out_specs = (P("sub", None), P("pln", None, "sub"))
    return jax.shard_map(body, mesh=mesh, in_specs=in_specs, out_specs=out_specs, check_vma=False)
```

```python
import jax
import jax.numpy as jnp
from jax import lax
from jax.experimental import pallas as pl
from jax.experimental.pallas import tpu as pltpu
from jax.sharding import PartitionSpec as P

CITERS = 2
STEP = 16
MODES = 8
CHUNK = 16
F32 = jnp.float32
BF16 = jnp.bfloat16
PRECISE = lax.Precision.HIGHEST
NT = (((1,), (1,)), ((), ()))
TN = (((0,), (0,)), ((), ()))
VMEM = pl.BlockSpec(memory_space=pltpu.VMEM)
SMEM = pl.BlockSpec(memory_space=pltpu.SMEM)
HBM = pl.BlockSpec(memory_space=pltpu.HBM)
ANY = pl.BlockSpec(memory_space=pl.ANY)


def call(kernel, outs, specs, scratch=(), flops=0, moved=0, limit=32, aliases=None):
    return pl.pallas_call(
        kernel,
        out_shape=outs,
        in_specs=specs,
        out_specs=[ANY if at in (aliases or {}).values() else VMEM for at in range(len(outs))],
        input_output_aliases=aliases or {},
        scratch_shapes=list(scratch),
        cost_estimate=pl.CostEstimate(flops=flops, bytes_accessed=moved, transcendentals=0),
        compiler_params=pltpu.CompilerParams(vmem_limit_bytes=limit << 20),
    )


def harmonic(left_value, right_value):
    return 2.0 * left_value * right_value / (left_value + right_value)


def coefficients(labels, levels_ref):
    weighted = jnp.zeros(labels.shape, F32)
    for level in range(levels_ref.shape[0]):
        weighted = weighted + jnp.where(labels == level, levels_ref[level], 0.0)
    return weighted


def lane_is(shape, lane):
    return lax.broadcasted_iota(jnp.int32, shape, len(shape) - 1) == lane


def pick_row(lane, width):
    row = lax.broadcasted_iota(jnp.int32, (16, width), 0)
    return ((row == 0) & lane_is((16, width), lane)).astype(BF16)


def stage_kernel(place, labels_far, zvec, outer_near, labels, label_sem, sem):
    modes, planes, rows, layers = zvec.shape
    half = rows // 2
    side = lax.rem(place[1], 2)
    start = pl.multiple_of((1 - side) * half, half)
    label_copy = pltpu.make_async_copy(labels_far, labels, label_sem)
    copy = pltpu.make_async_copy(
        zvec.at[:, side, pl.ds(start, half), :], outer_near.at[pl.ds(0, modes)], sem
    )
    copy.start()
    label_copy.start()
    label_copy.wait()
    outer_near[modes:] = labels[side].astype(F32).astype(BF16).reshape(rows // half, half, layers)
    copy.wait()


def plane_kernel(place, labels, held, staged, inner_send):
    modes = held.shape[0]
    side = lax.rem(place[1], 2)
    inner_send[:modes] = held[:, 1 - side]
    inner_send[modes] = labels[1 - side].astype(F32).astype(BF16)


def release_kernel(after, outer_rest, outer_out):
    pass


def prepare_kernel(place, labels, held, staged, planes_out, outer_rest, one_pack, two_pack):
    modes, planes, rows, layers = held.shape
    half = rows // 2
    width = planes * rows
    side = lax.rem(place[1], 2)
    odd = lax.rem(place[0], 2) == 1
    one_lane = jnp.where(odd, 0, layers - 1)
    two_lane = jnp.where(odd, layers - 1, 0)
    row = lax.broadcasted_iota(jnp.int32, (16, layers), 0)
    both = ((row == 0) & lane_is((16, layers), one_lane)) | ((row == 1) & lane_is((16, layers), two_lane))
    both = both.astype(BF16)
    flat = labels[...].astype(F32).astype(BF16).reshape(width, layers)
    for out, lane in ((one_pack, one_lane), (two_pack, two_lane)):
        out[modes:] = lax.dot_general(
            pick_row(lane, layers), flat, NT, preferred_element_type=F32
        ).astype(BF16)
    for k in range(0, modes, CHUNK):
        at = slice(k, k + CHUNK)
        ends = lax.dot_general(
            both, held[at].reshape(-1, layers), NT, preferred_element_type=F32
        )
        for out, index in ((one_pack, 0), (two_pack, 1)):
            out[at] = jnp.concatenate(
                [ends[index:index + 1, j * width:(j + 1) * width] for j in range(CHUNK)], axis=0
            ).astype(BF16)
        for slot, plane in ((0, 1 - side), (1, side)):
            planes_out[slot, :, at, :] = jnp.swapaxes(held[at, plane], 0, 1)
        outer_rest[at] = held[at, side, pl.ds(pl.multiple_of(side * half, half), half), :]


def block_kernel(
    place, levels, labels, resid, here, partial, weights, half_diag, link_y, link_z,
):
    planes, rows, layers = labels.shape
    modes = here.shape[2]
    side = lax.rem(place[1], 2)
    at_edge = (place[1] == 0) | (place[1] == place[2] - 1)
    held = (1 - side, side)
    coef = [coefficients(labels[x], levels) for x in held]
    middle = harmonic(coef[0], coef[1])
    weights[0] = middle
    row = lax.broadcasted_iota(jnp.int32, (rows, layers), 0)
    lane = lax.broadcasted_iota(jnp.int32, (rows, layers), 1)
    for x in range(2):
        c = coef[x]
        up_y = harmonic(c, jnp.where(row == rows - 1, c, pltpu.roll(c, rows - 1, 0)))
        up_z = harmonic(c, pltpu.roll(c, layers - 1, 1))
        down_y = jnp.where(row == 0, c, pltpu.roll(up_y, 1, 0))
        weights[1 + x] = up_y
        weights[3 + x] = up_z
        weights[5 + x] = c
        inner_z = jnp.where(lane == layers - 1, 0.0, up_z)
        total = middle + up_y + down_y + inner_z + pltpu.roll(inner_z, 1, 1)
        if x == 1:
            total = total + jnp.where(at_edge, c, 0.0)
        half_diag[x] = 0.5 * total
        link_y[x] = jnp.where(row == rows - 1, 0.0, up_y)
        link_z[x] = inner_z

    def step(j, carry):
        total, rhs, wide = carry
        for u in range(STEP):
            y = j * STEP + u
            at = pl.ds(y, 1)
            ahead = jnp.minimum(y + 1, rows - 1)
            up = [here[x, ahead].astype(F32) for x in range(2)]
            images = []
            for x in range(2):
                image = (
                    half_diag[x, at, :] * wide[x]
                    - link_y[x, at, :] * up[x]
                    - link_z[x, at, :] * pltpu.roll(wide[x], layers - 1, 1)
                )
                if x == 0:
                    image = image - weights[0, at, :] * wide[1]
                rhs = rhs + resid[held[x], at, :] * wide[x]
                images.append(image.astype(BF16))
            total = total + lax.dot_general(
                jnp.concatenate(images, axis=1),
                jnp.concatenate([here[0, y], here[1, y]], axis=1),
                NT,
                preferred_element_type=F32,
            )
            wide = up
        return total, rhs, wide

    total, rhs, _ = lax.fori_loop(
        0,
        rows // STEP,
        step,
        (
            jnp.zeros((modes, modes), F32),
            jnp.zeros((modes, layers), F32),
            [here[x, 0].astype(F32) for x in range(2)],
        ),
    )
    partial[:modes, :] = total
    partial[modes:, :] = lax.dot_general(
        jnp.ones((8, layers), F32), rhs, NT, precision=PRECISE, preferred_element_type=F32
    )


def turn(got, start, out):
    half, modes, layers = out.shape
    for k in range(0, modes, CHUNK):
        out[:, k:k + CHUNK, :] = jnp.swapaxes(got[k:k + CHUNK, pl.ds(start, half), :], 0, 1)


def face_product(weight_ref, base, own, other):
    half, modes, layers = other.shape

    def step(j, total):
        left, right = [], []
        for u in range(STEP):
            y = j * STEP + u
            weight = weight_ref[pl.ds(base + y, 1), :]
            image = weight * (own[base + y].astype(F32) - other[y].astype(F32))
            left.append(jnp.concatenate([own[base + y], other[y]], axis=0))
            right.append(image.astype(BF16))
        return total + lax.dot_general(
            jnp.concatenate(left, axis=1), jnp.concatenate(right, axis=1), NT,
            preferred_element_type=F32,
        )

    total = lax.fori_loop(0, half // STEP, step, jnp.zeros((2 * modes, modes), F32))
    return total[:modes] - total[modes:]


def inner_kernel(place, levels, partial, weights, here, inner_got, out, face, turned):
    planes, rows, modes, layers = here.shape
    half = rows // 2
    side = lax.rem(place[1], 2)
    base = pl.multiple_of(side * half, half)
    turn(inner_got, base, turned)
    face[...] = harmonic(weights[5], coefficients(inner_got[modes].astype(F32), levels))
    out[:modes, :] = partial[:modes, :] + 0.5 * face_product(face, base, here.at[0], turned)
    out[modes:, :] = partial[modes:, :]


def outer_kernel(
    place, levels, partial, weights, here, outer_got, one_pack, two_pack, one_got, two_got,
    out, face, turned, face_here,
):
    planes, rows, modes, layers = here.shape
    half = rows // 2
    side = lax.rem(place[1], 2)
    odd = lax.rem(place[0], 2) == 1
    at_edge = (place[1] == 0) | (place[1] == place[2] - 1)
    base = pl.multiple_of(side * half, half)
    turn(outer_got, 0, turned)
    coef = coefficients(outer_got[modes:].astype(F32).reshape(rows, layers), levels)
    between = harmonic(weights[6], coef)
    face[...] = jnp.where(at_edge, weights[6], between)
    face_here[...] = jnp.where(at_edge, 0.0, between)
    cross = face_product(face_here, base, here.at[1], turned)

    def coef_row(pack):
        return coefficients(pack[modes:modes + 16].astype(F32)[0:1], levels)

    one, two = one_pack[...].astype(F32), two_pack[...].astype(F32)
    one_other, two_other = one_got[...].astype(F32), two_got[...].astype(F32)
    first, last = jnp.where(odd, one, two), jnp.where(odd, two, one)
    next_first = jnp.where(odd, two_other, one_other)
    prev_last = jnp.where(odd, one_other, two_other)
    weight_low = harmonic(coef_row(first), coef_row(prev_last))
    weight_high = harmonic(coef_row(last), coef_row(next_first))

    def product(left, right):
        return lax.dot_general(left, right, NT, precision=PRECISE, preferred_element_type=F32)

    edge_rows = weight_high * last[:modes]
    ends = product(weight_low * first[:modes], first[:modes]) + product(edge_rows, last[:modes])
    square = partial[:modes, :] + 0.5 * (cross + ends)
    out[:modes, :modes] = square + square.T
    out[:modes, modes:] = -product(edge_rows, next_first[:modes])
    out[modes:, :modes] = partial[modes:, :]
    out[modes:, modes:] = jnp.zeros((8, modes), F32)


def terms_kernel(
    place, levels, pair, one_got, two_got, weights, inner_face, outer_face, terms, picked, coef_ref
):
    modes, width = picked.shape[1:]
    rows, layers = inner_face.shape
    side = lax.rem(place[1], 2)
    odd = lax.rem(place[0], 2) == 1
    one_other, two_other = one_got[...].astype(F32), two_got[...].astype(F32)
    next_first = jnp.where(odd, two_other, one_other)
    prev_last = jnp.where(odd, one_other, two_other)
    picked[0] = next_first[:modes]
    picked[1] = prev_last[:modes]
    end_labels = lax.dot_general(
        next_first[modes:].astype(BF16), pick_row(layers - 1, layers), TN, preferred_element_type=F32
    ) + lax.dot_general(
        prev_last[modes:].astype(BF16), pick_row(0, layers), TN, preferred_element_type=F32
    )
    coef_ref[...] = coefficients(end_labels, levels).reshape(width // rows, rows, layers)
    row = lax.broadcasted_iota(jnp.int32, (rows, layers), 0)
    lane = lax.broadcasted_iota(jnp.int32, (rows, layers), 1)
    for x, face in enumerate((inner_face, outer_face)):
        c = weights[5 + x]
        end_weight = harmonic(c, coef_ref[1 - side if x == 0 else side])
        up_y, up_z = weights[1 + x], weights[3 + x]
        down_y = jnp.where(row == 0, c, pltpu.roll(up_y, 1, 0))
        down_z = pltpu.roll(up_z, 1, 1)
        total = face[...] + weights[0] + up_y + down_y
        total = total + jnp.where(lane == layers - 1, end_weight, up_z)
        terms[x, 0] = total + jnp.where(lane == 0, end_weight, down_z)
        terms[x, 1] = jnp.where(row == 0, 0.0, down_y)
        terms[x, 2] = jnp.where(row == rows - 1, 0.0, up_y)
        terms[x, 3] = jnp.where(lane == 0, 0.0, down_z)
        terms[x, 4] = jnp.where(lane == layers - 1, 0.0, up_z)
        terms[x, 5] = end_weight


def sum_kernel(own, one, two, three, out):
    modes = own.shape[1] // 2
    total = (own[...] + one[...]) + (two[...] + three[...])
    encode(total, modes, out)


def encode(total, modes, out):
    row = lax.broadcasted_iota(jnp.int32, (modes, 2 * modes), 0)
    lane = lax.broadcasted_iota(jnp.int32, (modes, 2 * modes), 1)
    values = total[:modes]
    high = values.astype(BF16).astype(F32)
    low = values - high
    out[:modes] = jnp.where((lane <= row) | (lane >= modes), high, low).astype(BF16)
    diagonal = lane == row
    right = total[modes:modes + 1]
    parts = []
    for _ in range(3):
        part = right.astype(BF16).astype(F32)
        parts.append(part)
        right = right - part
    for part in (high, low):
        parts.append(jnp.sum(jnp.where(diagonal, part, 0.0), axis=0, keepdims=True))
    rows = lax.broadcasted_iota(jnp.int32, (16, 2 * modes), 0)
    extra = jnp.zeros((16, 2 * modes), F32)
    for index, part in enumerate(parts):
        extra = jnp.where(rows == index, part, extra)
    out[modes:] = extra.astype(BF16)


def finish_kernel(place, *refs):
    count = len(refs) - 17
    blocks, refs = refs[:count], refs[count:]
    zvec, inner_got, outer_got, outer_last, picked, terms, middle, inner_face, outer_face, resid = refs[:10]
    solution, deflated, direction_ref, image_ref, spread, outer_field, fix_ref = refs[10:]
    subs = direction_ref.shape[0]
    modes, planes, rows, layers = zvec.shape
    half = rows // 2
    me = place[0]
    side = lax.rem(place[1], 2)
    odd = lax.rem(me, 2) == 1
    at_edge = (place[1] == 0) | (place[1] == place[2] - 1)
    order = place[3]
    held = (1 - side, side)
    square = (modes, modes)
    eye = lax.broadcasted_iota(jnp.int32, square, 0) == lax.broadcasted_iota(jnp.int32, square, 1)

    def column(row):
        return jnp.sum(jnp.where(eye, row, 0.0), axis=1, keepdims=True)

    def each(body, carry):
        for index, block in enumerate(blocks):
            held_here = block.shape[0]
            if held_here <= 8:
                for entry in range(held_here):
                    s = jnp.bitwise_xor(order, index * held_here + entry)
                    carry = body(block.at[entry], s, carry)
            else:
                carry = lax.fori_loop(
                    0, held_here, lambda entry, c, block=block: body(block.at[entry], entry, c), carry
                )
        return carry

    def load(block, s, carry):
        extra = block[modes:modes + 16, :].astype(F32)
        direction_ref[pl.ds(s, 1), :] = (extra[0:1] + extra[1:2]) + extra[2:3]
        fix_ref[pl.ds(s, 1), :] = extra[4:5] - extra[3:4]
        return carry

    each(load, 0)
    fix = fix_ref[:, :modes]

    def turned(rows_of, by):
        by = by % subs
        return jnp.concatenate([rows_of[by:], rows_of[:by]], axis=0)

    def coarse_apply(direction):
        direction_ref[...] = jnp.concatenate([direction, turned(direction, 1)], axis=1)

        def one(block, s, carry):
            values = block[:modes, :].astype(F32)
            pair = direction_ref[pl.ds(s, 1), :]
            ahead = jnp.sum(values * pair, axis=1, keepdims=True)
            image_ref[pl.ds(s, 1), :] = jnp.sum(
                values * column(pair[:, :modes]), axis=0, keepdims=True
            )
            return jnp.where(lane_is((modes, 128), s), ahead, carry)

        ahead_all = each(one, jnp.zeros((modes, 128), F32))
        image = image_ref[...]
        square_part = ahead_all.T[:subs] + image[:, :modes] + fix * direction
        return square_part + turned(image[:, modes:], -1)

    def inner(left, right):
        return jnp.sum(jnp.sum(left * right, axis=0, keepdims=True), axis=1, keepdims=True)

    remain = direction_ref[:, :modes]
    direction = remain
    result = jnp.zeros_like(remain)
    norm_now = inner(remain, remain)
    for iteration in range(CITERS):
        image = coarse_apply(direction)
        step_size = norm_now / inner(direction, image)
        result = result + step_size * direction
        if iteration + 1 < CITERS:
            remain = remain - step_size * image
            norm_next = inner(remain, remain)
            direction = remain + (norm_next / norm_now) * direction
            norm_now = norm_next
    direction_ref[:, :modes] = result
    own = direction_ref[pl.ds(me, 1), :modes]
    solution[...] = own
    spread[...] = jnp.broadcast_to(column(own), (modes, layers))
    ahead_column = column(direction_ref[pl.ds(lax.rem(me + 1, subs), 1), :modes])
    behind_column = column(direction_ref[pl.ds(lax.rem(me + subs - 1, subs), 1), :modes])
    at_top = lane_is((modes, layers), layers - 1)
    at_bottom = lane_is((modes, layers), 0)

    def placed(pack, values):
        return lax.dot_general(
            pack, values, TN, precision=PRECISE, preferred_element_type=F32
        ).reshape(planes, rows, layers)

    ends = placed(picked[0], jnp.where(at_top, ahead_column, 0.0)) + placed(
        picked[1], jnp.where(at_bottom, behind_column, 0.0)
    )

    def add_mode(j, carry):
        fields, near, last = list(carry[0]), carry[1], carry[2]
        for u in range(MODES):
            k = j * MODES + u
            scale = spread[pl.ds(k, 1), :]
            for x, plane in enumerate((zvec[k, held[0]], zvec[k, held[1]], inner_got[k])):
                fields[x] = fields[x] + scale * plane.astype(F32)
            near = near + scale * outer_got[k].astype(F32)
            last = last + scale * outer_last[k].astype(F32)
        return tuple(fields), near, last

    zero, short = jnp.zeros((rows, layers), F32), jnp.zeros((half, layers), F32)
    field, near, last = lax.fori_loop(0, modes // MODES, add_mode, ((zero,) * 3, short, short))
    outer_field[pl.ds(pl.multiple_of(side * half, half), half), :] = near
    outer_field[pl.ds(pl.multiple_of((1 - side) * half, half), half), :] = last
    outside = (field[2], jnp.where(at_edge, 0.0, outer_field[...]))
    faces = (inner_face[...], outer_face[...])
    for x in range(2):
        f = field[x]
        end_field = jnp.where(side == x, ends[1], ends[0])
        image = (
            terms[x, 0] * f
            - middle[0] * field[1 - x]
            - faces[x] * outside[x]
            - terms[x, 1] * pltpu.roll(f, 1, 0)
            - terms[x, 2] * pltpu.roll(f, rows - 1, 0)
            - terms[x, 3] * pltpu.roll(f, 1, 1)
            - terms[x, 4] * pltpu.roll(f, layers - 1, 1)
            - terms[x, 5] * end_field
        )
        deflated[held[x]] = resid[held[x]] - image


def swapped(value, axis, first):
    count = lax.axis_size(axis)
    pairs = []
    for i in range(count):
        up = (i - first) % 2 == 0
        pairs.append((i, (i + 1) % count if up else (i - 1) % count))
    return lax.ppermute(value, axis, pairs)


def swapped_open(value):
    pairs = []
    for i in range(1, lax.axis_size("pln") - 1):
        pairs.append((i, i + 1 if i % 2 else i - 1))
    return lax.ppermute(value, "pln", pairs)


def swapped_all(value):
    subs, count = lax.axis_size("sub"), lax.axis_size("pln")
    pairs = []
    for s in range(subs):
        for i in range(count):
            if 0 < i < count - 1:
                to = (s, i + 1 if i % 2 else i - 1)
            else:
                to = (s ^ 1, i)
            pairs.append((s * count + i, to[0] * count + to[1]))
    return lax.ppermute(value, ("sub", "pln"), pairs)


def exchanged(value, axis, mask):
    return lax.ppermute(value, axis, [(i, i ^ mask) for i in range(lax.axis_size(axis))])


def gathered(value, axis):
    if lax.axis_size(axis) != 8:
        return [lax.all_gather(value, axis)]
    pair = jnp.stack([value, exchanged(value, axis, 1)])
    return [pair] + [exchanged(pair, axis, mask) for mask in (2, 4, 6)]


def body(labels, levels, zvec, resid):
    modes, planes, rows, layers = zvec.shape
    half = rows // 2
    subs, parts = lax.axis_size("sub"), lax.axis_size("pln")
    shape = jax.ShapeDtypeStruct
    order = lax.axis_index("sub") if subs == 8 else 0
    place = jnp.stack(
        [jnp.int32(v) for v in (lax.axis_index("sub"), lax.axis_index("pln"), parts, order)]
    )
    pack = shape((modes + 16, planes * rows), BF16)
    [outer_near] = call(
        stage_kernel,
        [shape((modes + rows // half, half, layers), BF16)],
        [SMEM, HBM, HBM],
        [pltpu.VMEM(labels.shape, jnp.int32), pltpu.SemaphoreType.DMA, pltpu.SemaphoreType.DMA],
        moved=1 << 20,
    )(place, *(pltpu.with_memory_space_constraint(v, pltpu.HBM) for v in (labels, zvec)))
    outer_got = swapped_all(outer_near)
    [inner_send] = call(
        plane_kernel, [shape((modes + 1, rows, layers), BF16)], [SMEM, VMEM, VMEM, ANY], moved=2 << 20
    )(place, labels, zvec, outer_near)
    inner_got = swapped(inner_send, "pln", 0)
    rest = shape((modes, half, layers), BF16)
    here, outer_rest, one_pack, two_pack = call(
        prepare_kernel,
        [shape((planes, rows, modes, layers), BF16), rest, pack, pack],
        [SMEM, VMEM, VMEM, ANY],
        flops=10_000_000,
        moved=6 << 20,
    )(place, labels, zvec, inner_send)
    one_got = swapped(one_pack, "sub", 0)
    two_got = swapped(two_pack, "sub", 1)
    field = (planes, rows, layers)
    plane = (rows, layers)
    partial, weights = call(
        block_kernel,
        [shape((modes + 8, modes), F32), shape((7,) + plane, F32)],
        [SMEM, SMEM] + [VMEM] * 3,
        [pltpu.VMEM(field, F32)] * 3,
        flops=400_000_000,
        moved=3 << 20,
    )(place, levels, labels, resid, here)
    turned = pltpu.VMEM((half, modes, layers), BF16)
    partial, inner_face = call(
        inner_kernel,
        [shape((modes + 8, modes), F32), shape(plane, F32)],
        [SMEM, SMEM] + [VMEM] * 4,
        [turned],
        flops=100_000_000,
        moved=1 << 20,
    )(place, levels, partial, weights, here, inner_got)
    block, outer_face = call(
        outer_kernel,
        [shape((modes + 8, 2 * modes), F32), shape(plane, F32)],
        [SMEM, SMEM] + [VMEM] * 8,
        [turned, pltpu.VMEM(plane, F32)],
        flops=100_000_000,
        moved=1 << 20,
    )(place, levels, partial, weights, here, outer_got, one_pack, two_pack, one_got, two_got)
    packed = shape((modes + 16, 2 * modes), BF16)
    if parts == 4:
        others = [exchanged(block, "pln", mask) for mask in (1, 2, 3)]
    else:
        block = lax.psum(block, "pln")
        others = [jnp.zeros_like(block)] * 3
    [packed] = call(sum_kernel, [packed], [VMEM] * 4)(block, *others)
    [outer_rest] = call(release_kernel, [rest], [ANY] * 2, aliases={1: 0})(packed, outer_rest)
    blocks = gathered(packed, "sub")
    outer_last = swapped_open(outer_rest)
    terms, picked = call(
        terms_kernel,
        [shape((planes, 6) + plane, F32), shape((2, modes, planes * rows), F32)],
        [SMEM, SMEM, ANY] + [VMEM] * 5,
        [pltpu.VMEM(field, F32)],

        flops=1 << 33,
        moved=1 << 20,
    )(place, levels, blocks[0], one_got, two_got, weights, inner_face, outer_face)
    return tuple(
        call(
            finish_kernel,
            [shape((1, modes), F32), shape(field, F32)],
            [SMEM] + [VMEM] * (10 + len(blocks)),
            [
                pltpu.VMEM((subs, 2 * modes), F32),
                pltpu.VMEM((subs, 2 * modes), F32),
                pltpu.VMEM((modes, layers), F32),
                pltpu.VMEM(plane, F32),
                pltpu.VMEM((subs, 2 * modes), F32),
            ],
            flops=10_000_000,
            moved=5 << 20,
        )(
            place, *blocks, zvec, inner_got, outer_got, outer_last, picked, terms, weights, inner_face,
            outer_face, resid,
        )
    )


def solution(mesh):
    in_specs = (P("pln", None, "sub"), P(), P(None, "pln", None, "sub"), P("pln", None, "sub"))
    out_specs = (P("sub", None), P("pln", None, "sub"))
    return jax.shard_map(body, mesh=mesh, in_specs=in_specs, out_specs=out_specs, check_vma=False)
```

```python
import jax
import jax.numpy as jnp
from jax import lax
from jax.experimental import pallas as pl
from jax.experimental.pallas import tpu as pltpu
from jax.sharding import PartitionSpec as P

CITERS = 2
STEP = 16
MODES = 8
CHUNK = 16
F32 = jnp.float32
BF16 = jnp.bfloat16
PRECISE = lax.Precision.HIGHEST
NT = (((1,), (1,)), ((), ()))
TN = (((0,), (0,)), ((), ()))
VMEM = pl.BlockSpec(memory_space=pltpu.VMEM)
SMEM = pl.BlockSpec(memory_space=pltpu.SMEM)
HBM = pl.BlockSpec(memory_space=pltpu.HBM)
ANY = pl.BlockSpec(memory_space=pl.ANY)


def call(kernel, outs, specs, scratch=(), flops=0, moved=0, limit=32, aliases=None):
    return pl.pallas_call(
        kernel,
        out_shape=outs,
        in_specs=specs,
        out_specs=[ANY if at in (aliases or {}).values() else VMEM for at in range(len(outs))],
        input_output_aliases=aliases or {},
        scratch_shapes=list(scratch),
        cost_estimate=pl.CostEstimate(flops=flops, bytes_accessed=moved, transcendentals=0),
        compiler_params=pltpu.CompilerParams(vmem_limit_bytes=limit << 20),
    )


def harmonic(left_value, right_value):
    return 2.0 * left_value * right_value / (left_value + right_value)


def coefficients(labels, levels_ref):
    weighted = jnp.zeros(labels.shape, F32)
    for level in range(levels_ref.shape[0]):
        weighted = weighted + jnp.where(labels == level, levels_ref[level], 0.0)
    return weighted


def lane_is(shape, lane):
    return lax.broadcasted_iota(jnp.int32, shape, len(shape) - 1) == lane


def pick_row(lane, width):
    row = lax.broadcasted_iota(jnp.int32, (16, width), 0)
    return ((row == 0) & lane_is((16, width), lane)).astype(BF16)


def stage_kernel(place, labels_far, zvec, inner_send, outer_near, labels, label_sem, sems):
    modes, planes, rows, layers = zvec.shape
    half = rows // 2
    side = lax.rem(place[1], 2)
    start = pl.multiple_of((1 - side) * half, half)
    label_copy = pltpu.make_async_copy(labels_far, labels, label_sem)
    copies = [
        pltpu.make_async_copy(
            zvec.at[:, side, pl.ds(start, half), :], outer_near.at[pl.ds(0, modes)], sems.at[0]
        ),
        pltpu.make_async_copy(zvec.at[:, 1 - side], inner_send.at[pl.ds(0, modes)], sems.at[1]),
    ]
    label_copy.start()
    for copy in copies:
        copy.start()
    label_copy.wait()
    outer_near[modes:] = labels[side].astype(F32).astype(BF16).reshape(rows // half, half, layers)
    inner_send[modes] = labels[1 - side].astype(F32).astype(BF16)
    for copy in copies:
        copy.wait()


def release_kernel(after, outer_rest, outer_out):
    pass


def prepare_kernel(place, labels, held, planes_out, outer_rest, one_pack, two_pack):
    modes, planes, rows, layers = held.shape
    half = rows // 2
    width = planes * rows
    side = lax.rem(place[1], 2)
    odd = lax.rem(place[0], 2) == 1
    one_lane = jnp.where(odd, 0, layers - 1)
    two_lane = jnp.where(odd, layers - 1, 0)
    row = lax.broadcasted_iota(jnp.int32, (16, layers), 0)
    both = ((row == 0) & lane_is((16, layers), one_lane)) | ((row == 1) & lane_is((16, layers), two_lane))
    both = both.astype(BF16)
    flat = labels[...].astype(F32).astype(BF16).reshape(width, layers)
    for out, lane in ((one_pack, one_lane), (two_pack, two_lane)):
        out[modes:] = lax.dot_general(
            pick_row(lane, layers), flat, NT, preferred_element_type=F32
        ).astype(BF16)
    for k in range(0, modes, CHUNK):
        at = slice(k, k + CHUNK)
        ends = lax.dot_general(
            both, held[at].reshape(-1, layers), NT, preferred_element_type=F32
        )
        for out, index in ((one_pack, 0), (two_pack, 1)):
            out[at] = jnp.concatenate(
                [ends[index:index + 1, j * width:(j + 1) * width] for j in range(CHUNK)], axis=0
            ).astype(BF16)
        for slot, plane in ((0, 1 - side), (1, side)):
            planes_out[slot, :, at, :] = jnp.swapaxes(held[at, plane], 0, 1)
        outer_rest[at] = held[at, side, pl.ds(pl.multiple_of(side * half, half), half), :]


def block_kernel(
    place, levels, labels, resid, here, partial, weights, half_diag, link_y, link_z,
):
    planes, rows, layers = labels.shape
    modes = here.shape[2]
    side = lax.rem(place[1], 2)
    at_edge = (place[1] == 0) | (place[1] == place[2] - 1)
    held = (1 - side, side)
    coef = [coefficients(labels[x], levels) for x in held]
    middle = harmonic(coef[0], coef[1])
    weights[0] = middle
    row = lax.broadcasted_iota(jnp.int32, (rows, layers), 0)
    lane = lax.broadcasted_iota(jnp.int32, (rows, layers), 1)
    for x in range(2):
        c = coef[x]
        up_y = harmonic(c, jnp.where(row == rows - 1, c, pltpu.roll(c, rows - 1, 0)))
        up_z = harmonic(c, pltpu.roll(c, layers - 1, 1))
        down_y = jnp.where(row == 0, c, pltpu.roll(up_y, 1, 0))
        weights[1 + x] = up_y
        weights[3 + x] = up_z
        weights[5 + x] = c
        inner_z = jnp.where(lane == layers - 1, 0.0, up_z)
        total = middle + up_y + down_y + inner_z + pltpu.roll(inner_z, 1, 1)
        if x == 1:
            total = total + jnp.where(at_edge, c, 0.0)
        half_diag[x] = 0.5 * total
        link_y[x] = jnp.where(row == rows - 1, 0.0, up_y)
        link_z[x] = inner_z

    def step(j, carry):
        total, rhs, wide = carry
        for u in range(STEP):
            y = j * STEP + u
            at = pl.ds(y, 1)
            ahead = jnp.minimum(y + 1, rows - 1)
            up = [here[x, ahead].astype(F32) for x in range(2)]
            images = []
            for x in range(2):
                image = (
                    half_diag[x, at, :] * wide[x]
                    - link_y[x, at, :] * up[x]
                    - link_z[x, at, :] * pltpu.roll(wide[x], layers - 1, 1)
                )
                if x == 0:
                    image = image - weights[0, at, :] * wide[1]
                rhs = rhs + resid[held[x], at, :] * wide[x]
                images.append(image.astype(BF16))
            total = total + lax.dot_general(
                jnp.concatenate(images, axis=1),
                jnp.concatenate([here[0, y], here[1, y]], axis=1),
                NT,
                preferred_element_type=F32,
            )
            wide = up
        return total, rhs, wide

    total, rhs, _ = lax.fori_loop(
        0,
        rows // STEP,
        step,
        (
            jnp.zeros((modes, modes), F32),
            jnp.zeros((modes, layers), F32),
            [here[x, 0].astype(F32) for x in range(2)],
        ),
    )
    partial[:modes, :] = total
    partial[modes:, :] = lax.dot_general(
        jnp.ones((8, layers), F32), rhs, NT, precision=PRECISE, preferred_element_type=F32
    )


def turn(got, start, out):
    half, modes, layers = out.shape
    for k in range(0, modes, CHUNK):
        out[:, k:k + CHUNK, :] = jnp.swapaxes(got[k:k + CHUNK, pl.ds(start, half), :], 0, 1)


def face_product(weight_ref, base, own, other):
    half, modes, layers = other.shape

    def step(j, total):
        left, right = [], []
        for u in range(STEP):
            y = j * STEP + u
            weight = weight_ref[pl.ds(base + y, 1), :]
            image = weight * (own[base + y].astype(F32) - other[y].astype(F32))
            left.append(jnp.concatenate([own[base + y], other[y]], axis=0))
            right.append(image.astype(BF16))
        return total + lax.dot_general(
            jnp.concatenate(left, axis=1), jnp.concatenate(right, axis=1), NT,
            preferred_element_type=F32,
        )

    total = lax.fori_loop(0, half // STEP, step, jnp.zeros((2 * modes, modes), F32))
    return total[:modes] - total[modes:]


def inner_kernel(place, levels, partial, weights, here, inner_got, out, face, turned):
    planes, rows, modes, layers = here.shape
    half = rows // 2
    side = lax.rem(place[1], 2)
    base = pl.multiple_of(side * half, half)
    turn(inner_got, base, turned)
    face[...] = harmonic(weights[5], coefficients(inner_got[modes].astype(F32), levels))
    out[:modes, :] = partial[:modes, :] + 0.5 * face_product(face, base, here.at[0], turned)
    out[modes:, :] = partial[modes:, :]


def outer_kernel(
    place, levels, partial, weights, here, outer_got, one_pack, two_pack, one_got, two_got,
    out, face, turned, face_here,
):
    planes, rows, modes, layers = here.shape
    half = rows // 2
    side = lax.rem(place[1], 2)
    odd = lax.rem(place[0], 2) == 1
    at_edge = (place[1] == 0) | (place[1] == place[2] - 1)
    base = pl.multiple_of(side * half, half)
    turn(outer_got, 0, turned)
    coef = coefficients(outer_got[modes:].astype(F32).reshape(rows, layers), levels)
    between = harmonic(weights[6], coef)
    face[...] = jnp.where(at_edge, weights[6], between)
    face_here[...] = jnp.where(at_edge, 0.0, between)
    cross = face_product(face_here, base, here.at[1], turned)

    def coef_row(pack):
        return coefficients(pack[modes:modes + 16].astype(F32)[0:1], levels)

    one, two = one_pack[...].astype(F32), two_pack[...].astype(F32)
    one_other, two_other = one_got[...].astype(F32), two_got[...].astype(F32)
    first, last = jnp.where(odd, one, two), jnp.where(odd, two, one)
    next_first = jnp.where(odd, two_other, one_other)
    prev_last = jnp.where(odd, one_other, two_other)
    weight_low = harmonic(coef_row(first), coef_row(prev_last))
    weight_high = harmonic(coef_row(last), coef_row(next_first))

    def product(left, right):
        return lax.dot_general(left, right, NT, precision=PRECISE, preferred_element_type=F32)

    edge_rows = weight_high * last[:modes]
    ends = product(weight_low * first[:modes], first[:modes]) + product(edge_rows, last[:modes])
    square = partial[:modes, :] + 0.5 * (cross + ends)
    out[:modes, :modes] = square + square.T
    out[:modes, modes:] = -product(edge_rows, next_first[:modes])
    out[modes:, :modes] = partial[modes:, :]
    out[modes:, modes:] = jnp.zeros((8, modes), F32)


def terms_kernel(
    place, levels, pair, one_got, two_got, weights, inner_face, outer_face, terms, picked, coef_ref
):
    modes, width = picked.shape[1:]
    rows, layers = inner_face.shape
    side = lax.rem(place[1], 2)
    odd = lax.rem(place[0], 2) == 1
    one_other, two_other = one_got[...].astype(F32), two_got[...].astype(F32)
    next_first = jnp.where(odd, two_other, one_other)
    prev_last = jnp.where(odd, one_other, two_other)
    picked[0] = next_first[:modes]
    picked[1] = prev_last[:modes]
    end_labels = lax.dot_general(
        next_first[modes:].astype(BF16), pick_row(layers - 1, layers), TN, preferred_element_type=F32
    ) + lax.dot_general(
        prev_last[modes:].astype(BF16), pick_row(0, layers), TN, preferred_element_type=F32
    )
    coef_ref[...] = coefficients(end_labels, levels).reshape(width // rows, rows, layers)
    row = lax.broadcasted_iota(jnp.int32, (rows, layers), 0)
    lane = lax.broadcasted_iota(jnp.int32, (rows, layers), 1)
    for x, face in enumerate((inner_face, outer_face)):
        c = weights[5 + x]
        end_weight = harmonic(c, coef_ref[1 - side if x == 0 else side])
        up_y, up_z = weights[1 + x], weights[3 + x]
        down_y = jnp.where(row == 0, c, pltpu.roll(up_y, 1, 0))
        down_z = pltpu.roll(up_z, 1, 1)
        total = face[...] + weights[0] + up_y + down_y
        total = total + jnp.where(lane == layers - 1, end_weight, up_z)
        terms[x, 0] = total + jnp.where(lane == 0, end_weight, down_z)
        terms[x, 1] = jnp.where(row == 0, 0.0, down_y)
        terms[x, 2] = jnp.where(row == rows - 1, 0.0, up_y)
        terms[x, 3] = jnp.where(lane == 0, 0.0, down_z)
        terms[x, 4] = jnp.where(lane == layers - 1, 0.0, up_z)
        terms[x, 5] = end_weight


def pair_kernel(own, across, beside, oblique, out):
    modes = own.shape[1] // 2
    encode(own[...] + across[...], modes, out.at[0])
    encode(beside[...] + oblique[...], modes, out.at[1])


def single_kernel(own, out):
    encode(own[...], own.shape[1] // 2, out)


def encode(total, modes, out):
    row = lax.broadcasted_iota(jnp.int32, (modes, 2 * modes), 0)
    lane = lax.broadcasted_iota(jnp.int32, (modes, 2 * modes), 1)
    values = total[:modes]
    high = values.astype(BF16).astype(F32)
    low = values - high
    out[:modes] = jnp.where((lane <= row) | (lane >= modes), high, low).astype(BF16)
    diagonal = lane == row
    right = total[modes:modes + 1]
    parts = []
    for _ in range(3):
        part = right.astype(BF16).astype(F32)
        parts.append(part)
        right = right - part
    for part in (high, low):
        parts.append(jnp.sum(jnp.where(diagonal, part, 0.0), axis=0, keepdims=True))
    rows = lax.broadcasted_iota(jnp.int32, (16, 2 * modes), 0)
    extra = jnp.zeros((16, 2 * modes), F32)
    for index, part in enumerate(parts):
        extra = jnp.where(rows == index, part, extra)
    out[modes:] = extra.astype(BF16)


def finish_kernel(place, *refs):
    count = len(refs) - 17
    blocks, refs = refs[:count], refs[count:]
    zvec, inner_got, outer_got, outer_last, picked, terms, middle, inner_face, outer_face, resid = refs[:10]
    solution, deflated, direction_ref, image_ref, spread, outer_field, fix_ref = refs[10:]
    subs = direction_ref.shape[0]
    modes, planes, rows, layers = zvec.shape
    half = rows // 2
    me = place[0]
    side = lax.rem(place[1], 2)
    odd = lax.rem(me, 2) == 1
    at_edge = (place[1] == 0) | (place[1] == place[2] - 1)
    order = place[3]
    held = (1 - side, side)
    square = (modes, modes)
    eye = lax.broadcasted_iota(jnp.int32, square, 0) == lax.broadcasted_iota(jnp.int32, square, 1)

    def column(row):
        return jnp.sum(jnp.where(eye, row, 0.0), axis=1, keepdims=True)

    def each(body, carry):
        for index, block in enumerate(blocks):
            held_here = block.shape[0]
            if held_here <= 8:
                for entry in range(held_here):
                    s = jnp.bitwise_xor(order, index * held_here + entry)
                    carry = body(block.at[entry], s, carry)
            else:
                carry = lax.fori_loop(
                    0, held_here, lambda entry, c, block=block: body(block.at[entry], entry, c), carry
                )
        return carry

    def load(block, s, carry):
        extra = block[modes:modes + 16, :].astype(F32)
        direction_ref[pl.ds(s, 1), :] = (extra[0:1] + extra[1:2]) + extra[2:3]
        fix_ref[pl.ds(s, 1), :] = extra[4:5] - extra[3:4]
        return carry

    each(load, 0)
    fix = fix_ref[:, :modes]

    def turned(rows_of, by):
        by = by % subs
        return jnp.concatenate([rows_of[by:], rows_of[:by]], axis=0)

    def coarse_apply(direction):
        direction_ref[...] = jnp.concatenate([direction, turned(direction, 1)], axis=1)

        def one(block, s, carry):
            values = block[:modes, :].astype(F32)
            pair = direction_ref[pl.ds(s, 1), :]
            ahead = jnp.sum(values * pair, axis=1, keepdims=True)
            image_ref[pl.ds(s, 1), :] = jnp.sum(
                values * column(pair[:, :modes]), axis=0, keepdims=True
            )
            return jnp.where(lane_is((modes, 128), s), ahead, carry)

        ahead_all = each(one, jnp.zeros((modes, 128), F32))
        image = image_ref[...]
        square_part = ahead_all.T[:subs] + image[:, :modes] + fix * direction
        return square_part + turned(image[:, modes:], -1)

    def inner(left, right):
        return jnp.sum(jnp.sum(left * right, axis=0, keepdims=True), axis=1, keepdims=True)

    remain = direction_ref[:, :modes]
    direction = remain
    result = jnp.zeros_like(remain)
    norm_now = inner(remain, remain)
    for iteration in range(CITERS):
        image = coarse_apply(direction)
        step_size = norm_now / inner(direction, image)
        result = result + step_size * direction
        if iteration + 1 < CITERS:
            remain = remain - step_size * image
            norm_next = inner(remain, remain)
            direction = remain + (norm_next / norm_now) * direction
            norm_now = norm_next
    direction_ref[:, :modes] = result
    own = direction_ref[pl.ds(me, 1), :modes]
    solution[...] = own
    spread[...] = jnp.broadcast_to(column(own), (modes, layers))
    ahead_column = column(direction_ref[pl.ds(lax.rem(me + 1, subs), 1), :modes])
    behind_column = column(direction_ref[pl.ds(lax.rem(me + subs - 1, subs), 1), :modes])
    ahead_row = jnp.sum(ahead_column * picked[0], axis=0, keepdims=True)
    behind_row = jnp.sum(behind_column * picked[1], axis=0, keepdims=True)
    width = planes * rows
    both_rows = jnp.where(
        lax.broadcasted_iota(jnp.int32, (8, width), 0) == 0,
        jnp.broadcast_to(ahead_row, (8, width)),
        jnp.broadcast_to(behind_row, (8, width)),
    )
    columns = both_rows.T
    ends = jnp.where(
        lane_is((width, layers), layers - 1),
        columns[:, 0:1],
        jnp.where(lane_is((width, layers), 0), columns[:, 1:2], 0.0),
    ).reshape(planes, rows, layers)

    def add_mode(j, carry):
        fields, near, last = list(carry[0]), carry[1], carry[2]
        for u in range(MODES):
            k = j * MODES + u
            scale = spread[pl.ds(k, 1), :]
            for x, plane in enumerate((zvec[k, held[0]], zvec[k, held[1]], inner_got[k])):
                fields[x] = fields[x] + scale * plane.astype(F32)
            near = near + scale * outer_got[k].astype(F32)
            last = last + scale * outer_last[k].astype(F32)
        return tuple(fields), near, last

    zero, short = jnp.zeros((rows, layers), F32), jnp.zeros((half, layers), F32)
    field, near, last = lax.fori_loop(0, modes // MODES, add_mode, ((zero,) * 3, short, short))
    outer_field[pl.ds(pl.multiple_of(side * half, half), half), :] = near
    outer_field[pl.ds(pl.multiple_of((1 - side) * half, half), half), :] = last
    outside = (field[2], jnp.where(at_edge, 0.0, outer_field[...]))
    faces = (inner_face[...], outer_face[...])
    for x in range(2):
        f = field[x]
        end_field = jnp.where(side == x, ends[1], ends[0])
        image = (
            terms[x, 0] * f
            - middle[0] * field[1 - x]
            - faces[x] * outside[x]
            - terms[x, 1] * pltpu.roll(f, 1, 0)
            - terms[x, 2] * pltpu.roll(f, rows - 1, 0)
            - terms[x, 3] * pltpu.roll(f, 1, 1)
            - terms[x, 4] * pltpu.roll(f, layers - 1, 1)
            - terms[x, 5] * end_field
        )
        deflated[held[x]] = resid[held[x]] - image


def swapped(value, axis, first):
    count = lax.axis_size(axis)
    pairs = []
    for i in range(count):
        up = (i - first) % 2 == 0
        pairs.append((i, (i + 1) % count if up else (i - 1) % count))
    return lax.ppermute(value, axis, pairs)


def swapped_all(value):
    subs, count = lax.axis_size("sub"), lax.axis_size("pln")
    pairs = []
    for s in range(subs):
        for i in range(count):
            if 0 < i < count - 1:
                to = (s, i + 1 if i % 2 else i - 1)
            else:
                to = (s ^ 1, i)
            pairs.append((s * count + i, to[0] * count + to[1]))
    return lax.ppermute(value, ("sub", "pln"), pairs)


def exchanged(value, axis, mask):
    return lax.ppermute(value, axis, [(i, i ^ mask) for i in range(lax.axis_size(axis))])


def partner(value, sub_mask, pln_mask):
    subs, count = lax.axis_size("sub"), lax.axis_size("pln")
    pairs = [
        (s * count + p, (s ^ sub_mask) * count + (p ^ pln_mask)) for s in range(subs) for p in range(count)
    ]
    return lax.ppermute(value, ("sub", "pln"), pairs)


def body(labels, levels, zvec, resid):
    modes, planes, rows, layers = zvec.shape
    half = rows // 2
    subs, parts = lax.axis_size("sub"), lax.axis_size("pln")
    shape = jax.ShapeDtypeStruct
    order = lax.axis_index("sub") if subs == 8 else 0
    place = jnp.stack(
        [jnp.int32(v) for v in (lax.axis_index("sub"), lax.axis_index("pln"), parts, order)]
    )
    pack = shape((modes + 16, planes * rows), BF16)
    inner_send, outer_near = call(
        stage_kernel,
        [shape((modes + 1, rows, layers), BF16), shape((modes + rows // half, half, layers), BF16)],
        [SMEM, HBM, HBM],
        [pltpu.VMEM(labels.shape, jnp.int32), pltpu.SemaphoreType.DMA, pltpu.SemaphoreType.DMA((2,))],
        moved=2 << 20,
    )(place, *(pltpu.with_memory_space_constraint(v, pltpu.HBM) for v in (labels, zvec)))
    outer_got = swapped_all(outer_near)
    inner_got = swapped(inner_send, "pln", 0)
    rest = shape((modes, half, layers), BF16)
    here, outer_rest, one_pack, two_pack = call(
        prepare_kernel,
        [shape((planes, rows, modes, layers), BF16), rest, pack, pack],
        [SMEM, VMEM, VMEM],
        flops=10_000_000,
        moved=6 << 20,
    )(place, labels, zvec)
    one_got = swapped(one_pack, "sub", 0)
    two_got = swapped(two_pack, "sub", 1)
    field = (planes, rows, layers)
    plane = (rows, layers)
    partial, weights = call(
        block_kernel,
        [shape((modes + 8, modes), F32), shape((7,) + plane, F32)],
        [SMEM, SMEM] + [VMEM] * 3,
        [pltpu.VMEM(field, F32)] * 3,
        flops=400_000_000,
        moved=3 << 20,
    )(place, levels, labels, resid, here)
    turned = pltpu.VMEM((half, modes, layers), BF16)
    partial, inner_face = call(
        inner_kernel,
        [shape((modes + 8, modes), F32), shape(plane, F32)],
        [SMEM, SMEM] + [VMEM] * 4,
        [turned],
        flops=100_000_000,
        moved=1 << 20,
    )(place, levels, partial, weights, here, inner_got)
    block, outer_face = call(
        outer_kernel,
        [shape((modes + 8, 2 * modes), F32), shape(plane, F32)],
        [SMEM, SMEM] + [VMEM] * 8,
        [turned, pltpu.VMEM(plane, F32)],
        flops=100_000_000,
        moved=1 << 20,
    )(place, levels, partial, weights, here, outer_got, one_pack, two_pack, one_got, two_got)
    packed = (modes + 16, 2 * modes)
    if parts == 4 and subs == 8:
        block = block + exchanged(block, "pln", 1)
        others = [partner(block, *masks) for masks in ((0, 2), (1, 0), (1, 2))]
        [pair] = call(pair_kernel, [shape((2,) + packed, BF16)], [VMEM] * 4)(block, *others)
        blocks = [pair] + [exchanged(pair, "sub", mask) for mask in (2, 4, 6)]
    else:
        [single] = call(single_kernel, [shape(packed, BF16)], [VMEM])(lax.psum(block, "pln"))
        blocks = [lax.all_gather(single, "sub")]
    [outer_rest] = call(release_kernel, [rest], [ANY] * 2, aliases={1: 0})(block, outer_rest)
    outer_last = swapped_all(outer_rest)
    terms, picked = call(
        terms_kernel,
        [shape((planes, 6) + plane, F32), shape((2, modes, planes * rows), F32)],
        [SMEM, SMEM, ANY] + [VMEM] * 5,
        [pltpu.VMEM(field, F32)],

        flops=1 << 33,
        moved=1 << 20,
    )(place, levels, blocks[0], one_got, two_got, weights, inner_face, outer_face)
    return tuple(
        call(
            finish_kernel,
            [shape((1, modes), F32), shape(field, F32)],
            [SMEM] + [VMEM] * (10 + len(blocks)),
            [
                pltpu.VMEM((subs, 2 * modes), F32),
                pltpu.VMEM((subs, 2 * modes), F32),
                pltpu.VMEM((modes, layers), F32),
                pltpu.VMEM(plane, F32),
                pltpu.VMEM((subs, 2 * modes), F32),
            ],
            flops=10_000_000,
            moved=5 << 20,
        )(
            place, *blocks, zvec, inner_got, outer_got, outer_last, picked, terms, weights, inner_face,
            outer_face, resid,
        )
    )


def solution(mesh):
    in_specs = (P("pln", None, "sub"), P(), P(None, "pln", None, "sub"), P("pln", None, "sub"))
    out_specs = (P("sub", None), P("pln", None, "sub"))
    return jax.shard_map(body, mesh=mesh, in_specs=in_specs, out_specs=out_specs, check_vma=False)
```

```python
import jax
import jax.numpy as jnp
from jax import lax
from jax.experimental import pallas as pl
from jax.experimental.pallas import tpu as pltpu
from jax.sharding import PartitionSpec as P

CITERS = 2
STEP = 16
MODES = 8
CHUNK = 16
F32 = jnp.float32
BF16 = jnp.bfloat16
PRECISE = lax.Precision.HIGHEST
NT = (((1,), (1,)), ((), ()))
TN = (((0,), (0,)), ((), ()))
VMEM = pl.BlockSpec(memory_space=pltpu.VMEM)
SMEM = pl.BlockSpec(memory_space=pltpu.SMEM)
HBM = pl.BlockSpec(memory_space=pltpu.HBM)
ANY = pl.BlockSpec(memory_space=pl.ANY)


def call(kernel, outs, specs, scratch=(), flops=0, moved=0, limit=32, aliases=None):
    return pl.pallas_call(
        kernel,
        out_shape=outs,
        in_specs=specs,
        out_specs=[ANY if at in (aliases or {}).values() else VMEM for at in range(len(outs))],
        input_output_aliases=aliases or {},
        scratch_shapes=list(scratch),
        cost_estimate=pl.CostEstimate(flops=flops, bytes_accessed=moved, transcendentals=0),
        compiler_params=pltpu.CompilerParams(vmem_limit_bytes=limit << 20),
    )


def harmonic(left_value, right_value):
    return 2.0 * left_value * right_value / (left_value + right_value)


def coefficients(labels, levels_ref):
    weighted = jnp.zeros(labels.shape, F32)
    for level in range(levels_ref.shape[0]):
        weighted = weighted + jnp.where(labels == level, levels_ref[level], 0.0)
    return weighted


def lane_is(shape, lane):
    return lax.broadcasted_iota(jnp.int32, shape, len(shape) - 1) == lane


def pick_row(lane, width):
    row = lax.broadcasted_iota(jnp.int32, (16, width), 0)
    return ((row == 0) & lane_is((16, width), lane)).astype(BF16)


def stage_kernel(place, labels_far, zvec, inner_send, outer_near, labels, label_sem, sems):
    modes, planes, rows, layers = zvec.shape
    half = rows // 2
    side = lax.rem(place[1], 2)
    start = pl.multiple_of((1 - side) * half, half)
    label_copy = pltpu.make_async_copy(labels_far, labels, label_sem)
    copies = [
        pltpu.make_async_copy(
            zvec.at[:, side, pl.ds(start, half), :], outer_near.at[pl.ds(0, modes)], sems.at[0]
        ),
        pltpu.make_async_copy(zvec.at[:, 1 - side], inner_send.at[pl.ds(0, modes)], sems.at[1]),
    ]
    label_copy.start()
    for copy in copies:
        copy.start()
    label_copy.wait()
    outer_near[modes:] = labels[side].astype(F32).astype(BF16).reshape(rows // half, half, layers)
    inner_send[modes] = labels[1 - side].astype(F32).astype(BF16)
    for copy in copies:
        copy.wait()


def release_kernel(after, outer_rest, outer_out):
    pass


def prepare_kernel(place, labels, held, outer_rest, one_pack, two_pack):
    modes, planes, rows, layers = held.shape
    half = rows // 2
    width = planes * rows
    side = lax.rem(place[1], 2)
    odd = lax.rem(place[0], 2) == 1
    one_lane = jnp.where(odd, 0, layers - 1)
    two_lane = jnp.where(odd, layers - 1, 0)
    row = lax.broadcasted_iota(jnp.int32, (16, layers), 0)
    both = ((row == 0) & lane_is((16, layers), one_lane)) | ((row == 1) & lane_is((16, layers), two_lane))
    both = both.astype(BF16)
    flat = labels[...].astype(F32).astype(BF16).reshape(width, layers)
    for out, lane in ((one_pack, one_lane), (two_pack, two_lane)):
        out[modes:] = lax.dot_general(
            pick_row(lane, layers), flat, NT, preferred_element_type=F32
        ).astype(BF16)
    for k in range(0, modes, CHUNK):
        at = slice(k, k + CHUNK)
        ends = lax.dot_general(
            both, held[at].reshape(-1, layers), NT, preferred_element_type=F32
        )
        for out, index in ((one_pack, 0), (two_pack, 1)):
            out[at] = jnp.concatenate(
                [ends[index:index + 1, j * width:(j + 1) * width] for j in range(CHUNK)], axis=0
            ).astype(BF16)
        outer_rest[at] = held[at, side, pl.ds(pl.multiple_of(side * half, half), half), :]


def block_kernel(
    place, levels, labels, resid, zvec, after, partial, weights, here, half_diag, link_y, link_z,
):
    planes, rows, layers = labels.shape
    modes = here.shape[2]
    side = lax.rem(place[1], 2)
    at_edge = (place[1] == 0) | (place[1] == place[2] - 1)
    held = (1 - side, side)
    for slot, plane in enumerate(held):
        for k in range(0, modes, CHUNK):
            here[slot, :, k:k + CHUNK, :] = jnp.swapaxes(zvec[k:k + CHUNK, plane], 0, 1)
    coef = [coefficients(labels[x], levels) for x in held]
    middle = harmonic(coef[0], coef[1])
    weights[0] = middle
    row = lax.broadcasted_iota(jnp.int32, (rows, layers), 0)
    lane = lax.broadcasted_iota(jnp.int32, (rows, layers), 1)
    for x in range(2):
        c = coef[x]
        up_y = harmonic(c, jnp.where(row == rows - 1, c, pltpu.roll(c, rows - 1, 0)))
        up_z = harmonic(c, pltpu.roll(c, layers - 1, 1))
        down_y = jnp.where(row == 0, c, pltpu.roll(up_y, 1, 0))
        weights[1 + x] = up_y
        weights[3 + x] = up_z
        weights[5 + x] = c
        inner_z = jnp.where(lane == layers - 1, 0.0, up_z)
        total = middle + up_y + down_y + inner_z + pltpu.roll(inner_z, 1, 1)
        if x == 1:
            total = total + jnp.where(at_edge, c, 0.0)
        half_diag[x] = 0.5 * total
        link_y[x] = jnp.where(row == rows - 1, 0.0, up_y)
        link_z[x] = inner_z

    def step(j, carry):
        total, rhs, wide = carry
        for u in range(STEP):
            y = j * STEP + u
            at = pl.ds(y, 1)
            ahead = jnp.minimum(y + 1, rows - 1)
            up = [here[x, ahead].astype(F32) for x in range(2)]
            images = []
            for x in range(2):
                image = (
                    half_diag[x, at, :] * wide[x]
                    - link_y[x, at, :] * up[x]
                    - link_z[x, at, :] * pltpu.roll(wide[x], layers - 1, 1)
                )
                if x == 0:
                    image = image - weights[0, at, :] * wide[1]
                rhs = rhs + resid[held[x], at, :] * wide[x]
                images.append(image.astype(BF16))
            total = total + lax.dot_general(
                jnp.concatenate(images, axis=1),
                jnp.concatenate([here[0, y], here[1, y]], axis=1),
                NT,
                preferred_element_type=F32,
            )
            wide = up
        return total, rhs, wide

    total, rhs, _ = lax.fori_loop(
        0,
        rows // STEP,
        step,
        (
            jnp.zeros((modes, modes), F32),
            jnp.zeros((modes, layers), F32),
            [here[x, 0].astype(F32) for x in range(2)],
        ),
    )
    partial[:modes, :] = total
    partial[modes:, :] = lax.dot_general(
        jnp.ones((8, layers), F32), rhs, NT, precision=PRECISE, preferred_element_type=F32
    )


def turn(got, start, out):
    half, modes, layers = out.shape
    for k in range(0, modes, CHUNK):
        out[:, k:k + CHUNK, :] = jnp.swapaxes(got[k:k + CHUNK, pl.ds(start, half), :], 0, 1)


def face_product(weight_ref, base, own, other):
    half, modes, layers = other.shape

    def step(j, total):
        left, right = [], []
        for u in range(STEP):
            y = j * STEP + u
            weight = weight_ref[pl.ds(base + y, 1), :]
            image = weight * (own[base + y].astype(F32) - other[y].astype(F32))
            left.append(jnp.concatenate([own[base + y], other[y]], axis=0))
            right.append(image.astype(BF16))
        return total + lax.dot_general(
            jnp.concatenate(left, axis=1), jnp.concatenate(right, axis=1), NT,
            preferred_element_type=F32,
        )

    total = lax.fori_loop(0, half // STEP, step, jnp.zeros((2 * modes, modes), F32))
    return total[:modes] - total[modes:]


def inner_kernel(place, levels, partial, weights, here, inner_got, out, face, turned):
    planes, rows, modes, layers = here.shape
    half = rows // 2
    side = lax.rem(place[1], 2)
    base = pl.multiple_of(side * half, half)
    turn(inner_got, base, turned)
    face[...] = harmonic(weights[5], coefficients(inner_got[modes].astype(F32), levels))
    out[:modes, :] = partial[:modes, :] + 0.5 * face_product(face, base, here.at[0], turned)
    out[modes:, :] = partial[modes:, :]


def outer_kernel(place, levels, partial, weights, here, outer_got, out, face, turned, face_here):
    planes, rows, modes, layers = here.shape
    half = rows // 2
    side = lax.rem(place[1], 2)
    at_edge = (place[1] == 0) | (place[1] == place[2] - 1)
    base = pl.multiple_of(side * half, half)
    turn(outer_got, 0, turned)
    coef = coefficients(outer_got[modes:].astype(F32).reshape(rows, layers), levels)
    between = harmonic(weights[6], coef)
    face[...] = jnp.where(at_edge, weights[6], between)
    face_here[...] = jnp.where(at_edge, 0.0, between)
    out[:modes, :] = partial[:modes, :] + 0.5 * face_product(face_here, base, here.at[1], turned)
    out[modes:, :] = partial[modes:, :]


def ends_kernel(place, levels, partial, one_pack, two_pack, one_got, two_got, out):
    modes = partial.shape[1]
    odd = lax.rem(place[0], 2) == 1

    def coef_row(pack):
        return coefficients(pack[modes:modes + 16].astype(F32)[0:1], levels)

    one, two = one_pack[...].astype(F32), two_pack[...].astype(F32)
    one_other, two_other = one_got[...].astype(F32), two_got[...].astype(F32)
    first, last = jnp.where(odd, one, two), jnp.where(odd, two, one)
    next_first = jnp.where(odd, two_other, one_other)
    prev_last = jnp.where(odd, one_other, two_other)
    weight_low = harmonic(coef_row(first), coef_row(prev_last))
    weight_high = harmonic(coef_row(last), coef_row(next_first))

    def product(left, right):
        return lax.dot_general(left, right, NT, precision=PRECISE, preferred_element_type=F32)

    edge_rows = weight_high * last[:modes]
    ends = product(weight_low * first[:modes], first[:modes]) + product(edge_rows, last[:modes])
    square = partial[:modes, :] + 0.5 * ends
    out[:modes, :modes] = square + square.T
    out[:modes, modes:] = -product(edge_rows, next_first[:modes])
    out[modes:, :modes] = partial[modes:, :]
    out[modes:, modes:] = jnp.zeros((8, modes), F32)


def terms_kernel(
    place, levels, pair, one_got, two_got, weights, inner_face, outer_face, terms, picked, coef_ref
):
    modes, width = picked.shape[1:]
    rows, layers = inner_face.shape
    side = lax.rem(place[1], 2)
    odd = lax.rem(place[0], 2) == 1
    one_other, two_other = one_got[...].astype(F32), two_got[...].astype(F32)
    next_first = jnp.where(odd, two_other, one_other)
    prev_last = jnp.where(odd, one_other, two_other)
    picked[0] = next_first[:modes]
    picked[1] = prev_last[:modes]
    end_labels = lax.dot_general(
        next_first[modes:].astype(BF16), pick_row(layers - 1, layers), TN, preferred_element_type=F32
    ) + lax.dot_general(
        prev_last[modes:].astype(BF16), pick_row(0, layers), TN, preferred_element_type=F32
    )
    coef_ref[...] = coefficients(end_labels, levels).reshape(width // rows, rows, layers)
    row = lax.broadcasted_iota(jnp.int32, (rows, layers), 0)
    lane = lax.broadcasted_iota(jnp.int32, (rows, layers), 1)
    for x, face in enumerate((inner_face, outer_face)):
        c = weights[5 + x]
        end_weight = harmonic(c, coef_ref[1 - side if x == 0 else side])
        up_y, up_z = weights[1 + x], weights[3 + x]
        down_y = jnp.where(row == 0, c, pltpu.roll(up_y, 1, 0))
        down_z = pltpu.roll(up_z, 1, 1)
        total = face[...] + weights[0] + up_y + down_y
        total = total + jnp.where(lane == layers - 1, end_weight, up_z)
        terms[x, 0] = total + jnp.where(lane == 0, end_weight, down_z)
        terms[x, 1] = jnp.where(row == 0, 0.0, down_y)
        terms[x, 2] = jnp.where(row == rows - 1, 0.0, up_y)
        terms[x, 3] = jnp.where(lane == 0, 0.0, down_z)
        terms[x, 4] = jnp.where(lane == layers - 1, 0.0, up_z)
        terms[x, 5] = end_weight


def pair_kernel(own, across, beside, oblique, out):
    modes = own.shape[1] // 2
    encode(own[...] + across[...], modes, out.at[0])
    encode(beside[...] + oblique[...], modes, out.at[1])


def single_kernel(own, out):
    encode(own[...], own.shape[1] // 2, out)


def encode(total, modes, out):
    row = lax.broadcasted_iota(jnp.int32, (modes, 2 * modes), 0)
    lane = lax.broadcasted_iota(jnp.int32, (modes, 2 * modes), 1)
    values = total[:modes]
    high = values.astype(BF16).astype(F32)
    low = values - high
    out[:modes] = jnp.where((lane <= row) | (lane >= modes), high, low).astype(BF16)
    diagonal = lane == row
    right = total[modes:modes + 1]
    parts = []
    for _ in range(3):
        part = right.astype(BF16).astype(F32)
        parts.append(part)
        right = right - part
    for part in (high, low):
        parts.append(jnp.sum(jnp.where(diagonal, part, 0.0), axis=0, keepdims=True))
    rows = lax.broadcasted_iota(jnp.int32, (16, 2 * modes), 0)
    extra = jnp.zeros((16, 2 * modes), F32)
    for index, part in enumerate(parts):
        extra = jnp.where(rows == index, part, extra)
    out[modes:] = extra.astype(BF16)


def finish_kernel(place, *refs):
    count = len(refs) - 17
    blocks, refs = refs[:count], refs[count:]
    zvec, inner_got, outer_got, outer_last, picked, terms, middle, inner_face, outer_face, resid = refs[:10]
    solution, deflated, direction_ref, image_ref, spread, outer_field, fix_ref = refs[10:]
    subs = direction_ref.shape[0]
    modes, planes, rows, layers = zvec.shape
    half = rows // 2
    me = place[0]
    side = lax.rem(place[1], 2)
    odd = lax.rem(me, 2) == 1
    at_edge = (place[1] == 0) | (place[1] == place[2] - 1)
    order = place[3]
    held = (1 - side, side)
    square = (modes, modes)
    eye = lax.broadcasted_iota(jnp.int32, square, 0) == lax.broadcasted_iota(jnp.int32, square, 1)

    def column(row):
        return jnp.sum(jnp.where(eye, row, 0.0), axis=1, keepdims=True)

    def each(body, carry):
        for index, block in enumerate(blocks):
            held_here = block.shape[0]
            if held_here <= 8:
                for entry in range(held_here):
                    s = jnp.bitwise_xor(order, index * held_here + entry)
                    carry = body(block.at[entry], s, carry)
            else:
                carry = lax.fori_loop(
                    0, held_here, lambda entry, c, block=block: body(block.at[entry], entry, c), carry
                )
        return carry

    def load(block, s, carry):
        extra = block[modes:modes + 16, :].astype(F32)
        direction_ref[pl.ds(s, 1), :] = (extra[0:1] + extra[1:2]) + extra[2:3]
        fix_ref[pl.ds(s, 1), :] = extra[4:5] - extra[3:4]
        return carry

    each(load, 0)
    fix = fix_ref[:, :modes]

    def turned(rows_of, by):
        by = by % subs
        return jnp.concatenate([rows_of[by:], rows_of[:by]], axis=0)

    def coarse_apply(direction):
        direction_ref[...] = jnp.concatenate([direction, turned(direction, 1)], axis=1)

        def one(block, s, carry):
            values = block[:modes, :].astype(F32)
            pair = direction_ref[pl.ds(s, 1), :]
            ahead = jnp.sum(values * pair, axis=1, keepdims=True)
            image_ref[pl.ds(s, 1), :] = jnp.sum(
                values * column(pair[:, :modes]), axis=0, keepdims=True
            )
            return jnp.where(lane_is((modes, 128), s), ahead, carry)

        ahead_all = each(one, jnp.zeros((modes, 128), F32))
        image = image_ref[...]
        square_part = ahead_all.T[:subs] + image[:, :modes] + fix * direction
        return square_part + turned(image[:, modes:], -1)

    def inner(left, right):
        return jnp.sum(jnp.sum(left * right, axis=0, keepdims=True), axis=1, keepdims=True)

    remain = direction_ref[:, :modes]
    direction = remain
    result = jnp.zeros_like(remain)
    norm_now = inner(remain, remain)
    for iteration in range(CITERS):
        image = coarse_apply(direction)
        step_size = norm_now / inner(direction, image)
        result = result + step_size * direction
        if iteration + 1 < CITERS:
            remain = remain - step_size * image
            norm_next = inner(remain, remain)
            direction = remain + (norm_next / norm_now) * direction
            norm_now = norm_next
    direction_ref[:, :modes] = result
    own = direction_ref[pl.ds(me, 1), :modes]
    solution[...] = own
    spread[...] = jnp.broadcast_to(column(own), (modes, layers))
    ahead_column = column(direction_ref[pl.ds(lax.rem(me + 1, subs), 1), :modes])
    behind_column = column(direction_ref[pl.ds(lax.rem(me + subs - 1, subs), 1), :modes])
    ahead_row = jnp.sum(ahead_column * picked[0], axis=0, keepdims=True)
    behind_row = jnp.sum(behind_column * picked[1], axis=0, keepdims=True)
    width = planes * rows
    both_rows = jnp.where(
        lax.broadcasted_iota(jnp.int32, (8, width), 0) == 0,
        jnp.broadcast_to(ahead_row, (8, width)),
        jnp.broadcast_to(behind_row, (8, width)),
    )
    columns = both_rows.T
    ends = jnp.where(
        lane_is((width, layers), layers - 1),
        columns[:, 0:1],
        jnp.where(lane_is((width, layers), 0), columns[:, 1:2], 0.0),
    ).reshape(planes, rows, layers)

    def add_mode(j, carry):
        fields, near, last = list(carry[0]), carry[1], carry[2]
        for u in range(MODES):
            k = j * MODES + u
            scale = spread[pl.ds(k, 1), :]
            for x, plane in enumerate((zvec[k, held[0]], zvec[k, held[1]], inner_got[k])):
                fields[x] = fields[x] + scale * plane.astype(F32)
            near = near + scale * outer_got[k].astype(F32)
            last = last + scale * outer_last[k].astype(F32)
        return tuple(fields), near, last

    zero, short = jnp.zeros((rows, layers), F32), jnp.zeros((half, layers), F32)
    field, near, last = lax.fori_loop(0, modes // MODES, add_mode, ((zero,) * 3, short, short))
    outer_field[pl.ds(pl.multiple_of(side * half, half), half), :] = near
    outer_field[pl.ds(pl.multiple_of((1 - side) * half, half), half), :] = last
    outside = (field[2], jnp.where(at_edge, 0.0, outer_field[...]))
    faces = (inner_face[...], outer_face[...])
    for x in range(2):
        f = field[x]
        end_field = jnp.where(side == x, ends[1], ends[0])
        image = (
            terms[x, 0] * f
            - middle[0] * field[1 - x]
            - faces[x] * outside[x]
            - terms[x, 1] * pltpu.roll(f, 1, 0)
            - terms[x, 2] * pltpu.roll(f, rows - 1, 0)
            - terms[x, 3] * pltpu.roll(f, 1, 1)
            - terms[x, 4] * pltpu.roll(f, layers - 1, 1)
            - terms[x, 5] * end_field
        )
        deflated[held[x]] = resid[held[x]] - image


def swapped(value, axis, first):
    count = lax.axis_size(axis)
    pairs = []
    for i in range(count):
        up = (i - first) % 2 == 0
        pairs.append((i, (i + 1) % count if up else (i - 1) % count))
    return lax.ppermute(value, axis, pairs)


def swapped_all(value):
    subs, count = lax.axis_size("sub"), lax.axis_size("pln")
    pairs = []
    for s in range(subs):
        for i in range(count):
            if 0 < i < count - 1:
                to = (s, i + 1 if i % 2 else i - 1)
            else:
                to = (s ^ 1, i)
            pairs.append((s * count + i, to[0] * count + to[1]))
    return lax.ppermute(value, ("sub", "pln"), pairs)


def exchanged(value, axis, mask):
    return lax.ppermute(value, axis, [(i, i ^ mask) for i in range(lax.axis_size(axis))])


def partner(value, sub_mask, pln_mask):
    subs, count = lax.axis_size("sub"), lax.axis_size("pln")
    pairs = [
        (s * count + p, (s ^ sub_mask) * count + (p ^ pln_mask)) for s in range(subs) for p in range(count)
    ]
    return lax.ppermute(value, ("sub", "pln"), pairs)


def body(labels, levels, zvec, resid):
    modes, planes, rows, layers = zvec.shape
    half = rows // 2
    subs, parts = lax.axis_size("sub"), lax.axis_size("pln")
    shape = jax.ShapeDtypeStruct
    order = lax.axis_index("sub") if subs == 8 else 0
    place = jnp.stack(
        [jnp.int32(v) for v in (lax.axis_index("sub"), lax.axis_index("pln"), parts, order)]
    )
    pack = shape((modes + 16, planes * rows), BF16)
    inner_send, outer_near = call(
        stage_kernel,
        [shape((modes + 1, rows, layers), BF16), shape((modes + rows // half, half, layers), BF16)],
        [SMEM, HBM, HBM],
        [pltpu.VMEM(labels.shape, jnp.int32), pltpu.SemaphoreType.DMA, pltpu.SemaphoreType.DMA((2,))],
        moved=2 << 20,
    )(place, *(pltpu.with_memory_space_constraint(v, pltpu.HBM) for v in (labels, zvec)))
    outer_got = swapped_all(outer_near)
    inner_got = swapped(inner_send, "pln", 0)
    rest = shape((modes, half, layers), BF16)
    outer_rest, one_pack, two_pack = call(
        prepare_kernel,
        [rest, pack, pack],
        [SMEM, VMEM, VMEM],
        flops=10_000_000,
        moved=6 << 20,
    )(place, labels, zvec)
    one_got = swapped(one_pack, "sub", 0)
    two_got = swapped(two_pack, "sub", 1)
    field = (planes, rows, layers)
    plane = (rows, layers)
    partial, weights, here = call(
        block_kernel,
        [
            shape((modes + 8, modes), F32),
            shape((7,) + plane, F32),
            shape((planes, rows, modes, layers), BF16),
        ],
        [SMEM, SMEM] + [VMEM] * 3 + [ANY],
        [pltpu.VMEM(field, F32)] * 3,
        flops=400_000_000,
        moved=3 << 20,
    )(place, levels, labels, resid, zvec, one_pack)
    turned = pltpu.VMEM((half, modes, layers), BF16)
    partial, inner_face = call(
        inner_kernel,
        [shape((modes + 8, modes), F32), shape(plane, F32)],
        [SMEM, SMEM] + [VMEM] * 4,
        [turned],
        flops=100_000_000,
        moved=1 << 20,
    )(place, levels, partial, weights, here, inner_got)
    partial, outer_face = call(
        outer_kernel,
        [shape((modes + 8, modes), F32), shape(plane, F32)],
        [SMEM, SMEM] + [VMEM] * 4,
        [turned, pltpu.VMEM(plane, F32)],
        flops=100_000_000,
        moved=1 << 20,
    )(place, levels, partial, weights, here, outer_got)
    [block] = call(
        ends_kernel, [shape((modes + 8, 2 * modes), F32)], [SMEM, SMEM] + [VMEM] * 5, flops=10_000_000
    )(place, levels, partial, one_pack, two_pack, one_got, two_got)
    packed = (modes + 16, 2 * modes)
    if parts == 4 and subs == 8:
        block = block + exchanged(block, "pln", 1)
        others = [partner(block, *masks) for masks in ((0, 2), (1, 0), (1, 2))]
        [pair] = call(pair_kernel, [shape((2,) + packed, BF16)], [VMEM] * 4)(block, *others)
        blocks = [pair] + [exchanged(pair, "sub", mask) for mask in (2, 4, 6)]
    else:
        [single] = call(single_kernel, [shape(packed, BF16)], [VMEM])(lax.psum(block, "pln"))
        blocks = [lax.all_gather(single, "sub")]
    [outer_rest] = call(release_kernel, [rest], [ANY] * 2, aliases={1: 0})(block, outer_rest)
    outer_last = swapped_all(outer_rest)
    terms, picked = call(
        terms_kernel,
        [shape((planes, 6) + plane, F32), shape((2, modes, planes * rows), F32)],
        [SMEM, SMEM, ANY] + [VMEM] * 5,
        [pltpu.VMEM(field, F32)],

        flops=1 << 33,
        moved=1 << 20,
    )(place, levels, blocks[0], one_got, two_got, weights, inner_face, outer_face)
    return tuple(
        call(
            finish_kernel,
            [shape((1, modes), F32), shape(field, F32)],
            [SMEM] + [VMEM] * (10 + len(blocks)),
            [
                pltpu.VMEM((subs, 2 * modes), F32),
                pltpu.VMEM((subs, 2 * modes), F32),
                pltpu.VMEM((modes, layers), F32),
                pltpu.VMEM(plane, F32),
                pltpu.VMEM((subs, 2 * modes), F32),
            ],
            flops=10_000_000,
            moved=5 << 20,
        )(
            place, *blocks, zvec, inner_got, outer_got, outer_last, picked, terms, weights, inner_face,
            outer_face, resid,
        )
    )


def solution(mesh):
    in_specs = (P("pln", None, "sub"), P(), P(None, "pln", None, "sub"), P("pln", None, "sub"))
    out_specs = (P("sub", None), P("pln", None, "sub"))
    return jax.shard_map(body, mesh=mesh, in_specs=in_specs, out_specs=out_specs, check_vma=False)
```

```python
import jax
import jax.numpy as jnp
from jax import lax
from jax.experimental import pallas as pl
from jax.experimental.pallas import tpu as pltpu
from jax.sharding import PartitionSpec as P

CITERS = 2
STEP = 16
MODES = 8
CHUNK = 16
F32 = jnp.float32
BF16 = jnp.bfloat16
PRECISE = lax.Precision.HIGHEST
NT = (((1,), (1,)), ((), ()))
TN = (((0,), (0,)), ((), ()))
VMEM = pl.BlockSpec(memory_space=pltpu.VMEM)
SMEM = pl.BlockSpec(memory_space=pltpu.SMEM)
HBM = pl.BlockSpec(memory_space=pltpu.HBM)
ANY = pl.BlockSpec(memory_space=pl.ANY)


def call(kernel, outs, specs, scratch=(), flops=0, moved=0, limit=32, aliases=None):
    return pl.pallas_call(
        kernel,
        out_shape=outs,
        in_specs=specs,
        out_specs=[ANY if at in (aliases or {}).values() else VMEM for at in range(len(outs))],
        input_output_aliases=aliases or {},
        scratch_shapes=list(scratch),
        cost_estimate=pl.CostEstimate(flops=flops, bytes_accessed=moved, transcendentals=0),
        compiler_params=pltpu.CompilerParams(vmem_limit_bytes=limit << 20),
    )


def harmonic(left_value, right_value):
    return 2.0 * left_value * right_value / (left_value + right_value)


def coefficients(labels, levels_ref):
    weighted = jnp.zeros(labels.shape, F32)
    for level in range(levels_ref.shape[0]):
        weighted = weighted + jnp.where(labels == level, levels_ref[level], 0.0)
    return weighted


def lane_is(shape, lane):
    return lax.broadcasted_iota(jnp.int32, shape, len(shape) - 1) == lane


def pick_row(lane, width):
    row = lax.broadcasted_iota(jnp.int32, (16, width), 0)
    return ((row == 0) & lane_is((16, width), lane)).astype(BF16)


def stage_kernel(place, labels_far, zvec, inner_send, outer_near, labels, label_sem, sems):
    modes, planes, rows, layers = zvec.shape
    half = rows // 2
    side = lax.rem(place[1], 2)
    start = pl.multiple_of((1 - side) * half, half)
    label_copy = pltpu.make_async_copy(labels_far, labels, label_sem)
    copies = [
        pltpu.make_async_copy(
            zvec.at[:, side, pl.ds(start, half), :], outer_near.at[pl.ds(0, modes)], sems.at[0]
        ),
        pltpu.make_async_copy(zvec.at[:, 1 - side], inner_send.at[pl.ds(0, modes)], sems.at[1]),
    ]
    label_copy.start()
    for copy in copies:
        copy.start()
    label_copy.wait()
    outer_near[modes:] = labels[side].astype(F32).astype(BF16).reshape(rows // half, half, layers)
    inner_send[modes] = labels[1 - side].astype(F32).astype(BF16)
    for copy in copies:
        copy.wait()


def release_kernel(after, outer_rest, outer_out):
    pass


def prepare_kernel(place, labels, held, outer_rest, one_pack, two_pack):
    modes, planes, rows, layers = held.shape
    half = rows // 2
    width = planes * rows
    side = lax.rem(place[1], 2)
    odd = lax.rem(place[0], 2) == 1
    one_lane = jnp.where(odd, 0, layers - 1)
    two_lane = jnp.where(odd, layers - 1, 0)
    row = lax.broadcasted_iota(jnp.int32, (16, layers), 0)
    both = ((row == 0) & lane_is((16, layers), one_lane)) | ((row == 1) & lane_is((16, layers), two_lane))
    both = both.astype(BF16)
    flat = labels[...].astype(F32).astype(BF16).reshape(width, layers)
    for out, lane in ((one_pack, one_lane), (two_pack, two_lane)):
        out[modes:] = lax.dot_general(
            pick_row(lane, layers), flat, NT, preferred_element_type=F32
        ).astype(BF16)
    for k in range(0, modes, CHUNK):
        at = slice(k, k + CHUNK)
        ends = lax.dot_general(
            both, held[at].reshape(-1, layers), NT, preferred_element_type=F32
        )
        for out, index in ((one_pack, 0), (two_pack, 1)):
            out[at] = jnp.concatenate(
                [ends[index:index + 1, j * width:(j + 1) * width] for j in range(CHUNK)], axis=0
            ).astype(BF16)
        outer_rest[at] = held[at, side, pl.ds(pl.multiple_of(side * half, half), half), :]


def block_kernel(
    place, levels, labels, resid, zvec, after, partial, weights, here, half_diag, link_y, link_z,
):
    planes, rows, layers = labels.shape
    modes = here.shape[2]
    side = lax.rem(place[1], 2)
    at_edge = (place[1] == 0) | (place[1] == place[2] - 1)
    held = (1 - side, side)

    def turn_rows(start):
        for slot, plane in enumerate(held):
            for k in range(0, modes, CHUNK):
                block = zvec[k:k + CHUNK, plane, pl.ds(start, STEP), :]
                here[slot, pl.ds(start, STEP), k:k + CHUNK, :] = jnp.swapaxes(block, 0, 1)

    turn_rows(0)
    coef = [coefficients(labels[x], levels) for x in held]
    middle = harmonic(coef[0], coef[1])
    weights[0] = middle
    row = lax.broadcasted_iota(jnp.int32, (rows, layers), 0)
    lane = lax.broadcasted_iota(jnp.int32, (rows, layers), 1)
    for x in range(2):
        c = coef[x]
        up_y = harmonic(c, jnp.where(row == rows - 1, c, pltpu.roll(c, rows - 1, 0)))
        up_z = harmonic(c, pltpu.roll(c, layers - 1, 1))
        down_y = jnp.where(row == 0, c, pltpu.roll(up_y, 1, 0))
        weights[1 + x] = up_y
        weights[3 + x] = up_z
        weights[5 + x] = c
        inner_z = jnp.where(lane == layers - 1, 0.0, up_z)
        total = middle + up_y + down_y + inner_z + pltpu.roll(inner_z, 1, 1)
        if x == 1:
            total = total + jnp.where(at_edge, c, 0.0)
        half_diag[x] = 0.5 * total
        link_y[x] = jnp.where(row == rows - 1, 0.0, up_y)
        link_z[x] = inner_z

    def step(j, carry):
        total, rhs, wide = carry
        turn_rows(pl.multiple_of(jnp.minimum((j + 1) * STEP, rows - STEP), STEP))
        for u in range(STEP):
            y = j * STEP + u
            at = pl.ds(y, 1)
            ahead = jnp.minimum(y + 1, rows - 1)
            up = [here[x, ahead].astype(F32) for x in range(2)]
            images = []
            for x in range(2):
                image = (
                    half_diag[x, at, :] * wide[x]
                    - link_y[x, at, :] * up[x]
                    - link_z[x, at, :] * pltpu.roll(wide[x], layers - 1, 1)
                )
                if x == 0:
                    image = image - weights[0, at, :] * wide[1]
                rhs = rhs + resid[held[x], at, :] * wide[x]
                images.append(image.astype(BF16))
            total = total + lax.dot_general(
                jnp.concatenate(images, axis=1),
                jnp.concatenate([here[0, y], here[1, y]], axis=1),
                NT,
                preferred_element_type=F32,
            )
            wide = up
        return total, rhs, wide

    total, rhs, _ = lax.fori_loop(
        0,
        rows // STEP,
        step,
        (
            jnp.zeros((modes, modes), F32),
            jnp.zeros((modes, layers), F32),
            [here[x, 0].astype(F32) for x in range(2)],
        ),
    )
    partial[:modes, :] = total
    partial[modes:, :] = lax.dot_general(
        jnp.ones((8, layers), F32), rhs, NT, precision=PRECISE, preferred_element_type=F32
    )


def turn(got, start, out):
    half, modes, layers = out.shape
    for k in range(0, modes, CHUNK):
        out[:, k:k + CHUNK, :] = jnp.swapaxes(got[k:k + CHUNK, pl.ds(start, half), :], 0, 1)


def face_product(weight_ref, base, own, other):
    half, modes, layers = other.shape

    def step(j, total):
        left, right = [], []
        for u in range(STEP):
            y = j * STEP + u
            weight = weight_ref[pl.ds(base + y, 1), :]
            image = weight * (own[base + y].astype(F32) - other[y].astype(F32))
            left.append(jnp.concatenate([own[base + y], other[y]], axis=0))
            right.append(image.astype(BF16))
        return total + lax.dot_general(
            jnp.concatenate(left, axis=1), jnp.concatenate(right, axis=1), NT,
            preferred_element_type=F32,
        )

    total = lax.fori_loop(0, half // STEP, step, jnp.zeros((2 * modes, modes), F32))
    return total[:modes] - total[modes:]


def inner_kernel(place, levels, partial, weights, here, inner_got, out, face, turned):
    planes, rows, modes, layers = here.shape
    half = rows // 2
    side = lax.rem(place[1], 2)
    base = pl.multiple_of(side * half, half)
    turn(inner_got, base, turned)
    face[...] = harmonic(weights[5], coefficients(inner_got[modes].astype(F32), levels))
    out[:modes, :] = partial[:modes, :] + 0.5 * face_product(face, base, here.at[0], turned)
    out[modes:, :] = partial[modes:, :]


def outer_kernel(
    place, levels, partial, weights, here, outer_got, one_pack, two_pack, one_got, two_got,
    out, face, turned, face_here,
):
    planes, rows, modes, layers = here.shape
    half = rows // 2
    side = lax.rem(place[1], 2)
    at_edge = (place[1] == 0) | (place[1] == place[2] - 1)
    base = pl.multiple_of(side * half, half)
    turn(outer_got, 0, turned)
    coef = coefficients(outer_got[modes:].astype(F32).reshape(rows, layers), levels)
    between = harmonic(weights[6], coef)
    face[...] = jnp.where(at_edge, weights[6], between)
    face_here[...] = jnp.where(at_edge, 0.0, between)
    cross = face_product(face_here, base, here.at[1], turned)
    odd = lax.rem(place[0], 2) == 1

    def coef_row(pack):
        return coefficients(pack[modes:modes + 16].astype(F32)[0:1], levels)

    one, two = one_pack[...].astype(F32), two_pack[...].astype(F32)
    one_other, two_other = one_got[...].astype(F32), two_got[...].astype(F32)
    first, last = jnp.where(odd, one, two), jnp.where(odd, two, one)
    next_first = jnp.where(odd, two_other, one_other)
    prev_last = jnp.where(odd, one_other, two_other)
    weight_low = harmonic(coef_row(first), coef_row(prev_last))
    weight_high = harmonic(coef_row(last), coef_row(next_first))

    def product(left, right):
        return lax.dot_general(
            left.astype(BF16), right.astype(BF16), NT, preferred_element_type=F32
        )

    edge_rows = weight_high * last[:modes]
    ends = product(
        jnp.concatenate([weight_low * first[:modes], edge_rows], axis=1),
        jnp.concatenate([first[:modes], last[:modes]], axis=1),
    )
    square = partial[:modes, :] + 0.5 * (cross + ends)
    out[:modes, :modes] = square + square.T
    out[:modes, modes:] = -product(edge_rows, next_first[:modes])
    out[modes:, :modes] = partial[modes:, :]
    out[modes:, modes:] = jnp.zeros((8, modes), F32)


def terms_kernel(
    place, levels, pair, one_got, two_got, weights, inner_face, outer_face, terms, picked, coef_ref
):
    modes, width = picked.shape[1:]
    rows, layers = inner_face.shape
    side = lax.rem(place[1], 2)
    odd = lax.rem(place[0], 2) == 1
    one_other, two_other = one_got[...].astype(F32), two_got[...].astype(F32)
    next_first = jnp.where(odd, two_other, one_other)
    prev_last = jnp.where(odd, one_other, two_other)
    picked[0] = next_first[:modes]
    picked[1] = prev_last[:modes]
    end_labels = lax.dot_general(
        next_first[modes:].astype(BF16), pick_row(layers - 1, layers), TN, preferred_element_type=F32
    ) + lax.dot_general(
        prev_last[modes:].astype(BF16), pick_row(0, layers), TN, preferred_element_type=F32
    )
    coef_ref[...] = coefficients(end_labels, levels).reshape(width // rows, rows, layers)
    row = lax.broadcasted_iota(jnp.int32, (rows, layers), 0)
    lane = lax.broadcasted_iota(jnp.int32, (rows, layers), 1)
    for x, face in enumerate((inner_face, outer_face)):
        c = weights[5 + x]
        end_weight = harmonic(c, coef_ref[1 - side if x == 0 else side])
        up_y, up_z = weights[1 + x], weights[3 + x]
        down_y = jnp.where(row == 0, c, pltpu.roll(up_y, 1, 0))
        down_z = pltpu.roll(up_z, 1, 1)
        total = face[...] + weights[0] + up_y + down_y
        total = total + jnp.where(lane == layers - 1, end_weight, up_z)
        terms[x, 0] = total + jnp.where(lane == 0, end_weight, down_z)
        terms[x, 1] = jnp.where(row == 0, 0.0, down_y)
        terms[x, 2] = jnp.where(row == rows - 1, 0.0, up_y)
        terms[x, 3] = jnp.where(lane == 0, 0.0, down_z)
        terms[x, 4] = jnp.where(lane == layers - 1, 0.0, up_z)
        terms[x, 5] = end_weight


def pair_kernel(own, across, beside, oblique, out):
    modes = own.shape[1] // 2
    encode(own[...] + across[...], modes, out.at[0])
    encode(beside[...] + oblique[...], modes, out.at[1])


def single_kernel(own, out):
    encode(own[...], own.shape[1] // 2, out)


def encode(total, modes, out):
    row = lax.broadcasted_iota(jnp.int32, (modes, 2 * modes), 0)
    lane = lax.broadcasted_iota(jnp.int32, (modes, 2 * modes), 1)
    values = total[:modes]
    high = values.astype(BF16).astype(F32)
    low = values - high
    out[:modes] = jnp.where((lane <= row) | (lane >= modes), high, low).astype(BF16)
    diagonal = lane == row
    right = total[modes:modes + 1]
    parts = []
    for _ in range(3):
        part = right.astype(BF16).astype(F32)
        parts.append(part)
        right = right - part
    for part in (high, low):
        parts.append(jnp.sum(jnp.where(diagonal, part, 0.0), axis=0, keepdims=True))
    rows = lax.broadcasted_iota(jnp.int32, (16, 2 * modes), 0)
    extra = jnp.zeros((16, 2 * modes), F32)
    for index, part in enumerate(parts):
        extra = jnp.where(rows == index, part, extra)
    out[modes:] = extra.astype(BF16)


def finish_kernel(place, *refs):
    count = len(refs) - 15
    blocks, refs = refs[:count], refs[count:]
    zvec, inner_got, outer_got, outer_last, picked, terms, middle, inner_face, outer_face, resid = refs[:10]
    solution, deflated, direction_ref, spread, outer_field = refs[10:]
    subs = direction_ref.shape[0]
    modes, planes, rows, layers = zvec.shape
    half = rows // 2
    me = place[0]
    side = lax.rem(place[1], 2)
    odd = lax.rem(me, 2) == 1
    at_edge = (place[1] == 0) | (place[1] == place[2] - 1)
    order = place[3]
    held = (1 - side, side)
    square = (modes, modes)
    eye = lax.broadcasted_iota(jnp.int32, square, 0) == lax.broadcasted_iota(jnp.int32, square, 1)

    def column(row):
        return jnp.sum(jnp.where(eye, row, 0.0), axis=1, keepdims=True)

    def each(body, carry):
        for index, block in enumerate(blocks):
            held_here = block.shape[0]
            if held_here <= 8:
                for entry in range(held_here):
                    s = jnp.bitwise_xor(order, index * held_here + entry)
                    carry = body(block.at[entry], s, carry)
            else:
                carry = lax.fori_loop(
                    0, held_here, lambda entry, c, block=block: body(block.at[entry], entry, c), carry
                )
        return carry

    def row_is(s, width):
        return lax.broadcasted_iota(jnp.int32, (subs, width), 0) == s

    def load(block, s, carry):
        extra = block[modes:modes + 16, :].astype(F32)
        right = (extra[0:1] + extra[1:2]) + extra[2:3]
        here = row_is(s, 2 * modes)
        return jnp.where(here, right, carry[0]), jnp.where(here, extra[4:5] - extra[3:4], carry[1])

    empty = jnp.zeros((subs, 2 * modes), F32)
    right_side, fix = each(load, (empty, empty))
    fix = fix[:, :modes]

    def turned(rows_of, by):
        by = by % subs
        return jnp.concatenate([rows_of[by:], rows_of[:by]], axis=0)

    def in_parts(value):
        parts = []
        for _ in range(3):
            part = value.astype(BF16)
            parts.append(part.astype(F32))
            value = value - parts[-1]
        return jnp.concatenate(parts, axis=0).astype(BF16)

    def joined(value):
        return (value[:subs] + value[subs:2 * subs]) + value[2 * subs:]

    def coarse_apply(direction):
        pairs = in_parts(jnp.concatenate([direction, turned(direction, 1)], axis=1))
        single = pairs[:, :modes]

        def one(block, s, carry):
            values = block[:modes, :]
            ahead = lax.dot_general(pairs, values, NT, preferred_element_type=F32)
            image = jnp.dot(single, values, preferred_element_type=F32)
            return (
                jnp.where(row_is(s, modes), joined(ahead), carry[0]),
                jnp.where(row_is(s, 2 * modes), joined(image), carry[1]),
            )

        ahead, image = each(one, (jnp.zeros((subs, modes), F32), empty))
        return ahead + image[:, :modes] + fix * direction + turned(image[:, modes:], -1)

    def inner(left, right):
        return jnp.sum(jnp.sum(left * right, axis=0, keepdims=True), axis=1, keepdims=True)

    remain = right_side[:, :modes]
    direction = remain
    result = jnp.zeros_like(remain)
    norm_now = inner(remain, remain)
    for iteration in range(CITERS):
        image = coarse_apply(direction)
        step_size = norm_now / inner(direction, image)
        result = result + step_size * direction
        if iteration + 1 < CITERS:
            remain = remain - step_size * image
            norm_next = inner(remain, remain)
            direction = remain + (norm_next / norm_now) * direction
            norm_now = norm_next
    direction_ref[...] = result
    own = direction_ref[pl.ds(me, 1), :]
    solution[...] = own
    spread[...] = jnp.broadcast_to(column(own), (modes, layers))
    ahead_column = column(direction_ref[pl.ds(lax.rem(me + 1, subs), 1), :])
    behind_column = column(direction_ref[pl.ds(lax.rem(me + subs - 1, subs), 1), :])
    ahead_row = jnp.sum(ahead_column * picked[0], axis=0, keepdims=True)
    behind_row = jnp.sum(behind_column * picked[1], axis=0, keepdims=True)
    width = planes * rows
    both_rows = jnp.where(
        lax.broadcasted_iota(jnp.int32, (8, width), 0) == 0,
        jnp.broadcast_to(ahead_row, (8, width)),
        jnp.broadcast_to(behind_row, (8, width)),
    )
    columns = both_rows.T
    ends = jnp.where(
        lane_is((width, layers), layers - 1),
        columns[:, 0:1],
        jnp.where(lane_is((width, layers), 0), columns[:, 1:2], 0.0),
    ).reshape(planes, rows, layers)

    def add_mode(j, carry):
        fields, near, last = list(carry[0]), carry[1], carry[2]
        for u in range(MODES):
            k = j * MODES + u
            scale = spread[pl.ds(k, 1), :]
            for x, plane in enumerate((zvec[k, held[0]], zvec[k, held[1]], inner_got[k])):
                fields[x] = fields[x] + scale * plane.astype(F32)
            near = near + scale * outer_got[k].astype(F32)
            last = last + scale * outer_last[k].astype(F32)
        return tuple(fields), near, last

    zero, short = jnp.zeros((rows, layers), F32), jnp.zeros((half, layers), F32)
    field, near, last = lax.fori_loop(0, modes // MODES, add_mode, ((zero,) * 3, short, short))
    outer_field[pl.ds(pl.multiple_of(side * half, half), half), :] = near
    outer_field[pl.ds(pl.multiple_of((1 - side) * half, half), half), :] = last
    outside = (field[2], jnp.where(at_edge, 0.0, outer_field[...]))
    faces = (inner_face[...], outer_face[...])
    for x in range(2):
        f = field[x]
        end_field = jnp.where(side == x, ends[1], ends[0])
        image = (
            terms[x, 0] * f
            - middle[0] * field[1 - x]
            - faces[x] * outside[x]
            - terms[x, 1] * pltpu.roll(f, 1, 0)
            - terms[x, 2] * pltpu.roll(f, rows - 1, 0)
            - terms[x, 3] * pltpu.roll(f, 1, 1)
            - terms[x, 4] * pltpu.roll(f, layers - 1, 1)
            - terms[x, 5] * end_field
        )
        deflated[held[x]] = resid[held[x]] - image


def swapped(value, axis, first):
    count = lax.axis_size(axis)
    pairs = []
    for i in range(count):
        up = (i - first) % 2 == 0
        pairs.append((i, (i + 1) % count if up else (i - 1) % count))
    return lax.ppermute(value, axis, pairs)


def swapped_all(value):
    subs, count = lax.axis_size("sub"), lax.axis_size("pln")
    pairs = []
    for s in range(subs):
        for i in range(count):
            if 0 < i < count - 1:
                to = (s, i + 1 if i % 2 else i - 1)
            else:
                to = (s ^ 1, i)
            pairs.append((s * count + i, to[0] * count + to[1]))
    return lax.ppermute(value, ("sub", "pln"), pairs)


def exchanged(value, axis, mask):
    return lax.ppermute(value, axis, [(i, i ^ mask) for i in range(lax.axis_size(axis))])


def partner(value, sub_mask, pln_mask):
    subs, count = lax.axis_size("sub"), lax.axis_size("pln")
    pairs = [
        (s * count + p, (s ^ sub_mask) * count + (p ^ pln_mask)) for s in range(subs) for p in range(count)
    ]
    return lax.ppermute(value, ("sub", "pln"), pairs)


def body(labels, levels, zvec, resid):
    modes, planes, rows, layers = zvec.shape
    half = rows // 2
    subs, parts = lax.axis_size("sub"), lax.axis_size("pln")
    shape = jax.ShapeDtypeStruct
    order = lax.axis_index("sub") if subs == 8 else 0
    place = jnp.stack(
        [jnp.int32(v) for v in (lax.axis_index("sub"), lax.axis_index("pln"), parts, order)]
    )
    pack = shape((modes + 16, planes * rows), BF16)
    inner_send, outer_near = call(
        stage_kernel,
        [shape((modes + 1, rows, layers), BF16), shape((modes + rows // half, half, layers), BF16)],
        [SMEM, HBM, HBM],
        [pltpu.VMEM(labels.shape, jnp.int32), pltpu.SemaphoreType.DMA, pltpu.SemaphoreType.DMA((2,))],
        moved=2 << 20,
    )(place, *(pltpu.with_memory_space_constraint(v, pltpu.HBM) for v in (labels, zvec)))
    outer_got = swapped_all(outer_near)
    inner_got = swapped(inner_send, "pln", 0)
    rest = shape((modes, half, layers), BF16)
    outer_rest, one_pack, two_pack = call(
        prepare_kernel,
        [rest, pack, pack],
        [SMEM, VMEM, VMEM],
        flops=10_000_000,
        moved=6 << 20,
    )(place, labels, zvec)
    one_got = swapped(one_pack, "sub", 0)
    two_got = swapped(two_pack, "sub", 1)
    field = (planes, rows, layers)
    plane = (rows, layers)
    partial, weights, here = call(
        block_kernel,
        [
            shape((modes + 8, modes), F32),
            shape((7,) + plane, F32),
            shape((planes, rows, modes, layers), BF16),
        ],
        [SMEM, SMEM] + [VMEM] * 3 + [ANY],
        [pltpu.VMEM(field, F32)] * 3,
        flops=400_000_000,
        moved=3 << 20,
    )(place, levels, labels, resid, zvec, one_pack)
    turned = pltpu.VMEM((half, modes, layers), BF16)
    partial, inner_face = call(
        inner_kernel,
        [shape((modes + 8, modes), F32), shape(plane, F32)],
        [SMEM, SMEM] + [VMEM] * 4,
        [turned],
        flops=100_000_000,
        moved=1 << 20,
    )(place, levels, partial, weights, here, inner_got)
    block, outer_face = call(
        outer_kernel,
        [shape((modes + 8, 2 * modes), F32), shape(plane, F32)],
        [SMEM, SMEM] + [VMEM] * 8,
        [turned, pltpu.VMEM(plane, F32)],
        flops=100_000_000,
        moved=1 << 20,
    )(place, levels, partial, weights, here, outer_got, one_pack, two_pack, one_got, two_got)
    packed = (modes + 16, 2 * modes)
    if parts == 4 and subs == 8:
        block = block + exchanged(block, "pln", 1)
        others = [partner(block, *masks) for masks in ((0, 2), (1, 0), (1, 2))]
        [pair] = call(pair_kernel, [shape((2,) + packed, BF16)], [VMEM] * 4)(block, *others)
        blocks = [pair] + [exchanged(pair, "sub", mask) for mask in (2, 4, 6)]
    else:
        [single] = call(single_kernel, [shape(packed, BF16)], [VMEM])(lax.psum(block, "pln"))
        blocks = [lax.all_gather(single, "sub")]
    [outer_rest] = call(release_kernel, [rest], [ANY] * 2, aliases={1: 0})(block, outer_rest)
    outer_last = swapped_all(outer_rest)
    terms, picked = call(
        terms_kernel,
        [shape((planes, 6) + plane, F32), shape((2, modes, planes * rows), F32)],
        [SMEM, SMEM, ANY] + [VMEM] * 5,
        [pltpu.VMEM(field, F32)],

        flops=1 << 33,
        moved=1 << 20,
    )(place, levels, blocks[0], one_got, two_got, weights, inner_face, outer_face)
    return tuple(
        call(
            finish_kernel,
            [shape((1, modes), F32), shape(field, F32)],
            [SMEM] + [VMEM] * (10 + len(blocks)),
            [
                pltpu.VMEM((subs, modes), F32),
                pltpu.VMEM((modes, layers), F32),
                pltpu.VMEM(plane, F32),
            ],
            flops=10_000_000,
            moved=5 << 20,
        )(
            place, *blocks, zvec, inner_got, outer_got, outer_last, picked, terms, weights, inner_face,
            outer_face, resid,
        )
    )


def solution(mesh):
    in_specs = (P("pln", None, "sub"), P(), P(None, "pln", None, "sub"), P("pln", None, "sub"))
    out_specs = (P("sub", None), P("pln", None, "sub"))
    return jax.shard_map(body, mesh=mesh, in_specs=in_specs, out_specs=out_specs, check_vma=False)
```

```python
import jax
import jax.numpy as jnp
from jax import lax
from jax.experimental import pallas as pl
from jax.experimental.pallas import tpu as pltpu
from jax.sharding import PartitionSpec as P

CITERS = 2
STEP = 16
MODES = 8
CHUNK = 16
F32 = jnp.float32
BF16 = jnp.bfloat16
PRECISE = lax.Precision.HIGHEST
NT = (((1,), (1,)), ((), ()))
TN = (((0,), (0,)), ((), ()))
VMEM = pl.BlockSpec(memory_space=pltpu.VMEM)
SMEM = pl.BlockSpec(memory_space=pltpu.SMEM)
HBM = pl.BlockSpec(memory_space=pltpu.HBM)
ANY = pl.BlockSpec(memory_space=pl.ANY)


def call(kernel, outs, specs, scratch=(), flops=0, moved=0, limit=32, aliases=None):
    return pl.pallas_call(
        kernel,
        out_shape=outs,
        in_specs=specs,
        out_specs=[ANY if at in (aliases or {}).values() else VMEM for at in range(len(outs))],
        input_output_aliases=aliases or {},
        scratch_shapes=list(scratch),
        cost_estimate=pl.CostEstimate(flops=flops, bytes_accessed=moved, transcendentals=0),
        compiler_params=pltpu.CompilerParams(vmem_limit_bytes=limit << 20),
    )


def harmonic(left_value, right_value):
    return 2.0 * left_value * right_value / (left_value + right_value)


def coefficients(labels, levels_ref):
    weighted = jnp.zeros(labels.shape, F32)
    for level in range(levels_ref.shape[0]):
        weighted = weighted + jnp.where(labels == level, levels_ref[level], 0.0)
    return weighted


def lane_is(shape, lane):
    return lax.broadcasted_iota(jnp.int32, shape, len(shape) - 1) == lane


def pick_row(lane, width):
    row = lax.broadcasted_iota(jnp.int32, (16, width), 0)
    return ((row == 0) & lane_is((16, width), lane)).astype(BF16)


def stage_kernel(place, labels_far, zvec, inner_send, outer_near, labels, label_sem, sems):
    modes, planes, rows, layers = zvec.shape
    half = rows // 2
    side = lax.rem(place[1], 2)
    start = pl.multiple_of((1 - side) * half, half)
    label_copy = pltpu.make_async_copy(labels_far, labels, label_sem)
    copies = [
        pltpu.make_async_copy(
            zvec.at[:, side, pl.ds(start, half), :], outer_near.at[pl.ds(0, modes)], sems.at[0]
        ),
        pltpu.make_async_copy(zvec.at[:, 1 - side], inner_send.at[pl.ds(0, modes)], sems.at[1]),
    ]
    label_copy.start()
    for copy in copies:
        copy.start()
    label_copy.wait()
    outer_near[modes:] = labels[side].astype(F32).astype(BF16).reshape(rows // half, half, layers)
    inner_send[modes] = labels[1 - side].astype(F32).astype(BF16)
    for copy in copies:
        copy.wait()


def release_kernel(after, outer_rest, outer_out):
    pass


def prepare_kernel(place, labels, held, outer_rest, one_pack, two_pack):
    modes, planes, rows, layers = held.shape
    half = rows // 2
    width = planes * rows
    side = lax.rem(place[1], 2)
    odd = lax.rem(place[0], 2) == 1
    one_lane = jnp.where(odd, 0, layers - 1)
    two_lane = jnp.where(odd, layers - 1, 0)
    row = lax.broadcasted_iota(jnp.int32, (16, layers), 0)
    both = ((row == 0) & lane_is((16, layers), one_lane)) | ((row == 1) & lane_is((16, layers), two_lane))
    both = both.astype(BF16)
    flat = labels[...].astype(F32).astype(BF16).reshape(width, layers)
    for out, lane in ((one_pack, one_lane), (two_pack, two_lane)):
        out[modes:] = lax.dot_general(
            pick_row(lane, layers), flat, NT, preferred_element_type=F32
        ).astype(BF16)
    for k in range(0, modes, CHUNK):
        at = slice(k, k + CHUNK)
        ends = lax.dot_general(
            both, held[at].reshape(-1, layers), NT, preferred_element_type=F32
        )
        for out, index in ((one_pack, 0), (two_pack, 1)):
            out[at] = jnp.concatenate(
                [ends[index:index + 1, j * width:(j + 1) * width] for j in range(CHUNK)], axis=0
            ).astype(BF16)
        outer_rest[at] = held[at, side, pl.ds(pl.multiple_of(side * half, half), half), :]


def block_kernel(
    place, levels, labels, resid, zvec, after, partial, weights, here, half_diag, link_y, link_z,
):
    planes, rows, layers = labels.shape
    modes = here.shape[2]
    side = lax.rem(place[1], 2)
    at_edge = (place[1] == 0) | (place[1] == place[2] - 1)
    held = (1 - side, side)

    def turn_rows(start):
        for slot, plane in enumerate(held):
            for k in range(0, modes, CHUNK):
                block = zvec[k:k + CHUNK, plane, pl.ds(start, STEP), :]
                here[slot, pl.ds(start, STEP), k:k + CHUNK, :] = jnp.swapaxes(block, 0, 1)

    turn_rows(0)
    coef = [coefficients(labels[x], levels) for x in held]
    middle = harmonic(coef[0], coef[1])
    weights[0] = middle
    row = lax.broadcasted_iota(jnp.int32, (rows, layers), 0)
    lane = lax.broadcasted_iota(jnp.int32, (rows, layers), 1)
    for x in range(2):
        c = coef[x]
        up_y = harmonic(c, jnp.where(row == rows - 1, c, pltpu.roll(c, rows - 1, 0)))
        up_z = harmonic(c, pltpu.roll(c, layers - 1, 1))
        down_y = jnp.where(row == 0, c, pltpu.roll(up_y, 1, 0))
        weights[1 + x] = up_y
        weights[3 + x] = up_z
        weights[5 + x] = c
        inner_z = jnp.where(lane == layers - 1, 0.0, up_z)
        total = middle + up_y + down_y + inner_z + pltpu.roll(inner_z, 1, 1)
        if x == 1:
            total = total + jnp.where(at_edge, c, 0.0)
        half_diag[x] = 0.5 * total
        link_y[x] = jnp.where(row == rows - 1, 0.0, up_y)
        link_z[x] = inner_z

    def step(j, carry):
        total, rhs, wide = carry
        turn_rows(pl.multiple_of(jnp.minimum((j + 1) * STEP, rows - STEP), STEP))
        for u in range(STEP):
            y = j * STEP + u
            at = pl.ds(y, 1)
            ahead = jnp.minimum(y + 1, rows - 1)
            up = [here[x, ahead].astype(F32) for x in range(2)]
            images = []
            for x in range(2):
                image = (
                    half_diag[x, at, :] * wide[x]
                    - link_y[x, at, :] * up[x]
                    - link_z[x, at, :] * pltpu.roll(wide[x], layers - 1, 1)
                )
                if x == 0:
                    image = image - weights[0, at, :] * wide[1]
                rhs = rhs + resid[held[x], at, :] * wide[x]
                images.append(image.astype(BF16))
            total = total + lax.dot_general(
                jnp.concatenate(images, axis=1),
                jnp.concatenate([here[0, y], here[1, y]], axis=1),
                NT,
                preferred_element_type=F32,
            )
            wide = up
        return total, rhs, wide

    total, rhs, _ = lax.fori_loop(
        0,
        rows // STEP,
        step,
        (
            jnp.zeros((modes, modes), F32),
            jnp.zeros((modes, layers), F32),
            [here[x, 0].astype(F32) for x in range(2)],
        ),
    )
    partial[:modes, :] = total
    partial[modes:, :] = lax.dot_general(
        jnp.ones((8, layers), F32), rhs, NT, precision=PRECISE, preferred_element_type=F32
    )


def turn(got, start, out):
    half, modes, layers = out.shape
    for k in range(0, modes, CHUNK):
        out[:, k:k + CHUNK, :] = jnp.swapaxes(got[k:k + CHUNK, pl.ds(start, half), :], 0, 1)


def face_product(weight_ref, base, own, other):
    half, modes, layers = other.shape

    def step(j, total):
        left, right = [], []
        for u in range(STEP):
            y = j * STEP + u
            weight = weight_ref[pl.ds(base + y, 1), :]
            image = weight * (own[base + y].astype(F32) - other[y].astype(F32))
            left.append(jnp.concatenate([own[base + y], other[y]], axis=0))
            right.append(image.astype(BF16))
        return total + lax.dot_general(
            jnp.concatenate(left, axis=1), jnp.concatenate(right, axis=1), NT,
            preferred_element_type=F32,
        )

    total = lax.fori_loop(0, half // STEP, step, jnp.zeros((2 * modes, modes), F32))
    return total[:modes] - total[modes:]


def inner_kernel(place, levels, partial, weights, here, inner_got, out, face, turned):
    planes, rows, modes, layers = here.shape
    half = rows // 2
    side = lax.rem(place[1], 2)
    base = pl.multiple_of(side * half, half)
    turn(inner_got, base, turned)
    face[...] = harmonic(weights[5], coefficients(inner_got[modes].astype(F32), levels))
    out[:modes, :] = partial[:modes, :] + 0.5 * face_product(face, base, here.at[0], turned)
    out[modes:, :] = partial[modes:, :]


def outer_kernel(
    place, levels, partial, weights, here, outer_got, one_pack, two_pack, one_got, two_got,
    out, face, turned, face_here,
):
    planes, rows, modes, layers = here.shape
    half = rows // 2
    side = lax.rem(place[1], 2)
    at_edge = (place[1] == 0) | (place[1] == place[2] - 1)
    base = pl.multiple_of(side * half, half)
    turn(outer_got, 0, turned)
    coef = coefficients(outer_got[modes:].astype(F32).reshape(rows, layers), levels)
    between = harmonic(weights[6], coef)
    face[...] = jnp.where(at_edge, weights[6], between)
    face_here[...] = jnp.where(at_edge, 0.0, between)
    cross = face_product(face_here, base, here.at[1], turned)
    odd = lax.rem(place[0], 2) == 1

    def coef_row(pack):
        return coefficients(pack[modes:modes + 16].astype(F32)[0:1], levels)

    one, two = one_pack[...].astype(F32), two_pack[...].astype(F32)
    one_other, two_other = one_got[...].astype(F32), two_got[...].astype(F32)
    first, last = jnp.where(odd, one, two), jnp.where(odd, two, one)
    next_first = jnp.where(odd, two_other, one_other)
    prev_last = jnp.where(odd, one_other, two_other)
    weight_low = harmonic(coef_row(first), coef_row(prev_last))
    weight_high = harmonic(coef_row(last), coef_row(next_first))

    def product(left, right):
        return lax.dot_general(
            left.astype(BF16), right.astype(BF16), NT, preferred_element_type=F32
        )

    edge_rows = weight_high * last[:modes]
    ends = product(
        jnp.concatenate([weight_low * first[:modes], edge_rows], axis=1),
        jnp.concatenate([first[:modes], last[:modes]], axis=1),
    )
    square = partial[:modes, :] + 0.5 * (cross + ends)
    out[:modes, :modes] = square + square.T
    out[:modes, modes:] = -product(edge_rows, next_first[:modes])
    out[modes:, :modes] = partial[modes:, :]
    out[modes:, modes:] = jnp.zeros((8, modes), F32)


def terms_kernel(
    place, levels, pair, one_got, two_got, weights, inner_face, outer_face, terms, picked, coef_ref
):
    modes, width = picked.shape[1:]
    rows, layers = inner_face.shape
    side = lax.rem(place[1], 2)
    odd = lax.rem(place[0], 2) == 1
    one_other, two_other = one_got[...].astype(F32), two_got[...].astype(F32)
    next_first = jnp.where(odd, two_other, one_other)
    prev_last = jnp.where(odd, one_other, two_other)
    picked[0] = next_first[:modes]
    picked[1] = prev_last[:modes]
    end_labels = lax.dot_general(
        next_first[modes:].astype(BF16), pick_row(layers - 1, layers), TN, preferred_element_type=F32
    ) + lax.dot_general(
        prev_last[modes:].astype(BF16), pick_row(0, layers), TN, preferred_element_type=F32
    )
    coef_ref[...] = coefficients(end_labels, levels).reshape(width // rows, rows, layers)
    row = lax.broadcasted_iota(jnp.int32, (rows, layers), 0)
    lane = lax.broadcasted_iota(jnp.int32, (rows, layers), 1)
    for x, face in enumerate((inner_face, outer_face)):
        c = weights[5 + x]
        end_weight = harmonic(c, coef_ref[1 - side if x == 0 else side])
        up_y, up_z = weights[1 + x], weights[3 + x]
        down_y = jnp.where(row == 0, c, pltpu.roll(up_y, 1, 0))
        down_z = pltpu.roll(up_z, 1, 1)
        total = face[...] + weights[0] + up_y + down_y
        total = total + jnp.where(lane == layers - 1, end_weight, up_z)
        terms[x, 0] = total + jnp.where(lane == 0, end_weight, down_z)
        terms[x, 1] = jnp.where(row == 0, 0.0, down_y)
        terms[x, 2] = jnp.where(row == rows - 1, 0.0, up_y)
        terms[x, 3] = jnp.where(lane == 0, 0.0, down_z)
        terms[x, 4] = jnp.where(lane == layers - 1, 0.0, up_z)
        terms[x, 5] = end_weight


def pair_kernel(own, across, beside, oblique, out):
    modes = own.shape[1] // 2
    encode(own[...] + across[...], modes, out.at[0])
    encode(beside[...] + oblique[...], modes, out.at[1])


def single_kernel(own, out):
    encode(own[...], own.shape[1] // 2, out)


def encode(total, modes, out):
    row = lax.broadcasted_iota(jnp.int32, (modes, 2 * modes), 0)
    lane = lax.broadcasted_iota(jnp.int32, (modes, 2 * modes), 1)
    values = total[:modes]
    high = values.astype(BF16).astype(F32)
    low = values - high
    out[:modes] = jnp.where((lane <= row) | (lane >= modes), high, low).astype(BF16)
    diagonal = lane == row
    right = total[modes:modes + 1]
    parts = []
    for _ in range(3):
        part = right.astype(BF16).astype(F32)
        parts.append(part)
        right = right - part
    for part in (high, low):
        parts.append(jnp.sum(jnp.where(diagonal, part, 0.0), axis=0, keepdims=True))
    rows = lax.broadcasted_iota(jnp.int32, (16, 2 * modes), 0)
    extra = jnp.zeros((16, 2 * modes), F32)
    for index, part in enumerate(parts):
        extra = jnp.where(rows == index, part, extra)
    out[modes:] = extra.astype(BF16)


def finish_kernel(place, *refs):
    count = len(refs) - 15
    blocks, refs = refs[:count], refs[count:]
    zvec, inner_got, outer_got, outer_last, picked, terms, middle, inner_face, outer_face, resid = refs[:10]
    solution, deflated, direction_ref, spread, outer_field = refs[10:]
    subs = direction_ref.shape[0]
    modes, planes, rows, layers = zvec.shape
    half = rows // 2
    me = place[0]
    side = lax.rem(place[1], 2)
    odd = lax.rem(me, 2) == 1
    at_edge = (place[1] == 0) | (place[1] == place[2] - 1)
    order = place[3]
    held = (1 - side, side)
    square = (modes, modes)
    eye = lax.broadcasted_iota(jnp.int32, square, 0) == lax.broadcasted_iota(jnp.int32, square, 1)

    def column(row):
        return jnp.sum(jnp.where(eye, row, 0.0), axis=1, keepdims=True)

    def each(body, carry):
        for index, block in enumerate(blocks):
            held_here = block.shape[0]
            if held_here <= 8:
                for entry in range(held_here):
                    s = jnp.bitwise_xor(order, index * held_here + entry)
                    carry = body(block.at[entry], s, carry)
            else:
                carry = lax.fori_loop(
                    0, held_here, lambda entry, c, block=block: body(block.at[entry], entry, c), carry
                )
        return carry

    def row_is(s, width):
        return lax.broadcasted_iota(jnp.int32, (subs, width), 0) == s

    def load(block, s, carry):
        extra = block[modes:modes + 16, :].astype(F32)
        right = (extra[0:1] + extra[1:2]) + extra[2:3]
        here = row_is(s, 2 * modes)
        return jnp.where(here, right, carry[0]), jnp.where(here, extra[4:5] - extra[3:4], carry[1])

    empty = jnp.zeros((subs, 2 * modes), F32)
    right_side, fix = each(load, (empty, empty))
    fix = fix[:, :modes]

    def turned(rows_of, by):
        by = by % subs
        return jnp.concatenate([rows_of[by:], rows_of[:by]], axis=0)

    def in_parts(value):
        parts = []
        for _ in range(3):
            part = value.astype(BF16)
            parts.append(part.astype(F32))
            value = value - parts[-1]
        return jnp.concatenate(parts, axis=0).astype(BF16)

    def joined(value):
        return (value[:subs] + value[subs:2 * subs]) + value[2 * subs:]

    def coarse_apply(direction):
        pairs = in_parts(jnp.concatenate([direction, turned(direction, 1)], axis=1))
        single = pairs[:, :modes]

        def one(block, s, carry):
            values = block[:modes, :]
            ahead = lax.dot_general(pairs, values, NT, preferred_element_type=F32)
            image = jnp.dot(single, values, preferred_element_type=F32)
            return (
                jnp.where(row_is(s, modes), joined(ahead), carry[0]),
                jnp.where(row_is(s, 2 * modes), joined(image), carry[1]),
            )

        ahead, image = each(one, (jnp.zeros((subs, modes), F32), empty))
        return ahead + image[:, :modes] + fix * direction + turned(image[:, modes:], -1)

    def inner(left, right):
        return jnp.sum(jnp.sum(left * right, axis=0, keepdims=True), axis=1, keepdims=True)

    remain = right_side[:, :modes]
    direction = remain
    result = jnp.zeros_like(remain)
    norm_now = inner(remain, remain)
    for iteration in range(CITERS):
        image = coarse_apply(direction)
        step_size = norm_now / inner(direction, image)
        result = result + step_size * direction
        if iteration + 1 < CITERS:
            remain = remain - step_size * image
            norm_next = inner(remain, remain)
            direction = remain + (norm_next / norm_now) * direction
            norm_now = norm_next
    direction_ref[...] = result
    own = direction_ref[pl.ds(me, 1), :]
    solution[...] = own
    spread[...] = jnp.broadcast_to(column(own), (modes, layers))
    ahead_column = column(direction_ref[pl.ds(lax.rem(me + 1, subs), 1), :])
    behind_column = column(direction_ref[pl.ds(lax.rem(me + subs - 1, subs), 1), :])
    ahead_row = jnp.sum(ahead_column * picked[0], axis=0, keepdims=True)
    behind_row = jnp.sum(behind_column * picked[1], axis=0, keepdims=True)
    width = planes * rows
    both_rows = jnp.where(
        lax.broadcasted_iota(jnp.int32, (8, width), 0) == 0,
        jnp.broadcast_to(ahead_row, (8, width)),
        jnp.broadcast_to(behind_row, (8, width)),
    )
    columns = both_rows.T
    ends = jnp.where(
        lane_is((width, layers), layers - 1),
        columns[:, 0:1],
        jnp.where(lane_is((width, layers), 0), columns[:, 1:2], 0.0),
    ).reshape(planes, rows, layers)

    def add_mode(j, carry):
        fields, near, last = list(carry[0]), carry[1], carry[2]
        for u in range(MODES):
            k = j * MODES + u
            scale = spread[pl.ds(k, 1), :]
            for x, plane in enumerate((zvec[k, held[0]], zvec[k, held[1]], inner_got[k])):
                fields[x] = fields[x] + scale * plane.astype(F32)
            near = near + scale * outer_got[k].astype(F32)
            last = last + scale * outer_last[k].astype(F32)
        return tuple(fields), near, last

    zero, short = jnp.zeros((rows, layers), F32), jnp.zeros((half, layers), F32)
    field, near, last = lax.fori_loop(0, modes // MODES, add_mode, ((zero,) * 3, short, short))
    outer_field[pl.ds(pl.multiple_of(side * half, half), half), :] = near
    outer_field[pl.ds(pl.multiple_of((1 - side) * half, half), half), :] = last
    outside = (field[2], jnp.where(at_edge, 0.0, outer_field[...]))
    faces = (inner_face[...], outer_face[...])
    for x in range(2):
        f = field[x]
        end_field = jnp.where(side == x, ends[1], ends[0])
        image = (
            terms[x, 0] * f
            - middle[0] * field[1 - x]
            - faces[x] * outside[x]
            - terms[x, 1] * pltpu.roll(f, 1, 0)
            - terms[x, 2] * pltpu.roll(f, rows - 1, 0)
            - terms[x, 3] * pltpu.roll(f, 1, 1)
            - terms[x, 4] * pltpu.roll(f, layers - 1, 1)
            - terms[x, 5] * end_field
        )
        deflated[held[x]] = resid[held[x]] - image


def swapped(value, axis, first):
    count = lax.axis_size(axis)
    pairs = []
    for i in range(count):
        up = (i - first) % 2 == 0
        pairs.append((i, (i + 1) % count if up else (i - 1) % count))
    return lax.ppermute(value, axis, pairs)


def swapped_all(value):
    subs, count = lax.axis_size("sub"), lax.axis_size("pln")
    pairs = []
    for s in range(subs):
        for i in range(count):
            if 0 < i < count - 1:
                to = (s, i + 1 if i % 2 else i - 1)
            else:
                to = (s ^ 1, i)
            pairs.append((s * count + i, to[0] * count + to[1]))
    return lax.ppermute(value, ("sub", "pln"), pairs)


def exchanged(value, axis, mask):
    return lax.ppermute(value, axis, [(i, i ^ mask) for i in range(lax.axis_size(axis))])


def partner(value, sub_mask, pln_mask):
    subs, count = lax.axis_size("sub"), lax.axis_size("pln")
    pairs = [
        (s * count + p, (s ^ sub_mask) * count + (p ^ pln_mask)) for s in range(subs) for p in range(count)
    ]
    return lax.ppermute(value, ("sub", "pln"), pairs)


def body(labels, levels, zvec, resid):
    modes, planes, rows, layers = zvec.shape
    half = rows // 2
    subs, parts = lax.axis_size("sub"), lax.axis_size("pln")
    shape = jax.ShapeDtypeStruct
    order = lax.axis_index("sub") if subs == 8 else 0
    place = jnp.stack(
        [jnp.int32(v) for v in (lax.axis_index("sub"), lax.axis_index("pln"), parts, order)]
    )
    pack = shape((modes + 16, planes * rows), BF16)
    inner_send, outer_near = call(
        stage_kernel,
        [shape((modes + 1, rows, layers), BF16), shape((modes + rows // half, half, layers), BF16)],
        [SMEM, HBM, HBM],
        [pltpu.VMEM(labels.shape, jnp.int32), pltpu.SemaphoreType.DMA, pltpu.SemaphoreType.DMA((2,))],
        moved=2 << 20,
    )(place, *(pltpu.with_memory_space_constraint(v, pltpu.HBM) for v in (labels, zvec)))
    outer_got = swapped_all(outer_near)
    inner_got = swapped(inner_send, "pln", 0)
    rest = shape((modes, half, layers), BF16)
    outer_rest, one_pack, two_pack = call(
        prepare_kernel,
        [rest, pack, pack],
        [SMEM, VMEM, VMEM],
        flops=10_000_000,
        moved=6 << 20,
    )(place, labels, zvec)
    one_got = swapped(one_pack, "sub", 0)
    two_got = swapped(two_pack, "sub", 1)
    field = (planes, rows, layers)
    plane = (rows, layers)
    partial, weights, here = call(
        block_kernel,
        [
            shape((modes + 8, modes), F32),
            shape((7,) + plane, F32),
            shape((planes, rows, modes, layers), BF16),
        ],
        [SMEM, SMEM] + [VMEM] * 3 + [ANY],
        [pltpu.VMEM(field, F32)] * 3,
        flops=400_000_000,
        moved=3 << 20,
    )(place, levels, labels, resid, zvec, one_pack)
    turned = pltpu.VMEM((half, modes, layers), BF16)
    partial, inner_face = call(
        inner_kernel,
        [shape((modes + 8, modes), F32), shape(plane, F32)],
        [SMEM, SMEM] + [VMEM] * 4,
        [turned],
        flops=100_000_000,
        moved=1 << 20,
    )(place, levels, partial, weights, here, inner_got)
    block, outer_face = call(
        outer_kernel,
        [shape((modes + 8, 2 * modes), F32), shape(plane, F32)],
        [SMEM, SMEM] + [VMEM] * 8,
        [turned, pltpu.VMEM(plane, F32)],
        flops=100_000_000,
        moved=1 << 20,
    )(place, levels, partial, weights, here, outer_got, one_pack, two_pack, one_got, two_got)
    packed = (modes + 16, 2 * modes)
    if parts == 4 and subs == 8:
        block = block + exchanged(block, "pln", 1)
        others = [partner(block, *masks) for masks in ((0, 3), (1, 1), (1, 3))]
        [pair] = call(pair_kernel, [shape((2,) + packed, BF16)], [VMEM] * 4)(block, *others)
        blocks = [pair] + [partner(pair, mask, 1) for mask in (2, 4, 6)]
    else:
        [single] = call(single_kernel, [shape(packed, BF16)], [VMEM])(lax.psum(block, "pln"))
        blocks = [lax.all_gather(single, "sub")]
    [outer_rest] = call(release_kernel, [rest], [ANY] * 2, aliases={1: 0})(block, outer_rest)
    outer_last = swapped_all(outer_rest)
    terms, picked = call(
        terms_kernel,
        [shape((planes, 6) + plane, F32), shape((2, modes, planes * rows), F32)],
        [SMEM, SMEM, ANY] + [VMEM] * 5,
        [pltpu.VMEM(field, F32)],

        flops=1 << 33,
        moved=1 << 20,
    )(place, levels, blocks[0], one_got, two_got, weights, inner_face, outer_face)
    return tuple(
        call(
            finish_kernel,
            [shape((1, modes), F32), shape(field, F32)],
            [SMEM] + [VMEM] * (10 + len(blocks)),
            [
                pltpu.VMEM((subs, modes), F32),
                pltpu.VMEM((modes, layers), F32),
                pltpu.VMEM(plane, F32),
            ],
            flops=10_000_000,
            moved=5 << 20,
        )(
            place, *blocks, zvec, inner_got, outer_got, outer_last, picked, terms, weights, inner_face,
            outer_face, resid,
        )
    )


def solution(mesh):
    in_specs = (P("pln", None, "sub"), P(), P(None, "pln", None, "sub"), P("pln", None, "sub"))
    out_specs = (P("sub", None), P("pln", None, "sub"))
    return jax.shard_map(body, mesh=mesh, in_specs=in_specs, out_specs=out_specs, check_vma=False)
```

```python
import jax
import jax.numpy as jnp
from jax import lax
from jax.experimental import pallas as pl
from jax.experimental.pallas import tpu as pltpu
from jax.sharding import PartitionSpec as P

CITERS = 2
STEP = 16
MODES = 8
CHUNK = 16
F32 = jnp.float32
BF16 = jnp.bfloat16
PRECISE = lax.Precision.HIGHEST
NT = (((1,), (1,)), ((), ()))
TN = (((0,), (0,)), ((), ()))
VMEM = pl.BlockSpec(memory_space=pltpu.VMEM)
SMEM = pl.BlockSpec(memory_space=pltpu.SMEM)
HBM = pl.BlockSpec(memory_space=pltpu.HBM)
ANY = pl.BlockSpec(memory_space=pl.ANY)


def call(kernel, outs, specs, scratch=(), flops=0, moved=0, limit=32, aliases=None):
    return pl.pallas_call(
        kernel,
        out_shape=outs,
        in_specs=specs,
        out_specs=[ANY if at in (aliases or {}).values() else VMEM for at in range(len(outs))],
        input_output_aliases=aliases or {},
        scratch_shapes=list(scratch),
        cost_estimate=pl.CostEstimate(flops=flops, bytes_accessed=moved, transcendentals=0),
        compiler_params=pltpu.CompilerParams(vmem_limit_bytes=limit << 20),
    )


def harmonic(left_value, right_value):
    return 2.0 * left_value * right_value / (left_value + right_value)


def coefficients(labels, levels_ref):
    weighted = jnp.zeros(labels.shape, F32)
    for level in range(levels_ref.shape[0]):
        weighted = weighted + jnp.where(labels == level, levels_ref[level], 0.0)
    return weighted


def lane_is(shape, lane):
    return lax.broadcasted_iota(jnp.int32, shape, len(shape) - 1) == lane


def pick_row(lane, width):
    row = lax.broadcasted_iota(jnp.int32, (16, width), 0)
    return ((row == 0) & lane_is((16, width), lane)).astype(BF16)


def stage_kernel(place, labels_far, zvec, inner_send, outer_near, labels, label_sem, sems):
    modes, planes, rows, layers = zvec.shape
    half = rows // 2
    side = lax.rem(place[1], 2)
    start = pl.multiple_of((1 - side) * half, half)
    label_copy = pltpu.make_async_copy(labels_far, labels, label_sem)
    copies = [
        pltpu.make_async_copy(
            zvec.at[:, side, pl.ds(start, half), :], outer_near.at[pl.ds(0, modes)], sems.at[0]
        ),
        pltpu.make_async_copy(zvec.at[:, 1 - side], inner_send.at[pl.ds(0, modes)], sems.at[1]),
    ]
    label_copy.start()
    for copy in copies:
        copy.start()
    label_copy.wait()
    outer_near[modes:] = labels[side].astype(F32).astype(BF16).reshape(rows // half, half, layers)
    inner_send[modes] = labels[1 - side].astype(F32).astype(BF16)
    for copy in copies:
        copy.wait()


def release_kernel(after, outer_rest, outer_out):
    pass


def prepare_kernel(place, labels, held, outer_rest, one_pack, two_pack):
    modes, planes, rows, layers = held.shape
    half = rows // 2
    width = planes * rows
    side = lax.rem(place[1], 2)
    odd = lax.rem(place[0], 2) == 1
    one_lane = jnp.where(odd, 0, layers - 1)
    two_lane = jnp.where(odd, layers - 1, 0)
    row = lax.broadcasted_iota(jnp.int32, (16, layers), 0)
    both = ((row == 0) & lane_is((16, layers), one_lane)) | ((row == 1) & lane_is((16, layers), two_lane))
    both = both.astype(BF16)
    flat = labels[...].astype(F32).astype(BF16).reshape(width, layers)
    for out, lane in ((one_pack, one_lane), (two_pack, two_lane)):
        out[modes:] = lax.dot_general(
            pick_row(lane, layers), flat, NT, preferred_element_type=F32
        ).astype(BF16)
    for k in range(0, modes, CHUNK):
        at = slice(k, k + CHUNK)
        ends = lax.dot_general(
            both, held[at].reshape(-1, layers), NT, preferred_element_type=F32
        )
        for out, index in ((one_pack, 0), (two_pack, 1)):
            out[at] = jnp.concatenate(
                [ends[index:index + 1, j * width:(j + 1) * width] for j in range(CHUNK)], axis=0
            ).astype(BF16)
        outer_rest[at] = held[at, side, pl.ds(pl.multiple_of(side * half, half), half), :]


def block_kernel(
    place, levels, labels, resid, zvec, after, partial, weights, here, half_diag, link_y, link_z,
):
    planes, rows, layers = labels.shape
    modes = here.shape[2]
    side = lax.rem(place[1], 2)
    at_edge = (place[1] == 0) | (place[1] == place[2] - 1)
    held = (1 - side, side)

    def turn_rows(start):
        for slot, plane in enumerate(held):
            for k in range(0, modes, CHUNK):
                block = zvec[k:k + CHUNK, plane, pl.ds(start, STEP), :]
                here[slot, pl.ds(start, STEP), k:k + CHUNK, :] = jnp.swapaxes(block, 0, 1)

    turn_rows(0)
    coef = [coefficients(labels[x], levels) for x in held]
    middle = harmonic(coef[0], coef[1])
    weights[0] = middle
    row = lax.broadcasted_iota(jnp.int32, (rows, layers), 0)
    lane = lax.broadcasted_iota(jnp.int32, (rows, layers), 1)
    for x in range(2):
        c = coef[x]
        up_y = harmonic(c, jnp.where(row == rows - 1, c, pltpu.roll(c, rows - 1, 0)))
        up_z = harmonic(c, pltpu.roll(c, layers - 1, 1))
        down_y = jnp.where(row == 0, c, pltpu.roll(up_y, 1, 0))
        weights[1 + x] = up_y
        weights[3 + x] = up_z
        weights[5 + x] = c
        inner_z = jnp.where(lane == layers - 1, 0.0, up_z)
        total = middle + up_y + down_y + inner_z + pltpu.roll(inner_z, 1, 1)
        if x == 1:
            total = total + jnp.where(at_edge, c, 0.0)
        half_diag[x] = 0.5 * total
        link_y[x] = jnp.where(row == rows - 1, 0.0, up_y)
        link_z[x] = inner_z

    def step(j, carry):
        total, rhs, wide = carry
        turn_rows(pl.multiple_of(jnp.minimum((j + 1) * STEP, rows - STEP), STEP))
        for u in range(STEP):
            y = j * STEP + u
            at = pl.ds(y, 1)
            ahead = jnp.minimum(y + 1, rows - 1)
            up = [here[x, ahead].astype(F32) for x in range(2)]
            images = []
            for x in range(2):
                image = (
                    half_diag[x, at, :] * wide[x]
                    - link_y[x, at, :] * up[x]
                    - link_z[x, at, :] * pltpu.roll(wide[x], layers - 1, 1)
                )
                if x == 0:
                    image = image - weights[0, at, :] * wide[1]
                rhs = rhs + resid[held[x], at, :] * wide[x]
                images.append(image.astype(BF16))
            total = total + lax.dot_general(
                jnp.concatenate(images, axis=1),
                jnp.concatenate([here[0, y], here[1, y]], axis=1),
                NT,
                preferred_element_type=F32,
            )
            wide = up
        return total, rhs, wide

    total, rhs, _ = lax.fori_loop(
        0,
        rows // STEP,
        step,
        (
            jnp.zeros((modes, modes), F32),
            jnp.zeros((modes, layers), F32),
            [here[x, 0].astype(F32) for x in range(2)],
        ),
    )
    partial[:modes, :] = total
    partial[modes:, :] = lax.dot_general(
        jnp.ones((8, layers), F32), rhs, NT, precision=PRECISE, preferred_element_type=F32
    )


def turn(got, start, out):
    half, modes, layers = out.shape
    for k in range(0, modes, CHUNK):
        out[:, k:k + CHUNK, :] = jnp.swapaxes(got[k:k + CHUNK, pl.ds(start, half), :], 0, 1)


def face_product(weight_ref, base, own, other):
    half, modes, layers = other.shape

    def step(j, total):
        left, right = [], []
        for u in range(STEP):
            y = j * STEP + u
            weight = weight_ref[pl.ds(base + y, 1), :]
            image = weight * (own[base + y].astype(F32) - other[y].astype(F32))
            left.append(jnp.concatenate([own[base + y], other[y]], axis=0))
            right.append(image.astype(BF16))
        return total + lax.dot_general(
            jnp.concatenate(left, axis=1), jnp.concatenate(right, axis=1), NT,
            preferred_element_type=F32,
        )

    total = lax.fori_loop(0, half // STEP, step, jnp.zeros((2 * modes, modes), F32))
    return total[:modes] - total[modes:]


def inner_kernel(place, levels, partial, weights, here, inner_got, out, face, turned):
    planes, rows, modes, layers = here.shape
    half = rows // 2
    side = lax.rem(place[1], 2)
    base = pl.multiple_of(side * half, half)
    turn(inner_got, base, turned)
    face[...] = harmonic(weights[5], coefficients(inner_got[modes].astype(F32), levels))
    out[:modes, :] = partial[:modes, :] + 0.5 * face_product(face, base, here.at[0], turned)
    out[modes:, :] = partial[modes:, :]


def outer_kernel(
    place, levels, partial, weights, here, outer_got, one_pack, two_pack, one_got, two_got,
    out, face, turned, face_here,
):
    planes, rows, modes, layers = here.shape
    half = rows // 2
    side = lax.rem(place[1], 2)
    at_edge = (place[1] == 0) | (place[1] == place[2] - 1)
    base = pl.multiple_of(side * half, half)
    turn(outer_got, 0, turned)
    coef = coefficients(outer_got[modes:].astype(F32).reshape(rows, layers), levels)
    between = harmonic(weights[6], coef)
    face[...] = jnp.where(at_edge, weights[6], between)
    face_here[...] = jnp.where(at_edge, 0.0, between)
    cross = face_product(face_here, base, here.at[1], turned)
    odd = lax.rem(place[0], 2) == 1

    def coef_row(pack):
        return coefficients(pack[modes:modes + 16].astype(F32)[0:1], levels)

    one, two = one_pack[...].astype(F32), two_pack[...].astype(F32)
    one_other, two_other = one_got[...].astype(F32), two_got[...].astype(F32)
    first, last = jnp.where(odd, one, two), jnp.where(odd, two, one)
    next_first = jnp.where(odd, two_other, one_other)
    prev_last = jnp.where(odd, one_other, two_other)
    weight_low = harmonic(coef_row(first), coef_row(prev_last))
    weight_high = harmonic(coef_row(last), coef_row(next_first))

    def product(left, right):
        return lax.dot_general(
            left.astype(BF16), right.astype(BF16), NT, preferred_element_type=F32
        )

    edge_rows = weight_high * last[:modes]
    ends = product(
        jnp.concatenate([weight_low * first[:modes], edge_rows], axis=1),
        jnp.concatenate([first[:modes], last[:modes]], axis=1),
    )
    square = partial[:modes, :] + 0.5 * (cross + ends)
    out[:modes, :modes] = square + square.T
    out[:modes, modes:] = -product(edge_rows, next_first[:modes])
    out[modes:, :modes] = partial[modes:, :]
    out[modes:, modes:] = jnp.zeros((8, modes), F32)


def terms_kernel(
    place, levels, pair, one_got, two_got, weights, inner_face, outer_face, terms, picked, coef_ref
):
    modes, width = picked.shape[1:]
    rows, layers = inner_face.shape
    side = lax.rem(place[1], 2)
    odd = lax.rem(place[0], 2) == 1
    one_other, two_other = one_got[...].astype(F32), two_got[...].astype(F32)
    next_first = jnp.where(odd, two_other, one_other)
    prev_last = jnp.where(odd, one_other, two_other)
    picked[0] = next_first[:modes]
    picked[1] = prev_last[:modes]
    end_labels = lax.dot_general(
        next_first[modes:].astype(BF16), pick_row(layers - 1, layers), TN, preferred_element_type=F32
    ) + lax.dot_general(
        prev_last[modes:].astype(BF16), pick_row(0, layers), TN, preferred_element_type=F32
    )
    coef_ref[...] = coefficients(end_labels, levels).reshape(width // rows, rows, layers)
    row = lax.broadcasted_iota(jnp.int32, (rows, layers), 0)
    lane = lax.broadcasted_iota(jnp.int32, (rows, layers), 1)
    for x, face in enumerate((inner_face, outer_face)):
        c = weights[5 + x]
        end_weight = harmonic(c, coef_ref[1 - side if x == 0 else side])
        up_y, up_z = weights[1 + x], weights[3 + x]
        down_y = jnp.where(row == 0, c, pltpu.roll(up_y, 1, 0))
        down_z = pltpu.roll(up_z, 1, 1)
        total = face[...] + weights[0] + up_y + down_y
        total = total + jnp.where(lane == layers - 1, end_weight, up_z)
        terms[x, 0] = total + jnp.where(lane == 0, end_weight, down_z)
        terms[x, 1] = jnp.where(row == 0, 0.0, down_y)
        terms[x, 2] = jnp.where(row == rows - 1, 0.0, up_y)
        terms[x, 3] = jnp.where(lane == 0, 0.0, down_z)
        terms[x, 4] = jnp.where(lane == layers - 1, 0.0, up_z)
        terms[x, 5] = end_weight


def pair_kernel(own, across, beside, oblique, out):
    modes = own.shape[1] // 2
    encode(own[...] + across[...], modes, out.at[0])
    encode(beside[...] + oblique[...], modes, out.at[1])


def single_kernel(own, out):
    encode(own[...], own.shape[1] // 2, out)


def encode(total, modes, out):
    row = lax.broadcasted_iota(jnp.int32, (modes, 2 * modes), 0)
    lane = lax.broadcasted_iota(jnp.int32, (modes, 2 * modes), 1)
    values = total[:modes]
    high = values.astype(BF16).astype(F32)
    low = values - high
    out[:modes] = jnp.where((lane <= row) | (lane >= modes), high, low).astype(BF16)
    diagonal = lane == row
    right = total[modes:modes + 1]
    parts = []
    for _ in range(3):
        part = right.astype(BF16).astype(F32)
        parts.append(part)
        right = right - part
    for part in (high, low):
        parts.append(jnp.sum(jnp.where(diagonal, part, 0.0), axis=0, keepdims=True))
    rows = lax.broadcasted_iota(jnp.int32, (16, 2 * modes), 0)
    extra = jnp.zeros((16, 2 * modes), F32)
    for index, part in enumerate(parts):
        extra = jnp.where(rows == index, part, extra)
    out[modes:] = extra.astype(BF16)


def finish_kernel(place, *refs):
    count = len(refs) - 15
    blocks, refs = refs[:count], refs[count:]
    zvec, inner_got, outer_got, outer_last, picked, terms, middle, inner_face, outer_face, resid = refs[:10]
    solution, deflated, direction_ref, spread, outer_field = refs[10:]
    subs = direction_ref.shape[0]
    modes, planes, rows, layers = zvec.shape
    half = rows // 2
    me = place[0]
    side = lax.rem(place[1], 2)
    odd = lax.rem(me, 2) == 1
    at_edge = (place[1] == 0) | (place[1] == place[2] - 1)
    held = (1 - side, side)
    square = (modes, modes)
    eye = lax.broadcasted_iota(jnp.int32, square, 0) == lax.broadcasted_iota(jnp.int32, square, 1)

    def column(row):
        return jnp.sum(jnp.where(eye, row, 0.0), axis=1, keepdims=True)

    def each(body, carry):
        for index, block in enumerate(blocks):
            held_here = block.shape[0]
            if held_here <= 8:
                for entry in range(held_here):
                    s = jnp.bitwise_xor(place[3 + index], entry)
                    carry = body(block.at[entry], s, carry)
            else:
                carry = lax.fori_loop(
                    0, held_here, lambda entry, c, block=block: body(block.at[entry], entry, c), carry
                )
        return carry

    def row_is(s, width):
        return lax.broadcasted_iota(jnp.int32, (subs, width), 0) == s

    def load(block, s, carry):
        extra = block[modes:modes + 16, :].astype(F32)
        right = (extra[0:1] + extra[1:2]) + extra[2:3]
        here = row_is(s, 2 * modes)
        return jnp.where(here, right, carry[0]), jnp.where(here, extra[4:5] - extra[3:4], carry[1])

    empty = jnp.zeros((subs, 2 * modes), F32)
    right_side, fix = each(load, (empty, empty))
    fix = fix[:, :modes]

    def turned(rows_of, by):
        by = by % subs
        return jnp.concatenate([rows_of[by:], rows_of[:by]], axis=0)

    def in_parts(value):
        parts = []
        for _ in range(3):
            part = value.astype(BF16)
            parts.append(part.astype(F32))
            value = value - parts[-1]
        return jnp.concatenate(parts, axis=0).astype(BF16)

    def joined(value):
        return (value[:subs] + value[subs:2 * subs]) + value[2 * subs:]

    def coarse_apply(direction):
        pairs = in_parts(jnp.concatenate([direction, turned(direction, 1)], axis=1))
        single = pairs[:, :modes]

        def one(block, s, carry):
            values = block[:modes, :]
            ahead = lax.dot_general(pairs, values, NT, preferred_element_type=F32)
            image = jnp.dot(single, values, preferred_element_type=F32)
            return (
                jnp.where(row_is(s, modes), joined(ahead), carry[0]),
                jnp.where(row_is(s, 2 * modes), joined(image), carry[1]),
            )

        ahead, image = each(one, (jnp.zeros((subs, modes), F32), empty))
        return ahead + image[:, :modes] + fix * direction + turned(image[:, modes:], -1)

    def inner(left, right):
        return jnp.sum(jnp.sum(left * right, axis=0, keepdims=True), axis=1, keepdims=True)

    remain = right_side[:, :modes]
    direction = remain
    result = jnp.zeros_like(remain)
    norm_now = inner(remain, remain)
    for iteration in range(CITERS):
        image = coarse_apply(direction)
        step_size = norm_now / inner(direction, image)
        result = result + step_size * direction
        if iteration + 1 < CITERS:
            remain = remain - step_size * image
            norm_next = inner(remain, remain)
            direction = remain + (norm_next / norm_now) * direction
            norm_now = norm_next
    direction_ref[...] = result
    own = direction_ref[pl.ds(me, 1), :]
    solution[...] = own
    spread[...] = jnp.broadcast_to(column(own), (modes, layers))
    ahead_column = column(direction_ref[pl.ds(lax.rem(me + 1, subs), 1), :])
    behind_column = column(direction_ref[pl.ds(lax.rem(me + subs - 1, subs), 1), :])
    ahead_row = jnp.sum(ahead_column * picked[0], axis=0, keepdims=True)
    behind_row = jnp.sum(behind_column * picked[1], axis=0, keepdims=True)
    width = planes * rows
    both_rows = jnp.where(
        lax.broadcasted_iota(jnp.int32, (8, width), 0) == 0,
        jnp.broadcast_to(ahead_row, (8, width)),
        jnp.broadcast_to(behind_row, (8, width)),
    )
    columns = both_rows.T
    ends = jnp.where(
        lane_is((width, layers), layers - 1),
        columns[:, 0:1],
        jnp.where(lane_is((width, layers), 0), columns[:, 1:2], 0.0),
    ).reshape(planes, rows, layers)

    def add_mode(j, carry):
        fields, near, last = list(carry[0]), carry[1], carry[2]
        for u in range(MODES):
            k = j * MODES + u
            scale = spread[pl.ds(k, 1), :]
            for x, plane in enumerate((zvec[k, held[0]], zvec[k, held[1]], inner_got[k])):
                fields[x] = fields[x] + scale * plane.astype(F32)
            near = near + scale * outer_got[k].astype(F32)
            last = last + scale * outer_last[k].astype(F32)
        return tuple(fields), near, last

    zero, short = jnp.zeros((rows, layers), F32), jnp.zeros((half, layers), F32)
    field, near, last = lax.fori_loop(0, modes // MODES, add_mode, ((zero,) * 3, short, short))
    outer_field[pl.ds(pl.multiple_of(side * half, half), half), :] = near
    outer_field[pl.ds(pl.multiple_of((1 - side) * half, half), half), :] = last
    outside = (field[2], jnp.where(at_edge, 0.0, outer_field[...]))
    faces = (inner_face[...], outer_face[...])
    for x in range(2):
        f = field[x]
        end_field = jnp.where(side == x, ends[1], ends[0])
        image = (
            terms[x, 0] * f
            - middle[0] * field[1 - x]
            - faces[x] * outside[x]
            - terms[x, 1] * pltpu.roll(f, 1, 0)
            - terms[x, 2] * pltpu.roll(f, rows - 1, 0)
            - terms[x, 3] * pltpu.roll(f, 1, 1)
            - terms[x, 4] * pltpu.roll(f, layers - 1, 1)
            - terms[x, 5] * end_field
        )
        deflated[held[x]] = resid[held[x]] - image


def swapped(value, axis, first):
    count = lax.axis_size(axis)
    pairs = []
    for i in range(count):
        up = (i - first) % 2 == 0
        pairs.append((i, (i + 1) % count if up else (i - 1) % count))
    return lax.ppermute(value, axis, pairs)


def swapped_all(value):
    subs, count = lax.axis_size("sub"), lax.axis_size("pln")
    pairs = []
    for s in range(subs):
        for i in range(count):
            if 0 < i < count - 1:
                to = (s, i + 1 if i % 2 else i - 1)
            else:
                to = (s ^ 1, i)
            pairs.append((s * count + i, to[0] * count + to[1]))
    return lax.ppermute(value, ("sub", "pln"), pairs)


def exchanged(value, axis, mask):
    return lax.ppermute(value, axis, [(i, i ^ mask) for i in range(lax.axis_size(axis))])


def partner(value, sub_mask, pln_mask):
    subs, count = lax.axis_size("sub"), lax.axis_size("pln")
    pairs = [
        (s * count + p, (s ^ sub_mask) * count + (p ^ pln_mask)) for s in range(subs) for p in range(count)
    ]
    return lax.ppermute(value, ("sub", "pln"), pairs)


FAR = (4, 6)


def far_partner(value):
    subs, count = lax.axis_size("sub"), lax.axis_size("pln")
    pairs = [(s * count + p, (s ^ FAR[p % 2]) * count + p) for s in range(subs) for p in range(count)]
    return lax.ppermute(value, ("sub", "pln"), pairs)


def body(labels, levels, zvec, resid):
    modes, planes, rows, layers = zvec.shape
    half = rows // 2
    subs, parts = lax.axis_size("sub"), lax.axis_size("pln")
    shape = jax.ShapeDtypeStruct
    at_sub, at_pln = lax.axis_index("sub"), lax.axis_index("pln")
    core = at_pln % 2
    masks = (0, FAR[0] + core * (FAR[1] - FAR[0]), 2, FAR[1] + core * (FAR[0] - FAR[1]))
    orders = [at_sub ^ mask for mask in masks] if parts == 4 and subs == 8 else [0] * 4
    place = jnp.stack([jnp.int32(v) for v in (at_sub, at_pln, parts, *orders)])
    pack = shape((modes + 16, planes * rows), BF16)
    inner_send, outer_near = call(
        stage_kernel,
        [shape((modes + 1, rows, layers), BF16), shape((modes + rows // half, half, layers), BF16)],
        [SMEM, HBM, HBM],
        [pltpu.VMEM(labels.shape, jnp.int32), pltpu.SemaphoreType.DMA, pltpu.SemaphoreType.DMA((2,))],
        moved=2 << 20,
    )(place, *(pltpu.with_memory_space_constraint(v, pltpu.HBM) for v in (labels, zvec)))
    outer_got = swapped_all(outer_near)
    inner_got = swapped(inner_send, "pln", 0)
    rest = shape((modes, half, layers), BF16)
    outer_rest, one_pack, two_pack = call(
        prepare_kernel,
        [rest, pack, pack],
        [SMEM, VMEM, VMEM],
        flops=10_000_000,
        moved=6 << 20,
    )(place, labels, zvec)
    one_got = swapped(one_pack, "sub", 0)
    two_got = swapped(two_pack, "sub", 1)
    field = (planes, rows, layers)
    plane = (rows, layers)
    partial, weights, here = call(
        block_kernel,
        [
            shape((modes + 8, modes), F32),
            shape((7,) + plane, F32),
            shape((planes, rows, modes, layers), BF16),
        ],
        [SMEM, SMEM] + [VMEM] * 3 + [ANY],
        [pltpu.VMEM(field, F32)] * 3,
        flops=400_000_000,
        moved=3 << 20,
    )(place, levels, labels, resid, zvec, one_pack)
    turned = pltpu.VMEM((half, modes, layers), BF16)
    partial, inner_face = call(
        inner_kernel,
        [shape((modes + 8, modes), F32), shape(plane, F32)],
        [SMEM, SMEM] + [VMEM] * 4,
        [turned],
        flops=100_000_000,
        moved=1 << 20,
    )(place, levels, partial, weights, here, inner_got)
    block, outer_face = call(
        outer_kernel,
        [shape((modes + 8, 2 * modes), F32), shape(plane, F32)],
        [SMEM, SMEM] + [VMEM] * 8,
        [turned, pltpu.VMEM(plane, F32)],
        flops=100_000_000,
        moved=1 << 20,
    )(place, levels, partial, weights, here, outer_got, one_pack, two_pack, one_got, two_got)
    packed = (modes + 16, 2 * modes)
    if parts == 4 and subs == 8:
        block = block + exchanged(block, "pln", 1)
        others = [partner(block, *masks) for masks in ((0, 3), (1, 1), (1, 3))]
        [pair] = call(pair_kernel, [shape((2,) + packed, BF16)], [VMEM] * 4)(block, *others)
        far = far_partner(pair)
        blocks = [pair, far, partner(pair, 2, 1), exchanged(far, "pln", 1)]
    else:
        [single] = call(single_kernel, [shape(packed, BF16)], [VMEM])(lax.psum(block, "pln"))
        blocks = [lax.all_gather(single, "sub")]
    [outer_rest] = call(release_kernel, [rest], [ANY] * 2, aliases={1: 0})(block, outer_rest)
    outer_last = swapped_all(outer_rest)
    terms, picked = call(
        terms_kernel,
        [shape((planes, 6) + plane, F32), shape((2, modes, planes * rows), F32)],
        [SMEM, SMEM, ANY] + [VMEM] * 5,
        [pltpu.VMEM(field, F32)],

        flops=1 << 33,
        moved=1 << 20,
    )(place, levels, blocks[0], one_got, two_got, weights, inner_face, outer_face)
    return tuple(
        call(
            finish_kernel,
            [shape((1, modes), F32), shape(field, F32)],
            [SMEM] + [VMEM] * (10 + len(blocks)),
            [
                pltpu.VMEM((subs, modes), F32),
                pltpu.VMEM((modes, layers), F32),
                pltpu.VMEM(plane, F32),
            ],
            flops=10_000_000,
            moved=5 << 20,
        )(
            place, *blocks, zvec, inner_got, outer_got, outer_last, picked, terms, weights, inner_face,
            outer_face, resid,
        )
    )


def solution(mesh):
    in_specs = (P("pln", None, "sub"), P(), P(None, "pln", None, "sub"), P("pln", None, "sub"))
    out_specs = (P("sub", None), P("pln", None, "sub"))
    return jax.shard_map(body, mesh=mesh, in_specs=in_specs, out_specs=out_specs, check_vma=False)
```

```python
import jax
import jax.numpy as jnp
from jax import lax
from jax.experimental import pallas as pl
from jax.experimental.pallas import tpu as pltpu
from jax.sharding import PartitionSpec as P

CITERS = 2
STEP = 16
MODES = 8
CHUNK = 16
F32 = jnp.float32
BF16 = jnp.bfloat16
PRECISE = lax.Precision.HIGHEST
NT = (((1,), (1,)), ((), ()))
TN = (((0,), (0,)), ((), ()))
VMEM = pl.BlockSpec(memory_space=pltpu.VMEM)
SMEM = pl.BlockSpec(memory_space=pltpu.SMEM)
HBM = pl.BlockSpec(memory_space=pltpu.HBM)
ANY = pl.BlockSpec(memory_space=pl.ANY)


def call(kernel, outs, specs, scratch=(), flops=0, moved=0, limit=32, aliases=None):
    return pl.pallas_call(
        kernel,
        out_shape=outs,
        in_specs=specs,
        out_specs=[ANY if at in (aliases or {}).values() else VMEM for at in range(len(outs))],
        input_output_aliases=aliases or {},
        scratch_shapes=list(scratch),
        cost_estimate=pl.CostEstimate(flops=flops, bytes_accessed=moved, transcendentals=0),
        compiler_params=pltpu.CompilerParams(vmem_limit_bytes=limit << 20),
    )


def harmonic(left_value, right_value):
    return 2.0 * left_value * right_value / (left_value + right_value)


def coefficients(labels, levels_ref):
    weighted = jnp.zeros(labels.shape, F32)
    for level in range(levels_ref.shape[0]):
        weighted = weighted + jnp.where(labels == level, levels_ref[level], 0.0)
    return weighted


def lane_is(shape, lane):
    return lax.broadcasted_iota(jnp.int32, shape, len(shape) - 1) == lane


def pick_row(lane, width):
    row = lax.broadcasted_iota(jnp.int32, (16, width), 0)
    return ((row == 0) & lane_is((16, width), lane)).astype(BF16)


def stage_kernel(place, labels_far, zvec, inner_send, outer_near, labels, label_sem, sems):
    modes, planes, rows, layers = zvec.shape
    half = rows // 2
    side = lax.rem(place[1], 2)
    start = pl.multiple_of((1 - side) * half, half)
    label_copy = pltpu.make_async_copy(labels_far, labels, label_sem)
    copies = [
        pltpu.make_async_copy(
            zvec.at[:, side, pl.ds(start, half), :], outer_near.at[pl.ds(0, modes)], sems.at[0]
        ),
        pltpu.make_async_copy(zvec.at[:, 1 - side], inner_send.at[pl.ds(0, modes)], sems.at[1]),
    ]
    label_copy.start()
    for copy in copies:
        copy.start()
    label_copy.wait()
    outer_near[modes:] = labels[side].astype(F32).astype(BF16).reshape(rows // half, half, layers)
    inner_send[modes] = labels[1 - side].astype(F32).astype(BF16)
    for copy in copies:
        copy.wait()


def release_kernel(after, outer_rest, outer_out):
    pass


def prepare_kernel(place, labels, held, outer_rest, one_pack, two_pack):
    modes, planes, rows, layers = held.shape
    half = rows // 2
    width = planes * rows
    side = lax.rem(place[1], 2)
    odd = lax.rem(place[0], 2) == 1
    one_lane = jnp.where(odd, 0, layers - 1)
    two_lane = jnp.where(odd, layers - 1, 0)
    row = lax.broadcasted_iota(jnp.int32, (16, layers), 0)
    both = ((row == 0) & lane_is((16, layers), one_lane)) | ((row == 1) & lane_is((16, layers), two_lane))
    both = both.astype(BF16)
    flat = labels[...].astype(F32).astype(BF16).reshape(width, layers)
    for out, lane in ((one_pack, one_lane), (two_pack, two_lane)):
        out[modes:] = lax.dot_general(
            pick_row(lane, layers), flat, NT, preferred_element_type=F32
        ).astype(BF16)
    for k in range(0, modes, CHUNK):
        at = slice(k, k + CHUNK)
        ends = lax.dot_general(
            both, held[at].reshape(-1, layers), NT, preferred_element_type=F32
        )
        for out, index in ((one_pack, 0), (two_pack, 1)):
            out[at] = jnp.concatenate(
                [ends[index:index + 1, j * width:(j + 1) * width] for j in range(CHUNK)], axis=0
            ).astype(BF16)
        outer_rest[at] = held[at, side, pl.ds(pl.multiple_of(side * half, half), half), :]


def block_kernel(
    place, levels, labels, resid, zvec, after, partial, weights, here, half_diag, link_y, link_z,
):
    planes, rows, layers = labels.shape
    modes = here.shape[2]
    side = lax.rem(place[1], 2)
    at_edge = (place[1] == 0) | (place[1] == place[2] - 1)
    held = (1 - side, side)

    def turn_rows(start):
        for slot, plane in enumerate(held):
            for k in range(0, modes, CHUNK):
                block = zvec[k:k + CHUNK, plane, pl.ds(start, STEP), :]
                here[slot, pl.ds(start, STEP), k:k + CHUNK, :] = jnp.swapaxes(block, 0, 1)

    turn_rows(0)
    coef = [coefficients(labels[x], levels) for x in held]
    middle = harmonic(coef[0], coef[1])
    weights[0] = middle
    row = lax.broadcasted_iota(jnp.int32, (rows, layers), 0)
    lane = lax.broadcasted_iota(jnp.int32, (rows, layers), 1)
    for x in range(2):
        c = coef[x]
        up_y = harmonic(c, jnp.where(row == rows - 1, c, pltpu.roll(c, rows - 1, 0)))
        up_z = harmonic(c, pltpu.roll(c, layers - 1, 1))
        down_y = jnp.where(row == 0, c, pltpu.roll(up_y, 1, 0))
        weights[1 + x] = up_y
        weights[3 + x] = up_z
        weights[5 + x] = c
        inner_z = jnp.where(lane == layers - 1, 0.0, up_z)
        total = middle + up_y + down_y + inner_z + pltpu.roll(inner_z, 1, 1)
        if x == 1:
            total = total + jnp.where(at_edge, c, 0.0)
        half_diag[x] = 0.5 * total
        link_y[x] = jnp.where(row == rows - 1, 0.0, up_y)
        link_z[x] = inner_z

    def step(j, carry):
        total, rhs, wide = carry
        turn_rows(pl.multiple_of(jnp.minimum((j + 1) * STEP, rows - STEP), STEP))
        for u in range(STEP):
            y = j * STEP + u
            at = pl.ds(y, 1)
            ahead = jnp.minimum(y + 1, rows - 1)
            up = [here[x, ahead].astype(F32) for x in range(2)]
            images = []
            for x in range(2):
                image = (
                    half_diag[x, at, :] * wide[x]
                    - link_y[x, at, :] * up[x]
                    - link_z[x, at, :] * pltpu.roll(wide[x], layers - 1, 1)
                )
                if x == 0:
                    image = image - weights[0, at, :] * wide[1]
                rhs = rhs + resid[held[x], at, :] * wide[x]
                images.append(image.astype(BF16))
            total = total + lax.dot_general(
                jnp.concatenate(images, axis=1),
                jnp.concatenate([here[0, y], here[1, y]], axis=1),
                NT,
                preferred_element_type=F32,
            )
            wide = up
        return total, rhs, wide

    total, rhs, _ = lax.fori_loop(
        0,
        rows // STEP,
        step,
        (
            jnp.zeros((modes, modes), F32),
            jnp.zeros((modes, layers), F32),
            [here[x, 0].astype(F32) for x in range(2)],
        ),
    )
    partial[:modes, :] = total
    partial[modes:, :] = lax.dot_general(
        jnp.ones((8, layers), F32), rhs, NT, precision=PRECISE, preferred_element_type=F32
    )


def turn(got, start, out):
    half, modes, layers = out.shape
    for k in range(0, modes, CHUNK):
        out[:, k:k + CHUNK, :] = jnp.swapaxes(got[k:k + CHUNK, pl.ds(start, half), :], 0, 1)


def face_product(weight_ref, base, own, other):
    half, modes, layers = other.shape

    def step(j, total):
        left, right = [], []
        for u in range(STEP):
            y = j * STEP + u
            weight = weight_ref[pl.ds(base + y, 1), :]
            image = weight * (own[base + y].astype(F32) - other[y].astype(F32))
            left.append(jnp.concatenate([own[base + y], other[y]], axis=0))
            right.append(image.astype(BF16))
        return total + lax.dot_general(
            jnp.concatenate(left, axis=1), jnp.concatenate(right, axis=1), NT,
            preferred_element_type=F32,
        )

    total = lax.fori_loop(0, half // STEP, step, jnp.zeros((2 * modes, modes), F32))
    return total[:modes] - total[modes:]


def inner_kernel(place, levels, partial, weights, here, inner_got, out, face, turned):
    planes, rows, modes, layers = here.shape
    half = rows // 2
    side = lax.rem(place[1], 2)
    base = pl.multiple_of(side * half, half)
    turn(inner_got, base, turned)
    face[...] = harmonic(weights[5], coefficients(inner_got[modes].astype(F32), levels))
    out[:modes, :] = partial[:modes, :] + 0.5 * face_product(face, base, here.at[0], turned)
    out[modes:, :] = partial[modes:, :]


def outer_kernel(
    place, levels, partial, weights, here, outer_got, one_pack, two_pack, one_got, two_got,
    out, face, turned, face_here,
):
    planes, rows, modes, layers = here.shape
    half = rows // 2
    side = lax.rem(place[1], 2)
    at_edge = (place[1] == 0) | (place[1] == place[2] - 1)
    base = pl.multiple_of(side * half, half)
    turn(outer_got, 0, turned)
    coef = coefficients(outer_got[modes:].astype(F32).reshape(rows, layers), levels)
    between = harmonic(weights[6], coef)
    face[...] = jnp.where(at_edge, weights[6], between)
    face_here[...] = jnp.where(at_edge, 0.0, between)
    cross = face_product(face_here, base, here.at[1], turned)
    odd = lax.rem(place[0], 2) == 1

    def coef_row(pack):
        return coefficients(pack[modes:modes + 16].astype(F32)[0:1], levels)

    one, two = one_pack[...].astype(F32), two_pack[...].astype(F32)
    one_other, two_other = one_got[...].astype(F32), two_got[...].astype(F32)
    first, last = jnp.where(odd, one, two), jnp.where(odd, two, one)
    next_first = jnp.where(odd, two_other, one_other)
    prev_last = jnp.where(odd, one_other, two_other)
    weight_low = harmonic(coef_row(first), coef_row(prev_last))
    weight_high = harmonic(coef_row(last), coef_row(next_first))

    def product(left, right):
        return lax.dot_general(
            left.astype(BF16), right.astype(BF16), NT, preferred_element_type=F32
        )

    edge_rows = weight_high * last[:modes]
    ends = product(
        jnp.concatenate([weight_low * first[:modes], edge_rows], axis=1),
        jnp.concatenate([first[:modes], last[:modes]], axis=1),
    )
    square = partial[:modes, :] + 0.5 * (cross + ends)
    out[:modes, :modes] = square + square.T
    out[:modes, modes:] = -product(edge_rows, next_first[:modes])
    out[modes:, :modes] = partial[modes:, :]
    out[modes:, modes:] = jnp.zeros((8, modes), F32)


def terms_kernel(
    place, levels, pair, one_got, two_got, weights, inner_face, outer_face, terms, picked, coef_ref
):
    modes, width = picked.shape[1:]
    rows, layers = inner_face.shape
    side = lax.rem(place[1], 2)
    odd = lax.rem(place[0], 2) == 1
    one_other, two_other = one_got[...].astype(F32), two_got[...].astype(F32)
    next_first = jnp.where(odd, two_other, one_other)
    prev_last = jnp.where(odd, one_other, two_other)
    picked[0] = next_first[:modes]
    picked[1] = prev_last[:modes]
    end_labels = lax.dot_general(
        next_first[modes:].astype(BF16), pick_row(layers - 1, layers), TN, preferred_element_type=F32
    ) + lax.dot_general(
        prev_last[modes:].astype(BF16), pick_row(0, layers), TN, preferred_element_type=F32
    )
    coef_ref[...] = coefficients(end_labels, levels).reshape(width // rows, rows, layers)
    row = lax.broadcasted_iota(jnp.int32, (rows, layers), 0)
    lane = lax.broadcasted_iota(jnp.int32, (rows, layers), 1)
    for x, face in enumerate((inner_face, outer_face)):
        c = weights[5 + x]
        end_weight = harmonic(c, coef_ref[1 - side if x == 0 else side])
        up_y, up_z = weights[1 + x], weights[3 + x]
        down_y = jnp.where(row == 0, c, pltpu.roll(up_y, 1, 0))
        down_z = pltpu.roll(up_z, 1, 1)
        total = face[...] + weights[0] + up_y + down_y
        total = total + jnp.where(lane == layers - 1, end_weight, up_z)
        terms[x, 0] = total + jnp.where(lane == 0, end_weight, down_z)
        terms[x, 1] = jnp.where(row == 0, 0.0, down_y)
        terms[x, 2] = jnp.where(row == rows - 1, 0.0, up_y)
        terms[x, 3] = jnp.where(lane == 0, 0.0, down_z)
        terms[x, 4] = jnp.where(lane == layers - 1, 0.0, up_z)
        terms[x, 5] = end_weight


def pair_kernel(own, across, beside, oblique, out):
    modes = own.shape[1] // 2
    encode(own[...] + across[...], modes, out.at[0])
    encode(beside[...] + oblique[...], modes, out.at[1])


def single_kernel(own, out):
    encode(own[...], own.shape[1] // 2, out)


def encode(total, modes, out):
    row = lax.broadcasted_iota(jnp.int32, (modes, 2 * modes), 0)
    lane = lax.broadcasted_iota(jnp.int32, (modes, 2 * modes), 1)
    values = total[:modes]
    high = values.astype(BF16).astype(F32)
    low = values - high
    out[:modes] = jnp.where((lane <= row) | (lane >= modes), high, low).astype(BF16)
    diagonal = lane == row
    right = total[modes:modes + 1]
    parts = []
    for _ in range(3):
        part = right.astype(BF16).astype(F32)
        parts.append(part)
        right = right - part
    for part in (high, low):
        parts.append(jnp.sum(jnp.where(diagonal, part, 0.0), axis=0, keepdims=True))
    rows = lax.broadcasted_iota(jnp.int32, (16, 2 * modes), 0)
    extra = jnp.zeros((16, 2 * modes), F32)
    for index, part in enumerate(parts):
        extra = jnp.where(rows == index, part, extra)
    out[modes:] = extra.astype(BF16)


def widen_kernel(place, pair, zvec, inner_got, outer_got, own_wide, inner_wide, outer_wide):
    modes, half = outer_wide.shape[:2]
    side = lax.rem(place[1], 2)

    def some(j, carry):
        at = pl.ds(pl.multiple_of(j * MODES, MODES), MODES)
        own_wide[at, 0] = zvec[at, 1 - side].astype(F32)
        own_wide[at, 1] = zvec[at, side].astype(F32)
        inner_wide[at] = inner_got[at].astype(F32)
        outer_wide[at] = outer_got[at].astype(F32)
        return carry

    lax.fori_loop(0, modes // MODES, some, 0)


def finish_kernel(place, *refs):
    count = len(refs) - 15
    blocks, refs = refs[:count], refs[count:]
    zvec, inner_got, outer_got, outer_last, picked, terms, middle, inner_face, outer_face, resid = refs[:10]
    solution, deflated, direction_ref, spread, outer_field = refs[10:]
    subs = direction_ref.shape[0]
    modes, planes, rows, layers = zvec.shape
    half = rows // 2
    me = place[0]
    side = lax.rem(place[1], 2)
    odd = lax.rem(me, 2) == 1
    at_edge = (place[1] == 0) | (place[1] == place[2] - 1)
    held = (1 - side, side)
    square = (modes, modes)
    eye = lax.broadcasted_iota(jnp.int32, square, 0) == lax.broadcasted_iota(jnp.int32, square, 1)

    def column(row):
        return jnp.sum(jnp.where(eye, row, 0.0), axis=1, keepdims=True)

    def each(body, carry):
        for index, block in enumerate(blocks):
            held_here = block.shape[0]
            if held_here <= 8:
                for entry in range(held_here):
                    s = jnp.bitwise_xor(place[3 + index], entry)
                    carry = body(block.at[entry], s, carry)
            else:
                carry = lax.fori_loop(
                    0, held_here, lambda entry, c, block=block: body(block.at[entry], entry, c), carry
                )
        return carry

    def row_is(s, width):
        return lax.broadcasted_iota(jnp.int32, (subs, width), 0) == s

    def load(block, s, carry):
        extra = block[modes:modes + 16, :].astype(F32)
        right = (extra[0:1] + extra[1:2]) + extra[2:3]
        here = row_is(s, 2 * modes)
        return jnp.where(here, right, carry[0]), jnp.where(here, extra[4:5] - extra[3:4], carry[1])

    empty = jnp.zeros((subs, 2 * modes), F32)
    right_side, fix = each(load, (empty, empty))
    fix = fix[:, :modes]

    def turned(rows_of, by):
        by = by % subs
        return jnp.concatenate([rows_of[by:], rows_of[:by]], axis=0)

    def in_parts(value):
        parts = []
        for _ in range(3):
            part = value.astype(BF16)
            parts.append(part.astype(F32))
            value = value - parts[-1]
        return jnp.concatenate(parts, axis=0).astype(BF16)

    def joined(value):
        return (value[:subs] + value[subs:2 * subs]) + value[2 * subs:]

    def coarse_apply(direction):
        pairs = in_parts(jnp.concatenate([direction, turned(direction, 1)], axis=1))
        single = pairs[:, :modes]

        def one(block, s, carry):
            values = block[:modes, :]
            ahead = lax.dot_general(pairs, values, NT, preferred_element_type=F32)
            image = jnp.dot(single, values, preferred_element_type=F32)
            return (
                jnp.where(row_is(s, modes), joined(ahead), carry[0]),
                jnp.where(row_is(s, 2 * modes), joined(image), carry[1]),
            )

        ahead, image = each(one, (jnp.zeros((subs, modes), F32), empty))
        return ahead + image[:, :modes] + fix * direction + turned(image[:, modes:], -1)

    def inner(left, right):
        return jnp.sum(jnp.sum(left * right, axis=0, keepdims=True), axis=1, keepdims=True)

    remain = right_side[:, :modes]
    direction = remain
    result = jnp.zeros_like(remain)
    norm_now = inner(remain, remain)
    for iteration in range(CITERS):
        image = coarse_apply(direction)
        step_size = norm_now / inner(direction, image)
        result = result + step_size * direction
        if iteration + 1 < CITERS:
            remain = remain - step_size * image
            norm_next = inner(remain, remain)
            direction = remain + (norm_next / norm_now) * direction
            norm_now = norm_next
    direction_ref[...] = result
    own = direction_ref[pl.ds(me, 1), :]
    solution[...] = own
    spread[...] = jnp.broadcast_to(column(own), (modes, layers))
    ahead_column = column(direction_ref[pl.ds(lax.rem(me + 1, subs), 1), :])
    behind_column = column(direction_ref[pl.ds(lax.rem(me + subs - 1, subs), 1), :])
    ahead_row = jnp.sum(ahead_column * picked[0], axis=0, keepdims=True)
    behind_row = jnp.sum(behind_column * picked[1], axis=0, keepdims=True)
    width = planes * rows
    both_rows = jnp.where(
        lax.broadcasted_iota(jnp.int32, (8, width), 0) == 0,
        jnp.broadcast_to(ahead_row, (8, width)),
        jnp.broadcast_to(behind_row, (8, width)),
    )
    columns = both_rows.T
    ends = jnp.where(
        lane_is((width, layers), layers - 1),
        columns[:, 0:1],
        jnp.where(lane_is((width, layers), 0), columns[:, 1:2], 0.0),
    ).reshape(planes, rows, layers)

    def add_mode(j, carry):
        fields, near, last = list(carry[0]), carry[1], carry[2]
        for u in range(MODES):
            k = j * MODES + u
            scale = spread[pl.ds(k, 1), :]
            for x, plane in enumerate((zvec[k, 0], zvec[k, 1], inner_got[k])):
                fields[x] = fields[x] + scale * plane
            near = near + scale * outer_got[k]
            last = last + scale * outer_last[k].astype(F32)
        return tuple(fields), near, last

    zero, short = jnp.zeros((rows, layers), F32), jnp.zeros((half, layers), F32)
    field, near, last = lax.fori_loop(0, modes // MODES, add_mode, ((zero,) * 3, short, short))
    outer_field[pl.ds(pl.multiple_of(side * half, half), half), :] = near
    outer_field[pl.ds(pl.multiple_of((1 - side) * half, half), half), :] = last
    outside = (field[2], jnp.where(at_edge, 0.0, outer_field[...]))
    faces = (inner_face[...], outer_face[...])
    for x in range(2):
        f = field[x]
        end_field = jnp.where(side == x, ends[1], ends[0])
        image = (
            terms[x, 0] * f
            - middle[0] * field[1 - x]
            - faces[x] * outside[x]
            - terms[x, 1] * pltpu.roll(f, 1, 0)
            - terms[x, 2] * pltpu.roll(f, rows - 1, 0)
            - terms[x, 3] * pltpu.roll(f, 1, 1)
            - terms[x, 4] * pltpu.roll(f, layers - 1, 1)
            - terms[x, 5] * end_field
        )
        deflated[held[x]] = resid[held[x]] - image


def swapped(value, axis, first):
    count = lax.axis_size(axis)
    pairs = []
    for i in range(count):
        up = (i - first) % 2 == 0
        pairs.append((i, (i + 1) % count if up else (i - 1) % count))
    return lax.ppermute(value, axis, pairs)


def swapped_all(value):
    subs, count = lax.axis_size("sub"), lax.axis_size("pln")
    pairs = []
    for s in range(subs):
        for i in range(count):
            if 0 < i < count - 1:
                to = (s, i + 1 if i % 2 else i - 1)
            else:
                to = (s ^ 1, i)
            pairs.append((s * count + i, to[0] * count + to[1]))
    return lax.ppermute(value, ("sub", "pln"), pairs)


def exchanged(value, axis, mask):
    return lax.ppermute(value, axis, [(i, i ^ mask) for i in range(lax.axis_size(axis))])


def partner(value, sub_mask, pln_mask):
    subs, count = lax.axis_size("sub"), lax.axis_size("pln")
    pairs = [
        (s * count + p, (s ^ sub_mask) * count + (p ^ pln_mask)) for s in range(subs) for p in range(count)
    ]
    return lax.ppermute(value, ("sub", "pln"), pairs)


FAR = (4, 6)


def far_partner(value):
    subs, count = lax.axis_size("sub"), lax.axis_size("pln")
    pairs = [(s * count + p, (s ^ FAR[p % 2]) * count + p) for s in range(subs) for p in range(count)]
    return lax.ppermute(value, ("sub", "pln"), pairs)


def body(labels, levels, zvec, resid):
    modes, planes, rows, layers = zvec.shape
    half = rows // 2
    subs, parts = lax.axis_size("sub"), lax.axis_size("pln")
    shape = jax.ShapeDtypeStruct
    at_sub, at_pln = lax.axis_index("sub"), lax.axis_index("pln")
    core = at_pln % 2
    masks = (0, FAR[0] + core * (FAR[1] - FAR[0]), 2, FAR[1] + core * (FAR[0] - FAR[1]))
    orders = [at_sub ^ mask for mask in masks] if parts == 4 and subs == 8 else [0] * 4
    place = jnp.stack([jnp.int32(v) for v in (at_sub, at_pln, parts, *orders)])
    pack = shape((modes + 16, planes * rows), BF16)
    inner_send, outer_near = call(
        stage_kernel,
        [shape((modes + 1, rows, layers), BF16), shape((modes + rows // half, half, layers), BF16)],
        [SMEM, HBM, HBM],
        [pltpu.VMEM(labels.shape, jnp.int32), pltpu.SemaphoreType.DMA, pltpu.SemaphoreType.DMA((2,))],
        moved=2 << 20,
    )(place, *(pltpu.with_memory_space_constraint(v, pltpu.HBM) for v in (labels, zvec)))
    outer_got = swapped_all(outer_near)
    inner_got = swapped(inner_send, "pln", 0)
    rest = shape((modes, half, layers), BF16)
    outer_rest, one_pack, two_pack = call(
        prepare_kernel,
        [rest, pack, pack],
        [SMEM, VMEM, VMEM],
        flops=10_000_000,
        moved=6 << 20,
    )(place, labels, zvec)
    one_got = swapped(one_pack, "sub", 0)
    two_got = swapped(two_pack, "sub", 1)
    field = (planes, rows, layers)
    plane = (rows, layers)
    partial, weights, here = call(
        block_kernel,
        [
            shape((modes + 8, modes), F32),
            shape((7,) + plane, F32),
            shape((planes, rows, modes, layers), BF16),
        ],
        [SMEM, SMEM] + [VMEM] * 3 + [ANY],
        [pltpu.VMEM(field, F32)] * 3,
        flops=400_000_000,
        moved=3 << 20,
    )(place, levels, labels, resid, zvec, one_pack)
    turned = pltpu.VMEM((half, modes, layers), BF16)
    partial, inner_face = call(
        inner_kernel,
        [shape((modes + 8, modes), F32), shape(plane, F32)],
        [SMEM, SMEM] + [VMEM] * 4,
        [turned],
        flops=100_000_000,
        moved=1 << 20,
    )(place, levels, partial, weights, here, inner_got)
    block, outer_face = call(
        outer_kernel,
        [shape((modes + 8, 2 * modes), F32), shape(plane, F32)],
        [SMEM, SMEM] + [VMEM] * 8,
        [turned, pltpu.VMEM(plane, F32)],
        flops=100_000_000,
        moved=1 << 20,
    )(place, levels, partial, weights, here, outer_got, one_pack, two_pack, one_got, two_got)
    packed = (modes + 16, 2 * modes)
    if parts == 4 and subs == 8:
        block = block + exchanged(block, "pln", 1)
        others = [partner(block, *masks) for masks in ((0, 3), (1, 1), (1, 3))]
        [pair] = call(
            pair_kernel, [shape((2,) + packed, BF16)], [VMEM] * 4, flops=1 << 33
        )(block, *others)
        far = far_partner(pair)
        blocks = [pair, far, partner(pair, 2, 1), exchanged(far, "pln", 1)]
    else:
        [single] = call(single_kernel, [shape(packed, BF16)], [VMEM])(lax.psum(block, "pln"))
        blocks = [lax.all_gather(single, "sub")]
    [outer_rest] = call(release_kernel, [rest], [ANY] * 2, aliases={1: 0})(block, outer_rest)
    outer_last = swapped_all(outer_rest)
    terms, picked = call(
        terms_kernel,
        [shape((planes, 6) + plane, F32), shape((2, modes, planes * rows), F32)],
        [SMEM, SMEM, ANY] + [VMEM] * 5,
        [pltpu.VMEM(field, F32)],

        flops=1 << 31,
        moved=1 << 20,
    )(place, levels, blocks[0], one_got, two_got, weights, inner_face, outer_face)
    wide = call(
        widen_kernel,
        [
            shape((modes,) + field, F32),
            shape((modes,) + plane, F32),
            shape((modes, half, layers), F32),
        ],
        [SMEM, ANY] + [VMEM] * 3,
        flops=1 << 30,
        moved=1 << 20,
    )(place, blocks[0], zvec, inner_got, outer_got)
    return tuple(
        call(
            finish_kernel,
            [shape((1, modes), F32), shape(field, F32)],
            [SMEM] + [VMEM] * (10 + len(blocks)),
            [
                pltpu.VMEM((subs, modes), F32),
                pltpu.VMEM((modes, layers), F32),
                pltpu.VMEM(plane, F32),
            ],
            flops=10_000_000,
            moved=5 << 20,
        )(
            place, *blocks, *wide, outer_last, picked, terms, weights, inner_face,
            outer_face, resid,
        )
    )


def solution(mesh):
    in_specs = (P("pln", None, "sub"), P(), P(None, "pln", None, "sub"), P("pln", None, "sub"))
    out_specs = (P("sub", None), P("pln", None, "sub"))
    return jax.shard_map(body, mesh=mesh, in_specs=in_specs, out_specs=out_specs, check_vma=False)
```

```python
import jax
import jax.numpy as jnp
from jax import lax
from jax.experimental import pallas as pl
from jax.experimental.pallas import tpu as pltpu
from jax.sharding import PartitionSpec as P

CITERS = 2
STEP = 16
MODES = 8
CHUNK = 16
F32 = jnp.float32
BF16 = jnp.bfloat16
PRECISE = lax.Precision.HIGHEST
NT = (((1,), (1,)), ((), ()))
TN = (((0,), (0,)), ((), ()))
VMEM = pl.BlockSpec(memory_space=pltpu.VMEM)
SMEM = pl.BlockSpec(memory_space=pltpu.SMEM)
HBM = pl.BlockSpec(memory_space=pltpu.HBM)
ANY = pl.BlockSpec(memory_space=pl.ANY)


def call(kernel, outs, specs, scratch=(), flops=0, moved=0, limit=32, aliases=None):
    return pl.pallas_call(
        kernel,
        out_shape=outs,
        in_specs=specs,
        out_specs=[ANY if at in (aliases or {}).values() else VMEM for at in range(len(outs))],
        input_output_aliases=aliases or {},
        scratch_shapes=list(scratch),
        cost_estimate=pl.CostEstimate(flops=flops, bytes_accessed=moved, transcendentals=0),
        compiler_params=pltpu.CompilerParams(vmem_limit_bytes=limit << 20),
    )


def harmonic(left_value, right_value):
    return 2.0 * left_value * right_value / (left_value + right_value)


def coefficients(labels, levels_ref):
    weighted = jnp.zeros(labels.shape, F32)
    for level in range(levels_ref.shape[0]):
        weighted = weighted + jnp.where(labels == level, levels_ref[level], 0.0)
    return weighted


def lane_is(shape, lane):
    return lax.broadcasted_iota(jnp.int32, shape, len(shape) - 1) == lane


def pick_row(lane, width):
    row = lax.broadcasted_iota(jnp.int32, (16, width), 0)
    return ((row == 0) & lane_is((16, width), lane)).astype(BF16)


def stage_kernel(place, labels_far, zvec, inner_send, outer_near, labels, label_sem, sems):
    modes, planes, rows, layers = zvec.shape
    half = rows // 2
    side = lax.rem(place[1], 2)
    start = pl.multiple_of((1 - side) * half, half)
    label_copy = pltpu.make_async_copy(labels_far, labels, label_sem)
    copies = [
        pltpu.make_async_copy(
            zvec.at[:, side, pl.ds(start, half), :], outer_near.at[pl.ds(0, modes)], sems.at[0]
        ),
        pltpu.make_async_copy(zvec.at[:, 1 - side], inner_send.at[pl.ds(0, modes)], sems.at[1]),
    ]
    label_copy.start()
    for copy in copies:
        copy.start()
    label_copy.wait()
    outer_near[modes:] = labels[side].astype(F32).astype(BF16).reshape(rows // half, half, layers)
    inner_send[modes] = labels[1 - side].astype(F32).astype(BF16)
    for copy in copies:
        copy.wait()


def release_kernel(after, outer_rest, outer_out):
    pass


def prepare_kernel(place, labels, held, outer_rest, one_pack, two_pack):
    modes, planes, rows, layers = held.shape
    half = rows // 2
    width = planes * rows
    side = lax.rem(place[1], 2)
    odd = lax.rem(place[0], 2) == 1
    one_lane = jnp.where(odd, 0, layers - 1)
    two_lane = jnp.where(odd, layers - 1, 0)
    row = lax.broadcasted_iota(jnp.int32, (16, layers), 0)
    both = ((row == 0) & lane_is((16, layers), one_lane)) | ((row == 1) & lane_is((16, layers), two_lane))
    both = both.astype(BF16)
    flat = labels[...].astype(F32).astype(BF16).reshape(width, layers)
    for out, lane in ((one_pack, one_lane), (two_pack, two_lane)):
        out[modes:] = lax.dot_general(
            pick_row(lane, layers), flat, NT, preferred_element_type=F32
        ).astype(BF16)
    for k in range(0, modes, CHUNK):
        at = slice(k, k + CHUNK)
        ends = lax.dot_general(
            both, held[at].reshape(-1, layers), NT, preferred_element_type=F32
        )
        for out, index in ((one_pack, 0), (two_pack, 1)):
            out[at] = jnp.concatenate(
                [ends[index:index + 1, j * width:(j + 1) * width] for j in range(CHUNK)], axis=0
            ).astype(BF16)
        outer_rest[at] = held[at, side, pl.ds(pl.multiple_of(side * half, half), half), :]


def block_kernel(
    place, levels, labels, resid, zvec, after, partial, weights, here, half_diag, link_y, link_z,
):
    planes, rows, layers = labels.shape
    modes = here.shape[2]
    side = lax.rem(place[1], 2)
    at_edge = (place[1] == 0) | (place[1] == place[2] - 1)
    held = (1 - side, side)

    def turn_rows(start):
        for slot, plane in enumerate(held):
            for k in range(0, modes, CHUNK):
                block = zvec[k:k + CHUNK, plane, pl.ds(start, STEP), :]
                here[slot, pl.ds(start, STEP), k:k + CHUNK, :] = jnp.swapaxes(block, 0, 1)

    turn_rows(0)
    coef = [coefficients(labels[x], levels) for x in held]
    middle = harmonic(coef[0], coef[1])
    weights[0] = middle
    row = lax.broadcasted_iota(jnp.int32, (rows, layers), 0)
    lane = lax.broadcasted_iota(jnp.int32, (rows, layers), 1)
    for x in range(2):
        c = coef[x]
        up_y = harmonic(c, jnp.where(row == rows - 1, c, pltpu.roll(c, rows - 1, 0)))
        up_z = harmonic(c, pltpu.roll(c, layers - 1, 1))
        down_y = jnp.where(row == 0, c, pltpu.roll(up_y, 1, 0))
        weights[1 + x] = up_y
        weights[3 + x] = up_z
        weights[5 + x] = c
        inner_z = jnp.where(lane == layers - 1, 0.0, up_z)
        total = middle + up_y + down_y + inner_z + pltpu.roll(inner_z, 1, 1)
        if x == 1:
            total = total + jnp.where(at_edge, c, 0.0)
        half_diag[x] = 0.5 * total
        link_y[x] = jnp.where(row == rows - 1, 0.0, up_y)
        link_z[x] = inner_z

    def step(j, carry):
        total, rhs, wide = carry
        turn_rows(pl.multiple_of(jnp.minimum((j + 1) * STEP, rows - STEP), STEP))
        for u in range(STEP):
            y = j * STEP + u
            at = pl.ds(y, 1)
            ahead = jnp.minimum(y + 1, rows - 1)
            up = [here[x, ahead].astype(F32) for x in range(2)]
            images = []
            for x in range(2):
                image = (
                    half_diag[x, at, :] * wide[x]
                    - link_y[x, at, :] * up[x]
                    - link_z[x, at, :] * pltpu.roll(wide[x], layers - 1, 1)
                )
                if x == 0:
                    image = image - weights[0, at, :] * wide[1]
                rhs = rhs + resid[held[x], at, :] * wide[x]
                images.append(image.astype(BF16))
            total = total + lax.dot_general(
                jnp.concatenate(images, axis=1),
                jnp.concatenate([here[0, y], here[1, y]], axis=1),
                NT,
                preferred_element_type=F32,
            )
            wide = up
        return total, rhs, wide

    total, rhs, _ = lax.fori_loop(
        0,
        rows // STEP,
        step,
        (
            jnp.zeros((modes, modes), F32),
            jnp.zeros((modes, layers), F32),
            [here[x, 0].astype(F32) for x in range(2)],
        ),
    )
    partial[:modes, :] = total
    partial[modes:, :] = lax.dot_general(
        jnp.ones((8, layers), F32), rhs, NT, precision=PRECISE, preferred_element_type=F32
    )


def turn(got, start, out):
    half, modes, layers = out.shape
    for k in range(0, modes, CHUNK):
        out[:, k:k + CHUNK, :] = jnp.swapaxes(got[k:k + CHUNK, pl.ds(start, half), :], 0, 1)


def face_product(weight_ref, base, own, other):
    half, modes, layers = other.shape

    def step(j, total):
        left, right = [], []
        for u in range(STEP):
            y = j * STEP + u
            weight = weight_ref[pl.ds(base + y, 1), :]
            image = weight * (own[base + y].astype(F32) - other[y].astype(F32))
            left.append(jnp.concatenate([own[base + y], other[y]], axis=0))
            right.append(image.astype(BF16))
        return total + lax.dot_general(
            jnp.concatenate(left, axis=1), jnp.concatenate(right, axis=1), NT,
            preferred_element_type=F32,
        )

    total = lax.fori_loop(0, half // STEP, step, jnp.zeros((2 * modes, modes), F32))
    return total[:modes] - total[modes:]


def inner_kernel(place, levels, partial, weights, here, inner_got, out, face, turned):
    planes, rows, modes, layers = here.shape
    half = rows // 2
    side = lax.rem(place[1], 2)
    base = pl.multiple_of(side * half, half)
    turn(inner_got, base, turned)
    face[...] = harmonic(weights[5], coefficients(inner_got[modes].astype(F32), levels))
    out[:modes, :] = partial[:modes, :] + 0.5 * face_product(face, base, here.at[0], turned)
    out[modes:, :] = partial[modes:, :]


def outer_kernel(
    place, levels, partial, weights, here, outer_got, one_pack, two_pack, one_got, two_got,
    out, face, turned, face_here,
):
    planes, rows, modes, layers = here.shape
    half = rows // 2
    side = lax.rem(place[1], 2)
    at_edge = (place[1] == 0) | (place[1] == place[2] - 1)
    base = pl.multiple_of(side * half, half)
    turn(outer_got, 0, turned)
    coef = coefficients(outer_got[modes:].astype(F32).reshape(rows, layers), levels)
    between = harmonic(weights[6], coef)
    face[...] = jnp.where(at_edge, weights[6], between)
    face_here[...] = jnp.where(at_edge, 0.0, between)
    cross = face_product(face_here, base, here.at[1], turned)
    odd = lax.rem(place[0], 2) == 1

    def coef_row(pack):
        return coefficients(pack[modes:modes + 16].astype(F32)[0:1], levels)

    one, two = one_pack[...].astype(F32), two_pack[...].astype(F32)
    one_other, two_other = one_got[...].astype(F32), two_got[...].astype(F32)
    first, last = jnp.where(odd, one, two), jnp.where(odd, two, one)
    next_first = jnp.where(odd, two_other, one_other)
    prev_last = jnp.where(odd, one_other, two_other)
    weight_low = harmonic(coef_row(first), coef_row(prev_last))
    weight_high = harmonic(coef_row(last), coef_row(next_first))

    def product(left, right):
        return lax.dot_general(
            left.astype(BF16), right.astype(BF16), NT, preferred_element_type=F32
        )

    edge_rows = weight_high * last[:modes]
    ends = product(
        jnp.concatenate([weight_low * first[:modes], edge_rows], axis=1),
        jnp.concatenate([first[:modes], last[:modes]], axis=1),
    )
    square = partial[:modes, :] + 0.5 * (cross + ends)
    out[:modes, :modes] = square + square.T
    out[:modes, modes:] = -product(edge_rows, next_first[:modes])
    out[modes:, :modes] = partial[modes:, :]
    out[modes:, modes:] = jnp.zeros((8, modes), F32)


def terms_kernel(
    place, levels, pair, one_got, two_got, weights, inner_face, outer_face, terms, picked, coef_ref
):
    modes, width = picked.shape[1:]
    rows, layers = inner_face.shape
    side = lax.rem(place[1], 2)
    odd = lax.rem(place[0], 2) == 1
    one_other, two_other = one_got[...].astype(F32), two_got[...].astype(F32)
    next_first = jnp.where(odd, two_other, one_other)
    prev_last = jnp.where(odd, one_other, two_other)
    picked[0] = next_first[:modes]
    picked[1] = prev_last[:modes]
    end_labels = lax.dot_general(
        next_first[modes:].astype(BF16), pick_row(layers - 1, layers), TN, preferred_element_type=F32
    ) + lax.dot_general(
        prev_last[modes:].astype(BF16), pick_row(0, layers), TN, preferred_element_type=F32
    )
    coef_ref[...] = coefficients(end_labels, levels).reshape(width // rows, rows, layers)
    row = lax.broadcasted_iota(jnp.int32, (rows, layers), 0)
    lane = lax.broadcasted_iota(jnp.int32, (rows, layers), 1)
    for x, face in enumerate((inner_face, outer_face)):
        c = weights[5 + x]
        end_weight = harmonic(c, coef_ref[1 - side if x == 0 else side])
        up_y, up_z = weights[1 + x], weights[3 + x]
        down_y = jnp.where(row == 0, c, pltpu.roll(up_y, 1, 0))
        down_z = pltpu.roll(up_z, 1, 1)
        total = face[...] + weights[0] + up_y + down_y
        total = total + jnp.where(lane == layers - 1, end_weight, up_z)
        terms[x, 0] = total + jnp.where(lane == 0, end_weight, down_z)
        terms[x, 1] = jnp.where(row == 0, 0.0, down_y)
        terms[x, 2] = jnp.where(row == rows - 1, 0.0, up_y)
        terms[x, 3] = jnp.where(lane == 0, 0.0, down_z)
        terms[x, 4] = jnp.where(lane == layers - 1, 0.0, up_z)
        terms[x, 5] = end_weight


def role_kernel(place, own, across, beside, out):
    modes = own.shape[1] // 2
    encode(jnp.where(place[3] == 0, own[...], beside[...]) + across[...], modes, out)


def single_kernel(own, out):
    encode(own[...], own.shape[1] // 2, out)


def encode(total, modes, out):
    row = lax.broadcasted_iota(jnp.int32, (modes, 2 * modes), 0)
    lane = lax.broadcasted_iota(jnp.int32, (modes, 2 * modes), 1)
    values = total[:modes]
    high = values.astype(BF16).astype(F32)
    low = values - high
    out[:modes] = jnp.where((lane <= row) | (lane >= modes), high, low).astype(BF16)
    diagonal = lane == row
    right = total[modes:modes + 1]
    parts = []
    for _ in range(3):
        part = right.astype(BF16).astype(F32)
        parts.append(part)
        right = right - part
    for part in (high, low):
        parts.append(jnp.sum(jnp.where(diagonal, part, 0.0), axis=0, keepdims=True))
    rows = lax.broadcasted_iota(jnp.int32, (16, 2 * modes), 0)
    extra = jnp.zeros((16, 2 * modes), F32)
    for index, part in enumerate(parts):
        extra = jnp.where(rows == index, part, extra)
    out[modes:] = extra.astype(BF16)


def widen_kernel(place, pair, zvec, inner_got, outer_got, own_wide, inner_wide, outer_wide):
    modes, half = outer_wide.shape[:2]
    side = lax.rem(place[1], 2)

    def some(j, carry):
        at = pl.ds(pl.multiple_of(j * MODES, MODES), MODES)
        own_wide[at, 0] = zvec[at, 1 - side].astype(F32)
        own_wide[at, 1] = zvec[at, side].astype(F32)
        inner_wide[at] = inner_got[at].astype(F32)
        outer_wide[at] = outer_got[at].astype(F32)
        return carry

    lax.fori_loop(0, modes // MODES, some, 0)


def finish_kernel(place, *refs):
    count = len(refs) - 15
    blocks, refs = refs[:count], refs[count:]
    zvec, inner_got, outer_got, outer_last, picked, terms, middle, inner_face, outer_face, resid = refs[:10]
    solution, deflated, direction_ref, spread, outer_field = refs[10:]
    subs = direction_ref.shape[0]
    modes, planes, rows, layers = zvec.shape
    half = rows // 2
    me = place[0]
    side = lax.rem(place[1], 2)
    odd = lax.rem(me, 2) == 1
    at_edge = (place[1] == 0) | (place[1] == place[2] - 1)
    held = (1 - side, side)
    square = (modes, modes)
    eye = lax.broadcasted_iota(jnp.int32, square, 0) == lax.broadcasted_iota(jnp.int32, square, 1)

    def column(row):
        return jnp.sum(jnp.where(eye, row, 0.0), axis=1, keepdims=True)

    def each(body, carry):
        for index, block in enumerate(blocks):
            held_here = block.shape[0]
            if held_here <= 8:
                for entry in range(held_here):
                    s = jnp.bitwise_xor(place[4 + index], entry * len(blocks))
                    carry = body(block.at[entry], s, carry)
            else:
                carry = lax.fori_loop(
                    0, held_here, lambda entry, c, block=block: body(block.at[entry], entry, c), carry
                )
        return carry

    def row_is(s, width):
        return lax.broadcasted_iota(jnp.int32, (subs, width), 0) == s

    def load(block, s, carry):
        extra = block[modes:modes + 16, :].astype(F32)
        right = (extra[0:1] + extra[1:2]) + extra[2:3]
        here = row_is(s, 2 * modes)
        return jnp.where(here, right, carry[0]), jnp.where(here, extra[4:5] - extra[3:4], carry[1])

    empty = jnp.zeros((subs, 2 * modes), F32)
    right_side, fix = each(load, (empty, empty))
    fix = fix[:, :modes]

    def turned(rows_of, by):
        by = by % subs
        return jnp.concatenate([rows_of[by:], rows_of[:by]], axis=0)

    def in_parts(value):
        parts = []
        for _ in range(3):
            part = value.astype(BF16)
            parts.append(part.astype(F32))
            value = value - parts[-1]
        return jnp.concatenate(parts, axis=0).astype(BF16)

    def joined(value):
        return (value[:subs] + value[subs:2 * subs]) + value[2 * subs:]

    def coarse_apply(direction):
        pairs = in_parts(jnp.concatenate([direction, turned(direction, 1)], axis=1))
        single = pairs[:, :modes]

        def one(block, s, carry):
            values = block[:modes, :]
            ahead = lax.dot_general(pairs, values, NT, preferred_element_type=F32)
            image = jnp.dot(single, values, preferred_element_type=F32)
            return (
                jnp.where(row_is(s, modes), joined(ahead), carry[0]),
                jnp.where(row_is(s, 2 * modes), joined(image), carry[1]),
            )

        ahead, image = each(one, (jnp.zeros((subs, modes), F32), empty))
        return ahead + image[:, :modes] + fix * direction + turned(image[:, modes:], -1)

    def inner(left, right):
        return jnp.sum(jnp.sum(left * right, axis=0, keepdims=True), axis=1, keepdims=True)

    remain = right_side[:, :modes]
    direction = remain
    result = jnp.zeros_like(remain)
    norm_now = inner(remain, remain)
    for iteration in range(CITERS):
        image = coarse_apply(direction)
        step_size = norm_now / inner(direction, image)
        result = result + step_size * direction
        if iteration + 1 < CITERS:
            remain = remain - step_size * image
            norm_next = inner(remain, remain)
            direction = remain + (norm_next / norm_now) * direction
            norm_now = norm_next
    direction_ref[...] = result
    own = direction_ref[pl.ds(me, 1), :]
    solution[...] = own
    spread[...] = jnp.broadcast_to(column(own), (modes, layers))
    ahead_column = column(direction_ref[pl.ds(lax.rem(me + 1, subs), 1), :])
    behind_column = column(direction_ref[pl.ds(lax.rem(me + subs - 1, subs), 1), :])
    ahead_row = jnp.sum(ahead_column * picked[0], axis=0, keepdims=True)
    behind_row = jnp.sum(behind_column * picked[1], axis=0, keepdims=True)
    width = planes * rows
    both_rows = jnp.where(
        lax.broadcasted_iota(jnp.int32, (8, width), 0) == 0,
        jnp.broadcast_to(ahead_row, (8, width)),
        jnp.broadcast_to(behind_row, (8, width)),
    )
    columns = both_rows.T
    ends = jnp.where(
        lane_is((width, layers), layers - 1),
        columns[:, 0:1],
        jnp.where(lane_is((width, layers), 0), columns[:, 1:2], 0.0),
    ).reshape(planes, rows, layers)

    def add_mode(j, carry):
        fields, near, last = list(carry[0]), carry[1], carry[2]
        for u in range(MODES):
            k = j * MODES + u
            scale = spread[pl.ds(k, 1), :]
            for x, plane in enumerate((zvec[k, 0], zvec[k, 1], inner_got[k])):
                fields[x] = fields[x] + scale * plane
            near = near + scale * outer_got[k]
            last = last + scale * outer_last[k].astype(F32)
        return tuple(fields), near, last

    zero, short = jnp.zeros((rows, layers), F32), jnp.zeros((half, layers), F32)
    field, near, last = lax.fori_loop(0, modes // MODES, add_mode, ((zero,) * 3, short, short))
    outer_field[pl.ds(pl.multiple_of(side * half, half), half), :] = near
    outer_field[pl.ds(pl.multiple_of((1 - side) * half, half), half), :] = last
    outside = (field[2], jnp.where(at_edge, 0.0, outer_field[...]))
    faces = (inner_face[...], outer_face[...])
    for x in range(2):
        f = field[x]
        end_field = jnp.where(side == x, ends[1], ends[0])
        image = (
            terms[x, 0] * f
            - middle[0] * field[1 - x]
            - faces[x] * outside[x]
            - terms[x, 1] * pltpu.roll(f, 1, 0)
            - terms[x, 2] * pltpu.roll(f, rows - 1, 0)
            - terms[x, 3] * pltpu.roll(f, 1, 1)
            - terms[x, 4] * pltpu.roll(f, layers - 1, 1)
            - terms[x, 5] * end_field
        )
        deflated[held[x]] = resid[held[x]] - image


def swapped(value, axis, first):
    count = lax.axis_size(axis)
    pairs = []
    for i in range(count):
        up = (i - first) % 2 == 0
        pairs.append((i, (i + 1) % count if up else (i - 1) % count))
    return lax.ppermute(value, axis, pairs)


def swapped_all(value):
    subs, count = lax.axis_size("sub"), lax.axis_size("pln")
    pairs = []
    for s in range(subs):
        for i in range(count):
            if 0 < i < count - 1:
                to = (s, i + 1 if i % 2 else i - 1)
            else:
                to = (s ^ 1, i)
            pairs.append((s * count + i, to[0] * count + to[1]))
    return lax.ppermute(value, ("sub", "pln"), pairs)


def exchanged(value, axis, mask):
    return lax.ppermute(value, axis, [(i, i ^ mask) for i in range(lax.axis_size(axis))])


def partner(value, sub_mask, pln_mask):
    subs, count = lax.axis_size("sub"), lax.axis_size("pln")
    pairs = [
        (s * count + p, (s ^ sub_mask) * count + (p ^ pln_mask)) for s in range(subs) for p in range(count)
    ]
    return lax.ppermute(value, ("sub", "pln"), pairs)


def role_of(s, p):
    return (p ^ (p >> 1) ^ (s >> 2)) & 1


def across(value):
    subs, count = lax.axis_size("sub"), lax.axis_size("pln")
    pairs = [
        (s * count + p, (s ^ role_of(s, p)) * count + (p ^ 3)) for s in range(subs) for p in range(count)
    ]
    return lax.ppermute(value, ("sub", "pln"), pairs)


def body(labels, levels, zvec, resid):
    modes, planes, rows, layers = zvec.shape
    half = rows // 2
    subs, parts = lax.axis_size("sub"), lax.axis_size("pln")
    shape = jax.ShapeDtypeStruct
    at_sub, at_pln = lax.axis_index("sub"), lax.axis_index("pln")
    split = parts == 4 and subs == 8
    role = role_of(at_sub, at_pln)
    orders = [at_sub ^ role, at_sub ^ role ^ 1] if split else [0, 0]
    place = jnp.stack([jnp.int32(v) for v in (at_sub, at_pln, parts, role, *orders)])
    pack = shape((modes + 16, planes * rows), BF16)
    inner_send, outer_near = call(
        stage_kernel,
        [shape((modes + 1, rows, layers), BF16), shape((modes + rows // half, half, layers), BF16)],
        [SMEM, HBM, HBM],
        [pltpu.VMEM(labels.shape, jnp.int32), pltpu.SemaphoreType.DMA, pltpu.SemaphoreType.DMA((2,))],
        moved=2 << 20,
    )(place, *(pltpu.with_memory_space_constraint(v, pltpu.HBM) for v in (labels, zvec)))
    outer_got = swapped_all(outer_near)
    inner_got = swapped(inner_send, "pln", 0)
    rest = shape((modes, half, layers), BF16)
    outer_rest, one_pack, two_pack = call(
        prepare_kernel,
        [rest, pack, pack],
        [SMEM, VMEM, VMEM],
        flops=10_000_000,
        moved=6 << 20,
    )(place, labels, zvec)
    one_got = swapped(one_pack, "sub", 0)
    two_got = swapped(two_pack, "sub", 1)
    field = (planes, rows, layers)
    plane = (rows, layers)
    partial, weights, here = call(
        block_kernel,
        [
            shape((modes + 8, modes), F32),
            shape((7,) + plane, F32),
            shape((planes, rows, modes, layers), BF16),
        ],
        [SMEM, SMEM] + [VMEM] * 3 + [ANY],
        [pltpu.VMEM(field, F32)] * 3,
        flops=400_000_000,
        moved=3 << 20,
    )(place, levels, labels, resid, zvec, one_pack)
    turned = pltpu.VMEM((half, modes, layers), BF16)
    partial, inner_face = call(
        inner_kernel,
        [shape((modes + 8, modes), F32), shape(plane, F32)],
        [SMEM, SMEM] + [VMEM] * 4,
        [turned],
        flops=100_000_000,
        moved=1 << 20,
    )(place, levels, partial, weights, here, inner_got)
    block, outer_face = call(
        outer_kernel,
        [shape((modes + 8, 2 * modes), F32), shape(plane, F32)],
        [SMEM, SMEM] + [VMEM] * 8,
        [turned, pltpu.VMEM(plane, F32)],
        flops=100_000_000,
        moved=1 << 20,
    )(place, levels, partial, weights, here, outer_got, one_pack, two_pack, one_got, two_got)
    packed = (modes + 16, 2 * modes)
    if split:
        block = block + exchanged(block, "pln", 1)
        [packed_here] = call(
            role_kernel, [shape(packed, BF16)], [SMEM] + [VMEM] * 3, flops=1 << 33
        )(place, block, across(block), partner(block, 1, 1))
        mine = jnp.stack([packed_here] + [partner(packed_here, *masks) for masks in ((2, 0), (4, 1), (6, 1))])
        blocks = [mine, exchanged(mine, "pln", 1)]
    else:
        [packed_here] = call(single_kernel, [shape(packed, BF16)], [VMEM])(lax.psum(block, "pln"))
        blocks = [lax.all_gather(packed_here, "sub")]
    [outer_rest] = call(release_kernel, [rest], [ANY] * 2, aliases={1: 0})(block, outer_rest)
    outer_last = swapped_all(outer_rest)
    terms, picked = call(
        terms_kernel,
        [shape((planes, 6) + plane, F32), shape((2, modes, planes * rows), F32)],
        [SMEM, SMEM, ANY] + [VMEM] * 5,
        [pltpu.VMEM(field, F32)],

        flops=1 << 31,
        moved=1 << 20,
    )(place, levels, packed_here, one_got, two_got, weights, inner_face, outer_face)
    wide = call(
        widen_kernel,
        [
            shape((modes,) + field, F32),
            shape((modes,) + plane, F32),
            shape((modes, half, layers), F32),
        ],
        [SMEM, ANY] + [VMEM] * 3,
        flops=1 << 30,
        moved=1 << 20,
    )(place, packed_here, zvec, inner_got, outer_got)
    return tuple(
        call(
            finish_kernel,
            [shape((1, modes), F32), shape(field, F32)],
            [SMEM] + [VMEM] * (10 + len(blocks)),
            [
                pltpu.VMEM((subs, modes), F32),
                pltpu.VMEM((modes, layers), F32),
                pltpu.VMEM(plane, F32),
            ],
            flops=10_000_000,
            moved=5 << 20,
        )(
            place, *blocks, *wide, outer_last, picked, terms, weights, inner_face,
            outer_face, resid,
        )
    )


def solution(mesh):
    in_specs = (P("pln", None, "sub"), P(), P(None, "pln", None, "sub"), P("pln", None, "sub"))
    out_specs = (P("sub", None), P("pln", None, "sub"))
    return jax.shard_map(body, mesh=mesh, in_specs=in_specs, out_specs=out_specs, check_vma=False)
```

```python
import jax
import jax.numpy as jnp
from jax import lax
from jax.experimental import pallas as pl
from jax.experimental.pallas import tpu as pltpu
from jax.sharding import PartitionSpec as P

CITERS = 2
STEP = 16
MODES = 8
CHUNK = 16
F32 = jnp.float32
BF16 = jnp.bfloat16
PRECISE = lax.Precision.HIGHEST
NT = (((1,), (1,)), ((), ()))
TN = (((0,), (0,)), ((), ()))
VMEM = pl.BlockSpec(memory_space=pltpu.VMEM)
HBM = pl.BlockSpec(memory_space=pltpu.HBM)
ANY = pl.BlockSpec(memory_space=pl.ANY)


def call(kernel, outs, specs, scratch=(), flops=0, moved=0, limit=32, aliases=None):
    return pl.pallas_call(
        kernel,
        out_shape=outs,
        in_specs=specs,
        out_specs=[ANY if at in (aliases or {}).values() else VMEM for at in range(len(outs))],
        input_output_aliases=aliases or {},
        scratch_shapes=list(scratch),
        cost_estimate=pl.CostEstimate(flops=flops, bytes_accessed=moved, transcendentals=0),
        compiler_params=pltpu.CompilerParams(vmem_limit_bytes=limit << 20),
    )


def here_on(axis):
    return lax.axis_index(axis).astype(jnp.int32)


def ends_the_line():
    p = here_on("pln")
    return (p == 0) | (p == lax.axis_size("pln") - 1)


def harmonic(left_value, right_value):
    return 2.0 * left_value * right_value / (left_value + right_value)


def coefficients(labels, levels_ref):
    weighted = jnp.zeros(labels.shape, F32)
    for level in range(levels_ref.shape[1]):
        weighted = weighted + jnp.where(labels == level, levels_ref[:, level:level + 1], 0.0)
    return weighted


def lane_is(shape, lane):
    return lax.broadcasted_iota(jnp.int32, shape, len(shape) - 1) == lane


def pick_row(lane, width):
    row = lax.broadcasted_iota(jnp.int32, (16, width), 0)
    return ((row == 0) & lane_is((16, width), lane)).astype(BF16)


def stage_kernel(labels_far, zvec, inner_send, outer_near, labels, label_sem, sems):
    modes, planes, rows, layers = zvec.shape
    half = rows // 2
    side = lax.rem(here_on("pln"), 2)
    start = pl.multiple_of((1 - side) * half, half)
    label_copy = pltpu.make_async_copy(labels_far, labels, label_sem)
    copies = [
        pltpu.make_async_copy(
            zvec.at[:, side, pl.ds(start, half), :], outer_near.at[pl.ds(0, modes)], sems.at[0]
        ),
        pltpu.make_async_copy(zvec.at[:, 1 - side], inner_send.at[pl.ds(0, modes)], sems.at[1]),
    ]
    label_copy.start()
    for copy in copies:
        copy.start()
    label_copy.wait()
    outer_near[modes:] = labels[side].astype(F32).astype(BF16).reshape(rows // half, half, layers)
    inner_send[modes] = labels[1 - side].astype(F32).astype(BF16)
    for copy in copies:
        copy.wait()


def release_kernel(after, outer_rest, outer_out):
    pass


def prepare_kernel(labels, held, outer_rest, one_pack, two_pack):
    modes, planes, rows, layers = held.shape
    half = rows // 2
    width = planes * rows
    side = lax.rem(here_on("pln"), 2)
    odd = lax.rem(here_on("sub"), 2) == 1
    one_lane = jnp.where(odd, 0, layers - 1)
    two_lane = jnp.where(odd, layers - 1, 0)
    row = lax.broadcasted_iota(jnp.int32, (16, layers), 0)
    both = ((row == 0) & lane_is((16, layers), one_lane)) | ((row == 1) & lane_is((16, layers), two_lane))
    both = both.astype(BF16)
    flat = labels[...].astype(F32).astype(BF16).reshape(width, layers)
    for out, lane in ((one_pack, one_lane), (two_pack, two_lane)):
        out[modes:] = lax.dot_general(
            pick_row(lane, layers), flat, NT, preferred_element_type=F32
        ).astype(BF16)
    for k in range(0, modes, CHUNK):
        at = slice(k, k + CHUNK)
        ends = lax.dot_general(
            both, held[at].reshape(-1, layers), NT, preferred_element_type=F32
        )
        for out, index in ((one_pack, 0), (two_pack, 1)):
            out[at] = jnp.concatenate(
                [ends[index:index + 1, j * width:(j + 1) * width] for j in range(CHUNK)], axis=0
            ).astype(BF16)
        outer_rest[at] = held[at, side, pl.ds(pl.multiple_of(side * half, half), half), :]


def block_kernel(
    levels, labels, resid, zvec, after, partial, weights, here, half_diag, link_y, link_z,
):
    planes, rows, layers = labels.shape
    modes = here.shape[2]
    side = lax.rem(here_on("pln"), 2)
    at_edge = ends_the_line()
    held = (1 - side, side)

    def turn_rows(start):
        for slot, plane in enumerate(held):
            for k in range(0, modes, CHUNK):
                block = zvec[k:k + CHUNK, plane, pl.ds(start, STEP), :]
                here[slot, pl.ds(start, STEP), k:k + CHUNK, :] = jnp.swapaxes(block, 0, 1)

    turn_rows(0)
    coef = [coefficients(labels[x], levels) for x in held]
    middle = harmonic(coef[0], coef[1])
    weights[0] = middle
    row = lax.broadcasted_iota(jnp.int32, (rows, layers), 0)
    lane = lax.broadcasted_iota(jnp.int32, (rows, layers), 1)
    for x in range(2):
        c = coef[x]
        up_y = harmonic(c, jnp.where(row == rows - 1, c, pltpu.roll(c, rows - 1, 0)))
        up_z = harmonic(c, pltpu.roll(c, layers - 1, 1))
        down_y = jnp.where(row == 0, c, pltpu.roll(up_y, 1, 0))
        weights[1 + x] = up_y
        weights[3 + x] = up_z
        weights[5 + x] = c
        inner_z = jnp.where(lane == layers - 1, 0.0, up_z)
        total = middle + up_y + down_y + inner_z + pltpu.roll(inner_z, 1, 1)
        if x == 1:
            total = total + jnp.where(at_edge, c, 0.0)
        half_diag[x] = 0.5 * total
        link_y[x] = jnp.where(row == rows - 1, 0.0, up_y)
        link_z[x] = inner_z

    def step(j, carry):
        total, rhs, wide = carry
        turn_rows(pl.multiple_of(jnp.minimum((j + 1) * STEP, rows - STEP), STEP))
        for u in range(STEP):
            y = j * STEP + u
            at = pl.ds(y, 1)
            ahead = jnp.minimum(y + 1, rows - 1)
            up = [here[x, ahead].astype(F32) for x in range(2)]
            images = []
            for x in range(2):
                image = (
                    half_diag[x, at, :] * wide[x]
                    - link_y[x, at, :] * up[x]
                    - link_z[x, at, :] * pltpu.roll(wide[x], layers - 1, 1)
                )
                if x == 0:
                    image = image - weights[0, at, :] * wide[1]
                rhs = rhs + resid[held[x], at, :] * wide[x]
                images.append(image.astype(BF16))
            total = total + lax.dot_general(
                jnp.concatenate(images, axis=1),
                jnp.concatenate([here[0, y], here[1, y]], axis=1),
                NT,
                preferred_element_type=F32,
            )
            wide = up
        return total, rhs, wide

    total, rhs, _ = lax.fori_loop(
        0,
        rows // STEP,
        step,
        (
            jnp.zeros((modes, modes), F32),
            jnp.zeros((modes, layers), F32),
            [here[x, 0].astype(F32) for x in range(2)],
        ),
    )
    partial[:modes, :] = total
    partial[modes:, :] = lax.dot_general(
        jnp.ones((8, layers), F32), rhs, NT, precision=PRECISE, preferred_element_type=F32
    )


def turn(got, start, out):
    half, modes, layers = out.shape
    for k in range(0, modes, CHUNK):
        out[:, k:k + CHUNK, :] = jnp.swapaxes(got[k:k + CHUNK, pl.ds(start, half), :], 0, 1)


def face_product(weight_ref, base, own, other):
    half, modes, layers = other.shape

    def step(j, total):
        left, right = [], []
        for u in range(STEP):
            y = j * STEP + u
            weight = weight_ref[pl.ds(base + y, 1), :]
            image = weight * (own[base + y].astype(F32) - other[y].astype(F32))
            left.append(jnp.concatenate([own[base + y], other[y]], axis=0))
            right.append(image.astype(BF16))
        return total + lax.dot_general(
            jnp.concatenate(left, axis=1), jnp.concatenate(right, axis=1), NT,
            preferred_element_type=F32,
        )

    total = lax.fori_loop(0, half // STEP, step, jnp.zeros((2 * modes, modes), F32))
    return total[:modes] - total[modes:]


def inner_kernel(levels, partial, weights, here, inner_got, out, face, turned):
    planes, rows, modes, layers = here.shape
    half = rows // 2
    side = lax.rem(here_on("pln"), 2)
    base = pl.multiple_of(side * half, half)
    turn(inner_got, base, turned)
    face[...] = harmonic(weights[5], coefficients(inner_got[modes].astype(F32), levels))
    out[:modes, :] = partial[:modes, :] + 0.5 * face_product(face, base, here.at[0], turned)
    out[modes:, :] = partial[modes:, :]


def outer_kernel(
    levels, partial, weights, here, outer_got, one_pack, two_pack, one_got, two_got,
    out, face, turned, face_here,
):
    planes, rows, modes, layers = here.shape
    half = rows // 2
    side = lax.rem(here_on("pln"), 2)
    at_edge = ends_the_line()
    base = pl.multiple_of(side * half, half)
    turn(outer_got, 0, turned)
    coef = coefficients(outer_got[modes:].astype(F32).reshape(rows, layers), levels)
    between = harmonic(weights[6], coef)
    face[...] = jnp.where(at_edge, weights[6], between)
    face_here[...] = jnp.where(at_edge, 0.0, between)
    cross = face_product(face_here, base, here.at[1], turned)
    odd = lax.rem(here_on("sub"), 2) == 1

    def coef_row(pack):
        return coefficients(pack[modes:modes + 16].astype(F32)[0:1], levels)

    one, two = one_pack[...].astype(F32), two_pack[...].astype(F32)
    one_other, two_other = one_got[...].astype(F32), two_got[...].astype(F32)
    first, last = jnp.where(odd, one, two), jnp.where(odd, two, one)
    next_first = jnp.where(odd, two_other, one_other)
    prev_last = jnp.where(odd, one_other, two_other)
    weight_low = harmonic(coef_row(first), coef_row(prev_last))
    weight_high = harmonic(coef_row(last), coef_row(next_first))

    def product(left, right):
        return lax.dot_general(
            left.astype(BF16), right.astype(BF16), NT, preferred_element_type=F32
        )

    edge_rows = weight_high * last[:modes]
    ends = product(
        jnp.concatenate([weight_low * first[:modes], edge_rows], axis=1),
        jnp.concatenate([first[:modes], last[:modes]], axis=1),
    )
    square = partial[:modes, :] + 0.5 * (cross + ends)
    out[:modes, :modes] = square + square.T
    out[:modes, modes:] = -product(edge_rows, next_first[:modes])
    out[modes:, :modes] = partial[modes:, :]
    out[modes:, modes:] = jnp.zeros((8, modes), F32)


def terms_kernel(
    levels, pair, one_got, two_got, weights, inner_face, outer_face, terms, picked, coef_ref
):
    modes, width = picked.shape[1:]
    rows, layers = inner_face.shape
    side = lax.rem(here_on("pln"), 2)
    odd = lax.rem(here_on("sub"), 2) == 1
    one_other, two_other = one_got[...].astype(F32), two_got[...].astype(F32)
    next_first = jnp.where(odd, two_other, one_other)
    prev_last = jnp.where(odd, one_other, two_other)
    picked[0] = next_first[:modes]
    picked[1] = prev_last[:modes]
    end_labels = lax.dot_general(
        next_first[modes:].astype(BF16), pick_row(layers - 1, layers), TN, preferred_element_type=F32
    ) + lax.dot_general(
        prev_last[modes:].astype(BF16), pick_row(0, layers), TN, preferred_element_type=F32
    )
    coef_ref[...] = coefficients(end_labels, levels).reshape(width // rows, rows, layers)
    row = lax.broadcasted_iota(jnp.int32, (rows, layers), 0)
    lane = lax.broadcasted_iota(jnp.int32, (rows, layers), 1)
    for x, face in enumerate((inner_face, outer_face)):
        c = weights[5 + x]
        end_weight = harmonic(c, coef_ref[1 - side if x == 0 else side])
        up_y, up_z = weights[1 + x], weights[3 + x]
        down_y = jnp.where(row == 0, c, pltpu.roll(up_y, 1, 0))
        down_z = pltpu.roll(up_z, 1, 1)
        total = face[...] + weights[0] + up_y + down_y
        total = total + jnp.where(lane == layers - 1, end_weight, up_z)
        terms[x, 0] = total + jnp.where(lane == 0, end_weight, down_z)
        terms[x, 1] = jnp.where(row == 0, 0.0, down_y)
        terms[x, 2] = jnp.where(row == rows - 1, 0.0, up_y)
        terms[x, 3] = jnp.where(lane == 0, 0.0, down_z)
        terms[x, 4] = jnp.where(lane == layers - 1, 0.0, up_z)
        terms[x, 5] = end_weight


def pair_kernel(own, across, beside, oblique, out):
    modes = own.shape[1] // 2
    encode(own[...] + across[...], modes, out.at[0])
    encode(beside[...] + oblique[...], modes, out.at[1])


def single_kernel(own, out):
    encode(own[...], own.shape[1] // 2, out)


def encode(total, modes, out):
    row = lax.broadcasted_iota(jnp.int32, (modes, 2 * modes), 0)
    lane = lax.broadcasted_iota(jnp.int32, (modes, 2 * modes), 1)
    values = total[:modes]
    high = values.astype(BF16).astype(F32)
    low = values - high
    out[:modes] = jnp.where((lane <= row) | (lane >= modes), high, low).astype(BF16)
    diagonal = lane == row
    right = total[modes:modes + 1]
    parts = []
    for _ in range(3):
        part = right.astype(BF16).astype(F32)
        parts.append(part)
        right = right - part
    for part in (high, low):
        parts.append(jnp.sum(jnp.where(diagonal, part, 0.0), axis=0, keepdims=True))
    rows = lax.broadcasted_iota(jnp.int32, (16, 2 * modes), 0)
    extra = jnp.zeros((16, 2 * modes), F32)
    for index, part in enumerate(parts):
        extra = jnp.where(rows == index, part, extra)
    out[modes:] = extra.astype(BF16)


def widen_kernel(pair, zvec, inner_got, outer_got, own_wide, inner_wide, outer_wide):
    modes, half = outer_wide.shape[:2]
    side = lax.rem(here_on("pln"), 2)

    def some(j, carry):
        at = pl.ds(pl.multiple_of(j * MODES, MODES), MODES)
        own_wide[at, 0] = zvec[at, 1 - side].astype(F32)
        own_wide[at, 1] = zvec[at, side].astype(F32)
        inner_wide[at] = inner_got[at].astype(F32)
        outer_wide[at] = outer_got[at].astype(F32)
        return carry

    lax.fori_loop(0, modes // MODES, some, 0)


def finish_kernel(*refs):
    count = len(refs) - 15
    blocks, refs = refs[:count], refs[count:]
    zvec, inner_got, outer_got, outer_last, picked, terms, middle, inner_face, outer_face, resid = refs[:10]
    solution, deflated, direction_ref, spread, outer_field = refs[10:]
    subs = direction_ref.shape[0]
    modes, planes, rows, layers = zvec.shape
    half = rows // 2
    me = here_on("sub")
    side = lax.rem(here_on("pln"), 2)
    odd = lax.rem(me, 2) == 1
    at_edge = ends_the_line()
    held = (1 - side, side)
    square = (modes, modes)
    eye = lax.broadcasted_iota(jnp.int32, square, 0) == lax.broadcasted_iota(jnp.int32, square, 1)

    def column(row):
        return jnp.sum(jnp.where(eye, row, 0.0), axis=1, keepdims=True)

    def each(body, carry):
        for index, block in enumerate(blocks):
            held_here = block.shape[0]
            if held_here <= 8:
                for entry in range(held_here):
                    s = jnp.bitwise_xor(jnp.bitwise_xor(me, mask_of(index, len(blocks))), entry)
                    carry = body(block.at[entry], s, carry)
            else:
                carry = lax.fori_loop(
                    0, held_here, lambda entry, c, block=block: body(block.at[entry], entry, c), carry
                )
        return carry

    def row_is(s, width):
        return lax.broadcasted_iota(jnp.int32, (subs, width), 0) == s

    def load(block, s, carry):
        extra = block[modes:modes + 16, :].astype(F32)
        right = (extra[0:1] + extra[1:2]) + extra[2:3]
        here = row_is(s, 2 * modes)
        return jnp.where(here, right, carry[0]), jnp.where(here, extra[4:5] - extra[3:4], carry[1])

    empty = jnp.zeros((subs, 2 * modes), F32)
    right_side, fix = each(load, (empty, empty))
    fix = fix[:, :modes]

    def turned(rows_of, by):
        by = by % subs
        return jnp.concatenate([rows_of[by:], rows_of[:by]], axis=0)

    def in_parts(value):
        parts = []
        for _ in range(3):
            part = value.astype(BF16)
            parts.append(part.astype(F32))
            value = value - parts[-1]
        return jnp.concatenate(parts, axis=0).astype(BF16)

    def joined(value):
        return (value[:subs] + value[subs:2 * subs]) + value[2 * subs:]

    def coarse_apply(direction):
        pairs = in_parts(jnp.concatenate([direction, turned(direction, 1)], axis=1))
        single = pairs[:, :modes]

        def one(block, s, carry):
            values = block[:modes, :]
            ahead = lax.dot_general(pairs, values, NT, preferred_element_type=F32)
            image = jnp.dot(single, values, preferred_element_type=F32)
            return (
                jnp.where(row_is(s, modes), joined(ahead), carry[0]),
                jnp.where(row_is(s, 2 * modes), joined(image), carry[1]),
            )

        ahead, image = each(one, (jnp.zeros((subs, modes), F32), empty))
        return ahead + image[:, :modes] + fix * direction + turned(image[:, modes:], -1)

    def inner(left, right):
        return jnp.sum(jnp.sum(left * right, axis=0, keepdims=True), axis=1, keepdims=True)

    remain = right_side[:, :modes]
    direction = remain
    result = jnp.zeros_like(remain)
    norm_now = inner(remain, remain)
    for iteration in range(CITERS):
        image = coarse_apply(direction)
        step_size = norm_now / inner(direction, image)
        result = result + step_size * direction
        if iteration + 1 < CITERS:
            remain = remain - step_size * image
            norm_next = inner(remain, remain)
            direction = remain + (norm_next / norm_now) * direction
            norm_now = norm_next
    direction_ref[...] = result
    own = direction_ref[pl.ds(me, 1), :]
    solution[...] = own
    spread[...] = jnp.broadcast_to(column(own), (modes, layers))
    ahead_column = column(direction_ref[pl.ds(lax.rem(me + 1, subs), 1), :])
    behind_column = column(direction_ref[pl.ds(lax.rem(me + subs - 1, subs), 1), :])
    ahead_row = jnp.sum(ahead_column * picked[0], axis=0, keepdims=True)
    behind_row = jnp.sum(behind_column * picked[1], axis=0, keepdims=True)
    width = planes * rows
    both_rows = jnp.where(
        lax.broadcasted_iota(jnp.int32, (8, width), 0) == 0,
        jnp.broadcast_to(ahead_row, (8, width)),
        jnp.broadcast_to(behind_row, (8, width)),
    )
    columns = both_rows.T
    ends = jnp.where(
        lane_is((width, layers), layers - 1),
        columns[:, 0:1],
        jnp.where(lane_is((width, layers), 0), columns[:, 1:2], 0.0),
    ).reshape(planes, rows, layers)

    def add_mode(j, carry):
        fields, near, last = list(carry[0]), carry[1], carry[2]
        for u in range(MODES):
            k = j * MODES + u
            scale = spread[pl.ds(k, 1), :]
            for x, plane in enumerate((zvec[k, 0], zvec[k, 1], inner_got[k])):
                fields[x] = fields[x] + scale * plane
            near = near + scale * outer_got[k]
            last = last + scale * outer_last[k].astype(F32)
        return tuple(fields), near, last

    zero, short = jnp.zeros((rows, layers), F32), jnp.zeros((half, layers), F32)
    field, near, last = lax.fori_loop(0, modes // MODES, add_mode, ((zero,) * 3, short, short))
    outer_field[pl.ds(pl.multiple_of(side * half, half), half), :] = near
    outer_field[pl.ds(pl.multiple_of((1 - side) * half, half), half), :] = last
    outside = (field[2], jnp.where(at_edge, 0.0, outer_field[...]))
    faces = (inner_face[...], outer_face[...])
    for x in range(2):
        f = field[x]
        end_field = jnp.where(side == x, ends[1], ends[0])
        image = (
            terms[x, 0] * f
            - middle[0] * field[1 - x]
            - faces[x] * outside[x]
            - terms[x, 1] * pltpu.roll(f, 1, 0)
            - terms[x, 2] * pltpu.roll(f, rows - 1, 0)
            - terms[x, 3] * pltpu.roll(f, 1, 1)
            - terms[x, 4] * pltpu.roll(f, layers - 1, 1)
            - terms[x, 5] * end_field
        )
        deflated[held[x]] = resid[held[x]] - image


def swapped(value, axis, first):
    count = lax.axis_size(axis)
    pairs = []
    for i in range(count):
        up = (i - first) % 2 == 0
        pairs.append((i, (i + 1) % count if up else (i - 1) % count))
    return lax.ppermute(value, axis, pairs)


def swapped_all(value):
    subs, count = lax.axis_size("sub"), lax.axis_size("pln")
    pairs = []
    for s in range(subs):
        for i in range(count):
            if 0 < i < count - 1:
                to = (s, i + 1 if i % 2 else i - 1)
            else:
                to = (s ^ 1, i)
            pairs.append((s * count + i, to[0] * count + to[1]))
    return lax.ppermute(value, ("sub", "pln"), pairs)


def exchanged(value, axis, mask):
    return lax.ppermute(value, axis, [(i, i ^ mask) for i in range(lax.axis_size(axis))])


def partner(value, sub_mask, pln_mask):
    subs, count = lax.axis_size("sub"), lax.axis_size("pln")
    pairs = [
        (s * count + p, (s ^ sub_mask) * count + (p ^ pln_mask)) for s in range(subs) for p in range(count)
    ]
    return lax.ppermute(value, ("sub", "pln"), pairs)


FAR = (4, 6)


def mask_of(index, count):
    if count == 1:
        return 0
    swap = lax.rem(here_on("pln"), 2) * (FAR[1] - FAR[0])
    return (0, FAR[0] + swap, 2, FAR[1] - swap)[index]


def far_partner(value):
    subs, count = lax.axis_size("sub"), lax.axis_size("pln")
    pairs = [(s * count + p, (s ^ FAR[p % 2]) * count + p) for s in range(subs) for p in range(count)]
    return lax.ppermute(value, ("sub", "pln"), pairs)


def body(labels, levels, zvec, resid):
    modes, planes, rows, layers = zvec.shape
    half = rows // 2
    subs, parts = lax.axis_size("sub"), lax.axis_size("pln")
    shape = jax.ShapeDtypeStruct
    levels = levels.reshape(1, -1)
    pack = shape((modes + 16, planes * rows), BF16)
    inner_send, outer_near = call(
        stage_kernel,
        [shape((modes + 1, rows, layers), BF16), shape((modes + rows // half, half, layers), BF16)],
        [HBM, HBM],
        [pltpu.VMEM(labels.shape, jnp.int32), pltpu.SemaphoreType.DMA, pltpu.SemaphoreType.DMA((2,))],
        moved=2 << 20,
    )(*(pltpu.with_memory_space_constraint(v, pltpu.HBM) for v in (labels, zvec)))
    outer_got = swapped_all(outer_near)
    inner_got = swapped(inner_send, "pln", 0)
    rest = shape((modes, half, layers), BF16)
    outer_rest, one_pack, two_pack = call(
        prepare_kernel,
        [rest, pack, pack],
        [VMEM, VMEM],
        flops=10_000_000,
        moved=6 << 20,
    )(labels, zvec)
    one_got = swapped(one_pack, "sub", 0)
    two_got = swapped(two_pack, "sub", 1)
    field = (planes, rows, layers)
    plane = (rows, layers)
    partial, weights, here = call(
        block_kernel,
        [
            shape((modes + 8, modes), F32),
            shape((7,) + plane, F32),
            shape((planes, rows, modes, layers), BF16),
        ],
        [VMEM] * 4 + [ANY],
        [pltpu.VMEM(field, F32)] * 3,
        flops=400_000_000,
        moved=3 << 20,
    )(levels, labels, resid, zvec, one_pack)
    turned = pltpu.VMEM((half, modes, layers), BF16)
    partial, inner_face = call(
        inner_kernel,
        [shape((modes + 8, modes), F32), shape(plane, F32)],
        [VMEM] * 5,
        [turned],
        flops=100_000_000,
        moved=1 << 20,
    )(levels, partial, weights, here, inner_got)
    block, outer_face = call(
        outer_kernel,
        [shape((modes + 8, 2 * modes), F32), shape(plane, F32)],
        [VMEM] * 9,
        [turned, pltpu.VMEM(plane, F32)],
        flops=100_000_000,
        moved=1 << 20,
    )(levels, partial, weights, here, outer_got, one_pack, two_pack, one_got, two_got)
    packed = (modes + 16, 2 * modes)
    if parts == 4 and subs == 8:
        block = block + exchanged(block, "pln", 1)
        others = [partner(block, *masks) for masks in ((0, 3), (1, 1), (1, 3))]
        [pair] = call(
            pair_kernel, [shape((2,) + packed, BF16)], [VMEM] * 4, flops=1 << 33
        )(block, *others)
        far = far_partner(pair)
        blocks = [pair, far, partner(pair, 2, 1), exchanged(far, "pln", 1)]
    else:
        [single] = call(single_kernel, [shape(packed, BF16)], [VMEM])(lax.psum(block, "pln"))
        blocks = [lax.all_gather(single, "sub")]
    [outer_rest] = call(release_kernel, [rest], [ANY] * 2, aliases={1: 0})(block, outer_rest)
    outer_last = swapped_all(outer_rest)
    terms, picked = call(
        terms_kernel,
        [shape((planes, 6) + plane, F32), shape((2, modes, planes * rows), F32)],
        [VMEM, ANY] + [VMEM] * 5,
        [pltpu.VMEM(field, F32)],

        flops=1 << 31,
        moved=1 << 20,
    )(levels, blocks[0], one_got, two_got, weights, inner_face, outer_face)
    wide = call(
        widen_kernel,
        [
            shape((modes,) + field, F32),
            shape((modes,) + plane, F32),
            shape((modes, half, layers), F32),
        ],
        [ANY] + [VMEM] * 3,
        flops=1 << 30,
        moved=1 << 20,
    )(blocks[0], zvec, inner_got, outer_got)
    return tuple(
        call(
            finish_kernel,
            [shape((1, modes), F32), shape(field, F32)],
            [VMEM] * (10 + len(blocks)),
            [
                pltpu.VMEM((subs, modes), F32),
                pltpu.VMEM((modes, layers), F32),
                pltpu.VMEM(plane, F32),
            ],
            flops=10_000_000,
            moved=5 << 20,
        )(
            *blocks, *wide, outer_last, picked, terms, weights, inner_face,
            outer_face, resid,
        )
    )


def solution(mesh):
    in_specs = (P("pln", None, "sub"), P(), P(None, "pln", None, "sub"), P("pln", None, "sub"))
    out_specs = (P("sub", None), P("pln", None, "sub"))
    return jax.shard_map(body, mesh=mesh, in_specs=in_specs, out_specs=out_specs, check_vma=False)
```

```python
import jax
import jax.numpy as jnp
from jax import lax
from jax.experimental import pallas as pl
from jax.experimental.pallas import tpu as pltpu
from jax.sharding import PartitionSpec as P

CITERS = 2
STEP = 16
MODES = 8
CHUNK = 16
F32 = jnp.float32
BF16 = jnp.bfloat16
PRECISE = lax.Precision.HIGHEST
NT = (((1,), (1,)), ((), ()))
TN = (((0,), (0,)), ((), ()))
VMEM = pl.BlockSpec(memory_space=pltpu.VMEM)
HBM = pl.BlockSpec(memory_space=pltpu.HBM)
ANY = pl.BlockSpec(memory_space=pl.ANY)


def call(kernel, outs, specs, scratch=(), flops=0, moved=0, limit=32, aliases=None):
    return pl.pallas_call(
        kernel,
        out_shape=outs,
        in_specs=specs,
        out_specs=[ANY if at in (aliases or {}).values() else VMEM for at in range(len(outs))],
        input_output_aliases=aliases or {},
        scratch_shapes=list(scratch),
        cost_estimate=pl.CostEstimate(flops=flops, bytes_accessed=moved, transcendentals=0),
        compiler_params=pltpu.CompilerParams(vmem_limit_bytes=limit << 20),
    )


def here_on(axis):
    return lax.axis_index(axis).astype(jnp.int32)


def ends_the_line():
    p = here_on("pln")
    return (p == 0) | (p == lax.axis_size("pln") - 1)


def harmonic(left_value, right_value):
    return 2.0 * left_value * right_value / (left_value + right_value)


def coefficients(labels, levels_ref):
    weighted = jnp.zeros(labels.shape, F32)
    for level in range(levels_ref.shape[1]):
        weighted = weighted + jnp.where(labels == level, levels_ref[:, level:level + 1], 0.0)
    return weighted


def lane_is(shape, lane):
    return lax.broadcasted_iota(jnp.int32, shape, len(shape) - 1) == lane


def pick_row(lane, width):
    row = lax.broadcasted_iota(jnp.int32, (16, width), 0)
    return ((row == 0) & lane_is((16, width), lane)).astype(BF16)


def stage_kernel(labels_far, zvec, inner_send, first_part, second_part, labels, label_sem, sems):
    modes, planes, rows, layers = zvec.shape
    quarter = second_part.shape[1]
    side = lax.rem(here_on("pln"), 2)
    start = pl.multiple_of((1 - side) * (rows // 2), quarter)
    label_copy = pltpu.make_async_copy(labels_far, labels, label_sem)
    copies = [
        pltpu.make_async_copy(
            zvec.at[:, side, pl.ds(start + index * quarter, quarter), :], out.at[pl.ds(0, modes)],
            sems.at[index],
        )
        for index, out in enumerate((first_part, second_part))
    ]
    copies.append(
        pltpu.make_async_copy(zvec.at[:, 1 - side], inner_send.at[pl.ds(0, modes)], sems.at[2])
    )
    label_copy.start()
    for copy in copies:
        copy.start()
    label_copy.wait()
    first_part[modes:] = labels[side].astype(F32).astype(BF16).reshape(rows // quarter, quarter, layers)
    inner_send[modes] = labels[1 - side].astype(F32).astype(BF16)
    for copy in copies:
        copy.wait()


def prepare_kernel(labels, held, outer_rest, one_pack, two_pack):
    modes, planes, rows, layers = held.shape
    half = rows // 2
    width = planes * rows
    side = lax.rem(here_on("pln"), 2)
    odd = lax.rem(here_on("sub"), 2) == 1
    one_lane = jnp.where(odd, 0, layers - 1)
    two_lane = jnp.where(odd, layers - 1, 0)
    row = lax.broadcasted_iota(jnp.int32, (16, layers), 0)
    both = ((row == 0) & lane_is((16, layers), one_lane)) | ((row == 1) & lane_is((16, layers), two_lane))
    both = both.astype(BF16)
    flat = labels[...].astype(F32).astype(BF16).reshape(width, layers)
    for out, lane in ((one_pack, one_lane), (two_pack, two_lane)):
        out[modes:] = lax.dot_general(
            pick_row(lane, layers), flat, NT, preferred_element_type=F32
        ).astype(BF16)
    for k in range(0, modes, CHUNK):
        at = slice(k, k + CHUNK)
        ends = lax.dot_general(
            both, held[at].reshape(-1, layers), NT, preferred_element_type=F32
        )
        for out, index in ((one_pack, 0), (two_pack, 1)):
            out[at] = jnp.concatenate(
                [ends[index:index + 1, j * width:(j + 1) * width] for j in range(CHUNK)], axis=0
            ).astype(BF16)
        outer_rest[at] = held[at, side, pl.ds(pl.multiple_of(side * half, half), half), :]


def release_kernel(after, outer_rest, outer_out):
    pass


def block_kernel(
    levels, labels, resid, zvec, after, partial, weights, here, half_diag, link_y, link_z,
):
    planes, rows, layers = labels.shape
    modes = here.shape[2]
    side = lax.rem(here_on("pln"), 2)
    at_edge = ends_the_line()
    held = (1 - side, side)

    def turn_rows(start):
        for slot, plane in enumerate(held):
            for k in range(0, modes, CHUNK):
                block = zvec[k:k + CHUNK, plane, pl.ds(start, STEP), :]
                here[slot, pl.ds(start, STEP), k:k + CHUNK, :] = jnp.swapaxes(block, 0, 1)

    turn_rows(0)
    coef = [coefficients(labels[x], levels) for x in held]
    middle = harmonic(coef[0], coef[1])
    weights[0] = middle
    row = lax.broadcasted_iota(jnp.int32, (rows, layers), 0)
    lane = lax.broadcasted_iota(jnp.int32, (rows, layers), 1)
    for x in range(2):
        c = coef[x]
        up_y = harmonic(c, jnp.where(row == rows - 1, c, pltpu.roll(c, rows - 1, 0)))
        up_z = harmonic(c, pltpu.roll(c, layers - 1, 1))
        down_y = jnp.where(row == 0, c, pltpu.roll(up_y, 1, 0))
        weights[1 + x] = up_y
        weights[3 + x] = up_z
        weights[5 + x] = c
        inner_z = jnp.where(lane == layers - 1, 0.0, up_z)
        total = middle + up_y + down_y + inner_z + pltpu.roll(inner_z, 1, 1)
        if x == 1:
            total = total + jnp.where(at_edge, c, 0.0)
        half_diag[x] = 0.5 * total
        link_y[x] = jnp.where(row == rows - 1, 0.0, up_y)
        link_z[x] = inner_z

    def step(j, carry):
        total, rhs, wide = carry
        turn_rows(pl.multiple_of(jnp.minimum((j + 1) * STEP, rows - STEP), STEP))
        for u in range(STEP):
            y = j * STEP + u
            at = pl.ds(y, 1)
            ahead = jnp.minimum(y + 1, rows - 1)
            up = [here[x, ahead].astype(F32) for x in range(2)]
            images = []
            for x in range(2):
                image = (
                    half_diag[x, at, :] * wide[x]
                    - link_y[x, at, :] * up[x]
                    - link_z[x, at, :] * pltpu.roll(wide[x], layers - 1, 1)
                )
                if x == 0:
                    image = image - weights[0, at, :] * wide[1]
                rhs = rhs + resid[held[x], at, :] * wide[x]
                images.append(image.astype(BF16))
            total = total + lax.dot_general(
                jnp.concatenate(images, axis=1),
                jnp.concatenate([here[0, y], here[1, y]], axis=1),
                NT,
                preferred_element_type=F32,
            )
            wide = up
        return total, rhs, wide

    total, rhs, _ = lax.fori_loop(
        0,
        rows // STEP,
        step,
        (
            jnp.zeros((modes, modes), F32),
            jnp.zeros((modes, layers), F32),
            [here[x, 0].astype(F32) for x in range(2)],
        ),
    )
    partial[:modes, :] = total
    partial[modes:, :] = lax.dot_general(
        jnp.ones((8, layers), F32), rhs, NT, precision=PRECISE, preferred_element_type=F32
    )


def turn(got, start, out):
    half, modes, layers = out.shape
    for k in range(0, modes, CHUNK):
        out[:, k:k + CHUNK, :] = jnp.swapaxes(got[k:k + CHUNK, pl.ds(start, half), :], 0, 1)


def face_product(weight_ref, base, own, other):
    half, modes, layers = other.shape

    def step(j, total):
        left, right = [], []
        for u in range(STEP):
            y = j * STEP + u
            weight = weight_ref[pl.ds(base + y, 1), :]
            image = weight * (own[base + y].astype(F32) - other[y].astype(F32))
            left.append(jnp.concatenate([own[base + y], other[y]], axis=0))
            right.append(image.astype(BF16))
        return total + lax.dot_general(
            jnp.concatenate(left, axis=1), jnp.concatenate(right, axis=1), NT,
            preferred_element_type=F32,
        )

    total = lax.fori_loop(0, half // STEP, step, jnp.zeros((2 * modes, modes), F32))
    return total[:modes] - total[modes:]


def inner_kernel(levels, partial, weights, here, inner_got, out, face, turned):
    planes, rows, modes, layers = here.shape
    half = rows // 2
    side = lax.rem(here_on("pln"), 2)
    base = pl.multiple_of(side * half, half)
    turn(inner_got, base, turned)
    face[...] = harmonic(weights[5], coefficients(inner_got[modes].astype(F32), levels))
    out[:modes, :] = partial[:modes, :] + 0.5 * face_product(face, base, here.at[0], turned)
    out[modes:, :] = partial[modes:, :]


def outer_kernel(levels, partial, weights, here, outer_got, out, face, face_here, turned):
    planes, rows, modes, layers = here.shape
    quarter = turned.shape[0]
    at_edge = ends_the_line()
    base = pl.multiple_of(lax.rem(here_on("pln"), 2) * (rows // 2), quarter)
    turn(outer_got, 0, turned)
    coef = coefficients(outer_got[modes:].astype(F32).reshape(rows, layers), levels)
    between = harmonic(weights[6], coef)
    face[...] = jnp.where(at_edge, weights[6], between)
    face_here[...] = jnp.where(at_edge, 0.0, between)
    out[:modes, :] = partial[:modes, :] + 0.5 * face_product(face_here, base, here.at[1], turned)
    out[modes:, :] = partial[modes:, :]


def last_kernel(
    levels, partial, face_here, here, outer_got, one_pack, two_pack, one_got, two_got, out, turned
):
    planes, rows, modes, layers = here.shape
    quarter = turned.shape[0]
    base = pl.multiple_of(lax.rem(here_on("pln"), 2) * (rows // 2) + quarter, quarter)
    turn(outer_got, 0, turned)
    cross = face_product(face_here, base, here.at[1], turned)
    odd = lax.rem(here_on("sub"), 2) == 1

    def coef_row(pack):
        return coefficients(pack[modes:modes + 16].astype(F32)[0:1], levels)

    one, two = one_pack[...].astype(F32), two_pack[...].astype(F32)
    one_other, two_other = one_got[...].astype(F32), two_got[...].astype(F32)
    first, last = jnp.where(odd, one, two), jnp.where(odd, two, one)
    next_first = jnp.where(odd, two_other, one_other)
    prev_last = jnp.where(odd, one_other, two_other)
    weight_low = harmonic(coef_row(first), coef_row(prev_last))
    weight_high = harmonic(coef_row(last), coef_row(next_first))

    def product(left, right):
        return lax.dot_general(
            left.astype(BF16), right.astype(BF16), NT, preferred_element_type=F32
        )

    edge_rows = weight_high * last[:modes]
    ends = product(
        jnp.concatenate([weight_low * first[:modes], edge_rows], axis=1),
        jnp.concatenate([first[:modes], last[:modes]], axis=1),
    )
    square = partial[:modes, :] + 0.5 * (cross + ends)
    out[:modes, :modes] = square + square.T
    out[:modes, modes:] = -product(edge_rows, next_first[:modes])
    out[modes:, :modes] = partial[modes:, :]
    out[modes:, modes:] = jnp.zeros((8, modes), F32)


def terms_kernel(
    levels, pair, one_got, two_got, weights, inner_face, outer_face, terms, picked, coef_ref
):
    modes, width = picked.shape[1:]
    rows, layers = inner_face.shape
    side = lax.rem(here_on("pln"), 2)
    odd = lax.rem(here_on("sub"), 2) == 1
    one_other, two_other = one_got[...].astype(F32), two_got[...].astype(F32)
    next_first = jnp.where(odd, two_other, one_other)
    prev_last = jnp.where(odd, one_other, two_other)
    picked[0] = next_first[:modes]
    picked[1] = prev_last[:modes]
    end_labels = lax.dot_general(
        next_first[modes:].astype(BF16), pick_row(layers - 1, layers), TN, preferred_element_type=F32
    ) + lax.dot_general(
        prev_last[modes:].astype(BF16), pick_row(0, layers), TN, preferred_element_type=F32
    )
    coef_ref[...] = coefficients(end_labels, levels).reshape(width // rows, rows, layers)
    row = lax.broadcasted_iota(jnp.int32, (rows, layers), 0)
    lane = lax.broadcasted_iota(jnp.int32, (rows, layers), 1)
    for x, face in enumerate((inner_face, outer_face)):
        c = weights[5 + x]
        end_weight = harmonic(c, coef_ref[1 - side if x == 0 else side])
        up_y, up_z = weights[1 + x], weights[3 + x]
        down_y = jnp.where(row == 0, c, pltpu.roll(up_y, 1, 0))
        down_z = pltpu.roll(up_z, 1, 1)
        total = face[...] + weights[0] + up_y + down_y
        total = total + jnp.where(lane == layers - 1, end_weight, up_z)
        terms[x, 0] = total + jnp.where(lane == 0, end_weight, down_z)
        terms[x, 1] = jnp.where(row == 0, 0.0, down_y)
        terms[x, 2] = jnp.where(row == rows - 1, 0.0, up_y)
        terms[x, 3] = jnp.where(lane == 0, 0.0, down_z)
        terms[x, 4] = jnp.where(lane == layers - 1, 0.0, up_z)
        terms[x, 5] = end_weight


def pair_kernel(own, across, beside, oblique, out):
    modes = own.shape[1] // 2
    encode(own[...] + across[...], modes, out.at[0])
    encode(beside[...] + oblique[...], modes, out.at[1])


def single_kernel(own, out):
    encode(own[...], own.shape[1] // 2, out)


def encode(total, modes, out):
    row = lax.broadcasted_iota(jnp.int32, (modes, 2 * modes), 0)
    lane = lax.broadcasted_iota(jnp.int32, (modes, 2 * modes), 1)
    values = total[:modes]
    high = values.astype(BF16).astype(F32)
    low = values - high
    out[:modes] = jnp.where((lane <= row) | (lane >= modes), high, low).astype(BF16)
    diagonal = lane == row
    right = total[modes:modes + 1]
    parts = []
    for _ in range(3):
        part = right.astype(BF16).astype(F32)
        parts.append(part)
        right = right - part
    for part in (high, low):
        parts.append(jnp.sum(jnp.where(diagonal, part, 0.0), axis=0, keepdims=True))
    rows = lax.broadcasted_iota(jnp.int32, (16, 2 * modes), 0)
    extra = jnp.zeros((16, 2 * modes), F32)
    for index, part in enumerate(parts):
        extra = jnp.where(rows == index, part, extra)
    out[modes:] = extra.astype(BF16)


def widen_kernel(
    packed, zvec, inner_got, outer_got, outer_next, own_wide, inner_wide, outer_wide
):
    modes, half = outer_wide.shape[:2]
    quarter = half // 2
    side = lax.rem(here_on("pln"), 2)

    def some(j, carry):
        at = pl.ds(pl.multiple_of(j * MODES, MODES), MODES)
        own_wide[at, 0] = zvec[at, 1 - side].astype(F32)
        own_wide[at, 1] = zvec[at, side].astype(F32)
        inner_wide[at] = inner_got[at].astype(F32)
        outer_wide[at, :quarter, :] = outer_got[at].astype(F32)
        outer_wide[at, quarter:, :] = outer_next[at].astype(F32)
        return carry

    lax.fori_loop(0, modes // MODES, some, 0)


def finish_kernel(*refs):
    count = len(refs) - 15
    blocks, refs = refs[:count], refs[count:]
    zvec, inner_got, outer_got, outer_last, picked, terms, middle, inner_face, outer_face, resid = refs[:10]
    solution, deflated, direction_ref, spread, outer_field = refs[10:]
    subs = direction_ref.shape[0]
    modes, planes, rows, layers = zvec.shape
    half = rows // 2
    me = here_on("sub")
    side = lax.rem(here_on("pln"), 2)
    odd = lax.rem(me, 2) == 1
    at_edge = ends_the_line()
    held = (1 - side, side)
    square = (modes, modes)
    eye = lax.broadcasted_iota(jnp.int32, square, 0) == lax.broadcasted_iota(jnp.int32, square, 1)

    def column(row):
        return jnp.sum(jnp.where(eye, row, 0.0), axis=1, keepdims=True)

    def each(body, carry):
        for index, block in enumerate(blocks):
            held_here = block.shape[0]
            if held_here <= 8:
                for entry in range(held_here):
                    s = jnp.bitwise_xor(jnp.bitwise_xor(me, mask_of(index, len(blocks))), entry)
                    carry = body(block.at[entry], s, carry)
            else:
                carry = lax.fori_loop(
                    0, held_here, lambda entry, c, block=block: body(block.at[entry], entry, c), carry
                )
        return carry

    def row_is(s, width):
        return lax.broadcasted_iota(jnp.int32, (subs, width), 0) == s

    def load(block, s, carry):
        extra = block[modes:modes + 16, :].astype(F32)
        right = (extra[0:1] + extra[1:2]) + extra[2:3]
        here = row_is(s, 2 * modes)
        return jnp.where(here, right, carry[0]), jnp.where(here, extra[4:5] - extra[3:4], carry[1])

    empty = jnp.zeros((subs, 2 * modes), F32)
    right_side, fix = each(load, (empty, empty))
    fix = fix[:, :modes]

    def turned(rows_of, by):
        by = by % subs
        return jnp.concatenate([rows_of[by:], rows_of[:by]], axis=0)

    def in_parts(value):
        parts = []
        for _ in range(3):
            part = value.astype(BF16)
            parts.append(part.astype(F32))
            value = value - parts[-1]
        return jnp.concatenate(parts, axis=0).astype(BF16)

    def joined(value):
        return (value[:subs] + value[subs:2 * subs]) + value[2 * subs:]

    def coarse_apply(direction):
        pairs = in_parts(jnp.concatenate([direction, turned(direction, 1)], axis=1))
        single = pairs[:, :modes]

        def one(block, s, carry):
            values = block[:modes, :]
            ahead = lax.dot_general(pairs, values, NT, preferred_element_type=F32)
            image = jnp.dot(single, values, preferred_element_type=F32)
            return (
                jnp.where(row_is(s, modes), joined(ahead), carry[0]),
                jnp.where(row_is(s, 2 * modes), joined(image), carry[1]),
            )

        ahead, image = each(one, (jnp.zeros((subs, modes), F32), empty))
        return ahead + image[:, :modes] + fix * direction + turned(image[:, modes:], -1)

    def inner(left, right):
        return jnp.sum(jnp.sum(left * right, axis=0, keepdims=True), axis=1, keepdims=True)

    remain = right_side[:, :modes]
    direction = remain
    result = jnp.zeros_like(remain)
    norm_now = inner(remain, remain)
    for iteration in range(CITERS):
        image = coarse_apply(direction)
        step_size = norm_now / inner(direction, image)
        result = result + step_size * direction
        if iteration + 1 < CITERS:
            remain = remain - step_size * image
            norm_next = inner(remain, remain)
            direction = remain + (norm_next / norm_now) * direction
            norm_now = norm_next
    direction_ref[...] = result
    own = direction_ref[pl.ds(me, 1), :]
    solution[...] = own
    spread[...] = jnp.broadcast_to(column(own), (modes, layers))
    ahead_column = column(direction_ref[pl.ds(lax.rem(me + 1, subs), 1), :])
    behind_column = column(direction_ref[pl.ds(lax.rem(me + subs - 1, subs), 1), :])
    ahead_row = jnp.sum(ahead_column * picked[0], axis=0, keepdims=True)
    behind_row = jnp.sum(behind_column * picked[1], axis=0, keepdims=True)
    width = planes * rows
    both_rows = jnp.where(
        lax.broadcasted_iota(jnp.int32, (8, width), 0) == 0,
        jnp.broadcast_to(ahead_row, (8, width)),
        jnp.broadcast_to(behind_row, (8, width)),
    )
    columns = both_rows.T
    ends = jnp.where(
        lane_is((width, layers), layers - 1),
        columns[:, 0:1],
        jnp.where(lane_is((width, layers), 0), columns[:, 1:2], 0.0),
    ).reshape(planes, rows, layers)

    def add_mode(j, carry):
        fields, near, last = list(carry[0]), carry[1], carry[2]
        for u in range(MODES):
            k = j * MODES + u
            scale = spread[pl.ds(k, 1), :]
            for x, plane in enumerate((zvec[k, 0], zvec[k, 1], inner_got[k])):
                fields[x] = fields[x] + scale * plane
            near = near + scale * outer_got[k]
            last = last + scale * outer_last[k].astype(F32)
        return tuple(fields), near, last

    zero, short = jnp.zeros((rows, layers), F32), jnp.zeros((half, layers), F32)
    field, near, last = lax.fori_loop(0, modes // MODES, add_mode, ((zero,) * 3, short, short))
    outer_field[pl.ds(pl.multiple_of(side * half, half), half), :] = near
    outer_field[pl.ds(pl.multiple_of((1 - side) * half, half), half), :] = last
    outside = (field[2], jnp.where(at_edge, 0.0, outer_field[...]))
    faces = (inner_face[...], outer_face[...])
    for x in range(2):
        f = field[x]
        end_field = jnp.where(side == x, ends[1], ends[0])
        image = (
            terms[x, 0] * f
            - middle[0] * field[1 - x]
            - faces[x] * outside[x]
            - terms[x, 1] * pltpu.roll(f, 1, 0)
            - terms[x, 2] * pltpu.roll(f, rows - 1, 0)
            - terms[x, 3] * pltpu.roll(f, 1, 1)
            - terms[x, 4] * pltpu.roll(f, layers - 1, 1)
            - terms[x, 5] * end_field
        )
        deflated[held[x]] = resid[held[x]] - image


def swapped(value, axis, first):
    count = lax.axis_size(axis)
    pairs = []
    for i in range(count):
        up = (i - first) % 2 == 0
        pairs.append((i, (i + 1) % count if up else (i - 1) % count))
    return lax.ppermute(value, axis, pairs)


def swapped_all(value, mask=1):
    subs, count = lax.axis_size("sub"), lax.axis_size("pln")
    pairs = []
    for s in range(subs):
        for i in range(count):
            if 0 < i < count - 1:
                to = (s, i + 1 if i % 2 else i - 1)
            else:
                to = (s ^ mask, i)
            pairs.append((s * count + i, to[0] * count + to[1]))
    return lax.ppermute(value, ("sub", "pln"), pairs)


def exchanged(value, axis, mask):
    return lax.ppermute(value, axis, [(i, i ^ mask) for i in range(lax.axis_size(axis))])


def partner(value, sub_mask, pln_mask):
    subs, count = lax.axis_size("sub"), lax.axis_size("pln")
    pairs = [
        (s * count + p, (s ^ sub_mask) * count + (p ^ pln_mask)) for s in range(subs) for p in range(count)
    ]
    return lax.ppermute(value, ("sub", "pln"), pairs)


FAR = (4, 6)


def mask_of(index, count):
    if count == 1:
        return 0
    swap = lax.rem(here_on("pln"), 2) * (FAR[1] - FAR[0])
    return (0, FAR[0] + swap, 2, FAR[1] - swap)[index]


def far_partner(value):
    subs, count = lax.axis_size("sub"), lax.axis_size("pln")
    pairs = [(s * count + p, (s ^ FAR[p % 2]) * count + p) for s in range(subs) for p in range(count)]
    return lax.ppermute(value, ("sub", "pln"), pairs)


def body(labels, levels, zvec, resid):
    modes, planes, rows, layers = zvec.shape
    half = rows // 2
    subs, parts = lax.axis_size("sub"), lax.axis_size("pln")
    shape = jax.ShapeDtypeStruct
    levels = levels.reshape(1, -1)
    pack = shape((modes + 16, planes * rows), BF16)
    quarter = half // 2
    inner_send, first_part, second_part = call(
        stage_kernel,
        [
            shape((modes + 1, rows, layers), BF16),
            shape((modes + rows // quarter, quarter, layers), BF16),
            shape((modes, quarter, layers), BF16),
        ],
        [HBM, HBM],
        [pltpu.VMEM(labels.shape, jnp.int32), pltpu.SemaphoreType.DMA, pltpu.SemaphoreType.DMA((3,))],
        moved=2 << 20,
    )(*(pltpu.with_memory_space_constraint(v, pltpu.HBM) for v in (labels, zvec)))
    outer_got = swapped_all(first_part)
    outer_next = swapped_all(second_part, 2 if subs % 4 == 0 else 1)
    inner_got = swapped(inner_send, "pln", 0)
    rest = shape((modes, half, layers), BF16)
    outer_rest, one_pack, two_pack = call(
        prepare_kernel,
        [rest, pack, pack],
        [VMEM, VMEM],
        flops=10_000_000,
        moved=6 << 20,
    )(labels, zvec)
    one_got = swapped(one_pack, "sub", 0)
    two_got = swapped(two_pack, "sub", 1)
    field = (planes, rows, layers)
    plane = (rows, layers)
    partial, weights, here = call(
        block_kernel,
        [
            shape((modes + 8, modes), F32),
            shape((7,) + plane, F32),
            shape((planes, rows, modes, layers), BF16),
        ],
        [VMEM] * 4 + [ANY],
        [pltpu.VMEM(field, F32)] * 3,
        flops=400_000_000,
        moved=3 << 20,
    )(levels, labels, resid, zvec, one_pack)
    turned = pltpu.VMEM((half, modes, layers), BF16)
    partial, inner_face = call(
        inner_kernel,
        [shape((modes + 8, modes), F32), shape(plane, F32)],
        [VMEM] * 5,
        [turned],
        flops=100_000_000,
        moved=1 << 20,
    )(levels, partial, weights, here, inner_got)
    turned = pltpu.VMEM((quarter, modes, layers), BF16)
    partial, outer_face, face_here = call(
        outer_kernel,
        [shape((modes + 8, modes), F32), shape(plane, F32), shape(plane, F32)],
        [VMEM] * 5,
        [turned],
        flops=100_000_000,
        moved=1 << 20,
    )(levels, partial, weights, here, outer_got)
    [block] = call(
        last_kernel,
        [shape((modes + 8, 2 * modes), F32)],
        [VMEM] * 9,
        [turned],
        flops=100_000_000,
        moved=1 << 20,
    )(levels, partial, face_here, here, outer_next, one_pack, two_pack, one_got, two_got)
    packed = (modes + 16, 2 * modes)
    if parts == 4 and subs == 8:
        block = block + exchanged(block, "pln", 1)
        others = [partner(block, *masks) for masks in ((0, 3), (1, 1), (1, 3))]
        [pair] = call(
            pair_kernel, [shape((2,) + packed, BF16)], [VMEM] * 4, flops=1 << 33
        )(block, *others)
        far = far_partner(pair)
        blocks = [pair, far, partner(pair, 2, 1), exchanged(far, "pln", 1)]
    else:
        [single] = call(single_kernel, [shape(packed, BF16)], [VMEM])(lax.psum(block, "pln"))
        blocks = [lax.all_gather(single, "sub")]
    [outer_rest] = call(release_kernel, [rest], [ANY] * 2, aliases={1: 0})(block, outer_rest)
    outer_last = swapped_all(outer_rest)
    terms, picked = call(
        terms_kernel,
        [shape((planes, 6) + plane, F32), shape((2, modes, planes * rows), F32)],
        [VMEM, ANY] + [VMEM] * 5,
        [pltpu.VMEM(field, F32)],

        flops=1 << 31,
        moved=1 << 20,
    )(levels, blocks[0], one_got, two_got, weights, inner_face, outer_face)
    wide = call(
        widen_kernel,
        [
            shape((modes,) + field, F32),
            shape((modes,) + plane, F32),
            shape((modes, half, layers), F32),
        ],
        [ANY] + [VMEM] * 4,
        flops=1 << 30,
        moved=1 << 20,
    )(blocks[0], zvec, inner_got, outer_got, outer_next)
    return tuple(
        call(
            finish_kernel,
            [shape((1, modes), F32), shape(field, F32)],
            [VMEM] * (10 + len(blocks)),
            [
                pltpu.VMEM((subs, modes), F32),
                pltpu.VMEM((modes, layers), F32),
                pltpu.VMEM(plane, F32),
            ],
            flops=10_000_000,
            moved=5 << 20,
        )(
            *blocks, *wide, outer_last, picked, terms, weights, inner_face,
            outer_face, resid,
        )
    )


def solution(mesh):
    in_specs = (P("pln", None, "sub"), P(), P(None, "pln", None, "sub"), P("pln", None, "sub"))
    out_specs = (P("sub", None), P("pln", None, "sub"))
    return jax.shard_map(body, mesh=mesh, in_specs=in_specs, out_specs=out_specs, check_vma=False)
```

```python
import jax
import jax.numpy as jnp
from jax import lax
from jax.experimental import pallas as pl
from jax.experimental.pallas import tpu as pltpu
from jax.sharding import PartitionSpec as P

CITERS = 2
STEP = 16
MODES = 8
CHUNK = 16
F32 = jnp.float32
BF16 = jnp.bfloat16
PRECISE = lax.Precision.HIGHEST
NT = (((1,), (1,)), ((), ()))
TN = (((0,), (0,)), ((), ()))
VMEM = pl.BlockSpec(memory_space=pltpu.VMEM)
HBM = pl.BlockSpec(memory_space=pltpu.HBM)
ANY = pl.BlockSpec(memory_space=pl.ANY)


def call(kernel, outs, specs, scratch=(), flops=0, moved=0, limit=32, aliases=None):
    return pl.pallas_call(
        kernel,
        out_shape=outs,
        in_specs=specs,
        out_specs=[ANY if at in (aliases or {}).values() else VMEM for at in range(len(outs))],
        input_output_aliases=aliases or {},
        scratch_shapes=list(scratch),
        cost_estimate=pl.CostEstimate(flops=flops, bytes_accessed=moved, transcendentals=0),
        compiler_params=pltpu.CompilerParams(vmem_limit_bytes=limit << 20),
    )


def here_on(axis):
    return lax.axis_index(axis).astype(jnp.int32)


def ends_the_line():
    p = here_on("pln")
    return (p == 0) | (p == lax.axis_size("pln") - 1)


def harmonic(left_value, right_value):
    return 2.0 * left_value * right_value / (left_value + right_value)


def coefficients(labels, levels_ref):
    weighted = jnp.zeros(labels.shape, F32)
    for level in range(levels_ref.shape[1]):
        weighted = weighted + jnp.where(labels == level, levels_ref[:, level:level + 1], 0.0)
    return weighted


def lane_is(shape, lane):
    return lax.broadcasted_iota(jnp.int32, shape, len(shape) - 1) == lane


def pick_row(lane, width):
    row = lax.broadcasted_iota(jnp.int32, (16, width), 0)
    return ((row == 0) & lane_is((16, width), lane)).astype(BF16)


def stage_kernel(labels_far, zvec, inner_send, first_part, second_part, labels, label_sem, sems):
    modes, planes, rows, layers = zvec.shape
    quarter = second_part.shape[1]
    side = lax.rem(here_on("pln"), 2)
    start = pl.multiple_of((1 - side) * (rows // 2), quarter)
    label_copy = pltpu.make_async_copy(labels_far, labels, label_sem)
    copies = [
        pltpu.make_async_copy(
            zvec.at[:, side, pl.ds(start + index * quarter, quarter), :], out.at[pl.ds(0, modes)],
            sems.at[index],
        )
        for index, out in enumerate((first_part, second_part))
    ]
    copies.append(
        pltpu.make_async_copy(zvec.at[:, 1 - side], inner_send.at[pl.ds(0, modes)], sems.at[2])
    )
    label_copy.start()
    for copy in copies:
        copy.start()
    label_copy.wait()
    first_part[modes:] = labels[side].astype(F32).astype(BF16).reshape(rows // quarter, quarter, layers)
    inner_send[modes] = labels[1 - side].astype(F32).astype(BF16)
    for copy in copies:
        copy.wait()


def prepare_kernel(labels, held, outer_rest, one_pack, two_pack):
    modes, planes, rows, layers = held.shape
    half = rows // 2
    width = planes * rows
    side = lax.rem(here_on("pln"), 2)
    odd = lax.rem(here_on("sub"), 2) == 1
    one_lane = jnp.where(odd, 0, layers - 1)
    two_lane = jnp.where(odd, layers - 1, 0)
    row = lax.broadcasted_iota(jnp.int32, (16, layers), 0)
    both = ((row == 0) & lane_is((16, layers), one_lane)) | ((row == 1) & lane_is((16, layers), two_lane))
    both = both.astype(BF16)
    flat = labels[...].astype(F32).astype(BF16).reshape(width, layers)
    for out, lane in ((one_pack, one_lane), (two_pack, two_lane)):
        out[modes:modes + 16] = lax.dot_general(
            pick_row(lane, layers), flat, NT, preferred_element_type=F32
        ).astype(BF16)
    two_pack[modes + 16:] = jnp.zeros((16, width), BF16)
    for k in range(0, modes, CHUNK):
        at = slice(k, k + CHUNK)
        ends = lax.dot_general(
            both, held[at].reshape(-1, layers), NT, preferred_element_type=F32
        )
        for out, index in ((one_pack, 0), (two_pack, 1)):
            out[at] = jnp.concatenate(
                [ends[index:index + 1, j * width:(j + 1) * width] for j in range(CHUNK)], axis=0
            ).astype(BF16)
        outer_rest[at] = held[at, side, pl.ds(pl.multiple_of(side * half, half), half), :]


def release_kernel(after, outer_rest, outer_out):
    pass


def block_kernel(
    levels, labels, resid, zvec, after, partial, weights, here, half_diag, link_y, link_z,
):
    planes, rows, layers = labels.shape
    modes = here.shape[2]
    side = lax.rem(here_on("pln"), 2)
    at_edge = ends_the_line()
    held = (1 - side, side)

    def turn_rows(start):
        for slot, plane in enumerate(held):
            for k in range(0, modes, CHUNK):
                block = zvec[k:k + CHUNK, plane, pl.ds(start, STEP), :]
                here[slot, pl.ds(start, STEP), k:k + CHUNK, :] = jnp.swapaxes(block, 0, 1)

    turn_rows(0)
    coef = [coefficients(labels[x], levels) for x in held]
    middle = harmonic(coef[0], coef[1])
    weights[0] = middle
    row = lax.broadcasted_iota(jnp.int32, (rows, layers), 0)
    lane = lax.broadcasted_iota(jnp.int32, (rows, layers), 1)
    for x in range(2):
        c = coef[x]
        up_y = harmonic(c, jnp.where(row == rows - 1, c, pltpu.roll(c, rows - 1, 0)))
        up_z = harmonic(c, pltpu.roll(c, layers - 1, 1))
        down_y = jnp.where(row == 0, c, pltpu.roll(up_y, 1, 0))
        weights[1 + x] = up_y
        weights[3 + x] = up_z
        weights[5 + x] = c
        inner_z = jnp.where(lane == layers - 1, 0.0, up_z)
        total = middle + up_y + down_y + inner_z + pltpu.roll(inner_z, 1, 1)
        if x == 1:
            total = total + jnp.where(at_edge, c, 0.0)
        half_diag[x] = 0.5 * total
        link_y[x] = jnp.where(row == rows - 1, 0.0, up_y)
        link_z[x] = inner_z

    def step(j, carry):
        total, rhs, wide = carry
        turn_rows(pl.multiple_of(jnp.minimum((j + 1) * STEP, rows - STEP), STEP))
        for u in range(STEP):
            y = j * STEP + u
            at = pl.ds(y, 1)
            ahead = jnp.minimum(y + 1, rows - 1)
            up = [here[x, ahead].astype(F32) for x in range(2)]
            images = []
            for x in range(2):
                image = (
                    half_diag[x, at, :] * wide[x]
                    - link_y[x, at, :] * up[x]
                    - link_z[x, at, :] * pltpu.roll(wide[x], layers - 1, 1)
                )
                if x == 0:
                    image = image - weights[0, at, :] * wide[1]
                rhs = rhs + resid[held[x], at, :] * wide[x]
                images.append(image.astype(BF16))
            total = total + lax.dot_general(
                jnp.concatenate(images, axis=1),
                jnp.concatenate([here[0, y], here[1, y]], axis=1),
                NT,
                preferred_element_type=F32,
            )
            wide = up
        return total, rhs, wide

    total, rhs, _ = lax.fori_loop(
        0,
        rows // STEP,
        step,
        (
            jnp.zeros((modes, modes), F32),
            jnp.zeros((modes, layers), F32),
            [here[x, 0].astype(F32) for x in range(2)],
        ),
    )
    partial[:modes, :] = total
    partial[modes:, :] = lax.dot_general(
        jnp.ones((8, layers), F32), rhs, NT, precision=PRECISE, preferred_element_type=F32
    )


def turn(got, start, out):
    half, modes, layers = out.shape
    for k in range(0, modes, CHUNK):
        out[:, k:k + CHUNK, :] = jnp.swapaxes(got[k:k + CHUNK, pl.ds(start, half), :], 0, 1)


def face_product(weight_ref, base, own, other):
    half, modes, layers = other.shape

    def step(j, total):
        left, right = [], []
        for u in range(STEP):
            y = j * STEP + u
            weight = weight_ref[pl.ds(base + y, 1), :]
            image = weight * (own[base + y].astype(F32) - other[y].astype(F32))
            left.append(jnp.concatenate([own[base + y], other[y]], axis=0))
            right.append(image.astype(BF16))
        return total + lax.dot_general(
            jnp.concatenate(left, axis=1), jnp.concatenate(right, axis=1), NT,
            preferred_element_type=F32,
        )

    total = lax.fori_loop(0, half // STEP, step, jnp.zeros((2 * modes, modes), F32))
    return total[:modes] - total[modes:]


def inner_kernel(levels, partial, weights, here, inner_got, out, face, turned):
    planes, rows, modes, layers = here.shape
    half = rows // 2
    side = lax.rem(here_on("pln"), 2)
    base = pl.multiple_of(side * half, half)
    turn(inner_got, base, turned)
    face[...] = harmonic(weights[5], coefficients(inner_got[modes].astype(F32), levels))
    out[:modes, :] = partial[:modes, :] + 0.5 * face_product(face, base, here.at[0], turned)
    out[modes:, :] = partial[modes:, :]


def outer_kernel(levels, partial, weights, here, outer_got, out, face, face_here, turned):
    planes, rows, modes, layers = here.shape
    quarter = turned.shape[0]
    at_edge = ends_the_line()
    base = pl.multiple_of(lax.rem(here_on("pln"), 2) * (rows // 2), quarter)
    turn(outer_got, 0, turned)
    coef = coefficients(outer_got[modes:].astype(F32).reshape(rows, layers), levels)
    between = harmonic(weights[6], coef)
    face[...] = jnp.where(at_edge, weights[6], between)
    face_here[...] = jnp.where(at_edge, 0.0, between)
    out[:modes, :] = partial[:modes, :] + 0.5 * face_product(face_here, base, here.at[1], turned)
    out[modes:, :] = partial[modes:, :]


def last_kernel(
    levels, partial, face_here, here, outer_got, two_pack, one_pack, two_got, one_got, out, turned
):
    planes, rows, modes, layers = here.shape
    quarter = turned.shape[0]
    base = pl.multiple_of(lax.rem(here_on("pln"), 2) * (rows // 2) + quarter, quarter)
    turn(outer_got, 0, turned)
    cross = face_product(face_here, base, here.at[1], turned)
    odd = lax.rem(here_on("sub"), 2) == 1

    def coef_row(pack):
        return coefficients(pack[modes:modes + 16].astype(F32)[0:1], levels)

    one, two, one_other, two_other = (
        ref[:modes + 16].astype(F32) for ref in (one_pack, two_pack, one_got, two_got)
    )
    first, last = jnp.where(odd, one, two), jnp.where(odd, two, one)
    next_first = jnp.where(odd, two_other, one_other)
    prev_last = jnp.where(odd, one_other, two_other)
    weight_low = harmonic(coef_row(first), coef_row(prev_last))
    weight_high = harmonic(coef_row(last), coef_row(next_first))

    def product(left, right):
        return lax.dot_general(
            left.astype(BF16), right.astype(BF16), NT, preferred_element_type=F32
        )

    edge_rows = weight_high * last[:modes]
    ends = product(
        jnp.concatenate([weight_low * first[:modes], edge_rows], axis=1),
        jnp.concatenate([first[:modes], last[:modes]], axis=1),
    )
    square = partial[:modes, :] + 0.5 * (cross + ends)
    out[:modes, :modes] = square + square.T
    out[:modes, modes:] = -product(edge_rows, next_first[:modes])
    out[modes:, :modes] = partial[modes:, :]
    out[modes:, modes:] = jnp.zeros((8, modes), F32)


def terms_kernel(
    levels, pair, one_got, two_got, weights, inner_face, outer_face, terms, picked, coef_ref
):
    modes, width = picked.shape[1:]
    rows, layers = inner_face.shape
    side = lax.rem(here_on("pln"), 2)
    odd = lax.rem(here_on("sub"), 2) == 1
    one_other, two_other = (ref[:modes + 16].astype(F32) for ref in (one_got, two_got))
    next_first = jnp.where(odd, two_other, one_other)
    prev_last = jnp.where(odd, one_other, two_other)
    picked[0] = next_first[:modes]
    picked[1] = prev_last[:modes]
    end_labels = lax.dot_general(
        next_first[modes:].astype(BF16), pick_row(layers - 1, layers), TN, preferred_element_type=F32
    ) + lax.dot_general(
        prev_last[modes:].astype(BF16), pick_row(0, layers), TN, preferred_element_type=F32
    )
    coef_ref[...] = coefficients(end_labels, levels).reshape(width // rows, rows, layers)
    row = lax.broadcasted_iota(jnp.int32, (rows, layers), 0)
    lane = lax.broadcasted_iota(jnp.int32, (rows, layers), 1)
    for x, face in enumerate((inner_face, outer_face)):
        c = weights[5 + x]
        end_weight = harmonic(c, coef_ref[1 - side if x == 0 else side])
        up_y, up_z = weights[1 + x], weights[3 + x]
        down_y = jnp.where(row == 0, c, pltpu.roll(up_y, 1, 0))
        down_z = pltpu.roll(up_z, 1, 1)
        total = face[...] + weights[0] + up_y + down_y
        total = total + jnp.where(lane == layers - 1, end_weight, up_z)
        terms[x, 0] = total + jnp.where(lane == 0, end_weight, down_z)
        terms[x, 1] = jnp.where(row == 0, 0.0, down_y)
        terms[x, 2] = jnp.where(row == rows - 1, 0.0, up_y)
        terms[x, 3] = jnp.where(lane == 0, 0.0, down_z)
        terms[x, 4] = jnp.where(lane == layers - 1, 0.0, up_z)
        terms[x, 5] = end_weight


def pair_kernel(own, across, beside, oblique, out):
    modes = own.shape[1] // 2
    encode(own[...] + across[...], modes, out.at[0])
    encode(beside[...] + oblique[...], modes, out.at[1])


def single_kernel(own, out):
    encode(own[...], own.shape[1] // 2, out)


def encode(total, modes, out):
    row = lax.broadcasted_iota(jnp.int32, (modes, 2 * modes), 0)
    lane = lax.broadcasted_iota(jnp.int32, (modes, 2 * modes), 1)
    values = total[:modes]
    high = values.astype(BF16).astype(F32)
    low = values - high
    out[:modes] = jnp.where((lane <= row) | (lane >= modes), high, low).astype(BF16)
    diagonal = lane == row
    right = total[modes:modes + 1]
    parts = []
    for _ in range(3):
        part = right.astype(BF16).astype(F32)
        parts.append(part)
        right = right - part
    for part in (high, low):
        parts.append(jnp.sum(jnp.where(diagonal, part, 0.0), axis=0, keepdims=True))
    rows = lax.broadcasted_iota(jnp.int32, (16, 2 * modes), 0)
    extra = jnp.zeros((16, 2 * modes), F32)
    for index, part in enumerate(parts):
        extra = jnp.where(rows == index, part, extra)
    out[modes:] = extra.astype(BF16)


def widen_kernel(
    packed, zvec, inner_got, outer_got, outer_next, own_wide, inner_wide, outer_wide
):
    modes, half = outer_wide.shape[:2]
    quarter = half // 2
    side = lax.rem(here_on("pln"), 2)

    def some(j, carry):
        at = pl.ds(pl.multiple_of(j * MODES, MODES), MODES)
        own_wide[at, 0] = zvec[at, 1 - side].astype(F32)
        own_wide[at, 1] = zvec[at, side].astype(F32)
        inner_wide[at] = inner_got[at].astype(F32)
        outer_wide[at, :quarter, :] = outer_got[at].astype(F32)
        outer_wide[at, quarter:, :] = outer_next[at].astype(F32)
        return carry

    lax.fori_loop(0, modes // MODES, some, 0)


def finish_kernel(*refs):
    count = len(refs) - 15
    blocks, refs = refs[:count], refs[count:]
    zvec, inner_got, outer_got, outer_last, picked, terms, middle, inner_face, outer_face, resid = refs[:10]
    solution, deflated, direction_ref, spread, outer_field = refs[10:]
    subs = direction_ref.shape[0]
    modes, planes, rows, layers = zvec.shape
    half = rows // 2
    me = here_on("sub")
    side = lax.rem(here_on("pln"), 2)
    odd = lax.rem(me, 2) == 1
    at_edge = ends_the_line()
    held = (1 - side, side)
    square = (modes, modes)
    eye = lax.broadcasted_iota(jnp.int32, square, 0) == lax.broadcasted_iota(jnp.int32, square, 1)

    def column(row):
        return jnp.sum(jnp.where(eye, row, 0.0), axis=1, keepdims=True)

    def each(body, carry):
        for index, block in enumerate(blocks):
            held_here = block.shape[0]
            if held_here <= 8:
                for entry in range(held_here):
                    s = jnp.bitwise_xor(jnp.bitwise_xor(me, mask_of(index, len(blocks))), entry)
                    carry = body(block.at[entry], s, carry)
            else:
                carry = lax.fori_loop(
                    0, held_here, lambda entry, c, block=block: body(block.at[entry], entry, c), carry
                )
        return carry

    def row_is(s, width):
        return lax.broadcasted_iota(jnp.int32, (subs, width), 0) == s

    def load(block, s, carry):
        extra = block[modes:modes + 16, :].astype(F32)
        right = (extra[0:1] + extra[1:2]) + extra[2:3]
        here = row_is(s, 2 * modes)
        return jnp.where(here, right, carry[0]), jnp.where(here, extra[4:5] - extra[3:4], carry[1])

    empty = jnp.zeros((subs, 2 * modes), F32)
    right_side, fix = each(load, (empty, empty))
    fix = fix[:, :modes]

    def turned(rows_of, by):
        by = by % subs
        return jnp.concatenate([rows_of[by:], rows_of[:by]], axis=0)

    def in_parts(value):
        parts = []
        for _ in range(3):
            part = value.astype(BF16)
            parts.append(part.astype(F32))
            value = value - parts[-1]
        return jnp.concatenate(parts, axis=0).astype(BF16)

    def joined(value):
        return (value[:subs] + value[subs:2 * subs]) + value[2 * subs:]

    def coarse_apply(direction):
        pairs = in_parts(jnp.concatenate([direction, turned(direction, 1)], axis=1))
        single = pairs[:, :modes]

        def one(block, s, carry):
            values = block[:modes, :]
            ahead = lax.dot_general(pairs, values, NT, preferred_element_type=F32)
            image = jnp.dot(single, values, preferred_element_type=F32)
            return (
                jnp.where(row_is(s, modes), joined(ahead), carry[0]),
                jnp.where(row_is(s, 2 * modes), joined(image), carry[1]),
            )

        ahead, image = each(one, (jnp.zeros((subs, modes), F32), empty))
        return ahead + image[:, :modes] + fix * direction + turned(image[:, modes:], -1)

    def inner(left, right):
        return jnp.sum(jnp.sum(left * right, axis=0, keepdims=True), axis=1, keepdims=True)

    remain = right_side[:, :modes]
    direction = remain
    result = jnp.zeros_like(remain)
    norm_now = inner(remain, remain)
    for iteration in range(CITERS):
        image = coarse_apply(direction)
        step_size = norm_now / inner(direction, image)
        result = result + step_size * direction
        if iteration + 1 < CITERS:
            remain = remain - step_size * image
            norm_next = inner(remain, remain)
            direction = remain + (norm_next / norm_now) * direction
            norm_now = norm_next
    direction_ref[...] = result
    own = direction_ref[pl.ds(me, 1), :]
    solution[...] = own
    spread[...] = jnp.broadcast_to(column(own), (modes, layers))
    ahead_column = column(direction_ref[pl.ds(lax.rem(me + 1, subs), 1), :])
    behind_column = column(direction_ref[pl.ds(lax.rem(me + subs - 1, subs), 1), :])
    ahead_row = jnp.sum(ahead_column * picked[0], axis=0, keepdims=True)
    behind_row = jnp.sum(behind_column * picked[1], axis=0, keepdims=True)
    width = planes * rows
    both_rows = jnp.where(
        lax.broadcasted_iota(jnp.int32, (8, width), 0) == 0,
        jnp.broadcast_to(ahead_row, (8, width)),
        jnp.broadcast_to(behind_row, (8, width)),
    )
    columns = both_rows.T
    ends = jnp.where(
        lane_is((width, layers), layers - 1),
        columns[:, 0:1],
        jnp.where(lane_is((width, layers), 0), columns[:, 1:2], 0.0),
    ).reshape(planes, rows, layers)

    def add_mode(j, carry):
        fields, near, last = list(carry[0]), carry[1], carry[2]
        for u in range(MODES):
            k = j * MODES + u
            scale = spread[pl.ds(k, 1), :]
            for x, plane in enumerate((zvec[k, 0], zvec[k, 1], inner_got[k])):
                fields[x] = fields[x] + scale * plane
            near = near + scale * outer_got[k]
            last = last + scale * outer_last[k].astype(F32)
        return tuple(fields), near, last

    zero, short = jnp.zeros((rows, layers), F32), jnp.zeros((half, layers), F32)
    field, near, last = lax.fori_loop(0, modes // MODES, add_mode, ((zero,) * 3, short, short))
    outer_field[pl.ds(pl.multiple_of(side * half, half), half), :] = near
    outer_field[pl.ds(pl.multiple_of((1 - side) * half, half), half), :] = last
    outside = (field[2], jnp.where(at_edge, 0.0, outer_field[...]))
    faces = (inner_face[...], outer_face[...])
    for x in range(2):
        f = field[x]
        end_field = jnp.where(side == x, ends[1], ends[0])
        image = (
            terms[x, 0] * f
            - middle[0] * field[1 - x]
            - faces[x] * outside[x]
            - terms[x, 1] * pltpu.roll(f, 1, 0)
            - terms[x, 2] * pltpu.roll(f, rows - 1, 0)
            - terms[x, 3] * pltpu.roll(f, 1, 1)
            - terms[x, 4] * pltpu.roll(f, layers - 1, 1)
            - terms[x, 5] * end_field
        )
        deflated[held[x]] = resid[held[x]] - image


def swapped(value, axis, first):
    count = lax.axis_size(axis)
    pairs = []
    for i in range(count):
        up = (i - first) % 2 == 0
        pairs.append((i, (i + 1) % count if up else (i - 1) % count))
    return lax.ppermute(value, axis, pairs)


def swapped_all(value, mask=1):
    subs, count = lax.axis_size("sub"), lax.axis_size("pln")
    pairs = []
    for s in range(subs):
        for i in range(count):
            if 0 < i < count - 1:
                to = (s, i + 1 if i % 2 else i - 1)
            else:
                to = (s ^ mask, i)
            pairs.append((s * count + i, to[0] * count + to[1]))
    return lax.ppermute(value, ("sub", "pln"), pairs)


def exchanged(value, axis, mask):
    return lax.ppermute(value, axis, [(i, i ^ mask) for i in range(lax.axis_size(axis))])


def partner(value, sub_mask, pln_mask):
    subs, count = lax.axis_size("sub"), lax.axis_size("pln")
    pairs = [
        (s * count + p, (s ^ sub_mask) * count + (p ^ pln_mask)) for s in range(subs) for p in range(count)
    ]
    return lax.ppermute(value, ("sub", "pln"), pairs)


FAR = (4, 6)


def mask_of(index, count):
    if count == 1:
        return 0
    swap = lax.rem(here_on("pln"), 2) * (FAR[1] - FAR[0])
    return (0, FAR[0] + swap, 2, FAR[1] - swap)[index]


def far_partner(value):
    subs, count = lax.axis_size("sub"), lax.axis_size("pln")
    pairs = [(s * count + p, (s ^ FAR[p % 2]) * count + p) for s in range(subs) for p in range(count)]
    return lax.ppermute(value, ("sub", "pln"), pairs)


def body(labels, levels, zvec, resid):
    modes, planes, rows, layers = zvec.shape
    half = rows // 2
    subs, parts = lax.axis_size("sub"), lax.axis_size("pln")
    shape = jax.ShapeDtypeStruct
    levels = levels.reshape(1, -1)
    pack = shape((modes + 16, planes * rows), BF16)
    quarter = half // 2
    inner_send, first_part, second_part = call(
        stage_kernel,
        [
            shape((modes + 1, rows, layers), BF16),
            shape((modes + rows // quarter, quarter, layers), BF16),
            shape((modes, quarter, layers), BF16),
        ],
        [HBM, HBM],
        [pltpu.VMEM(labels.shape, jnp.int32), pltpu.SemaphoreType.DMA, pltpu.SemaphoreType.DMA((3,))],
        moved=2 << 20,
    )(*(pltpu.with_memory_space_constraint(v, pltpu.HBM) for v in (labels, zvec)))
    outer_got = swapped_all(first_part)
    outer_next = swapped_all(second_part, 2 if subs % 4 == 0 else 1)
    inner_got = swapped(inner_send, "pln", 0)
    rest = shape((modes, half, layers), BF16)
    outer_rest, one_pack, two_pack = call(
        prepare_kernel,
        [rest, pack, shape((modes + 32, planes * rows), BF16)],
        [VMEM, VMEM],
        flops=10_000_000,
        moved=6 << 20,
    )(labels, zvec)
    one_got = swapped(one_pack, "sub", 0)
    two_got = swapped(two_pack, "sub", 1)
    field = (planes, rows, layers)
    plane = (rows, layers)
    partial, weights, here = call(
        block_kernel,
        [
            shape((modes + 8, modes), F32),
            shape((7,) + plane, F32),
            shape((planes, rows, modes, layers), BF16),
        ],
        [VMEM] * 4 + [ANY],
        [pltpu.VMEM(field, F32)] * 3,
        flops=400_000_000,
        moved=3 << 20,
    )(levels, labels, resid, zvec, one_pack)
    turned = pltpu.VMEM((half, modes, layers), BF16)
    partial, inner_face = call(
        inner_kernel,
        [shape((modes + 8, modes), F32), shape(plane, F32)],
        [VMEM] * 5,
        [turned],
        flops=100_000_000,
        moved=1 << 20,
    )(levels, partial, weights, here, inner_got)
    turned = pltpu.VMEM((quarter, modes, layers), BF16)
    partial, outer_face, face_here = call(
        outer_kernel,
        [shape((modes + 8, modes), F32), shape(plane, F32), shape(plane, F32)],
        [VMEM] * 5,
        [turned],
        flops=100_000_000,
        moved=1 << 20,
    )(levels, partial, weights, here, outer_got)
    [block] = call(
        last_kernel,
        [shape((modes + 8, 2 * modes), F32)],
        [VMEM] * 9,
        [turned],
        flops=100_000_000,
        moved=1 << 20,
    )(levels, partial, face_here, here, outer_next, two_pack, one_pack, two_got, one_got)
    packed = (modes + 16, 2 * modes)
    if parts == 4 and subs == 8:
        block = block + exchanged(block, "pln", 1)
        others = [partner(block, *masks) for masks in ((0, 3), (1, 1), (1, 3))]
        [pair] = call(
            pair_kernel, [shape((2,) + packed, BF16)], [VMEM] * 4, flops=1 << 33
        )(block, *others)
        far = far_partner(pair)
        blocks = [pair, far, partner(pair, 2, 1), exchanged(far, "pln", 1)]
    else:
        [single] = call(single_kernel, [shape(packed, BF16)], [VMEM])(lax.psum(block, "pln"))
        blocks = [lax.all_gather(single, "sub")]
    [outer_rest] = call(release_kernel, [rest], [ANY] * 2, aliases={1: 0})(block, outer_rest)
    outer_last = swapped_all(outer_rest)
    terms, picked = call(
        terms_kernel,
        [shape((planes, 6) + plane, F32), shape((2, modes, planes * rows), F32)],
        [VMEM, ANY] + [VMEM] * 5,
        [pltpu.VMEM(field, F32)],

        flops=1 << 31,
        moved=1 << 20,
    )(levels, blocks[0], one_got, two_got, weights, inner_face, outer_face)
    wide = call(
        widen_kernel,
        [
            shape((modes,) + field, F32),
            shape((modes,) + plane, F32),
            shape((modes, half, layers), F32),
        ],
        [ANY] + [VMEM] * 4,
        flops=1 << 30,
        moved=1 << 20,
    )(blocks[0], zvec, inner_got, outer_got, outer_next)
    return tuple(
        call(
            finish_kernel,
            [shape((1, modes), F32), shape(field, F32)],
            [VMEM] * (10 + len(blocks)),
            [
                pltpu.VMEM((subs, modes), F32),
                pltpu.VMEM((modes, layers), F32),
                pltpu.VMEM(plane, F32),
            ],
            flops=10_000_000,
            moved=5 << 20,
        )(
            *blocks, *wide, outer_last, picked, terms, weights, inner_face,
            outer_face, resid,
        )
    )


def solution(mesh):
    in_specs = (P("pln", None, "sub"), P(), P(None, "pln", None, "sub"), P("pln", None, "sub"))
    out_specs = (P("sub", None), P("pln", None, "sub"))
    return jax.shard_map(body, mesh=mesh, in_specs=in_specs, out_specs=out_specs, check_vma=False)
```

```python
import jax
import jax.numpy as jnp
from jax import lax
from jax.experimental import pallas as pl
from jax.experimental.pallas import tpu as pltpu
from jax.sharding import PartitionSpec as P

CITERS = 2
STEP = 16
MODES = 8
CHUNK = 16
F32 = jnp.float32
BF16 = jnp.bfloat16
PRECISE = lax.Precision.HIGHEST
NT = (((1,), (1,)), ((), ()))
TN = (((0,), (0,)), ((), ()))
VMEM = pl.BlockSpec(memory_space=pltpu.VMEM)
HBM = pl.BlockSpec(memory_space=pltpu.HBM)
ANY = pl.BlockSpec(memory_space=pl.ANY)


def call(kernel, outs, specs, scratch=(), flops=0, moved=0, limit=32, aliases=None):
    return pl.pallas_call(
        kernel,
        out_shape=outs,
        in_specs=specs,
        out_specs=[ANY if at in (aliases or {}).values() else VMEM for at in range(len(outs))],
        input_output_aliases=aliases or {},
        scratch_shapes=list(scratch),
        cost_estimate=pl.CostEstimate(flops=flops, bytes_accessed=moved, transcendentals=0),
        compiler_params=pltpu.CompilerParams(vmem_limit_bytes=limit << 20),
    )


def here_on(axis):
    return lax.axis_index(axis).astype(jnp.int32)


def ends_the_line():
    p = here_on("pln")
    return (p == 0) | (p == lax.axis_size("pln") - 1)


def harmonic(left_value, right_value):
    return 2.0 * left_value * right_value / (left_value + right_value)


def coefficients(labels, levels_ref):
    weighted = jnp.zeros(labels.shape, F32)
    for level in range(levels_ref.shape[1]):
        weighted = weighted + jnp.where(labels == level, levels_ref[:, level:level + 1], 0.0)
    return weighted


def lane_is(shape, lane):
    return lax.broadcasted_iota(jnp.int32, shape, len(shape) - 1) == lane


def pick_row(lane, width):
    row = lax.broadcasted_iota(jnp.int32, (16, width), 0)
    return ((row == 0) & lane_is((16, width), lane)).astype(BF16)


def stage_kernel(labels_far, zvec, inner_send, outer_near, labels, label_sem, sems):
    modes, planes, rows, layers = zvec.shape
    half = rows // 2
    side = lax.rem(here_on("pln"), 2)
    start = pl.multiple_of((1 - side) * half, half)
    label_copy = pltpu.make_async_copy(labels_far, labels, label_sem)
    copies = [
        pltpu.make_async_copy(
            zvec.at[:, side, pl.ds(start, half), :], outer_near.at[pl.ds(0, modes)], sems.at[0]
        ),
        pltpu.make_async_copy(zvec.at[:, 1 - side], inner_send.at[pl.ds(0, modes)], sems.at[1]),
    ]
    label_copy.start()
    for copy in copies:
        copy.start()
    label_copy.wait()
    outer_near[modes:] = labels[side].astype(F32).astype(BF16).reshape(rows // half, half, layers)
    inner_send[modes] = labels[1 - side].astype(F32).astype(BF16)
    for copy in copies:
        copy.wait()


def release_kernel(after, outer_rest, outer_out):
    pass


def prepare_kernel(labels, held, outer_rest, one_pack, two_pack):
    modes, planes, rows, layers = held.shape
    half = rows // 2
    width = planes * rows
    side = lax.rem(here_on("pln"), 2)
    odd = lax.rem(here_on("sub"), 2) == 1
    one_lane = jnp.where(odd, 0, layers - 1)
    two_lane = jnp.where(odd, layers - 1, 0)
    row = lax.broadcasted_iota(jnp.int32, (16, layers), 0)
    both = ((row == 0) & lane_is((16, layers), one_lane)) | ((row == 1) & lane_is((16, layers), two_lane))
    both = both.astype(BF16)
    flat = labels[...].astype(F32).astype(BF16).reshape(width, layers)
    for out, lane in ((one_pack, one_lane), (two_pack, two_lane)):
        out[modes:] = lax.dot_general(
            pick_row(lane, layers), flat, NT, preferred_element_type=F32
        ).astype(BF16)
    for k in range(0, modes, CHUNK):
        at = slice(k, k + CHUNK)
        ends = lax.dot_general(
            both, held[at].reshape(-1, layers), NT, preferred_element_type=F32
        )
        for out, index in ((one_pack, 0), (two_pack, 1)):
            out[at] = jnp.concatenate(
                [ends[index:index + 1, j * width:(j + 1) * width] for j in range(CHUNK)], axis=0
            ).astype(BF16)
        outer_rest[at] = held[at, side, pl.ds(pl.multiple_of(side * half, half), half), :]


def block_kernel(
    levels, labels, resid, zvec, after, partial, weights, here, half_diag, link_y, link_z,
):
    planes, rows, layers = labels.shape
    modes = here.shape[2]
    side = lax.rem(here_on("pln"), 2)
    at_edge = ends_the_line()
    held = (1 - side, side)

    def turn_rows(start):
        for slot, plane in enumerate(held):
            for k in range(0, modes, CHUNK):
                block = zvec[k:k + CHUNK, plane, pl.ds(start, STEP), :]
                here[slot, pl.ds(start, STEP), k:k + CHUNK, :] = jnp.swapaxes(block, 0, 1)

    turn_rows(0)
    coef = [coefficients(labels[x], levels) for x in held]
    middle = harmonic(coef[0], coef[1])
    weights[0] = middle
    row = lax.broadcasted_iota(jnp.int32, (rows, layers), 0)
    lane = lax.broadcasted_iota(jnp.int32, (rows, layers), 1)
    for x in range(2):
        c = coef[x]
        up_y = harmonic(c, jnp.where(row == rows - 1, c, pltpu.roll(c, rows - 1, 0)))
        up_z = harmonic(c, pltpu.roll(c, layers - 1, 1))
        down_y = jnp.where(row == 0, c, pltpu.roll(up_y, 1, 0))
        weights[1 + x] = up_y
        weights[3 + x] = up_z
        weights[5 + x] = c
        inner_z = jnp.where(lane == layers - 1, 0.0, up_z)
        total = middle + up_y + down_y + inner_z + pltpu.roll(inner_z, 1, 1)
        if x == 1:
            total = total + jnp.where(at_edge, c, 0.0)
        half_diag[x] = 0.5 * total
        link_y[x] = jnp.where(row == rows - 1, 0.0, up_y)
        link_z[x] = inner_z

    def step(j, carry):
        total, wide = carry
        turn_rows(pl.multiple_of(jnp.minimum((j + 1) * STEP, rows - STEP), STEP))
        for u in range(STEP):
            y = j * STEP + u
            at = pl.ds(y, 1)
            ahead = jnp.minimum(y + 1, rows - 1)
            up = [here[x, ahead].astype(F32) for x in range(2)]
            images, parts = [], []
            for x in range(2):
                image = (
                    half_diag[x, at, :] * wide[x]
                    - link_y[x, at, :] * up[x]
                    - link_z[x, at, :] * pltpu.roll(wide[x], layers - 1, 1)
                )
                if x == 0:
                    image = image - weights[0, at, :] * wide[1]
                images.append(image.astype(BF16))
                value = resid[held[x], at, :]
                high = value.astype(BF16).astype(F32)
                part = jnp.where(part_row == 0, high, jnp.where(part_row == 1, value - high, 0.0))
                parts.append(part.astype(BF16))
            total = total + lax.dot_general(
                jnp.concatenate(
                    [jnp.concatenate(images, axis=1), jnp.concatenate(parts, axis=1)], axis=0
                ),
                jnp.concatenate([here[0, y], here[1, y]], axis=1),
                NT,
                preferred_element_type=F32,
            )
            wide = up
        return total, wide

    part_row = lax.broadcasted_iota(jnp.int32, (16, layers), 0)
    total, _ = lax.fori_loop(
        0,
        rows // STEP,
        step,
        (
            jnp.zeros((modes + 16, modes), F32),
            [here[x, 0].astype(F32) for x in range(2)],
        ),
    )
    partial[:modes, :] = total[:modes]
    partial[modes:, :] = jnp.broadcast_to(total[modes:modes + 1] + total[modes + 1:modes + 2], (8, modes))


def turn(got, start, out):
    half, modes, layers = out.shape
    for k in range(0, modes, CHUNK):
        out[:, k:k + CHUNK, :] = jnp.swapaxes(got[k:k + CHUNK, pl.ds(start, half), :], 0, 1)


def face_product(weight_ref, base, own, other):
    half, modes, layers = other.shape

    def step(j, total):
        left, right = [], []
        for u in range(STEP):
            y = j * STEP + u
            weight = weight_ref[pl.ds(base + y, 1), :]
            image = weight * (own[base + y].astype(F32) - other[y].astype(F32))
            left.append(jnp.concatenate([own[base + y], other[y]], axis=0))
            right.append(image.astype(BF16))
        return total + lax.dot_general(
            jnp.concatenate(left, axis=1), jnp.concatenate(right, axis=1), NT,
            preferred_element_type=F32,
        )

    total = lax.fori_loop(0, half // STEP, step, jnp.zeros((2 * modes, modes), F32))
    return total[:modes] - total[modes:]


def inner_kernel(levels, partial, weights, here, inner_got, out, face, turned):
    planes, rows, modes, layers = here.shape
    half = rows // 2
    side = lax.rem(here_on("pln"), 2)
    base = pl.multiple_of(side * half, half)
    turn(inner_got, base, turned)
    face[...] = harmonic(weights[5], coefficients(inner_got[modes].astype(F32), levels))
    out[:modes, :] = partial[:modes, :] + 0.5 * face_product(face, base, here.at[0], turned)
    out[modes:, :] = partial[modes:, :]


def outer_kernel(
    levels, partial, weights, here, outer_got, one_pack, two_pack, one_got, two_got,
    out, face, turned, face_here,
):
    planes, rows, modes, layers = here.shape
    half = rows // 2
    side = lax.rem(here_on("pln"), 2)
    at_edge = ends_the_line()
    base = pl.multiple_of(side * half, half)
    turn(outer_got, 0, turned)
    coef = coefficients(outer_got[modes:].astype(F32).reshape(rows, layers), levels)
    between = harmonic(weights[6], coef)
    face[...] = jnp.where(at_edge, weights[6], between)
    face_here[...] = jnp.where(at_edge, 0.0, between)
    cross = face_product(face_here, base, here.at[1], turned)
    odd = lax.rem(here_on("sub"), 2) == 1

    def coef_row(pack):
        return coefficients(pack[modes:modes + 16].astype(F32)[0:1], levels)

    one, two = one_pack[...].astype(F32), two_pack[...].astype(F32)
    one_other, two_other = one_got[...].astype(F32), two_got[...].astype(F32)
    first, last = jnp.where(odd, one, two), jnp.where(odd, two, one)
    next_first = jnp.where(odd, two_other, one_other)
    prev_last = jnp.where(odd, one_other, two_other)
    weight_low = harmonic(coef_row(first), coef_row(prev_last))
    weight_high = harmonic(coef_row(last), coef_row(next_first))

    def product(left, right):
        return lax.dot_general(
            left.astype(BF16), right.astype(BF16), NT, preferred_element_type=F32
        )

    edge_rows = weight_high * last[:modes]
    ends = product(
        jnp.concatenate([weight_low * first[:modes], edge_rows], axis=1),
        jnp.concatenate([first[:modes], last[:modes]], axis=1),
    )
    square = partial[:modes, :] + 0.5 * (cross + ends)
    out[:modes, :modes] = square + square.T
    out[:modes, modes:] = -product(edge_rows, next_first[:modes])
    out[modes:, :modes] = partial[modes:, :]
    out[modes:, modes:] = jnp.zeros((8, modes), F32)


def terms_kernel(
    levels, pair, one_got, two_got, weights, inner_face, outer_face, terms, picked, coef_ref
):
    modes, width = picked.shape[1:]
    rows, layers = inner_face.shape
    side = lax.rem(here_on("pln"), 2)
    odd = lax.rem(here_on("sub"), 2) == 1
    one_other, two_other = one_got[...].astype(F32), two_got[...].astype(F32)
    next_first = jnp.where(odd, two_other, one_other)
    prev_last = jnp.where(odd, one_other, two_other)
    picked[0] = next_first[:modes]
    picked[1] = prev_last[:modes]
    end_labels = lax.dot_general(
        next_first[modes:].astype(BF16), pick_row(layers - 1, layers), TN, preferred_element_type=F32
    ) + lax.dot_general(
        prev_last[modes:].astype(BF16), pick_row(0, layers), TN, preferred_element_type=F32
    )
    coef_ref[...] = coefficients(end_labels, levels).reshape(width // rows, rows, layers)
    row = lax.broadcasted_iota(jnp.int32, (rows, layers), 0)
    lane = lax.broadcasted_iota(jnp.int32, (rows, layers), 1)
    for x, face in enumerate((inner_face, outer_face)):
        c = weights[5 + x]
        end_weight = harmonic(c, coef_ref[1 - side if x == 0 else side])
        up_y, up_z = weights[1 + x], weights[3 + x]
        down_y = jnp.where(row == 0, c, pltpu.roll(up_y, 1, 0))
        down_z = pltpu.roll(up_z, 1, 1)
        total = face[...] + weights[0] + up_y + down_y
        total = total + jnp.where(lane == layers - 1, end_weight, up_z)
        terms[x, 0] = total + jnp.where(lane == 0, end_weight, down_z)
        terms[x, 1] = jnp.where(row == 0, 0.0, down_y)
        terms[x, 2] = jnp.where(row == rows - 1, 0.0, up_y)
        terms[x, 3] = jnp.where(lane == 0, 0.0, down_z)
        terms[x, 4] = jnp.where(lane == layers - 1, 0.0, up_z)
        terms[x, 5] = end_weight


def pair_kernel(own, across, beside, oblique, out):
    modes = own.shape[1] // 2
    encode(own[...] + across[...], modes, out.at[0])
    encode(beside[...] + oblique[...], modes, out.at[1])


def single_kernel(own, out):
    encode(own[...], own.shape[1] // 2, out)


def encode(total, modes, out):
    row = lax.broadcasted_iota(jnp.int32, (modes, 2 * modes), 0)
    lane = lax.broadcasted_iota(jnp.int32, (modes, 2 * modes), 1)
    values = total[:modes]
    high = values.astype(BF16).astype(F32)
    low = values - high
    out[:modes] = jnp.where((lane <= row) | (lane >= modes), high, low).astype(BF16)
    diagonal = lane == row
    right = total[modes:modes + 1]
    parts = []
    for _ in range(3):
        part = right.astype(BF16).astype(F32)
        parts.append(part)
        right = right - part
    for part in (high, low):
        parts.append(jnp.sum(jnp.where(diagonal, part, 0.0), axis=0, keepdims=True))
    rows = lax.broadcasted_iota(jnp.int32, (16, 2 * modes), 0)
    extra = jnp.zeros((16, 2 * modes), F32)
    for index, part in enumerate(parts):
        extra = jnp.where(rows == index, part, extra)
    out[modes:] = extra.astype(BF16)


def widen_kernel(pair, zvec, inner_got, outer_got, own_wide, inner_wide, outer_wide):
    modes, half = outer_wide.shape[:2]
    side = lax.rem(here_on("pln"), 2)

    def some(j, carry):
        at = pl.ds(pl.multiple_of(j * MODES, MODES), MODES)
        own_wide[at, 0] = zvec[at, 1 - side].astype(F32)
        own_wide[at, 1] = zvec[at, side].astype(F32)
        inner_wide[at] = inner_got[at].astype(F32)
        outer_wide[at] = outer_got[at].astype(F32)
        return carry

    lax.fori_loop(0, modes // MODES, some, 0)


def finish_kernel(*refs):
    count = len(refs) - 15
    blocks, refs = refs[:count], refs[count:]
    zvec, inner_got, outer_got, outer_last, picked, terms, middle, inner_face, outer_face, resid = refs[:10]
    solution, deflated, direction_ref, spread, outer_field = refs[10:]
    subs = direction_ref.shape[0]
    modes, planes, rows, layers = zvec.shape
    half = rows // 2
    me = here_on("sub")
    side = lax.rem(here_on("pln"), 2)
    odd = lax.rem(me, 2) == 1
    at_edge = ends_the_line()
    held = (1 - side, side)
    square = (modes, modes)
    eye = lax.broadcasted_iota(jnp.int32, square, 0) == lax.broadcasted_iota(jnp.int32, square, 1)

    def column(row):
        return jnp.sum(jnp.where(eye, row, 0.0), axis=1, keepdims=True)

    def each(body, carry):
        for index, block in enumerate(blocks):
            held_here = block.shape[0]
            if held_here <= 8:
                for entry in range(held_here):
                    s = jnp.bitwise_xor(jnp.bitwise_xor(me, mask_of(index, len(blocks))), entry)
                    carry = body(block.at[entry], s, carry)
            else:
                carry = lax.fori_loop(
                    0, held_here, lambda entry, c, block=block: body(block.at[entry], entry, c), carry
                )
        return carry

    def row_is(s, width):
        return lax.broadcasted_iota(jnp.int32, (subs, width), 0) == s

    def load(block, s, carry):
        extra = block[modes:modes + 16, :].astype(F32)
        right = (extra[0:1] + extra[1:2]) + extra[2:3]
        here = row_is(s, 2 * modes)
        return jnp.where(here, right, carry[0]), jnp.where(here, extra[4:5] - extra[3:4], carry[1])

    empty = jnp.zeros((subs, 2 * modes), F32)
    right_side, fix = each(load, (empty, empty))
    fix = fix[:, :modes]

    def turned(rows_of, by):
        by = by % subs
        return jnp.concatenate([rows_of[by:], rows_of[:by]], axis=0)

    def in_parts(value):
        parts = []
        for _ in range(3):
            part = value.astype(BF16)
            parts.append(part.astype(F32))
            value = value - parts[-1]
        return jnp.concatenate(parts, axis=0).astype(BF16)

    def joined(value):
        return (value[:subs] + value[subs:2 * subs]) + value[2 * subs:]

    def coarse_apply(direction):
        pairs = in_parts(jnp.concatenate([direction, turned(direction, 1)], axis=1))
        single = pairs[:, :modes]

        def one(block, s, carry):
            values = block[:modes, :]
            ahead = lax.dot_general(pairs, values, NT, preferred_element_type=F32)
            image = jnp.dot(single, values, preferred_element_type=F32)
            return (
                jnp.where(row_is(s, modes), joined(ahead), carry[0]),
                jnp.where(row_is(s, 2 * modes), joined(image), carry[1]),
            )

        ahead, image = each(one, (jnp.zeros((subs, modes), F32), empty))
        return ahead + image[:, :modes] + fix * direction + turned(image[:, modes:], -1)

    def inner(left, right):
        return jnp.sum(jnp.sum(left * right, axis=0, keepdims=True), axis=1, keepdims=True)

    remain = right_side[:, :modes]
    direction = remain
    result = jnp.zeros_like(remain)
    norm_now = inner(remain, remain)
    for iteration in range(CITERS):
        image = coarse_apply(direction)
        step_size = norm_now / inner(direction, image)
        result = result + step_size * direction
        if iteration + 1 < CITERS:
            remain = remain - step_size * image
            norm_next = inner(remain, remain)
            direction = remain + (norm_next / norm_now) * direction
            norm_now = norm_next
    direction_ref[...] = result
    own = direction_ref[pl.ds(me, 1), :]
    solution[...] = own
    spread[...] = jnp.broadcast_to(column(own), (modes, layers))
    ahead_column = column(direction_ref[pl.ds(lax.rem(me + 1, subs), 1), :])
    behind_column = column(direction_ref[pl.ds(lax.rem(me + subs - 1, subs), 1), :])
    ahead_row = jnp.sum(ahead_column * picked[0], axis=0, keepdims=True)
    behind_row = jnp.sum(behind_column * picked[1], axis=0, keepdims=True)
    width = planes * rows
    both_rows = jnp.where(
        lax.broadcasted_iota(jnp.int32, (8, width), 0) == 0,
        jnp.broadcast_to(ahead_row, (8, width)),
        jnp.broadcast_to(behind_row, (8, width)),
    )
    columns = both_rows.T
    ends = jnp.where(
        lane_is((width, layers), layers - 1),
        columns[:, 0:1],
        jnp.where(lane_is((width, layers), 0), columns[:, 1:2], 0.0),
    ).reshape(planes, rows, layers)

    def add_mode(j, carry):
        fields, near, last = list(carry[0]), carry[1], carry[2]
        for u in range(MODES):
            k = j * MODES + u
            scale = spread[pl.ds(k, 1), :]
            for x, plane in enumerate((zvec[k, 0], zvec[k, 1], inner_got[k])):
                fields[x] = fields[x] + scale * plane
            near = near + scale * outer_got[k]
            last = last + scale * outer_last[k].astype(F32)
        return tuple(fields), near, last

    zero, short = jnp.zeros((rows, layers), F32), jnp.zeros((half, layers), F32)
    field, near, last = lax.fori_loop(0, modes // MODES, add_mode, ((zero,) * 3, short, short))
    outer_field[pl.ds(pl.multiple_of(side * half, half), half), :] = near
    outer_field[pl.ds(pl.multiple_of((1 - side) * half, half), half), :] = last
    outside = (field[2], jnp.where(at_edge, 0.0, outer_field[...]))
    faces = (inner_face[...], outer_face[...])
    for x in range(2):
        f = field[x]
        end_field = jnp.where(side == x, ends[1], ends[0])
        image = (
            terms[x, 0] * f
            - middle[0] * field[1 - x]
            - faces[x] * outside[x]
            - terms[x, 1] * pltpu.roll(f, 1, 0)
            - terms[x, 2] * pltpu.roll(f, rows - 1, 0)
            - terms[x, 3] * pltpu.roll(f, 1, 1)
            - terms[x, 4] * pltpu.roll(f, layers - 1, 1)
            - terms[x, 5] * end_field
        )
        deflated[held[x]] = resid[held[x]] - image


def swapped(value, axis, first):
    count = lax.axis_size(axis)
    pairs = []
    for i in range(count):
        up = (i - first) % 2 == 0
        pairs.append((i, (i + 1) % count if up else (i - 1) % count))
    return lax.ppermute(value, axis, pairs)


def swapped_all(value):
    subs, count = lax.axis_size("sub"), lax.axis_size("pln")
    pairs = []
    for s in range(subs):
        for i in range(count):
            if 0 < i < count - 1:
                to = (s, i + 1 if i % 2 else i - 1)
            else:
                to = (s ^ 1, i)
            pairs.append((s * count + i, to[0] * count + to[1]))
    return lax.ppermute(value, ("sub", "pln"), pairs)


def exchanged(value, axis, mask):
    return lax.ppermute(value, axis, [(i, i ^ mask) for i in range(lax.axis_size(axis))])


def partner(value, sub_mask, pln_mask):
    subs, count = lax.axis_size("sub"), lax.axis_size("pln")
    pairs = [
        (s * count + p, (s ^ sub_mask) * count + (p ^ pln_mask)) for s in range(subs) for p in range(count)
    ]
    return lax.ppermute(value, ("sub", "pln"), pairs)


FAR = (4, 6)


def mask_of(index, count):
    if count == 1:
        return 0
    swap = far_role(here_on("sub"), here_on("pln")) * (FAR[1] - FAR[0])
    return (0, FAR[0] + swap, 2, FAR[1] - swap)[index]


def far_role(s, p):
    return (p ^ (s >> 2)) & 1


def far_partner(value):
    subs, count = lax.axis_size("sub"), lax.axis_size("pln")
    pairs = [
        (s * count + p, (s ^ FAR[far_role(s, p)]) * count + (p ^ 1)) for s in range(subs) for p in range(count)
    ]
    return lax.ppermute(value, ("sub", "pln"), pairs)


def body(labels, levels, zvec, resid):
    modes, planes, rows, layers = zvec.shape
    half = rows // 2
    subs, parts = lax.axis_size("sub"), lax.axis_size("pln")
    shape = jax.ShapeDtypeStruct
    levels = levels.reshape(1, -1)
    pack = shape((modes + 16, planes * rows), BF16)
    inner_send, outer_near = call(
        stage_kernel,
        [shape((modes + 1, rows, layers), BF16), shape((modes + rows // half, half, layers), BF16)],
        [HBM, HBM],
        [pltpu.VMEM(labels.shape, jnp.int32), pltpu.SemaphoreType.DMA, pltpu.SemaphoreType.DMA((2,))],
        moved=2 << 20,
    )(*(pltpu.with_memory_space_constraint(v, pltpu.HBM) for v in (labels, zvec)))
    outer_got = swapped_all(outer_near)
    inner_got = swapped(inner_send, "pln", 0)
    rest = shape((modes, half, layers), BF16)
    outer_rest, one_pack, two_pack = call(
        prepare_kernel,
        [rest, pack, pack],
        [VMEM, VMEM],
        flops=10_000_000,
        moved=6 << 20,
    )(labels, zvec)
    one_got = swapped(one_pack, "sub", 0)
    two_got = swapped(two_pack, "sub", 1)
    field = (planes, rows, layers)
    plane = (rows, layers)
    partial, weights, here = call(
        block_kernel,
        [
            shape((modes + 8, modes), F32),
            shape((7,) + plane, F32),
            shape((planes, rows, modes, layers), BF16),
        ],
        [VMEM] * 4 + [ANY],
        [pltpu.VMEM(field, F32)] * 3,
        flops=400_000_000,
        moved=3 << 20,
    )(levels, labels, resid, zvec, one_pack)
    turned = pltpu.VMEM((half, modes, layers), BF16)
    partial, inner_face = call(
        inner_kernel,
        [shape((modes + 8, modes), F32), shape(plane, F32)],
        [VMEM] * 5,
        [turned],
        flops=100_000_000,
        moved=1 << 20,
    )(levels, partial, weights, here, inner_got)
    block, outer_face = call(
        outer_kernel,
        [shape((modes + 8, 2 * modes), F32), shape(plane, F32)],
        [VMEM] * 9,
        [turned, pltpu.VMEM(plane, F32)],
        flops=100_000_000,
        moved=1 << 20,
    )(levels, partial, weights, here, outer_got, one_pack, two_pack, one_got, two_got)
    packed = (modes + 16, 2 * modes)
    if parts == 4 and subs == 8:
        block = block + exchanged(block, "pln", 1)
        others = [partner(block, *masks) for masks in ((0, 3), (1, 1), (1, 3))]
        [pair] = call(
            pair_kernel, [shape((2,) + packed, BF16)], [VMEM] * 4, flops=1 << 33
        )(block, *others)
        far = far_partner(pair)
        blocks = [pair, far, partner(pair, 2, 1), exchanged(far, "pln", 1)]
    else:
        [single] = call(single_kernel, [shape(packed, BF16)], [VMEM])(lax.psum(block, "pln"))
        blocks = [lax.all_gather(single, "sub")]
    [outer_rest] = call(release_kernel, [rest], [ANY] * 2, aliases={1: 0})(block, outer_rest)
    outer_last = swapped_all(outer_rest)
    terms, picked = call(
        terms_kernel,
        [shape((planes, 6) + plane, F32), shape((2, modes, planes * rows), F32)],
        [VMEM, ANY] + [VMEM] * 5,
        [pltpu.VMEM(field, F32)],

        flops=1 << 31,
        moved=1 << 20,
    )(levels, blocks[0], one_got, two_got, weights, inner_face, outer_face)
    wide = call(
        widen_kernel,
        [
            shape((modes,) + field, F32),
            shape((modes,) + plane, F32),
            shape((modes, half, layers), F32),
        ],
        [ANY] + [VMEM] * 3,
        flops=1 << 30,
        moved=1 << 20,
    )(blocks[0], zvec, inner_got, outer_got)
    return tuple(
        call(
            finish_kernel,
            [shape((1, modes), F32), shape(field, F32)],
            [VMEM] * (10 + len(blocks)),
            [
                pltpu.VMEM((subs, modes), F32),
                pltpu.VMEM((modes, layers), F32),
                pltpu.VMEM(plane, F32),
            ],
            flops=10_000_000,
            moved=5 << 20,
        )(
            *blocks, *wide, outer_last, picked, terms, weights, inner_face,
            outer_face, resid,
        )
    )


def solution(mesh):
    in_specs = (P("pln", None, "sub"), P(), P(None, "pln", None, "sub"), P("pln", None, "sub"))
    out_specs = (P("sub", None), P("pln", None, "sub"))
    return jax.shard_map(body, mesh=mesh, in_specs=in_specs, out_specs=out_specs, check_vma=False)
```

```python
import jax
import jax.numpy as jnp
from jax import lax
from jax.experimental import pallas as pl
from jax.experimental.pallas import tpu as pltpu
from jax.sharding import PartitionSpec as P

CITERS = 2
STEP = 16
MODES = 8
CHUNK = 16
F32 = jnp.float32
BF16 = jnp.bfloat16
PRECISE = lax.Precision.HIGHEST
NT = (((1,), (1,)), ((), ()))
TN = (((0,), (0,)), ((), ()))
VMEM = pl.BlockSpec(memory_space=pltpu.VMEM)
HBM = pl.BlockSpec(memory_space=pltpu.HBM)
ANY = pl.BlockSpec(memory_space=pl.ANY)


def call(kernel, outs, specs, scratch=(), flops=0, moved=0, limit=32, aliases=None):
    return pl.pallas_call(
        kernel,
        out_shape=outs,
        in_specs=specs,
        out_specs=[ANY if at in (aliases or {}).values() else VMEM for at in range(len(outs))],
        input_output_aliases=aliases or {},
        scratch_shapes=list(scratch),
        cost_estimate=pl.CostEstimate(flops=flops, bytes_accessed=moved, transcendentals=0),
        compiler_params=pltpu.CompilerParams(vmem_limit_bytes=limit << 20),
    )


def here_on(axis):
    return lax.axis_index(axis).astype(jnp.int32)


def ends_the_line():
    p = here_on("pln")
    return (p == 0) | (p == lax.axis_size("pln") - 1)


def harmonic(left_value, right_value):
    return 2.0 * left_value * right_value / (left_value + right_value)


def coefficients(labels, levels_ref):
    weighted = jnp.zeros(labels.shape, F32)
    for level in range(levels_ref.shape[1]):
        weighted = weighted + jnp.where(labels == level, levels_ref[:, level:level + 1], 0.0)
    return weighted


def lane_is(shape, lane):
    return lax.broadcasted_iota(jnp.int32, shape, len(shape) - 1) == lane


def pick_row(lane, width):
    row = lax.broadcasted_iota(jnp.int32, (16, width), 0)
    return ((row == 0) & lane_is((16, width), lane)).astype(BF16)


def stage_kernel(labels_far, zvec, inner_send, outer_near, labels, label_sem, sems):
    modes, planes, rows, layers = zvec.shape
    half = rows // 2
    side = lax.rem(here_on("pln"), 2)
    start = pl.multiple_of((1 - side) * half, half)
    label_copy = pltpu.make_async_copy(labels_far, labels, label_sem)
    copies = [
        pltpu.make_async_copy(
            zvec.at[:, side, pl.ds(start, half), :], outer_near.at[pl.ds(0, modes)], sems.at[0]
        ),
        pltpu.make_async_copy(zvec.at[:, 1 - side], inner_send.at[pl.ds(0, modes)], sems.at[1]),
    ]
    label_copy.start()
    for copy in copies:
        copy.start()
    label_copy.wait()
    outer_near[modes:] = labels[side].astype(F32).astype(BF16).reshape(rows // half, half, layers)
    inner_send[modes] = labels[1 - side].astype(F32).astype(BF16)
    for copy in copies:
        copy.wait()


def release_kernel(after, outer_rest, outer_out):
    pass


def prepare_kernel(labels, held, outer_rest, one_pack, two_pack):
    modes, planes, rows, layers = held.shape
    half = rows // 2
    width = planes * rows
    side = lax.rem(here_on("pln"), 2)
    odd = lax.rem(here_on("sub"), 2) == 1
    one_lane = jnp.where(odd, 0, layers - 1)
    two_lane = jnp.where(odd, layers - 1, 0)
    row = lax.broadcasted_iota(jnp.int32, (16, layers), 0)
    both = ((row == 0) & lane_is((16, layers), one_lane)) | ((row == 1) & lane_is((16, layers), two_lane))
    both = both.astype(BF16)
    flat = labels[...].astype(F32).astype(BF16).reshape(width, layers)
    for out, lane in ((one_pack, one_lane), (two_pack, two_lane)):
        out[modes:] = lax.dot_general(
            pick_row(lane, layers), flat, NT, preferred_element_type=F32
        ).astype(BF16)
    for k in range(0, modes, CHUNK):
        at = slice(k, k + CHUNK)
        ends = lax.dot_general(
            both, held[at].reshape(-1, layers), NT, preferred_element_type=F32
        )
        for out, index in ((one_pack, 0), (two_pack, 1)):
            out[at] = jnp.concatenate(
                [ends[index:index + 1, j * width:(j + 1) * width] for j in range(CHUNK)], axis=0
            ).astype(BF16)
        outer_rest[at] = held[at, side, pl.ds(pl.multiple_of(side * half, half), half), :]


def block_kernel(
    levels, labels, resid, zvec, after, partial, weights, here, half_diag, link_y, link_z,
):
    planes, rows, layers = labels.shape
    modes = here.shape[2]
    side = lax.rem(here_on("pln"), 2)
    at_edge = ends_the_line()
    held = (1 - side, side)

    def turn_rows(start):
        for slot, plane in enumerate(held):
            for k in range(0, modes, CHUNK):
                block = zvec[k:k + CHUNK, plane, pl.ds(start, STEP), :]
                here[slot, pl.ds(start, STEP), k:k + CHUNK, :] = jnp.swapaxes(block, 0, 1)

    turn_rows(0)
    coef = [coefficients(labels[x], levels) for x in held]
    middle = harmonic(coef[0], coef[1])
    weights[0] = middle
    row = lax.broadcasted_iota(jnp.int32, (rows, layers), 0)
    lane = lax.broadcasted_iota(jnp.int32, (rows, layers), 1)
    for x in range(2):
        c = coef[x]
        up_y = harmonic(c, jnp.where(row == rows - 1, c, pltpu.roll(c, rows - 1, 0)))
        up_z = harmonic(c, pltpu.roll(c, layers - 1, 1))
        down_y = jnp.where(row == 0, c, pltpu.roll(up_y, 1, 0))
        weights[1 + x] = up_y
        weights[3 + x] = up_z
        weights[5 + x] = c
        inner_z = jnp.where(lane == layers - 1, 0.0, up_z)
        total = middle + up_y + down_y + inner_z + pltpu.roll(inner_z, 1, 1)
        if x == 1:
            total = total + jnp.where(at_edge, c, 0.0)
        half_diag[x] = 0.5 * total
        link_y[x] = jnp.where(row == rows - 1, 0.0, up_y)
        link_z[x] = inner_z

    def step(j, carry):
        total, wide = carry
        turn_rows(pl.multiple_of(jnp.minimum((j + 1) * STEP, rows - STEP), STEP))
        for u in range(STEP):
            y = j * STEP + u
            at = pl.ds(y, 1)
            ahead = jnp.minimum(y + 1, rows - 1)
            up = [here[x, ahead].astype(F32) for x in range(2)]
            images, parts = [], []
            for x in range(2):
                image = (
                    half_diag[x, at, :] * wide[x]
                    - link_y[x, at, :] * up[x]
                    - link_z[x, at, :] * pltpu.roll(wide[x], layers - 1, 1)
                )
                if x == 0:
                    image = image - weights[0, at, :] * wide[1]
                images.append(image.astype(BF16))
                value = resid[held[x], at, :]
                high = value.astype(BF16).astype(F32)
                part = jnp.where(part_row == 0, high, jnp.where(part_row == 1, value - high, 0.0))
                parts.append(part.astype(BF16))
            total = total + lax.dot_general(
                jnp.concatenate(
                    [jnp.concatenate(images, axis=1), jnp.concatenate(parts, axis=1)], axis=0
                ),
                jnp.concatenate([here[0, y], here[1, y]], axis=1),
                NT,
                preferred_element_type=F32,
            )
            wide = up
        return total, wide

    part_row = lax.broadcasted_iota(jnp.int32, (16, layers), 0)
    total, _ = lax.fori_loop(
        0,
        rows // STEP,
        step,
        (
            jnp.zeros((modes + 16, modes), F32),
            [here[x, 0].astype(F32) for x in range(2)],
        ),
    )
    partial[:modes, :] = total[:modes]
    partial[modes:, :] = jnp.broadcast_to(total[modes:modes + 1] + total[modes + 1:modes + 2], (8, modes))


def turn(got, start, out):
    half, modes, layers = out.shape
    for k in range(0, modes, CHUNK):
        out[:, k:k + CHUNK, :] = jnp.swapaxes(got[k:k + CHUNK, pl.ds(start, half), :], 0, 1)


def face_product(weight_ref, base, own, other):
    half, modes, layers = other.shape

    def step(j, total):
        left, right = [], []
        for u in range(STEP):
            y = j * STEP + u
            weight = weight_ref[pl.ds(base + y, 1), :]
            image = weight * (own[base + y].astype(F32) - other[y].astype(F32))
            left.append(jnp.concatenate([own[base + y], other[y]], axis=0))
            right.append(image.astype(BF16))
        return total + lax.dot_general(
            jnp.concatenate(left, axis=1), jnp.concatenate(right, axis=1), NT,
            preferred_element_type=F32,
        )

    total = lax.fori_loop(0, half // STEP, step, jnp.zeros((2 * modes, modes), F32))
    return total[:modes] - total[modes:]


def inner_kernel(levels, partial, weights, here, inner_got, out, face, turned):
    planes, rows, modes, layers = here.shape
    half = rows // 2
    side = lax.rem(here_on("pln"), 2)
    base = pl.multiple_of(side * half, half)
    turn(inner_got, base, turned)
    face[...] = harmonic(weights[5], coefficients(inner_got[modes].astype(F32), levels))
    out[:modes, :] = partial[:modes, :] + 0.5 * face_product(face, base, here.at[0], turned)
    out[modes:, :] = partial[modes:, :]


def outer_kernel(
    levels, partial, weights, here, outer_got, one_pack, two_pack, one_got, two_got,
    out, face, turned, face_here,
):
    planes, rows, modes, layers = here.shape
    half = rows // 2
    side = lax.rem(here_on("pln"), 2)
    at_edge = ends_the_line()
    base = pl.multiple_of(side * half, half)
    turn(outer_got, 0, turned)
    coef = coefficients(outer_got[modes:].astype(F32).reshape(rows, layers), levels)
    between = harmonic(weights[6], coef)
    face[...] = jnp.where(at_edge, weights[6], between)
    face_here[...] = jnp.where(at_edge, 0.0, between)
    cross = face_product(face_here, base, here.at[1], turned)
    odd = lax.rem(here_on("sub"), 2) == 1

    def coef_row(pack):
        return coefficients(pack[modes:modes + 16].astype(F32)[0:1], levels)

    one, two = one_pack[...].astype(F32), two_pack[...].astype(F32)
    one_other, two_other = one_got[...].astype(F32), two_got[...].astype(F32)
    first, last = jnp.where(odd, one, two), jnp.where(odd, two, one)
    next_first = jnp.where(odd, two_other, one_other)
    prev_last = jnp.where(odd, one_other, two_other)
    weight_low = harmonic(coef_row(first), coef_row(prev_last))
    weight_high = harmonic(coef_row(last), coef_row(next_first))

    def product(left, right):
        return lax.dot_general(
            left.astype(BF16), right.astype(BF16), NT, preferred_element_type=F32
        )

    edge_rows = weight_high * last[:modes]
    ends = product(
        jnp.concatenate([weight_low * first[:modes], edge_rows], axis=1),
        jnp.concatenate([first[:modes], last[:modes]], axis=1),
    )
    square = partial[:modes, :] + 0.5 * (cross + ends)
    out[:modes, :modes] = square + square.T
    out[:modes, modes:] = -product(edge_rows, next_first[:modes])
    out[modes:, :modes] = partial[modes:, :]
    out[modes:, modes:] = jnp.zeros((8, modes), F32)


def terms_kernel(
    levels, pair, one_got, two_got, weights, inner_face, outer_face, terms, picked, coef_ref
):
    modes, width = picked.shape[1:]
    rows, layers = inner_face.shape
    side = lax.rem(here_on("pln"), 2)
    odd = lax.rem(here_on("sub"), 2) == 1
    one_other, two_other = one_got[...].astype(F32), two_got[...].astype(F32)
    next_first = jnp.where(odd, two_other, one_other)
    prev_last = jnp.where(odd, one_other, two_other)
    picked[0] = next_first[:modes]
    picked[1] = prev_last[:modes]
    end_labels = lax.dot_general(
        next_first[modes:].astype(BF16), pick_row(layers - 1, layers), TN, preferred_element_type=F32
    ) + lax.dot_general(
        prev_last[modes:].astype(BF16), pick_row(0, layers), TN, preferred_element_type=F32
    )
    coef_ref[...] = coefficients(end_labels, levels).reshape(width // rows, rows, layers)
    row = lax.broadcasted_iota(jnp.int32, (rows, layers), 0)
    lane = lax.broadcasted_iota(jnp.int32, (rows, layers), 1)
    for x, face in enumerate((inner_face, outer_face)):
        c = weights[5 + x]
        end_weight = harmonic(c, coef_ref[1 - side if x == 0 else side])
        up_y, up_z = weights[1 + x], weights[3 + x]
        down_y = jnp.where(row == 0, c, pltpu.roll(up_y, 1, 0))
        down_z = pltpu.roll(up_z, 1, 1)
        total = face[...] + weights[0] + up_y + down_y
        total = total + jnp.where(lane == layers - 1, end_weight, up_z)
        terms[x, 0] = total + jnp.where(lane == 0, end_weight, down_z)
        terms[x, 1] = jnp.where(row == 0, 0.0, down_y)
        terms[x, 2] = jnp.where(row == rows - 1, 0.0, up_y)
        terms[x, 3] = jnp.where(lane == 0, 0.0, down_z)
        terms[x, 4] = jnp.where(lane == layers - 1, 0.0, up_z)
        terms[x, 5] = end_weight


def pair_kernel(own, across, beside, oblique, out):
    modes = own.shape[1] // 2
    encode(own[...] + across[...], modes, out.at[0])
    encode(beside[...] + oblique[...], modes, out.at[1])


def single_kernel(own, out):
    encode(own[...], own.shape[1] // 2, out)


def encode(total, modes, out):
    row = lax.broadcasted_iota(jnp.int32, (modes, 2 * modes), 0)
    lane = lax.broadcasted_iota(jnp.int32, (modes, 2 * modes), 1)
    values = total[:modes]
    high = values.astype(BF16).astype(F32)
    low = values - high
    out[:modes] = jnp.where((lane <= row) | (lane >= modes), high, low).astype(BF16)
    diagonal = lane == row
    right = total[modes:modes + 1]
    parts = []
    for _ in range(3):
        part = right.astype(BF16).astype(F32)
        parts.append(part)
        right = right - part
    for part in (high, low):
        parts.append(jnp.sum(jnp.where(diagonal, part, 0.0), axis=0, keepdims=True))
    rows = lax.broadcasted_iota(jnp.int32, (16, 2 * modes), 0)
    extra = jnp.zeros((16, 2 * modes), F32)
    for index, part in enumerate(parts):
        extra = jnp.where(rows == index, part, extra)
    out[modes:] = extra.astype(BF16)


def widen_kernel(pair, zvec, inner_got, outer_got, own_wide, inner_wide, outer_wide):
    modes, half = outer_wide.shape[:2]
    side = lax.rem(here_on("pln"), 2)

    def some(j, carry):
        at = pl.ds(pl.multiple_of(j * MODES, MODES), MODES)
        own_wide[at, 0] = zvec[at, 1 - side].astype(F32)
        own_wide[at, 1] = zvec[at, side].astype(F32)
        inner_wide[at] = inner_got[at].astype(F32)
        outer_wide[at] = outer_got[at].astype(F32)
        return carry

    lax.fori_loop(0, modes // MODES, some, 0)


def finish_kernel(*refs):
    count = len(refs) - 15
    blocks, refs = refs[:count], refs[count:]
    zvec, inner_got, outer_got, outer_last, picked, terms, middle, inner_face, outer_face, resid = refs[:10]
    solution, deflated, direction_ref, spread, outer_field = refs[10:]
    subs = direction_ref.shape[0]
    modes, planes, rows, layers = zvec.shape
    half = rows // 2
    me = here_on("sub")
    side = lax.rem(here_on("pln"), 2)
    odd = lax.rem(me, 2) == 1
    at_edge = ends_the_line()
    held = (1 - side, side)
    square = (modes, modes)
    eye = lax.broadcasted_iota(jnp.int32, square, 0) == lax.broadcasted_iota(jnp.int32, square, 1)

    def column(row):
        return jnp.sum(jnp.where(eye, row, 0.0), axis=1, keepdims=True)

    def each(body, carry):
        for index, block in enumerate(blocks):
            held_here = block.shape[0]
            if held_here <= 8:
                for entry in range(held_here):
                    s = jnp.bitwise_xor(jnp.bitwise_xor(me, mask_of(index, len(blocks))), entry)
                    carry = body(block.at[entry], s, carry)
            else:
                carry = lax.fori_loop(
                    0, held_here, lambda entry, c, block=block: body(block.at[entry], entry, c), carry
                )
        return carry

    def row_is(s, width):
        return lax.broadcasted_iota(jnp.int32, (subs, width), 0) == s

    def load(block, s, carry):
        extra = block[modes:modes + 16, :].astype(F32)
        right = (extra[0:1] + extra[1:2]) + extra[2:3]
        here = row_is(s, 2 * modes)
        return jnp.where(here, right, carry[0]), jnp.where(here, extra[4:5] - extra[3:4], carry[1])

    empty = jnp.zeros((subs, 2 * modes), F32)
    right_side, fix = each(load, (empty, empty))
    fix = fix[:, :modes]

    def turned(rows_of, by):
        by = by % subs
        return jnp.concatenate([rows_of[by:], rows_of[:by]], axis=0)

    def in_parts(value):
        parts = []
        for _ in range(3):
            part = value.astype(BF16)
            parts.append(part.astype(F32))
            value = value - parts[-1]
        return jnp.concatenate(parts, axis=0).astype(BF16)

    def joined(value):
        return (value[:subs] + value[subs:2 * subs]) + value[2 * subs:]

    def coarse_apply(direction):
        pairs = in_parts(jnp.concatenate([direction, turned(direction, 1)], axis=1))
        single = pairs[:, :modes]

        def one(block, s, carry):
            values = block[:modes, :]
            ahead = lax.dot_general(pairs, values, NT, preferred_element_type=F32)
            image = jnp.dot(single, values, preferred_element_type=F32)
            return (
                jnp.where(row_is(s, modes), joined(ahead), carry[0]),
                jnp.where(row_is(s, 2 * modes), joined(image), carry[1]),
            )

        ahead, image = each(one, (jnp.zeros((subs, modes), F32), empty))
        return ahead + image[:, :modes] + fix * direction + turned(image[:, modes:], -1)

    def inner(left, right):
        return jnp.sum(jnp.sum(left * right, axis=0, keepdims=True), axis=1, keepdims=True)

    remain = right_side[:, :modes]
    direction = remain
    result = jnp.zeros_like(remain)
    norm_now = inner(remain, remain)
    for iteration in range(CITERS):
        image = coarse_apply(direction)
        step_size = norm_now / inner(direction, image)
        result = result + step_size * direction
        if iteration + 1 < CITERS:
            remain = remain - step_size * image
            norm_next = inner(remain, remain)
            direction = remain + (norm_next / norm_now) * direction
            norm_now = norm_next
    direction_ref[...] = result
    own = direction_ref[pl.ds(me, 1), :]
    solution[...] = own
    spread[...] = jnp.broadcast_to(column(own), (modes, layers))
    ahead_column = column(direction_ref[pl.ds(lax.rem(me + 1, subs), 1), :])
    behind_column = column(direction_ref[pl.ds(lax.rem(me + subs - 1, subs), 1), :])
    ahead_row = jnp.sum(ahead_column * picked[0], axis=0, keepdims=True)
    behind_row = jnp.sum(behind_column * picked[1], axis=0, keepdims=True)
    width = planes * rows
    both_rows = jnp.where(
        lax.broadcasted_iota(jnp.int32, (8, width), 0) == 0,
        jnp.broadcast_to(ahead_row, (8, width)),
        jnp.broadcast_to(behind_row, (8, width)),
    )
    columns = both_rows.T
    ends = jnp.where(
        lane_is((width, layers), layers - 1),
        columns[:, 0:1],
        jnp.where(lane_is((width, layers), 0), columns[:, 1:2], 0.0),
    ).reshape(planes, rows, layers)

    def add_mode(j, carry):
        fields, near, last = list(carry[0]), carry[1], carry[2]
        for u in range(MODES):
            k = j * MODES + u
            scale = spread[pl.ds(k, 1), :]
            for x, plane in enumerate((zvec[k, 0], zvec[k, 1], inner_got[k])):
                fields[x] = fields[x] + scale * plane
            near = near + scale * outer_got[k]
            last = last + scale * outer_last[k].astype(F32)
        return tuple(fields), near, last

    zero, short = jnp.zeros((rows, layers), F32), jnp.zeros((half, layers), F32)
    field, near, last = lax.fori_loop(0, modes // MODES, add_mode, ((zero,) * 3, short, short))
    outer_field[pl.ds(pl.multiple_of(side * half, half), half), :] = near
    outer_field[pl.ds(pl.multiple_of((1 - side) * half, half), half), :] = last
    outside = (field[2], jnp.where(at_edge, 0.0, outer_field[...]))
    faces = (inner_face[...], outer_face[...])
    for x in range(2):
        f = field[x]
        end_field = jnp.where(side == x, ends[1], ends[0])
        image = (
            terms[x, 0] * f
            - middle[0] * field[1 - x]
            - faces[x] * outside[x]
            - terms[x, 1] * pltpu.roll(f, 1, 0)
            - terms[x, 2] * pltpu.roll(f, rows - 1, 0)
            - terms[x, 3] * pltpu.roll(f, 1, 1)
            - terms[x, 4] * pltpu.roll(f, layers - 1, 1)
            - terms[x, 5] * end_field
        )
        deflated[held[x]] = resid[held[x]] - image


def swapped(value, axis, first):
    count = lax.axis_size(axis)
    pairs = []
    for i in range(count):
        up = (i - first) % 2 == 0
        pairs.append((i, (i + 1) % count if up else (i - 1) % count))
    return lax.ppermute(value, axis, pairs)


def swapped_all(value, mask=1):
    subs, count = lax.axis_size("sub"), lax.axis_size("pln")
    pairs = []
    for s in range(subs):
        for i in range(count):
            if 0 < i < count - 1:
                to = (s, i + 1 if i % 2 else i - 1)
            else:
                to = (s ^ mask, i)
            pairs.append((s * count + i, to[0] * count + to[1]))
    return lax.ppermute(value, ("sub", "pln"), pairs)


def exchanged(value, axis, mask):
    return lax.ppermute(value, axis, [(i, i ^ mask) for i in range(lax.axis_size(axis))])


def partner(value, sub_mask, pln_mask):
    subs, count = lax.axis_size("sub"), lax.axis_size("pln")
    pairs = [
        (s * count + p, (s ^ sub_mask) * count + (p ^ pln_mask)) for s in range(subs) for p in range(count)
    ]
    return lax.ppermute(value, ("sub", "pln"), pairs)


FAR = (4, 6)


def mask_of(index, count):
    if count == 1:
        return 0
    swap = far_role(here_on("sub"), here_on("pln")) * (FAR[1] - FAR[0])
    return (0, FAR[0] + swap, 2, FAR[1] - swap)[index]


def far_role(s, p):
    return (p ^ (s >> 2)) & 1


def far_partner(value):
    subs, count = lax.axis_size("sub"), lax.axis_size("pln")
    pairs = [
        (s * count + p, (s ^ FAR[far_role(s, p)]) * count + (p ^ 1)) for s in range(subs) for p in range(count)
    ]
    return lax.ppermute(value, ("sub", "pln"), pairs)


def body(labels, levels, zvec, resid):
    modes, planes, rows, layers = zvec.shape
    half = rows // 2
    subs, parts = lax.axis_size("sub"), lax.axis_size("pln")
    shape = jax.ShapeDtypeStruct
    levels = levels.reshape(1, -1)
    pack = shape((modes + 16, planes * rows), BF16)
    inner_send, outer_near = call(
        stage_kernel,
        [shape((modes + 1, rows, layers), BF16), shape((modes + rows // half, half, layers), BF16)],
        [HBM, HBM],
        [pltpu.VMEM(labels.shape, jnp.int32), pltpu.SemaphoreType.DMA, pltpu.SemaphoreType.DMA((2,))],
        moved=2 << 20,
    )(*(pltpu.with_memory_space_constraint(v, pltpu.HBM) for v in (labels, zvec)))
    outer_got = swapped_all(outer_near, 2 if subs % 4 == 0 else 1)
    inner_got = swapped(inner_send, "pln", 0)
    rest = shape((modes, half, layers), BF16)
    outer_rest, one_pack, two_pack = call(
        prepare_kernel,
        [rest, pack, pack],
        [VMEM, VMEM],
        flops=10_000_000,
        moved=6 << 20,
    )(labels, zvec)
    one_got = swapped(one_pack, "sub", 0)
    two_got = swapped(two_pack, "sub", 1)
    field = (planes, rows, layers)
    plane = (rows, layers)
    partial, weights, here = call(
        block_kernel,
        [
            shape((modes + 8, modes), F32),
            shape((7,) + plane, F32),
            shape((planes, rows, modes, layers), BF16),
        ],
        [VMEM] * 4 + [ANY],
        [pltpu.VMEM(field, F32)] * 3,
        flops=400_000_000,
        moved=3 << 20,
    )(levels, labels, resid, zvec, one_pack)
    turned = pltpu.VMEM((half, modes, layers), BF16)
    partial, inner_face = call(
        inner_kernel,
        [shape((modes + 8, modes), F32), shape(plane, F32)],
        [VMEM] * 5,
        [turned],
        flops=100_000_000,
        moved=1 << 20,
    )(levels, partial, weights, here, inner_got)
    block, outer_face = call(
        outer_kernel,
        [shape((modes + 8, 2 * modes), F32), shape(plane, F32)],
        [VMEM] * 9,
        [turned, pltpu.VMEM(plane, F32)],
        flops=100_000_000,
        moved=1 << 20,
    )(levels, partial, weights, here, outer_got, one_pack, two_pack, one_got, two_got)
    packed = (modes + 16, 2 * modes)
    if parts == 4 and subs == 8:
        block = block + exchanged(block, "pln", 1)
        others = [partner(block, *masks) for masks in ((0, 3), (1, 1), (1, 3))]
        [pair] = call(
            pair_kernel, [shape((2,) + packed, BF16)], [VMEM] * 4, flops=1 << 33
        )(block, *others)
        far = far_partner(pair)
        blocks = [pair, far, partner(pair, 2, 1), exchanged(far, "pln", 1)]
    else:
        [single] = call(single_kernel, [shape(packed, BF16)], [VMEM])(lax.psum(block, "pln"))
        blocks = [lax.all_gather(single, "sub")]
    [outer_rest] = call(release_kernel, [rest], [ANY] * 2, aliases={1: 0})(block, outer_rest)
    outer_last = swapped_all(outer_rest)
    terms, picked = call(
        terms_kernel,
        [shape((planes, 6) + plane, F32), shape((2, modes, planes * rows), F32)],
        [VMEM, ANY] + [VMEM] * 5,
        [pltpu.VMEM(field, F32)],

        flops=1 << 31,
        moved=1 << 20,
    )(levels, blocks[0], one_got, two_got, weights, inner_face, outer_face)
    wide = call(
        widen_kernel,
        [
            shape((modes,) + field, F32),
            shape((modes,) + plane, F32),
            shape((modes, half, layers), F32),
        ],
        [ANY] + [VMEM] * 3,
        flops=1 << 30,
        moved=1 << 20,
    )(blocks[0], zvec, inner_got, outer_got)
    return tuple(
        call(
            finish_kernel,
            [shape((1, modes), F32), shape(field, F32)],
            [VMEM] * (10 + len(blocks)),
            [
                pltpu.VMEM((subs, modes), F32),
                pltpu.VMEM((modes, layers), F32),
                pltpu.VMEM(plane, F32),
            ],
            flops=10_000_000,
            moved=5 << 20,
        )(
            *blocks, *wide, outer_last, picked, terms, weights, inner_face,
            outer_face, resid,
        )
    )


def solution(mesh):
    in_specs = (P("pln", None, "sub"), P(), P(None, "pln", None, "sub"), P("pln", None, "sub"))
    out_specs = (P("sub", None), P("pln", None, "sub"))
    return jax.shard_map(body, mesh=mesh, in_specs=in_specs, out_specs=out_specs, check_vma=False)
```

```python
import jax
import jax.numpy as jnp
from jax import lax
from jax.experimental import pallas as pl
from jax.experimental.pallas import tpu as pltpu
from jax.sharding import PartitionSpec as P

CITERS = 2
STEP = 32
MODES = 16
CHUNK = 16
F32 = jnp.float32
BF16 = jnp.bfloat16
PRECISE = lax.Precision.HIGHEST
NT = (((1,), (1,)), ((), ()))
TN = (((0,), (0,)), ((), ()))
VMEM = pl.BlockSpec(memory_space=pltpu.VMEM)
HBM = pl.BlockSpec(memory_space=pltpu.HBM)
ANY = pl.BlockSpec(memory_space=pl.ANY)


def call(kernel, outs, specs, scratch=(), flops=0, moved=0, limit=32, aliases=None):
    return pl.pallas_call(
        kernel,
        out_shape=outs,
        in_specs=specs,
        out_specs=[ANY if at in (aliases or {}).values() else VMEM for at in range(len(outs))],
        input_output_aliases=aliases or {},
        scratch_shapes=list(scratch),
        cost_estimate=pl.CostEstimate(flops=flops, bytes_accessed=moved, transcendentals=0),
        compiler_params=pltpu.CompilerParams(vmem_limit_bytes=limit << 20),
    )


def here_on(axis):
    return lax.axis_index(axis).astype(jnp.int32)


def ends_the_line():
    p = here_on("pln")
    return (p == 0) | (p == lax.axis_size("pln") - 1)


def harmonic(left_value, right_value):
    return 2.0 * left_value * right_value / (left_value + right_value)


def coefficients(labels, levels_ref):
    weighted = jnp.zeros(labels.shape, F32)
    for level in range(levels_ref.shape[1]):
        weighted = weighted + jnp.where(labels == level, levels_ref[:, level:level + 1], 0.0)
    return weighted


def lane_is(shape, lane):
    return lax.broadcasted_iota(jnp.int32, shape, len(shape) - 1) == lane


def pick_row(lane, width):
    row = lax.broadcasted_iota(jnp.int32, (16, width), 0)
    return ((row == 0) & lane_is((16, width), lane)).astype(BF16)


def stage_kernel(labels_far, zvec, inner_send, outer_near, labels, label_sem, sems):
    modes, planes, rows, layers = zvec.shape
    half = rows // 2
    side = lax.rem(here_on("pln"), 2)
    start = pl.multiple_of((1 - side) * half, half)
    label_copy = pltpu.make_async_copy(labels_far, labels, label_sem)
    copies = [
        pltpu.make_async_copy(
            zvec.at[:, side, pl.ds(start, half), :], outer_near.at[pl.ds(0, modes)], sems.at[0]
        ),
        pltpu.make_async_copy(zvec.at[:, 1 - side], inner_send.at[pl.ds(0, modes)], sems.at[1]),
    ]
    label_copy.start()
    for copy in copies:
        copy.start()
    label_copy.wait()
    outer_near[modes:] = labels[side].astype(F32).astype(BF16).reshape(rows // half, half, layers)
    inner_send[modes] = labels[1 - side].astype(F32).astype(BF16)
    for copy in copies:
        copy.wait()


def release_kernel(after, outer_rest, outer_out):
    pass


def prepare_kernel(labels, held, outer_rest, one_pack, two_pack):
    modes, planes, rows, layers = held.shape
    half = rows // 2
    width = planes * rows
    side = lax.rem(here_on("pln"), 2)
    odd = lax.rem(here_on("sub"), 2) == 1
    one_lane = jnp.where(odd, 0, layers - 1)
    two_lane = jnp.where(odd, layers - 1, 0)
    row = lax.broadcasted_iota(jnp.int32, (16, layers), 0)
    both = ((row == 0) & lane_is((16, layers), one_lane)) | ((row == 1) & lane_is((16, layers), two_lane))
    both = both.astype(BF16)
    flat = labels[...].astype(F32).astype(BF16).reshape(width, layers)
    for out, lane in ((one_pack, one_lane), (two_pack, two_lane)):
        out[modes:] = lax.dot_general(
            pick_row(lane, layers), flat, NT, preferred_element_type=F32
        ).astype(BF16)
    for k in range(0, modes, CHUNK):
        at = slice(k, k + CHUNK)
        ends = lax.dot_general(
            both, held[at].reshape(-1, layers), NT, preferred_element_type=F32
        )
        for out, index in ((one_pack, 0), (two_pack, 1)):
            out[at] = jnp.concatenate(
                [ends[index:index + 1, j * width:(j + 1) * width] for j in range(CHUNK)], axis=0
            ).astype(BF16)
        outer_rest[at] = held[at, side, pl.ds(pl.multiple_of(side * half, half), half), :]


def block_kernel(
    levels, labels, resid, zvec, after, partial, weights, here, half_diag, link_y, link_z,
):
    planes, rows, layers = labels.shape
    modes = here.shape[2]
    side = lax.rem(here_on("pln"), 2)
    at_edge = ends_the_line()
    held = (1 - side, side)

    def turn_rows(start):
        for slot, plane in enumerate(held):
            for k in range(0, modes, CHUNK):
                block = zvec[k:k + CHUNK, plane, pl.ds(start, STEP), :]
                here[slot, pl.ds(start, STEP), k:k + CHUNK, :] = jnp.swapaxes(block, 0, 1)

    turn_rows(0)
    coef = [coefficients(labels[x], levels) for x in held]
    middle = harmonic(coef[0], coef[1])
    weights[0] = middle
    row = lax.broadcasted_iota(jnp.int32, (rows, layers), 0)
    lane = lax.broadcasted_iota(jnp.int32, (rows, layers), 1)
    for x in range(2):
        c = coef[x]
        up_y = harmonic(c, jnp.where(row == rows - 1, c, pltpu.roll(c, rows - 1, 0)))
        up_z = harmonic(c, pltpu.roll(c, layers - 1, 1))
        down_y = jnp.where(row == 0, c, pltpu.roll(up_y, 1, 0))
        weights[1 + x] = up_y
        weights[3 + x] = up_z
        weights[5 + x] = c
        inner_z = jnp.where(lane == layers - 1, 0.0, up_z)
        total = middle + up_y + down_y + inner_z + pltpu.roll(inner_z, 1, 1)
        if x == 1:
            total = total + jnp.where(at_edge, c, 0.0)
        half_diag[x] = 0.5 * total
        link_y[x] = jnp.where(row == rows - 1, 0.0, up_y)
        link_z[x] = inner_z

    def step(j, carry):
        total, wide = carry
        turn_rows(pl.multiple_of(jnp.minimum((j + 1) * STEP, rows - STEP), STEP))
        for u in range(STEP):
            y = j * STEP + u
            at = pl.ds(y, 1)
            ahead = jnp.minimum(y + 1, rows - 1)
            up = [here[x, ahead].astype(F32) for x in range(2)]
            images, parts = [], []
            for x in range(2):
                image = (
                    half_diag[x, at, :] * wide[x]
                    - link_y[x, at, :] * up[x]
                    - link_z[x, at, :] * pltpu.roll(wide[x], layers - 1, 1)
                )
                if x == 0:
                    image = image - weights[0, at, :] * wide[1]
                images.append(image.astype(BF16))
                value = resid[held[x], at, :]
                high = value.astype(BF16).astype(F32)
                part = jnp.where(part_row == 0, high, jnp.where(part_row == 1, value - high, 0.0))
                parts.append(part.astype(BF16))
            total = total + lax.dot_general(
                jnp.concatenate(
                    [jnp.concatenate(images, axis=1), jnp.concatenate(parts, axis=1)], axis=0
                ),
                jnp.concatenate([here[0, y], here[1, y]], axis=1),
                NT,
                preferred_element_type=F32,
            )
            wide = up
        return total, wide

    part_row = lax.broadcasted_iota(jnp.int32, (16, layers), 0)
    total, _ = lax.fori_loop(
        0,
        rows // STEP,
        step,
        (
            jnp.zeros((modes + 16, modes), F32),
            [here[x, 0].astype(F32) for x in range(2)],
        ),
    )
    partial[:modes, :] = total[:modes]
    partial[modes:, :] = jnp.broadcast_to(total[modes:modes + 1] + total[modes + 1:modes + 2], (8, modes))


def turn(got, start, out):
    half, modes, layers = out.shape
    for k in range(0, modes, CHUNK):
        out[:, k:k + CHUNK, :] = jnp.swapaxes(got[k:k + CHUNK, pl.ds(start, half), :], 0, 1)


def face_product(weight_ref, base, own, other):
    half, modes, layers = other.shape

    def step(j, total):
        left, right = [], []
        for u in range(STEP):
            y = j * STEP + u
            weight = weight_ref[pl.ds(base + y, 1), :]
            image = weight * (own[base + y].astype(F32) - other[y].astype(F32))
            left.append(jnp.concatenate([own[base + y], other[y]], axis=0))
            right.append(image.astype(BF16))
        return total + lax.dot_general(
            jnp.concatenate(left, axis=1), jnp.concatenate(right, axis=1), NT,
            preferred_element_type=F32,
        )

    total = lax.fori_loop(0, half // STEP, step, jnp.zeros((2 * modes, modes), F32))
    return total[:modes] - total[modes:]


def inner_kernel(levels, partial, weights, here, inner_got, out, face, turned):
    planes, rows, modes, layers = here.shape
    half = rows // 2
    side = lax.rem(here_on("pln"), 2)
    base = pl.multiple_of(side * half, half)
    turn(inner_got, base, turned)
    face[...] = harmonic(weights[5], coefficients(inner_got[modes].astype(F32), levels))
    out[:modes, :] = partial[:modes, :] + 0.5 * face_product(face, base, here.at[0], turned)
    out[modes:, :] = partial[modes:, :]


def outer_kernel(
    levels, partial, weights, here, outer_got, one_pack, two_pack, one_got, two_got,
    out, face, turned, face_here,
):
    planes, rows, modes, layers = here.shape
    half = rows // 2
    side = lax.rem(here_on("pln"), 2)
    at_edge = ends_the_line()
    base = pl.multiple_of(side * half, half)
    turn(outer_got, 0, turned)
    coef = coefficients(outer_got[modes:].astype(F32).reshape(rows, layers), levels)
    between = harmonic(weights[6], coef)
    face[...] = jnp.where(at_edge, weights[6], between)
    face_here[...] = jnp.where(at_edge, 0.0, between)
    cross = face_product(face_here, base, here.at[1], turned)
    odd = lax.rem(here_on("sub"), 2) == 1

    def coef_row(pack):
        return coefficients(pack[modes:modes + 16].astype(F32)[0:1], levels)

    one, two = one_pack[...].astype(F32), two_pack[...].astype(F32)
    one_other, two_other = one_got[...].astype(F32), two_got[...].astype(F32)
    first, last = jnp.where(odd, one, two), jnp.where(odd, two, one)
    next_first = jnp.where(odd, two_other, one_other)
    prev_last = jnp.where(odd, one_other, two_other)
    weight_low = harmonic(coef_row(first), coef_row(prev_last))
    weight_high = harmonic(coef_row(last), coef_row(next_first))

    def product(left, right):
        return lax.dot_general(
            left.astype(BF16), right.astype(BF16), NT, preferred_element_type=F32
        )

    edge_rows = weight_high * last[:modes]
    ends = product(
        jnp.concatenate([weight_low * first[:modes], edge_rows], axis=1),
        jnp.concatenate([first[:modes], last[:modes]], axis=1),
    )
    square = partial[:modes, :] + 0.5 * (cross + ends)
    out[:modes, :modes] = square + square.T
    out[:modes, modes:] = -product(edge_rows, next_first[:modes])
    out[modes:, :modes] = partial[modes:, :]
    out[modes:, modes:] = jnp.zeros((8, modes), F32)


def terms_kernel(
    levels, pair, one_got, two_got, weights, inner_face, outer_face, terms, picked, coef_ref
):
    modes, width = picked.shape[1:]
    rows, layers = inner_face.shape
    side = lax.rem(here_on("pln"), 2)
    odd = lax.rem(here_on("sub"), 2) == 1
    one_other, two_other = one_got[...].astype(F32), two_got[...].astype(F32)
    next_first = jnp.where(odd, two_other, one_other)
    prev_last = jnp.where(odd, one_other, two_other)
    picked[0] = next_first[:modes]
    picked[1] = prev_last[:modes]
    end_labels = lax.dot_general(
        next_first[modes:].astype(BF16), pick_row(layers - 1, layers), TN, preferred_element_type=F32
    ) + lax.dot_general(
        prev_last[modes:].astype(BF16), pick_row(0, layers), TN, preferred_element_type=F32
    )
    coef_ref[...] = coefficients(end_labels, levels).reshape(width // rows, rows, layers)
    row = lax.broadcasted_iota(jnp.int32, (rows, layers), 0)
    lane = lax.broadcasted_iota(jnp.int32, (rows, layers), 1)
    for x, face in enumerate((inner_face, outer_face)):
        c = weights[5 + x]
        end_weight = harmonic(c, coef_ref[1 - side if x == 0 else side])
        up_y, up_z = weights[1 + x], weights[3 + x]
        down_y = jnp.where(row == 0, c, pltpu.roll(up_y, 1, 0))
        down_z = pltpu.roll(up_z, 1, 1)
        total = face[...] + weights[0] + up_y + down_y
        total = total + jnp.where(lane == layers - 1, end_weight, up_z)
        terms[x, 0] = total + jnp.where(lane == 0, end_weight, down_z)
        terms[x, 1] = jnp.where(row == 0, 0.0, down_y)
        terms[x, 2] = jnp.where(row == rows - 1, 0.0, up_y)
        terms[x, 3] = jnp.where(lane == 0, 0.0, down_z)
        terms[x, 4] = jnp.where(lane == layers - 1, 0.0, up_z)
        terms[x, 5] = end_weight


def pair_kernel(own, across, beside, oblique, out):
    modes = own.shape[1] // 2
    encode(own[...] + across[...], modes, out.at[0])
    encode(beside[...] + oblique[...], modes, out.at[1])


def single_kernel(own, out):
    encode(own[...], own.shape[1] // 2, out)


def encode(total, modes, out):
    row = lax.broadcasted_iota(jnp.int32, (modes, 2 * modes), 0)
    lane = lax.broadcasted_iota(jnp.int32, (modes, 2 * modes), 1)
    values = total[:modes]
    high = values.astype(BF16).astype(F32)
    low = values - high
    out[:modes] = jnp.where((lane <= row) | (lane >= modes), high, low).astype(BF16)
    diagonal = lane == row
    right = total[modes:modes + 1]
    parts = []
    for _ in range(3):
        part = right.astype(BF16).astype(F32)
        parts.append(part)
        right = right - part
    for part in (high, low):
        parts.append(jnp.sum(jnp.where(diagonal, part, 0.0), axis=0, keepdims=True))
    rows = lax.broadcasted_iota(jnp.int32, (16, 2 * modes), 0)
    extra = jnp.zeros((16, 2 * modes), F32)
    for index, part in enumerate(parts):
        extra = jnp.where(rows == index, part, extra)
    out[modes:] = extra.astype(BF16)


def widen_kernel(pair, zvec, inner_got, outer_got, own_wide, inner_wide, outer_wide):
    modes, half = outer_wide.shape[:2]
    side = lax.rem(here_on("pln"), 2)

    def some(j, carry):
        at = pl.ds(pl.multiple_of(j * MODES, MODES), MODES)
        own_wide[at, 0] = zvec[at, 1 - side].astype(F32)
        own_wide[at, 1] = zvec[at, side].astype(F32)
        inner_wide[at] = inner_got[at].astype(F32)
        outer_wide[at] = outer_got[at].astype(F32)
        return carry

    lax.fori_loop(0, modes // MODES, some, 0)


def finish_kernel(*refs):
    count = len(refs) - 15
    blocks, refs = refs[:count], refs[count:]
    zvec, inner_got, outer_got, outer_last, picked, terms, middle, inner_face, outer_face, resid = refs[:10]
    solution, deflated, direction_ref, spread, outer_field = refs[10:]
    subs = direction_ref.shape[0]
    modes, planes, rows, layers = zvec.shape
    half = rows // 2
    me = here_on("sub")
    side = lax.rem(here_on("pln"), 2)
    odd = lax.rem(me, 2) == 1
    at_edge = ends_the_line()
    held = (1 - side, side)
    square = (modes, modes)
    eye = lax.broadcasted_iota(jnp.int32, square, 0) == lax.broadcasted_iota(jnp.int32, square, 1)

    def column(row):
        return jnp.sum(jnp.where(eye, row, 0.0), axis=1, keepdims=True)

    def each(body, carry):
        for index, block in enumerate(blocks):
            held_here = block.shape[0]
            if held_here <= 8:
                for entry in range(held_here):
                    s = jnp.bitwise_xor(jnp.bitwise_xor(me, mask_of(index, len(blocks))), entry)
                    carry = body(block.at[entry], s, carry)
            else:
                carry = lax.fori_loop(
                    0, held_here, lambda entry, c, block=block: body(block.at[entry], entry, c), carry
                )
        return carry

    def row_is(s, width):
        return lax.broadcasted_iota(jnp.int32, (subs, width), 0) == s

    def load(block, s, carry):
        extra = block[modes:modes + 16, :].astype(F32)
        right = (extra[0:1] + extra[1:2]) + extra[2:3]
        here = row_is(s, 2 * modes)
        return jnp.where(here, right, carry[0]), jnp.where(here, extra[4:5] - extra[3:4], carry[1])

    empty = jnp.zeros((subs, 2 * modes), F32)
    right_side, fix = each(load, (empty, empty))
    fix = fix[:, :modes]

    def turned(rows_of, by):
        by = by % subs
        return jnp.concatenate([rows_of[by:], rows_of[:by]], axis=0)

    def in_parts(value):
        parts = []
        for _ in range(3):
            part = value.astype(BF16)
            parts.append(part.astype(F32))
            value = value - parts[-1]
        return jnp.concatenate(parts, axis=0).astype(BF16)

    def joined(value):
        return (value[:subs] + value[subs:2 * subs]) + value[2 * subs:]

    def coarse_apply(direction):
        pairs = in_parts(jnp.concatenate([direction, turned(direction, 1)], axis=1))
        single = pairs[:, :modes]

        def one(block, s, carry):
            values = block[:modes, :]
            ahead = lax.dot_general(pairs, values, NT, preferred_element_type=F32)
            image = jnp.dot(single, values, preferred_element_type=F32)
            return (
                jnp.where(row_is(s, modes), joined(ahead), carry[0]),
                jnp.where(row_is(s, 2 * modes), joined(image), carry[1]),
            )

        ahead, image = each(one, (jnp.zeros((subs, modes), F32), empty))
        return ahead + image[:, :modes] + fix * direction + turned(image[:, modes:], -1)

    def inner(left, right):
        return jnp.sum(jnp.sum(left * right, axis=0, keepdims=True), axis=1, keepdims=True)

    remain = right_side[:, :modes]
    direction = remain
    result = jnp.zeros_like(remain)
    norm_now = inner(remain, remain)
    for iteration in range(CITERS):
        image = coarse_apply(direction)
        step_size = norm_now / inner(direction, image)
        result = result + step_size * direction
        if iteration + 1 < CITERS:
            remain = remain - step_size * image
            norm_next = inner(remain, remain)
            direction = remain + (norm_next / norm_now) * direction
            norm_now = norm_next
    direction_ref[...] = result
    own = direction_ref[pl.ds(me, 1), :]
    solution[...] = own
    spread[...] = jnp.broadcast_to(column(own), (modes, layers))
    ahead_column = column(direction_ref[pl.ds(lax.rem(me + 1, subs), 1), :])
    behind_column = column(direction_ref[pl.ds(lax.rem(me + subs - 1, subs), 1), :])
    ahead_row = jnp.sum(ahead_column * picked[0], axis=0, keepdims=True)
    behind_row = jnp.sum(behind_column * picked[1], axis=0, keepdims=True)
    width = planes * rows
    both_rows = jnp.where(
        lax.broadcasted_iota(jnp.int32, (8, width), 0) == 0,
        jnp.broadcast_to(ahead_row, (8, width)),
        jnp.broadcast_to(behind_row, (8, width)),
    )
    columns = both_rows.T
    ends = jnp.where(
        lane_is((width, layers), layers - 1),
        columns[:, 0:1],
        jnp.where(lane_is((width, layers), 0), columns[:, 1:2], 0.0),
    ).reshape(planes, rows, layers)

    def add_mode(j, carry):
        fields, near, last = list(carry[0]), carry[1], carry[2]
        for u in range(MODES):
            k = j * MODES + u
            scale = spread[pl.ds(k, 1), :]
            for x, plane in enumerate((zvec[k, 0], zvec[k, 1], inner_got[k])):
                fields[x] = fields[x] + scale * plane
            near = near + scale * outer_got[k]
            last = last + scale * outer_last[k].astype(F32)
        return tuple(fields), near, last

    zero, short = jnp.zeros((rows, layers), F32), jnp.zeros((half, layers), F32)
    field, near, last = lax.fori_loop(0, modes // MODES, add_mode, ((zero,) * 3, short, short))
    outer_field[pl.ds(pl.multiple_of(side * half, half), half), :] = near
    outer_field[pl.ds(pl.multiple_of((1 - side) * half, half), half), :] = last
    outside = (field[2], jnp.where(at_edge, 0.0, outer_field[...]))
    faces = (inner_face[...], outer_face[...])
    for x in range(2):
        f = field[x]
        end_field = jnp.where(side == x, ends[1], ends[0])
        image = (
            terms[x, 0] * f
            - middle[0] * field[1 - x]
            - faces[x] * outside[x]
            - terms[x, 1] * pltpu.roll(f, 1, 0)
            - terms[x, 2] * pltpu.roll(f, rows - 1, 0)
            - terms[x, 3] * pltpu.roll(f, 1, 1)
            - terms[x, 4] * pltpu.roll(f, layers - 1, 1)
            - terms[x, 5] * end_field
        )
        deflated[held[x]] = resid[held[x]] - image


def swapped(value, axis, first):
    count = lax.axis_size(axis)
    pairs = []
    for i in range(count):
        up = (i - first) % 2 == 0
        pairs.append((i, (i + 1) % count if up else (i - 1) % count))
    return lax.ppermute(value, axis, pairs)


def swapped_all(value):
    subs, count = lax.axis_size("sub"), lax.axis_size("pln")
    pairs = []
    for s in range(subs):
        for i in range(count):
            if 0 < i < count - 1:
                to = (s, i + 1 if i % 2 else i - 1)
            else:
                to = (s ^ 1, i)
            pairs.append((s * count + i, to[0] * count + to[1]))
    return lax.ppermute(value, ("sub", "pln"), pairs)


def exchanged(value, axis, mask):
    return lax.ppermute(value, axis, [(i, i ^ mask) for i in range(lax.axis_size(axis))])


def partner(value, sub_mask, pln_mask):
    subs, count = lax.axis_size("sub"), lax.axis_size("pln")
    pairs = [
        (s * count + p, (s ^ sub_mask) * count + (p ^ pln_mask)) for s in range(subs) for p in range(count)
    ]
    return lax.ppermute(value, ("sub", "pln"), pairs)


FAR = (4, 6)


def mask_of(index, count):
    if count == 1:
        return 0
    swap = far_role(here_on("sub"), here_on("pln")) * (FAR[1] - FAR[0])
    return (0, FAR[0] + swap, 2, FAR[1] - swap)[index]


def far_role(s, p):
    return (p ^ (s >> 2)) & 1


def far_partner(value):
    subs, count = lax.axis_size("sub"), lax.axis_size("pln")
    pairs = [
        (s * count + p, (s ^ FAR[far_role(s, p)]) * count + (p ^ 1)) for s in range(subs) for p in range(count)
    ]
    return lax.ppermute(value, ("sub", "pln"), pairs)


def body(labels, levels, zvec, resid):
    modes, planes, rows, layers = zvec.shape
    half = rows // 2
    subs, parts = lax.axis_size("sub"), lax.axis_size("pln")
    shape = jax.ShapeDtypeStruct
    levels = levels.reshape(1, -1)
    pack = shape((modes + 16, planes * rows), BF16)
    inner_send, outer_near = call(
        stage_kernel,
        [shape((modes + 1, rows, layers), BF16), shape((modes + rows // half, half, layers), BF16)],
        [HBM, HBM],
        [pltpu.VMEM(labels.shape, jnp.int32), pltpu.SemaphoreType.DMA, pltpu.SemaphoreType.DMA((2,))],
        moved=2 << 20,
    )(*(pltpu.with_memory_space_constraint(v, pltpu.HBM) for v in (labels, zvec)))
    outer_got = swapped_all(outer_near)
    inner_got = swapped(inner_send, "pln", 0)
    rest = shape((modes, half, layers), BF16)
    outer_rest, one_pack, two_pack = call(
        prepare_kernel,
        [rest, pack, pack],
        [VMEM, VMEM],
        flops=10_000_000,
        moved=6 << 20,
    )(labels, zvec)
    one_got = swapped(one_pack, "sub", 0)
    two_got = swapped(two_pack, "sub", 1)
    field = (planes, rows, layers)
    plane = (rows, layers)
    partial, weights, here = call(
        block_kernel,
        [
            shape((modes + 8, modes), F32),
            shape((7,) + plane, F32),
            shape((planes, rows, modes, layers), BF16),
        ],
        [VMEM] * 4 + [ANY],
        [pltpu.VMEM(field, F32)] * 3,
        flops=400_000_000,
        moved=3 << 20,
    )(levels, labels, resid, zvec, one_pack)
    turned = pltpu.VMEM((half, modes, layers), BF16)
    partial, inner_face = call(
        inner_kernel,
        [shape((modes + 8, modes), F32), shape(plane, F32)],
        [VMEM] * 5,
        [turned],
        flops=100_000_000,
        moved=1 << 20,
    )(levels, partial, weights, here, inner_got)
    block, outer_face = call(
        outer_kernel,
        [shape((modes + 8, 2 * modes), F32), shape(plane, F32)],
        [VMEM] * 9,
        [turned, pltpu.VMEM(plane, F32)],
        flops=100_000_000,
        moved=1 << 20,
    )(levels, partial, weights, here, outer_got, one_pack, two_pack, one_got, two_got)
    packed = (modes + 16, 2 * modes)
    if parts == 4 and subs == 8:
        block = block + exchanged(block, "pln", 1)
        others = [partner(block, *masks) for masks in ((0, 3), (1, 1), (1, 3))]
        [pair] = call(
            pair_kernel, [shape((2,) + packed, BF16)], [VMEM] * 4, flops=1 << 33
        )(block, *others)
        far = far_partner(pair)
        blocks = [pair, far, partner(pair, 2, 1), exchanged(far, "pln", 1)]
    else:
        [single] = call(single_kernel, [shape(packed, BF16)], [VMEM])(lax.psum(block, "pln"))
        blocks = [lax.all_gather(single, "sub")]
    [outer_rest] = call(release_kernel, [rest], [ANY] * 2, aliases={1: 0})(block, outer_rest)
    outer_last = swapped_all(outer_rest)
    terms, picked = call(
        terms_kernel,
        [shape((planes, 6) + plane, F32), shape((2, modes, planes * rows), F32)],
        [VMEM, ANY] + [VMEM] * 5,
        [pltpu.VMEM(field, F32)],

        flops=1 << 31,
        moved=1 << 20,
    )(levels, blocks[0], one_got, two_got, weights, inner_face, outer_face)
    wide = call(
        widen_kernel,
        [
            shape((modes,) + field, F32),
            shape((modes,) + plane, F32),
            shape((modes, half, layers), F32),
        ],
        [ANY] + [VMEM] * 3,
        flops=1 << 30,
        moved=1 << 20,
    )(blocks[0], zvec, inner_got, outer_got)
    return tuple(
        call(
            finish_kernel,
            [shape((1, modes), F32), shape(field, F32)],
            [VMEM] * (10 + len(blocks)),
            [
                pltpu.VMEM((subs, modes), F32),
                pltpu.VMEM((modes, layers), F32),
                pltpu.VMEM(plane, F32),
            ],
            flops=10_000_000,
            moved=5 << 20,
        )(
            *blocks, *wide, outer_last, picked, terms, weights, inner_face,
            outer_face, resid,
        )
    )


def solution(mesh):
    in_specs = (P("pln", None, "sub"), P(), P(None, "pln", None, "sub"), P("pln", None, "sub"))
    out_specs = (P("sub", None), P("pln", None, "sub"))
    return jax.shard_map(body, mesh=mesh, in_specs=in_specs, out_specs=out_specs, check_vma=False)
```

```python
import jax
import jax.numpy as jnp
from jax import lax
from jax.experimental import pallas as pl
from jax.experimental.pallas import tpu as pltpu
from jax.sharding import PartitionSpec as P

CITERS = 2
STEP = 32
MODES = 16
CHUNK = 16
F32 = jnp.float32
BF16 = jnp.bfloat16
PRECISE = lax.Precision.HIGHEST
NT = (((1,), (1,)), ((), ()))
TN = (((0,), (0,)), ((), ()))
VMEM = pl.BlockSpec(memory_space=pltpu.VMEM)
HBM = pl.BlockSpec(memory_space=pltpu.HBM)
ANY = pl.BlockSpec(memory_space=pl.ANY)


def call(kernel, outs, specs, scratch=(), flops=0, moved=0, limit=32, aliases=None):
    return pl.pallas_call(
        kernel,
        out_shape=outs,
        in_specs=specs,
        out_specs=[ANY if at in (aliases or {}).values() else VMEM for at in range(len(outs))],
        input_output_aliases=aliases or {},
        scratch_shapes=list(scratch),
        cost_estimate=pl.CostEstimate(flops=flops, bytes_accessed=moved, transcendentals=0),
        compiler_params=pltpu.CompilerParams(vmem_limit_bytes=limit << 20),
    )


def here_on(axis):
    return lax.axis_index(axis).astype(jnp.int32)


def ends_the_line():
    p = here_on("pln")
    return (p == 0) | (p == lax.axis_size("pln") - 1)


def harmonic(left_value, right_value):
    return 2.0 * left_value * right_value / (left_value + right_value)


def coefficients(labels, levels_ref):
    weighted = jnp.zeros(labels.shape, F32)
    for level in range(levels_ref.shape[1]):
        weighted = weighted + jnp.where(labels == level, levels_ref[:, level:level + 1], 0.0)
    return weighted


def lane_is(shape, lane):
    return lax.broadcasted_iota(jnp.int32, shape, len(shape) - 1) == lane


def pick_row(lane, width):
    row = lax.broadcasted_iota(jnp.int32, (16, width), 0)
    return ((row == 0) & lane_is((16, width), lane)).astype(BF16)


def stage_kernel(labels_far, zvec, inner_send, outer_near, labels, label_sem, sems):
    modes, planes, rows, layers = zvec.shape
    half = rows // 2
    side = lax.rem(here_on("pln"), 2)
    start = pl.multiple_of((1 - side) * half, half)
    label_copy = pltpu.make_async_copy(labels_far, labels, label_sem)
    copies = [
        pltpu.make_async_copy(
            zvec.at[:, side, pl.ds(start, half), :], outer_near.at[pl.ds(0, modes)], sems.at[0]
        ),
        pltpu.make_async_copy(zvec.at[:, 1 - side], inner_send.at[pl.ds(0, modes)], sems.at[1]),
    ]
    label_copy.start()
    for copy in copies:
        copy.start()
    label_copy.wait()
    outer_near[modes:] = labels[side].astype(F32).astype(BF16).reshape(rows // half, half, layers)
    inner_send[modes] = labels[1 - side].astype(F32).astype(BF16)
    for copy in copies:
        copy.wait()


def release_kernel(after, outer_rest, outer_out):
    pass


def prepare_kernel(labels, held, outer_rest, one_pack, two_pack):
    modes, planes, rows, layers = held.shape
    half = rows // 2
    width = planes * rows
    side = lax.rem(here_on("pln"), 2)
    odd = lax.rem(here_on("sub"), 2) == 1
    one_lane = jnp.where(odd, 0, layers - 1)
    two_lane = jnp.where(odd, layers - 1, 0)
    row = lax.broadcasted_iota(jnp.int32, (16, layers), 0)
    both = ((row == 0) & lane_is((16, layers), one_lane)) | ((row == 1) & lane_is((16, layers), two_lane))
    both = both.astype(BF16)
    flat = labels[...].astype(F32).astype(BF16).reshape(width, layers)
    for out, lane in ((one_pack, one_lane), (two_pack, two_lane)):
        out[modes:] = lax.dot_general(
            pick_row(lane, layers), flat, NT, preferred_element_type=F32
        ).astype(BF16)
    for k in range(0, modes, CHUNK):
        at = slice(k, k + CHUNK)
        ends = lax.dot_general(
            both, held[at].reshape(-1, layers), NT, preferred_element_type=F32
        )
        for out, index in ((one_pack, 0), (two_pack, 1)):
            out[at] = jnp.concatenate(
                [ends[index:index + 1, j * width:(j + 1) * width] for j in range(CHUNK)], axis=0
            ).astype(BF16)
        outer_rest[at] = held[at, side, pl.ds(pl.multiple_of(side * half, half), half), :]


def block_kernel(
    levels, labels, resid, zvec, after, partial, weights, here, half_diag, link_y, link_z,
):
    planes, rows, layers = labels.shape
    modes = here.shape[2]
    side = lax.rem(here_on("pln"), 2)
    at_edge = ends_the_line()
    held = (1 - side, side)

    def turn_rows(start):
        for slot, plane in enumerate(held):
            for k in range(0, modes, CHUNK):
                block = zvec[k:k + CHUNK, plane, pl.ds(start, STEP), :]
                here[slot, pl.ds(start, STEP), k:k + CHUNK, :] = jnp.swapaxes(block, 0, 1)

    turn_rows(0)
    coef = [coefficients(labels[x], levels) for x in held]
    middle = harmonic(coef[0], coef[1])
    weights[0] = middle
    row = lax.broadcasted_iota(jnp.int32, (rows, layers), 0)
    lane = lax.broadcasted_iota(jnp.int32, (rows, layers), 1)
    for x in range(2):
        c = coef[x]
        up_y = harmonic(c, jnp.where(row == rows - 1, c, pltpu.roll(c, rows - 1, 0)))
        up_z = harmonic(c, pltpu.roll(c, layers - 1, 1))
        down_y = jnp.where(row == 0, c, pltpu.roll(up_y, 1, 0))
        weights[1 + x] = up_y
        weights[3 + x] = up_z
        weights[5 + x] = c
        inner_z = jnp.where(lane == layers - 1, 0.0, up_z)
        total = middle + up_y + down_y + inner_z + pltpu.roll(inner_z, 1, 1)
        if x == 1:
            total = total + jnp.where(at_edge, c, 0.0)
        half_diag[x] = 0.5 * total
        link_y[x] = jnp.where(row == rows - 1, 0.0, up_y)
        link_z[x] = inner_z

    def step(j, carry):
        total, wide = carry
        turn_rows(pl.multiple_of(jnp.minimum((j + 1) * STEP, rows - STEP), STEP))
        for u in range(STEP):
            y = j * STEP + u
            at = pl.ds(y, 1)
            ahead = jnp.minimum(y + 1, rows - 1)
            up = [here[x, ahead].astype(F32) for x in range(2)]
            images, parts = [], []
            for x in range(2):
                image = (
                    half_diag[x, at, :] * wide[x]
                    - link_y[x, at, :] * up[x]
                    - link_z[x, at, :] * pltpu.roll(here[x, y], layers - 1, 1).astype(F32)
                )
                if x == 0:
                    image = image - weights[0, at, :] * wide[1]
                images.append(image.astype(BF16))
                value = resid[held[x], at, :]
                high = value.astype(BF16).astype(F32)
                part = jnp.where(part_row == 0, high, jnp.where(part_row == 1, value - high, 0.0))
                parts.append(part.astype(BF16))
            total = total + lax.dot_general(
                jnp.concatenate(
                    [jnp.concatenate(images, axis=1), jnp.concatenate(parts, axis=1)], axis=0
                ),
                jnp.concatenate([here[0, y], here[1, y]], axis=1),
                NT,
                preferred_element_type=F32,
            )
            wide = up
        return total, wide

    part_row = lax.broadcasted_iota(jnp.int32, (16, layers), 0)
    total, _ = lax.fori_loop(
        0,
        rows // STEP,
        step,
        (
            jnp.zeros((modes + 16, modes), F32),
            [here[x, 0].astype(F32) for x in range(2)],
        ),
    )
    partial[:modes, :] = total[:modes]
    partial[modes:, :] = jnp.broadcast_to(total[modes:modes + 1] + total[modes + 1:modes + 2], (8, modes))


def turn(got, start, out):
    half, modes, layers = out.shape
    for k in range(0, modes, CHUNK):
        out[:, k:k + CHUNK, :] = jnp.swapaxes(got[k:k + CHUNK, pl.ds(start, half), :], 0, 1)


def face_product(weight_ref, base, own, other):
    half, modes, layers = other.shape

    def step(j, total):
        left, right = [], []
        for u in range(STEP):
            y = j * STEP + u
            weight = weight_ref[pl.ds(base + y, 1), :]
            image = weight * (own[base + y].astype(F32) - other[y].astype(F32))
            left.append(jnp.concatenate([own[base + y], other[y]], axis=0))
            right.append(image.astype(BF16))
        return total + lax.dot_general(
            jnp.concatenate(left, axis=1), jnp.concatenate(right, axis=1), NT,
            preferred_element_type=F32,
        )

    total = lax.fori_loop(0, half // STEP, step, jnp.zeros((2 * modes, modes), F32))
    return total[:modes] - total[modes:]


def inner_kernel(levels, partial, weights, here, inner_got, out, face, turned):
    planes, rows, modes, layers = here.shape
    half = rows // 2
    side = lax.rem(here_on("pln"), 2)
    base = pl.multiple_of(side * half, half)
    turn(inner_got, base, turned)
    face[...] = harmonic(weights[5], coefficients(inner_got[modes].astype(F32), levels))
    out[:modes, :] = partial[:modes, :] + 0.5 * face_product(face, base, here.at[0], turned)
    out[modes:, :] = partial[modes:, :]


def outer_kernel(
    levels, partial, weights, here, outer_got, one_pack, two_pack, one_got, two_got,
    out, face, turned, face_here,
):
    planes, rows, modes, layers = here.shape
    half = rows // 2
    side = lax.rem(here_on("pln"), 2)
    at_edge = ends_the_line()
    base = pl.multiple_of(side * half, half)
    turn(outer_got, 0, turned)
    coef = coefficients(outer_got[modes:].astype(F32).reshape(rows, layers), levels)
    between = harmonic(weights[6], coef)
    face[...] = jnp.where(at_edge, weights[6], between)
    face_here[...] = jnp.where(at_edge, 0.0, between)
    cross = face_product(face_here, base, here.at[1], turned)
    odd = lax.rem(here_on("sub"), 2) == 1

    def coef_row(pack):
        return coefficients(pack[modes:modes + 16].astype(F32)[0:1], levels)

    one, two = one_pack[...].astype(F32), two_pack[...].astype(F32)
    one_other, two_other = one_got[...].astype(F32), two_got[...].astype(F32)
    first, last = jnp.where(odd, one, two), jnp.where(odd, two, one)
    next_first = jnp.where(odd, two_other, one_other)
    prev_last = jnp.where(odd, one_other, two_other)
    weight_low = harmonic(coef_row(first), coef_row(prev_last))
    weight_high = harmonic(coef_row(last), coef_row(next_first))

    def product(left, right):
        return lax.dot_general(
            left.astype(BF16), right.astype(BF16), NT, preferred_element_type=F32
        )

    edge_rows = weight_high * last[:modes]
    ends = product(
        jnp.concatenate([weight_low * first[:modes], edge_rows], axis=1),
        jnp.concatenate([first[:modes], last[:modes]], axis=1),
    )
    square = partial[:modes, :] + 0.5 * (cross + ends)
    out[:modes, :modes] = square + square.T
    out[:modes, modes:] = -product(edge_rows, next_first[:modes])
    out[modes:, :modes] = partial[modes:, :]
    out[modes:, modes:] = jnp.zeros((8, modes), F32)


def terms_kernel(
    levels, pair, one_got, two_got, weights, inner_face, outer_face, terms, picked, coef_ref
):
    modes, width = picked.shape[1:]
    rows, layers = inner_face.shape
    side = lax.rem(here_on("pln"), 2)
    odd = lax.rem(here_on("sub"), 2) == 1
    one_other, two_other = one_got[...].astype(F32), two_got[...].astype(F32)
    next_first = jnp.where(odd, two_other, one_other)
    prev_last = jnp.where(odd, one_other, two_other)
    picked[0] = next_first[:modes]
    picked[1] = prev_last[:modes]
    end_labels = lax.dot_general(
        next_first[modes:].astype(BF16), pick_row(layers - 1, layers), TN, preferred_element_type=F32
    ) + lax.dot_general(
        prev_last[modes:].astype(BF16), pick_row(0, layers), TN, preferred_element_type=F32
    )
    coef_ref[...] = coefficients(end_labels, levels).reshape(width // rows, rows, layers)
    row = lax.broadcasted_iota(jnp.int32, (rows, layers), 0)
    lane = lax.broadcasted_iota(jnp.int32, (rows, layers), 1)
    for x, face in enumerate((inner_face, outer_face)):
        c = weights[5 + x]
        end_weight = harmonic(c, coef_ref[1 - side if x == 0 else side])
        up_y, up_z = weights[1 + x], weights[3 + x]
        down_y = jnp.where(row == 0, c, pltpu.roll(up_y, 1, 0))
        down_z = pltpu.roll(up_z, 1, 1)
        total = face[...] + weights[0] + up_y + down_y
        total = total + jnp.where(lane == layers - 1, end_weight, up_z)
        terms[x, 0] = total + jnp.where(lane == 0, end_weight, down_z)
        terms[x, 1] = jnp.where(row == 0, 0.0, down_y)
        terms[x, 2] = jnp.where(row == rows - 1, 0.0, up_y)
        terms[x, 3] = jnp.where(lane == 0, 0.0, down_z)
        terms[x, 4] = jnp.where(lane == layers - 1, 0.0, up_z)
        terms[x, 5] = end_weight


def pair_kernel(own, across, beside, oblique, out):
    modes = own.shape[1] // 2
    encode(own[...] + across[...], modes, out.at[0])
    encode(beside[...] + oblique[...], modes, out.at[1])


def single_kernel(own, out):
    encode(own[...], own.shape[1] // 2, out)


def encode(total, modes, out):
    row = lax.broadcasted_iota(jnp.int32, (modes, 2 * modes), 0)
    lane = lax.broadcasted_iota(jnp.int32, (modes, 2 * modes), 1)
    values = total[:modes]
    high = values.astype(BF16).astype(F32)
    low = values - high
    out[:modes] = jnp.where((lane <= row) | (lane >= modes), high, low).astype(BF16)
    diagonal = lane == row
    right = total[modes:modes + 1]
    parts = []
    for _ in range(3):
        part = right.astype(BF16).astype(F32)
        parts.append(part)
        right = right - part
    for part in (high, low):
        parts.append(jnp.sum(jnp.where(diagonal, part, 0.0), axis=0, keepdims=True))
    rows = lax.broadcasted_iota(jnp.int32, (16, 2 * modes), 0)
    extra = jnp.zeros((16, 2 * modes), F32)
    for index, part in enumerate(parts):
        extra = jnp.where(rows == index, part, extra)
    out[modes:] = extra.astype(BF16)


def widen_kernel(pair, zvec, inner_got, outer_got, own_wide, inner_wide, outer_wide):
    modes, half = outer_wide.shape[:2]
    side = lax.rem(here_on("pln"), 2)

    def some(j, carry):
        at = pl.ds(pl.multiple_of(j * MODES, MODES), MODES)
        own_wide[at, 0] = zvec[at, 1 - side].astype(F32)
        own_wide[at, 1] = zvec[at, side].astype(F32)
        inner_wide[at] = inner_got[at].astype(F32)
        outer_wide[at] = outer_got[at].astype(F32)
        return carry

    lax.fori_loop(0, modes // MODES, some, 0)


def finish_kernel(*refs):
    count = len(refs) - 15
    blocks, refs = refs[:count], refs[count:]
    zvec, inner_got, outer_got, outer_last, picked, terms, middle, inner_face, outer_face, resid = refs[:10]
    solution, deflated, direction_ref, spread, outer_field = refs[10:]
    subs = direction_ref.shape[0]
    modes, planes, rows, layers = zvec.shape
    half = rows // 2
    me = here_on("sub")
    side = lax.rem(here_on("pln"), 2)
    odd = lax.rem(me, 2) == 1
    at_edge = ends_the_line()
    held = (1 - side, side)
    square = (modes, modes)
    eye = lax.broadcasted_iota(jnp.int32, square, 0) == lax.broadcasted_iota(jnp.int32, square, 1)

    def column(row):
        return jnp.sum(jnp.where(eye, row, 0.0), axis=1, keepdims=True)

    def each(body, carry):
        for index, block in enumerate(blocks):
            held_here = block.shape[0]
            if held_here <= 8:
                for entry in range(held_here):
                    s = jnp.bitwise_xor(jnp.bitwise_xor(me, mask_of(index, len(blocks))), entry)
                    carry = body(block.at[entry], s, carry)
            else:
                carry = lax.fori_loop(
                    0, held_here, lambda entry, c, block=block: body(block.at[entry], entry, c), carry
                )
        return carry

    def row_is(s, width):
        return lax.broadcasted_iota(jnp.int32, (subs, width), 0) == s

    def load(block, s, carry):
        extra = block[modes:modes + 16, :].astype(F32)
        right = (extra[0:1] + extra[1:2]) + extra[2:3]
        here = row_is(s, 2 * modes)
        return jnp.where(here, right, carry[0]), jnp.where(here, extra[4:5] - extra[3:4], carry[1])

    empty = jnp.zeros((subs, 2 * modes), F32)
    right_side, fix = each(load, (empty, empty))
    fix = fix[:, :modes]

    def turned(rows_of, by):
        by = by % subs
        return jnp.concatenate([rows_of[by:], rows_of[:by]], axis=0)

    def in_parts(value):
        parts = []
        for _ in range(3):
            part = value.astype(BF16)
            parts.append(part.astype(F32))
            value = value - parts[-1]
        return jnp.concatenate(parts, axis=0).astype(BF16)

    def joined(value):
        return (value[:subs] + value[subs:2 * subs]) + value[2 * subs:]

    def coarse_apply(direction):
        pairs = in_parts(jnp.concatenate([direction, turned(direction, 1)], axis=1))
        single = pairs[:, :modes]

        def one(block, s, carry):
            values = block[:modes, :]
            ahead = lax.dot_general(pairs, values, NT, preferred_element_type=F32)
            image = jnp.dot(single, values, preferred_element_type=F32)
            return (
                jnp.where(row_is(s, modes), joined(ahead), carry[0]),
                jnp.where(row_is(s, 2 * modes), joined(image), carry[1]),
            )

        ahead, image = each(one, (jnp.zeros((subs, modes), F32), empty))
        return ahead + image[:, :modes] + fix * direction + turned(image[:, modes:], -1)

    def inner(left, right):
        return jnp.sum(jnp.sum(left * right, axis=0, keepdims=True), axis=1, keepdims=True)

    remain = right_side[:, :modes]
    direction = remain
    result = jnp.zeros_like(remain)
    norm_now = inner(remain, remain)
    for iteration in range(CITERS):
        image = coarse_apply(direction)
        step_size = norm_now / inner(direction, image)
        result = result + step_size * direction
        if iteration + 1 < CITERS:
            remain = remain - step_size * image
            norm_next = inner(remain, remain)
            direction = remain + (norm_next / norm_now) * direction
            norm_now = norm_next
    direction_ref[...] = result
    own = direction_ref[pl.ds(me, 1), :]
    solution[...] = own
    spread[...] = jnp.broadcast_to(column(own), (modes, layers))
    ahead_column = column(direction_ref[pl.ds(lax.rem(me + 1, subs), 1), :])
    behind_column = column(direction_ref[pl.ds(lax.rem(me + subs - 1, subs), 1), :])
    ahead_row = jnp.sum(ahead_column * picked[0], axis=0, keepdims=True)
    behind_row = jnp.sum(behind_column * picked[1], axis=0, keepdims=True)
    width = planes * rows
    both_rows = jnp.where(
        lax.broadcasted_iota(jnp.int32, (8, width), 0) == 0,
        jnp.broadcast_to(ahead_row, (8, width)),
        jnp.broadcast_to(behind_row, (8, width)),
    )
    columns = both_rows.T
    ends = jnp.where(
        lane_is((width, layers), layers - 1),
        columns[:, 0:1],
        jnp.where(lane_is((width, layers), 0), columns[:, 1:2], 0.0),
    ).reshape(planes, rows, layers)

    def add_mode(j, carry):
        fields, near, last = list(carry[0]), carry[1], carry[2]
        for u in range(MODES):
            k = j * MODES + u
            scale = spread[pl.ds(k, 1), :]
            for x, plane in enumerate((zvec[k, 0], zvec[k, 1], inner_got[k])):
                fields[x] = fields[x] + scale * plane
            near = near + scale * outer_got[k]
            last = last + scale * outer_last[k].astype(F32)
        return tuple(fields), near, last

    zero, short = jnp.zeros((rows, layers), F32), jnp.zeros((half, layers), F32)
    field, near, last = lax.fori_loop(0, modes // MODES, add_mode, ((zero,) * 3, short, short))
    outer_field[pl.ds(pl.multiple_of(side * half, half), half), :] = near
    outer_field[pl.ds(pl.multiple_of((1 - side) * half, half), half), :] = last
    outside = (field[2], jnp.where(at_edge, 0.0, outer_field[...]))
    faces = (inner_face[...], outer_face[...])
    for x in range(2):
        f = field[x]
        end_field = jnp.where(side == x, ends[1], ends[0])
        image = (
            terms[x, 0] * f
            - middle[0] * field[1 - x]
            - faces[x] * outside[x]
            - terms[x, 1] * pltpu.roll(f, 1, 0)
            - terms[x, 2] * pltpu.roll(f, rows - 1, 0)
            - terms[x, 3] * pltpu.roll(f, 1, 1)
            - terms[x, 4] * pltpu.roll(f, layers - 1, 1)
            - terms[x, 5] * end_field
        )
        deflated[held[x]] = resid[held[x]] - image


def swapped(value, axis, first):
    count = lax.axis_size(axis)
    pairs = []
    for i in range(count):
        up = (i - first) % 2 == 0
        pairs.append((i, (i + 1) % count if up else (i - 1) % count))
    return lax.ppermute(value, axis, pairs)


def swapped_all(value):
    subs, count = lax.axis_size("sub"), lax.axis_size("pln")
    pairs = []
    for s in range(subs):
        for i in range(count):
            if 0 < i < count - 1:
                to = (s, i + 1 if i % 2 else i - 1)
            else:
                to = (s ^ 1, i)
            pairs.append((s * count + i, to[0] * count + to[1]))
    return lax.ppermute(value, ("sub", "pln"), pairs)


def exchanged(value, axis, mask):
    return lax.ppermute(value, axis, [(i, i ^ mask) for i in range(lax.axis_size(axis))])


def partner(value, sub_mask, pln_mask):
    subs, count = lax.axis_size("sub"), lax.axis_size("pln")
    pairs = [
        (s * count + p, (s ^ sub_mask) * count + (p ^ pln_mask)) for s in range(subs) for p in range(count)
    ]
    return lax.ppermute(value, ("sub", "pln"), pairs)


FAR = (4, 6)


def mask_of(index, count):
    if count == 1:
        return 0
    swap = far_role(here_on("sub"), here_on("pln")) * (FAR[1] - FAR[0])
    return (0, FAR[0] + swap, 2, FAR[1] - swap)[index]


def far_role(s, p):
    return (p ^ (s >> 2)) & 1


def far_partner(value):
    subs, count = lax.axis_size("sub"), lax.axis_size("pln")
    pairs = [
        (s * count + p, (s ^ FAR[far_role(s, p)]) * count + (p ^ 1)) for s in range(subs) for p in range(count)
    ]
    return lax.ppermute(value, ("sub", "pln"), pairs)


def body(labels, levels, zvec, resid):
    modes, planes, rows, layers = zvec.shape
    half = rows // 2
    subs, parts = lax.axis_size("sub"), lax.axis_size("pln")
    shape = jax.ShapeDtypeStruct
    levels = levels.reshape(1, -1)
    pack = shape((modes + 16, planes * rows), BF16)
    inner_send, outer_near = call(
        stage_kernel,
        [shape((modes + 1, rows, layers), BF16), shape((modes + rows // half, half, layers), BF16)],
        [HBM, HBM],
        [pltpu.VMEM(labels.shape, jnp.int32), pltpu.SemaphoreType.DMA, pltpu.SemaphoreType.DMA((2,))],
        moved=2 << 20,
    )(*(pltpu.with_memory_space_constraint(v, pltpu.HBM) for v in (labels, zvec)))
    outer_got = swapped_all(outer_near)
    inner_got = swapped(inner_send, "pln", 0)
    rest = shape((modes, half, layers), BF16)
    outer_rest, one_pack, two_pack = call(
        prepare_kernel,
        [rest, pack, pack],
        [VMEM, VMEM],
        flops=10_000_000,
        moved=6 << 20,
    )(labels, zvec)
    one_got = swapped(one_pack, "sub", 0)
    two_got = swapped(two_pack, "sub", 1)
    field = (planes, rows, layers)
    plane = (rows, layers)
    partial, weights, here = call(
        block_kernel,
        [
            shape((modes + 8, modes), F32),
            shape((7,) + plane, F32),
            shape((planes, rows, modes, layers), BF16),
        ],
        [VMEM] * 4 + [ANY],
        [pltpu.VMEM(field, F32)] * 3,
        flops=400_000_000,
        moved=3 << 20,
    )(levels, labels, resid, zvec, one_pack)
    turned = pltpu.VMEM((half, modes, layers), BF16)
    partial, inner_face = call(
        inner_kernel,
        [shape((modes + 8, modes), F32), shape(plane, F32)],
        [VMEM] * 5,
        [turned],
        flops=100_000_000,
        moved=1 << 20,
    )(levels, partial, weights, here, inner_got)
    block, outer_face = call(
        outer_kernel,
        [shape((modes + 8, 2 * modes), F32), shape(plane, F32)],
        [VMEM] * 9,
        [turned, pltpu.VMEM(plane, F32)],
        flops=100_000_000,
        moved=1 << 20,
    )(levels, partial, weights, here, outer_got, one_pack, two_pack, one_got, two_got)
    packed = (modes + 16, 2 * modes)
    if parts == 4 and subs == 8:
        block = block + exchanged(block, "pln", 1)
        others = [partner(block, *masks) for masks in ((0, 3), (1, 1), (1, 3))]
        [pair] = call(
            pair_kernel, [shape((2,) + packed, BF16)], [VMEM] * 4, flops=1 << 33
        )(block, *others)
        far = far_partner(pair)
        blocks = [pair, far, partner(pair, 2, 1), exchanged(far, "pln", 1)]
    else:
        [single] = call(single_kernel, [shape(packed, BF16)], [VMEM])(lax.psum(block, "pln"))
        blocks = [lax.all_gather(single, "sub")]
    [outer_rest] = call(release_kernel, [rest], [ANY] * 2, aliases={1: 0})(block, outer_rest)
    outer_last = swapped_all(outer_rest)
    terms, picked = call(
        terms_kernel,
        [shape((planes, 6) + plane, F32), shape((2, modes, planes * rows), F32)],
        [VMEM, ANY] + [VMEM] * 5,
        [pltpu.VMEM(field, F32)],

        flops=1 << 31,
        moved=1 << 20,
    )(levels, blocks[0], one_got, two_got, weights, inner_face, outer_face)
    wide = call(
        widen_kernel,
        [
            shape((modes,) + field, F32),
            shape((modes,) + plane, F32),
            shape((modes, half, layers), F32),
        ],
        [ANY] + [VMEM] * 3,
        flops=1 << 30,
        moved=1 << 20,
    )(blocks[0], zvec, inner_got, outer_got)
    return tuple(
        call(
            finish_kernel,
            [shape((1, modes), F32), shape(field, F32)],
            [VMEM] * (10 + len(blocks)),
            [
                pltpu.VMEM((subs, modes), F32),
                pltpu.VMEM((modes, layers), F32),
                pltpu.VMEM(plane, F32),
            ],
            flops=10_000_000,
            moved=5 << 20,
        )(
            *blocks, *wide, outer_last, picked, terms, weights, inner_face,
            outer_face, resid,
        )
    )


def solution(mesh):
    in_specs = (P("pln", None, "sub"), P(), P(None, "pln", None, "sub"), P("pln", None, "sub"))
    out_specs = (P("sub", None), P("pln", None, "sub"))
    return jax.shard_map(body, mesh=mesh, in_specs=in_specs, out_specs=out_specs, check_vma=False)
```

```python
import jax
import jax.numpy as jnp
from jax import lax
from jax.experimental import pallas as pl
from jax.experimental.pallas import tpu as pltpu
from jax.sharding import PartitionSpec as P

CITERS = 2
STEP = 32
MODES = 16
GROUP = 4
CHUNK = 16
F32 = jnp.float32
BF16 = jnp.bfloat16
PRECISE = lax.Precision.HIGHEST
NT = (((1,), (1,)), ((), ()))
TN = (((0,), (0,)), ((), ()))
VMEM = pl.BlockSpec(memory_space=pltpu.VMEM)
HBM = pl.BlockSpec(memory_space=pltpu.HBM)
ANY = pl.BlockSpec(memory_space=pl.ANY)


def call(kernel, outs, specs, scratch=(), flops=0, moved=0, limit=32, aliases=None):
    return pl.pallas_call(
        kernel,
        out_shape=outs,
        in_specs=specs,
        out_specs=[ANY if at in (aliases or {}).values() else VMEM for at in range(len(outs))],
        input_output_aliases=aliases or {},
        scratch_shapes=list(scratch),
        cost_estimate=pl.CostEstimate(flops=flops, bytes_accessed=moved, transcendentals=0),
        compiler_params=pltpu.CompilerParams(vmem_limit_bytes=limit << 20),
    )


def here_on(axis):
    return lax.axis_index(axis).astype(jnp.int32)


def ends_the_line():
    p = here_on("pln")
    return (p == 0) | (p == lax.axis_size("pln") - 1)


def harmonic(left_value, right_value):
    return 2.0 * left_value * right_value / (left_value + right_value)


def coefficients(labels, levels_ref):
    weighted = jnp.zeros(labels.shape, F32)
    for level in range(levels_ref.shape[1]):
        weighted = weighted + jnp.where(labels == level, levels_ref[:, level:level + 1], 0.0)
    return weighted


def lane_is(shape, lane):
    return lax.broadcasted_iota(jnp.int32, shape, len(shape) - 1) == lane


def pick_row(lane, width):
    row = lax.broadcasted_iota(jnp.int32, (16, width), 0)
    return ((row == 0) & lane_is((16, width), lane)).astype(BF16)


def stage_kernel(labels_far, zvec, inner_send, outer_near, labels, label_sem, sems):
    modes, planes, rows, layers = zvec.shape
    half = rows // 2
    side = lax.rem(here_on("pln"), 2)
    start = pl.multiple_of((1 - side) * half, half)
    label_copy = pltpu.make_async_copy(labels_far, labels, label_sem)
    copies = [
        pltpu.make_async_copy(
            zvec.at[:, side, pl.ds(start, half), :], outer_near.at[pl.ds(0, modes)], sems.at[0]
        ),
        pltpu.make_async_copy(zvec.at[:, 1 - side], inner_send.at[pl.ds(0, modes)], sems.at[1]),
    ]
    label_copy.start()
    for copy in copies:
        copy.start()
    label_copy.wait()
    outer_near[modes:] = labels[side].astype(F32).astype(BF16).reshape(rows // half, half, layers)
    inner_send[modes] = labels[1 - side].astype(F32).astype(BF16)
    for copy in copies:
        copy.wait()


def release_kernel(after, outer_rest, outer_out):
    pass


def prepare_kernel(labels, held, outer_rest, one_pack, two_pack):
    modes, planes, rows, layers = held.shape
    half = rows // 2
    width = planes * rows
    side = lax.rem(here_on("pln"), 2)
    odd = lax.rem(here_on("sub"), 2) == 1
    one_lane = jnp.where(odd, 0, layers - 1)
    two_lane = jnp.where(odd, layers - 1, 0)
    row = lax.broadcasted_iota(jnp.int32, (16, layers), 0)
    both = ((row == 0) & lane_is((16, layers), one_lane)) | ((row == 1) & lane_is((16, layers), two_lane))
    both = both.astype(BF16)
    flat = labels[...].astype(F32).astype(BF16).reshape(width, layers)
    for out, lane in ((one_pack, one_lane), (two_pack, two_lane)):
        out[modes:] = lax.dot_general(
            pick_row(lane, layers), flat, NT, preferred_element_type=F32
        ).astype(BF16)
    for k in range(0, modes, CHUNK):
        at = slice(k, k + CHUNK)
        ends = lax.dot_general(
            both, held[at].reshape(-1, layers), NT, preferred_element_type=F32
        )
        for out, index in ((one_pack, 0), (two_pack, 1)):
            out[at] = jnp.concatenate(
                [ends[index:index + 1, j * width:(j + 1) * width] for j in range(CHUNK)], axis=0
            ).astype(BF16)
        outer_rest[at] = held[at, side, pl.ds(pl.multiple_of(side * half, half), half), :]


def block_kernel(
    levels, labels, resid, zvec, after, partial, weights, here, half_diag, link_y, link_z,
):
    planes, rows, layers = labels.shape
    modes = here.shape[2]
    side = lax.rem(here_on("pln"), 2)
    at_edge = ends_the_line()
    held = (1 - side, side)

    def turn_rows(start):
        for slot, plane in enumerate(held):
            for k in range(0, modes, CHUNK):
                block = zvec[k:k + CHUNK, plane, pl.ds(start, STEP), :]
                here[slot, pl.ds(start, STEP), k:k + CHUNK, :] = jnp.swapaxes(block, 0, 1)

    turn_rows(0)
    coef = [coefficients(labels[x], levels) for x in held]
    middle = harmonic(coef[0], coef[1])
    weights[0] = middle
    row = lax.broadcasted_iota(jnp.int32, (rows, layers), 0)
    lane = lax.broadcasted_iota(jnp.int32, (rows, layers), 1)
    for x in range(2):
        c = coef[x]
        up_y = harmonic(c, jnp.where(row == rows - 1, c, pltpu.roll(c, rows - 1, 0)))
        up_z = harmonic(c, pltpu.roll(c, layers - 1, 1))
        down_y = jnp.where(row == 0, c, pltpu.roll(up_y, 1, 0))
        weights[1 + x] = up_y
        weights[3 + x] = up_z
        weights[5 + x] = c
        inner_z = jnp.where(lane == layers - 1, 0.0, up_z)
        total = middle + up_y + down_y + inner_z + pltpu.roll(inner_z, 1, 1)
        if x == 1:
            total = total + jnp.where(at_edge, c, 0.0)
        half_diag[x] = 0.5 * total
        link_y[x] = jnp.where(row == rows - 1, 0.0, up_y)
        link_z[x] = inner_z

    def step(j, carry):
        total, wide = carry
        turn_rows(pl.multiple_of(jnp.minimum((j + 1) * STEP, rows - STEP), STEP))
        left, right = [], []
        for u in range(STEP):
            y = j * STEP + u
            at = pl.ds(y, 1)
            ahead = jnp.minimum(y + 1, rows - 1)
            up = [here[x, ahead].astype(F32) for x in range(2)]
            images, parts = [], []
            for x in range(2):
                image = (
                    half_diag[x, at, :] * wide[x]
                    - link_y[x, at, :] * up[x]
                    - link_z[x, at, :] * pltpu.roll(here[x, y], layers - 1, 1).astype(F32)
                )
                if x == 0:
                    image = image - weights[0, at, :] * wide[1]
                images.append(image.astype(BF16))
                value = resid[held[x], at, :]
                high = value.astype(BF16).astype(F32)
                part = jnp.where(part_row == 0, high, jnp.where(part_row == 1, value - high, 0.0))
                parts.append(part.astype(BF16))
            left.append(
                jnp.concatenate(
                    [jnp.concatenate(images, axis=1), jnp.concatenate(parts, axis=1)], axis=0
                )
            )
            right.append(jnp.concatenate([here[0, y], here[1, y]], axis=1))
            if len(left) == GROUP:
                total = total + lax.dot_general(
                    jnp.concatenate(left, axis=1), jnp.concatenate(right, axis=1), NT,
                    preferred_element_type=F32,
                )
                left, right = [], []
            wide = up
        return total, wide

    part_row = lax.broadcasted_iota(jnp.int32, (16, layers), 0)
    total, _ = lax.fori_loop(
        0,
        rows // STEP,
        step,
        (
            jnp.zeros((modes + 16, modes), F32),
            [here[x, 0].astype(F32) for x in range(2)],
        ),
    )
    partial[:modes, :] = total[:modes]
    partial[modes:, :] = jnp.broadcast_to(total[modes:modes + 1] + total[modes + 1:modes + 2], (8, modes))


def turn(got, start, out):
    half, modes, layers = out.shape
    for k in range(0, modes, CHUNK):
        out[:, k:k + CHUNK, :] = jnp.swapaxes(got[k:k + CHUNK, pl.ds(start, half), :], 0, 1)


def face_product(weight_ref, base, own, other):
    half, modes, layers = other.shape

    def step(j, total):
        left, right = [], []
        for u in range(STEP):
            y = j * STEP + u
            weight = weight_ref[pl.ds(base + y, 1), :]
            image = weight * (own[base + y].astype(F32) - other[y].astype(F32))
            left.append(jnp.concatenate([own[base + y], other[y]], axis=0))
            right.append(image.astype(BF16))
        return total + lax.dot_general(
            jnp.concatenate(left, axis=1), jnp.concatenate(right, axis=1), NT,
            preferred_element_type=F32,
        )

    total = lax.fori_loop(0, half // STEP, step, jnp.zeros((2 * modes, modes), F32))
    return total[:modes] - total[modes:]


def inner_kernel(levels, partial, weights, here, inner_got, out, face, turned):
    planes, rows, modes, layers = here.shape
    half = rows // 2
    side = lax.rem(here_on("pln"), 2)
    base = pl.multiple_of(side * half, half)
    turn(inner_got, base, turned)
    face[...] = harmonic(weights[5], coefficients(inner_got[modes].astype(F32), levels))
    out[:modes, :] = partial[:modes, :] + 0.5 * face_product(face, base, here.at[0], turned)
    out[modes:, :] = partial[modes:, :]


def outer_kernel(
    levels, partial, weights, here, outer_got, one_pack, two_pack, one_got, two_got,
    out, face, turned, face_here,
):
    planes, rows, modes, layers = here.shape
    half = rows // 2
    side = lax.rem(here_on("pln"), 2)
    at_edge = ends_the_line()
    base = pl.multiple_of(side * half, half)
    turn(outer_got, 0, turned)
    coef = coefficients(outer_got[modes:].astype(F32).reshape(rows, layers), levels)
    between = harmonic(weights[6], coef)
    face[...] = jnp.where(at_edge, weights[6], between)
    face_here[...] = jnp.where(at_edge, 0.0, between)
    cross = face_product(face_here, base, here.at[1], turned)
    odd = lax.rem(here_on("sub"), 2) == 1

    def coef_row(pack):
        return coefficients(pack[modes:modes + 16].astype(F32)[0:1], levels)

    one, two = one_pack[...].astype(F32), two_pack[...].astype(F32)
    one_other, two_other = one_got[...].astype(F32), two_got[...].astype(F32)
    first, last = jnp.where(odd, one, two), jnp.where(odd, two, one)
    next_first = jnp.where(odd, two_other, one_other)
    prev_last = jnp.where(odd, one_other, two_other)
    weight_low = harmonic(coef_row(first), coef_row(prev_last))
    weight_high = harmonic(coef_row(last), coef_row(next_first))

    def product(left, right):
        return lax.dot_general(
            left.astype(BF16), right.astype(BF16), NT, preferred_element_type=F32
        )

    edge_rows = weight_high * last[:modes]
    ends = product(
        jnp.concatenate([weight_low * first[:modes], edge_rows], axis=1),
        jnp.concatenate([first[:modes], last[:modes]], axis=1),
    )
    square = partial[:modes, :] + 0.5 * (cross + ends)
    out[:modes, :modes] = square + square.T
    out[:modes, modes:] = -product(edge_rows, next_first[:modes])
    out[modes:, :modes] = partial[modes:, :]
    out[modes:, modes:] = jnp.zeros((8, modes), F32)


def terms_kernel(
    levels, pair, one_got, two_got, weights, inner_face, outer_face, terms, picked, coef_ref
):
    modes, width = picked.shape[1:]
    rows, layers = inner_face.shape
    side = lax.rem(here_on("pln"), 2)
    odd = lax.rem(here_on("sub"), 2) == 1
    one_other, two_other = one_got[...].astype(F32), two_got[...].astype(F32)
    next_first = jnp.where(odd, two_other, one_other)
    prev_last = jnp.where(odd, one_other, two_other)
    picked[0] = next_first[:modes]
    picked[1] = prev_last[:modes]
    end_labels = lax.dot_general(
        next_first[modes:].astype(BF16), pick_row(layers - 1, layers), TN, preferred_element_type=F32
    ) + lax.dot_general(
        prev_last[modes:].astype(BF16), pick_row(0, layers), TN, preferred_element_type=F32
    )
    coef_ref[...] = coefficients(end_labels, levels).reshape(width // rows, rows, layers)
    row = lax.broadcasted_iota(jnp.int32, (rows, layers), 0)
    lane = lax.broadcasted_iota(jnp.int32, (rows, layers), 1)
    for x, face in enumerate((inner_face, outer_face)):
        c = weights[5 + x]
        end_weight = harmonic(c, coef_ref[1 - side if x == 0 else side])
        up_y, up_z = weights[1 + x], weights[3 + x]
        down_y = jnp.where(row == 0, c, pltpu.roll(up_y, 1, 0))
        down_z = pltpu.roll(up_z, 1, 1)
        total = face[...] + weights[0] + up_y + down_y
        total = total + jnp.where(lane == layers - 1, end_weight, up_z)
        terms[x, 0] = total + jnp.where(lane == 0, end_weight, down_z)
        terms[x, 1] = jnp.where(row == 0, 0.0, down_y)
        terms[x, 2] = jnp.where(row == rows - 1, 0.0, up_y)
        terms[x, 3] = jnp.where(lane == 0, 0.0, down_z)
        terms[x, 4] = jnp.where(lane == layers - 1, 0.0, up_z)
        terms[x, 5] = end_weight


def pair_kernel(own, across, beside, oblique, out):
    modes = own.shape[1] // 2
    encode(own[...] + across[...], modes, out.at[0])
    encode(beside[...] + oblique[...], modes, out.at[1])


def single_kernel(own, out):
    encode(own[...], own.shape[1] // 2, out)


def encode(total, modes, out):
    row = lax.broadcasted_iota(jnp.int32, (modes, 2 * modes), 0)
    lane = lax.broadcasted_iota(jnp.int32, (modes, 2 * modes), 1)
    values = total[:modes]
    high = values.astype(BF16).astype(F32)
    low = values - high
    out[:modes] = jnp.where((lane <= row) | (lane >= modes), high, low).astype(BF16)
    diagonal = lane == row
    right = total[modes:modes + 1]
    parts = []
    for _ in range(3):
        part = right.astype(BF16).astype(F32)
        parts.append(part)
        right = right - part
    for part in (high, low):
        parts.append(jnp.sum(jnp.where(diagonal, part, 0.0), axis=0, keepdims=True))
    rows = lax.broadcasted_iota(jnp.int32, (16, 2 * modes), 0)
    extra = jnp.zeros((16, 2 * modes), F32)
    for index, part in enumerate(parts):
        extra = jnp.where(rows == index, part, extra)
    out[modes:] = extra.astype(BF16)


def widen_kernel(pair, zvec, inner_got, outer_got, own_wide, inner_wide, outer_wide):
    modes, half = outer_wide.shape[:2]
    side = lax.rem(here_on("pln"), 2)

    def some(j, carry):
        at = pl.ds(pl.multiple_of(j * MODES, MODES), MODES)
        own_wide[at, 0] = zvec[at, 1 - side].astype(F32)
        own_wide[at, 1] = zvec[at, side].astype(F32)
        inner_wide[at] = inner_got[at].astype(F32)
        outer_wide[at] = outer_got[at].astype(F32)
        return carry

    lax.fori_loop(0, modes // MODES, some, 0)


def finish_kernel(*refs):
    count = len(refs) - 15
    blocks, refs = refs[:count], refs[count:]
    zvec, inner_got, outer_got, outer_last, picked, terms, middle, inner_face, outer_face, resid = refs[:10]
    solution, deflated, direction_ref, spread, outer_field = refs[10:]
    subs = direction_ref.shape[0]
    modes, planes, rows, layers = zvec.shape
    half = rows // 2
    me = here_on("sub")
    side = lax.rem(here_on("pln"), 2)
    odd = lax.rem(me, 2) == 1
    at_edge = ends_the_line()
    held = (1 - side, side)
    square = (modes, modes)
    eye = lax.broadcasted_iota(jnp.int32, square, 0) == lax.broadcasted_iota(jnp.int32, square, 1)

    def column(row):
        return jnp.sum(jnp.where(eye, row, 0.0), axis=1, keepdims=True)

    def each(body, carry):
        for index, block in enumerate(blocks):
            held_here = block.shape[0]
            if held_here <= 8:
                for entry in range(held_here):
                    s = jnp.bitwise_xor(jnp.bitwise_xor(me, mask_of(index, len(blocks))), entry)
                    carry = body(block.at[entry], s, carry)
            else:
                carry = lax.fori_loop(
                    0, held_here, lambda entry, c, block=block: body(block.at[entry], entry, c), carry
                )
        return carry

    def row_is(s, width):
        return lax.broadcasted_iota(jnp.int32, (subs, width), 0) == s

    def load(block, s, carry):
        extra = block[modes:modes + 16, :].astype(F32)
        right = (extra[0:1] + extra[1:2]) + extra[2:3]
        here = row_is(s, 2 * modes)
        return jnp.where(here, right, carry[0]), jnp.where(here, extra[4:5] - extra[3:4], carry[1])

    empty = jnp.zeros((subs, 2 * modes), F32)
    right_side, fix = each(load, (empty, empty))
    fix = fix[:, :modes]

    def turned(rows_of, by):
        by = by % subs
        return jnp.concatenate([rows_of[by:], rows_of[:by]], axis=0)

    def in_parts(value):
        parts = []
        for _ in range(3):
            part = value.astype(BF16)
            parts.append(part.astype(F32))
            value = value - parts[-1]
        return jnp.concatenate(parts, axis=0).astype(BF16)

    def joined(value):
        return (value[:subs] + value[subs:2 * subs]) + value[2 * subs:]

    def coarse_apply(direction):
        pairs = in_parts(jnp.concatenate([direction, turned(direction, 1)], axis=1))
        single = pairs[:, :modes]

        def one(block, s, carry):
            values = block[:modes, :]
            ahead = lax.dot_general(pairs, values, NT, preferred_element_type=F32)
            image = jnp.dot(single, values, preferred_element_type=F32)
            return (
                jnp.where(row_is(s, modes), joined(ahead), carry[0]),
                jnp.where(row_is(s, 2 * modes), joined(image), carry[1]),
            )

        ahead, image = each(one, (jnp.zeros((subs, modes), F32), empty))
        return ahead + image[:, :modes] + fix * direction + turned(image[:, modes:], -1)

    def inner(left, right):
        return jnp.sum(jnp.sum(left * right, axis=0, keepdims=True), axis=1, keepdims=True)

    remain = right_side[:, :modes]
    direction = remain
    result = jnp.zeros_like(remain)
    norm_now = inner(remain, remain)
    for iteration in range(CITERS):
        image = coarse_apply(direction)
        step_size = norm_now / inner(direction, image)
        result = result + step_size * direction
        if iteration + 1 < CITERS:
            remain = remain - step_size * image
            norm_next = inner(remain, remain)
            direction = remain + (norm_next / norm_now) * direction
            norm_now = norm_next
    direction_ref[...] = result
    own = direction_ref[pl.ds(me, 1), :]
    solution[...] = own
    spread[...] = jnp.broadcast_to(column(own), (modes, layers))
    ahead_column = column(direction_ref[pl.ds(lax.rem(me + 1, subs), 1), :])
    behind_column = column(direction_ref[pl.ds(lax.rem(me + subs - 1, subs), 1), :])
    ahead_row = jnp.sum(ahead_column * picked[0], axis=0, keepdims=True)
    behind_row = jnp.sum(behind_column * picked[1], axis=0, keepdims=True)
    width = planes * rows
    both_rows = jnp.where(
        lax.broadcasted_iota(jnp.int32, (8, width), 0) == 0,
        jnp.broadcast_to(ahead_row, (8, width)),
        jnp.broadcast_to(behind_row, (8, width)),
    )
    columns = both_rows.T
    ends = jnp.where(
        lane_is((width, layers), layers - 1),
        columns[:, 0:1],
        jnp.where(lane_is((width, layers), 0), columns[:, 1:2], 0.0),
    ).reshape(planes, rows, layers)

    def add_mode(j, carry):
        fields, near, last = list(carry[0]), carry[1], carry[2]
        for u in range(MODES):
            k = j * MODES + u
            scale = spread[pl.ds(k, 1), :]
            for x, plane in enumerate((zvec[k, 0], zvec[k, 1], inner_got[k])):
                fields[x] = fields[x] + scale * plane
            near = near + scale * outer_got[k]
            last = last + scale * outer_last[k].astype(F32)
        return tuple(fields), near, last

    zero, short = jnp.zeros((rows, layers), F32), jnp.zeros((half, layers), F32)
    field, near, last = lax.fori_loop(0, modes // MODES, add_mode, ((zero,) * 3, short, short))
    outer_field[pl.ds(pl.multiple_of(side * half, half), half), :] = near
    outer_field[pl.ds(pl.multiple_of((1 - side) * half, half), half), :] = last
    outside = (field[2], jnp.where(at_edge, 0.0, outer_field[...]))
    faces = (inner_face[...], outer_face[...])
    for x in range(2):
        f = field[x]
        end_field = jnp.where(side == x, ends[1], ends[0])
        image = (
            terms[x, 0] * f
            - middle[0] * field[1 - x]
            - faces[x] * outside[x]
            - terms[x, 1] * pltpu.roll(f, 1, 0)
            - terms[x, 2] * pltpu.roll(f, rows - 1, 0)
            - terms[x, 3] * pltpu.roll(f, 1, 1)
            - terms[x, 4] * pltpu.roll(f, layers - 1, 1)
            - terms[x, 5] * end_field
        )
        deflated[held[x]] = resid[held[x]] - image


def swapped(value, axis, first):
    count = lax.axis_size(axis)
    pairs = []
    for i in range(count):
        up = (i - first) % 2 == 0
        pairs.append((i, (i + 1) % count if up else (i - 1) % count))
    return lax.ppermute(value, axis, pairs)


def swapped_all(value):
    subs, count = lax.axis_size("sub"), lax.axis_size("pln")
    pairs = []
    for s in range(subs):
        for i in range(count):
            if 0 < i < count - 1:
                to = (s, i + 1 if i % 2 else i - 1)
            else:
                to = (s ^ 1, i)
            pairs.append((s * count + i, to[0] * count + to[1]))
    return lax.ppermute(value, ("sub", "pln"), pairs)


def exchanged(value, axis, mask):
    return lax.ppermute(value, axis, [(i, i ^ mask) for i in range(lax.axis_size(axis))])


def partner(value, sub_mask, pln_mask):
    subs, count = lax.axis_size("sub"), lax.axis_size("pln")
    pairs = [
        (s * count + p, (s ^ sub_mask) * count + (p ^ pln_mask)) for s in range(subs) for p in range(count)
    ]
    return lax.ppermute(value, ("sub", "pln"), pairs)


FAR = (4, 6)


def mask_of(index, count):
    if count == 1:
        return 0
    swap = far_role(here_on("sub"), here_on("pln")) * (FAR[1] - FAR[0])
    return (0, FAR[0] + swap, 2, FAR[1] - swap)[index]


def far_role(s, p):
    return (p ^ (s >> 2)) & 1


def far_partner(value):
    subs, count = lax.axis_size("sub"), lax.axis_size("pln")
    pairs = [
        (s * count + p, (s ^ FAR[far_role(s, p)]) * count + (p ^ 1)) for s in range(subs) for p in range(count)
    ]
    return lax.ppermute(value, ("sub", "pln"), pairs)


def body(labels, levels, zvec, resid):
    modes, planes, rows, layers = zvec.shape
    half = rows // 2
    subs, parts = lax.axis_size("sub"), lax.axis_size("pln")
    shape = jax.ShapeDtypeStruct
    levels = levels.reshape(1, -1)
    pack = shape((modes + 16, planes * rows), BF16)
    inner_send, outer_near = call(
        stage_kernel,
        [shape((modes + 1, rows, layers), BF16), shape((modes + rows // half, half, layers), BF16)],
        [HBM, HBM],
        [pltpu.VMEM(labels.shape, jnp.int32), pltpu.SemaphoreType.DMA, pltpu.SemaphoreType.DMA((2,))],
        moved=2 << 20,
    )(*(pltpu.with_memory_space_constraint(v, pltpu.HBM) for v in (labels, zvec)))
    outer_got = swapped_all(outer_near)
    inner_got = swapped(inner_send, "pln", 0)
    rest = shape((modes, half, layers), BF16)
    outer_rest, one_pack, two_pack = call(
        prepare_kernel,
        [rest, pack, pack],
        [VMEM, VMEM],
        flops=10_000_000,
        moved=6 << 20,
    )(labels, zvec)
    one_got = swapped(one_pack, "sub", 0)
    two_got = swapped(two_pack, "sub", 1)
    field = (planes, rows, layers)
    plane = (rows, layers)
    partial, weights, here = call(
        block_kernel,
        [
            shape((modes + 8, modes), F32),
            shape((7,) + plane, F32),
            shape((planes, rows, modes, layers), BF16),
        ],
        [VMEM] * 4 + [ANY],
        [pltpu.VMEM(field, F32)] * 3,
        flops=400_000_000,
        moved=3 << 20,
    )(levels, labels, resid, zvec, one_pack)
    turned = pltpu.VMEM((half, modes, layers), BF16)
    partial, inner_face = call(
        inner_kernel,
        [shape((modes + 8, modes), F32), shape(plane, F32)],
        [VMEM] * 5,
        [turned],
        flops=100_000_000,
        moved=1 << 20,
    )(levels, partial, weights, here, inner_got)
    block, outer_face = call(
        outer_kernel,
        [shape((modes + 8, 2 * modes), F32), shape(plane, F32)],
        [VMEM] * 9,
        [turned, pltpu.VMEM(plane, F32)],
        flops=100_000_000,
        moved=1 << 20,
    )(levels, partial, weights, here, outer_got, one_pack, two_pack, one_got, two_got)
    packed = (modes + 16, 2 * modes)
    if parts == 4 and subs == 8:
        block = block + exchanged(block, "pln", 1)
        others = [partner(block, *masks) for masks in ((0, 3), (1, 1), (1, 3))]
        [pair] = call(
            pair_kernel, [shape((2,) + packed, BF16)], [VMEM] * 4, flops=1 << 33
        )(block, *others)
        far = far_partner(pair)
        blocks = [pair, far, partner(pair, 2, 1), exchanged(far, "pln", 1)]
    else:
        [single] = call(single_kernel, [shape(packed, BF16)], [VMEM])(lax.psum(block, "pln"))
        blocks = [lax.all_gather(single, "sub")]
    [outer_rest] = call(release_kernel, [rest], [ANY] * 2, aliases={1: 0})(block, outer_rest)
    outer_last = swapped_all(outer_rest)
    terms, picked = call(
        terms_kernel,
        [shape((planes, 6) + plane, F32), shape((2, modes, planes * rows), F32)],
        [VMEM, ANY] + [VMEM] * 5,
        [pltpu.VMEM(field, F32)],

        flops=1 << 31,
        moved=1 << 20,
    )(levels, blocks[0], one_got, two_got, weights, inner_face, outer_face)
    wide = call(
        widen_kernel,
        [
            shape((modes,) + field, F32),
            shape((modes,) + plane, F32),
            shape((modes, half, layers), F32),
        ],
        [ANY] + [VMEM] * 3,
        flops=1 << 30,
        moved=1 << 20,
    )(blocks[0], zvec, inner_got, outer_got)
    return tuple(
        call(
            finish_kernel,
            [shape((1, modes), F32), shape(field, F32)],
            [VMEM] * (10 + len(blocks)),
            [
                pltpu.VMEM((subs, modes), F32),
                pltpu.VMEM((modes, layers), F32),
                pltpu.VMEM(plane, F32),
            ],
            flops=10_000_000,
            moved=5 << 20,
        )(
            *blocks, *wide, outer_last, picked, terms, weights, inner_face,
            outer_face, resid,
        )
    )


def solution(mesh):
    in_specs = (P("pln", None, "sub"), P(), P(None, "pln", None, "sub"), P("pln", None, "sub"))
    out_specs = (P("sub", None), P("pln", None, "sub"))
    return jax.shard_map(body, mesh=mesh, in_specs=in_specs, out_specs=out_specs, check_vma=False)
```

```python
import jax
import jax.numpy as jnp
from jax import lax
from jax.experimental import pallas as pl
from jax.experimental.pallas import tpu as pltpu
from jax.sharding import PartitionSpec as P

CITERS = 2
STEP = 32
MODES = 16
CHUNK = 16
F32 = jnp.float32
BF16 = jnp.bfloat16
PRECISE = lax.Precision.HIGHEST
NT = (((1,), (1,)), ((), ()))
TN = (((0,), (0,)), ((), ()))
VMEM = pl.BlockSpec(memory_space=pltpu.VMEM)
HBM = pl.BlockSpec(memory_space=pltpu.HBM)
ANY = pl.BlockSpec(memory_space=pl.ANY)


def call(kernel, outs, specs, scratch=(), flops=0, moved=0, limit=32, aliases=None, far=()):
    return pl.pallas_call(
        kernel,
        out_shape=outs,
        in_specs=specs,
        out_specs=[
            HBM if at in far else ANY if at in (aliases or {}).values() else VMEM for at in range(len(outs))
        ],
        input_output_aliases=aliases or {},
        scratch_shapes=list(scratch),
        cost_estimate=pl.CostEstimate(flops=flops, bytes_accessed=moved, transcendentals=0),
        compiler_params=pltpu.CompilerParams(vmem_limit_bytes=limit << 20),
    )


def here_on(axis):
    return lax.axis_index(axis).astype(jnp.int32)


def ends_the_line():
    p = here_on("pln")
    return (p == 0) | (p == lax.axis_size("pln") - 1)


def harmonic(left_value, right_value):
    return 2.0 * left_value * right_value / (left_value + right_value)


def coefficients(labels, levels_ref):
    weighted = jnp.zeros(labels.shape, F32)
    for level in range(levels_ref.shape[1]):
        weighted = weighted + jnp.where(labels == level, levels_ref[:, level:level + 1], 0.0)
    return weighted


def lane_is(shape, lane):
    return lax.broadcasted_iota(jnp.int32, shape, len(shape) - 1) == lane


def pick_row(lane, width):
    row = lax.broadcasted_iota(jnp.int32, (16, width), 0)
    return ((row == 0) & lane_is((16, width), lane)).astype(BF16)


def stage_kernel(labels_far, zvec, inner_send, outer_near, labels, label_sem, sems):
    modes, planes, rows, layers = zvec.shape
    half = rows // 2
    side = lax.rem(here_on("pln"), 2)
    start = pl.multiple_of((1 - side) * half, half)
    label_copy = pltpu.make_async_copy(labels_far, labels, label_sem)
    copies = [
        pltpu.make_async_copy(
            zvec.at[:, side, pl.ds(start, half), :], outer_near.at[pl.ds(0, modes)], sems.at[0]
        ),
        pltpu.make_async_copy(zvec.at[:, 1 - side], inner_send.at[pl.ds(0, modes)], sems.at[1]),
    ]
    label_copy.start()
    for copy in copies:
        copy.start()
    label_copy.wait()
    outer_near[modes:] = labels[side].astype(F32).astype(BF16).reshape(rows // half, half, layers)
    inner_send[modes] = labels[1 - side].astype(F32).astype(BF16)
    for copy in copies:
        copy.wait()


def release_kernel(after, outer_rest, outer_out):
    pass


def prepare_kernel(labels, held, outer_rest, one_pack, two_pack):
    modes, planes, rows, layers = held.shape
    half = rows // 2
    width = planes * rows
    side = lax.rem(here_on("pln"), 2)
    odd = lax.rem(here_on("sub"), 2) == 1
    one_lane = jnp.where(odd, 0, layers - 1)
    two_lane = jnp.where(odd, layers - 1, 0)
    row = lax.broadcasted_iota(jnp.int32, (16, layers), 0)
    both = ((row == 0) & lane_is((16, layers), one_lane)) | ((row == 1) & lane_is((16, layers), two_lane))
    both = both.astype(BF16)
    flat = labels[...].astype(F32).astype(BF16).reshape(width, layers)
    for out, lane in ((one_pack, one_lane), (two_pack, two_lane)):
        out[modes:] = lax.dot_general(
            pick_row(lane, layers), flat, NT, preferred_element_type=F32
        ).astype(BF16)
    for k in range(0, modes, CHUNK):
        at = slice(k, k + CHUNK)
        ends = lax.dot_general(
            both, held[at].reshape(-1, layers), NT, preferred_element_type=F32
        )
        for out, index in ((one_pack, 0), (two_pack, 1)):
            out[at] = jnp.concatenate(
                [ends[index:index + 1, j * width:(j + 1) * width] for j in range(CHUNK)], axis=0
            ).astype(BF16)
        outer_rest[at] = held[at, side, pl.ds(pl.multiple_of(side * half, half), half), :]


def block_kernel(
    levels, labels, resid, zvec, after, partial, weights, here, half_diag, link_y, link_z,
):
    planes, rows, layers = labels.shape
    modes = here.shape[2]
    side = lax.rem(here_on("pln"), 2)
    at_edge = ends_the_line()
    held = (1 - side, side)

    def turn_rows(start):
        for slot, plane in enumerate(held):
            for k in range(0, modes, CHUNK):
                block = zvec[k:k + CHUNK, plane, pl.ds(start, STEP), :]
                here[slot, pl.ds(start, STEP), k:k + CHUNK, :] = jnp.swapaxes(block, 0, 1)

    turn_rows(0)
    coef = [coefficients(labels[x], levels) for x in held]
    middle = harmonic(coef[0], coef[1])
    weights[0] = middle
    row = lax.broadcasted_iota(jnp.int32, (rows, layers), 0)
    lane = lax.broadcasted_iota(jnp.int32, (rows, layers), 1)
    for x in range(2):
        c = coef[x]
        up_y = harmonic(c, jnp.where(row == rows - 1, c, pltpu.roll(c, rows - 1, 0)))
        up_z = harmonic(c, pltpu.roll(c, layers - 1, 1))
        down_y = jnp.where(row == 0, c, pltpu.roll(up_y, 1, 0))
        weights[1 + x] = up_y
        weights[3 + x] = up_z
        weights[5 + x] = c
        inner_z = jnp.where(lane == layers - 1, 0.0, up_z)
        total = middle + up_y + down_y + inner_z + pltpu.roll(inner_z, 1, 1)
        if x == 1:
            total = total + jnp.where(at_edge, c, 0.0)
        half_diag[x] = 0.5 * total
        link_y[x] = jnp.where(row == rows - 1, 0.0, up_y)
        link_z[x] = inner_z

    def step(j, carry):
        total, wide = carry
        turn_rows(pl.multiple_of(jnp.minimum((j + 1) * STEP, rows - STEP), STEP))
        for u in range(STEP):
            y = j * STEP + u
            at = pl.ds(y, 1)
            ahead = jnp.minimum(y + 1, rows - 1)
            up = [here[x, ahead].astype(F32) for x in range(2)]
            images, parts = [], []
            for x in range(2):
                image = (
                    half_diag[x, at, :] * wide[x]
                    - link_y[x, at, :] * up[x]
                    - link_z[x, at, :] * pltpu.roll(here[x, y], layers - 1, 1).astype(F32)
                )
                if x == 0:
                    image = image - weights[0, at, :] * wide[1]
                images.append(image.astype(BF16))
                value = resid[held[x], at, :]
                high = value.astype(BF16).astype(F32)
                part = jnp.where(part_row == 0, high, jnp.where(part_row == 1, value - high, 0.0))
                parts.append(part.astype(BF16))
            total = total + lax.dot_general(
                jnp.concatenate(
                    [jnp.concatenate(images, axis=1), jnp.concatenate(parts, axis=1)], axis=0
                ),
                jnp.concatenate([here[0, y], here[1, y]], axis=1),
                NT,
                preferred_element_type=F32,
            )
            wide = up
        return total, wide

    part_row = lax.broadcasted_iota(jnp.int32, (16, layers), 0)
    total, _ = lax.fori_loop(
        0,
        rows // STEP,
        step,
        (
            jnp.zeros((modes + 16, modes), F32),
            [here[x, 0].astype(F32) for x in range(2)],
        ),
    )
    partial[:modes, :] = total[:modes]
    partial[modes:, :] = jnp.broadcast_to(total[modes:modes + 1] + total[modes + 1:modes + 2], (8, modes))


def turn(got, start, out):
    half, modes, layers = out.shape
    for k in range(0, modes, CHUNK):
        out[:, k:k + CHUNK, :] = jnp.swapaxes(got[k:k + CHUNK, pl.ds(start, half), :], 0, 1)


def face_product(weight_ref, base, own, other):
    half, modes, layers = other.shape

    def step(j, total):
        left, right = [], []
        for u in range(STEP):
            y = j * STEP + u
            weight = weight_ref[pl.ds(base + y, 1), :]
            image = weight * (own[base + y].astype(F32) - other[y].astype(F32))
            left.append(jnp.concatenate([own[base + y], other[y]], axis=0))
            right.append(image.astype(BF16))
        return total + lax.dot_general(
            jnp.concatenate(left, axis=1), jnp.concatenate(right, axis=1), NT,
            preferred_element_type=F32,
        )

    total = lax.fori_loop(0, half // STEP, step, jnp.zeros((2 * modes, modes), F32))
    return total[:modes] - total[modes:]


def inner_kernel(levels, partial, weights, here, inner_got, out, face, turned):
    planes, rows, modes, layers = here.shape
    half = rows // 2
    side = lax.rem(here_on("pln"), 2)
    base = pl.multiple_of(side * half, half)
    turn(inner_got, base, turned)
    face[...] = harmonic(weights[5], coefficients(inner_got[modes].astype(F32), levels))
    out[:modes, :] = partial[:modes, :] + 0.5 * face_product(face, base, here.at[0], turned)
    out[modes:, :] = partial[modes:, :]


def outer_kernel(
    levels, partial, weights, here, outer_got, one_pack, two_pack, one_got, two_got,
    out, face, turned, face_here,
):
    planes, rows, modes, layers = here.shape
    half = rows // 2
    side = lax.rem(here_on("pln"), 2)
    at_edge = ends_the_line()
    base = pl.multiple_of(side * half, half)
    turn(outer_got, 0, turned)
    coef = coefficients(outer_got[modes:].astype(F32).reshape(rows, layers), levels)
    between = harmonic(weights[6], coef)
    face[...] = jnp.where(at_edge, weights[6], between)
    face_here[...] = jnp.where(at_edge, 0.0, between)
    cross = face_product(face_here, base, here.at[1], turned)
    odd = lax.rem(here_on("sub"), 2) == 1

    def coef_row(pack):
        return coefficients(pack[modes:modes + 16].astype(F32)[0:1], levels)

    one, two = one_pack[...].astype(F32), two_pack[...].astype(F32)
    one_other, two_other = one_got[...].astype(F32), two_got[...].astype(F32)
    first, last = jnp.where(odd, one, two), jnp.where(odd, two, one)
    next_first = jnp.where(odd, two_other, one_other)
    prev_last = jnp.where(odd, one_other, two_other)
    weight_low = harmonic(coef_row(first), coef_row(prev_last))
    weight_high = harmonic(coef_row(last), coef_row(next_first))

    def product(left, right):
        return lax.dot_general(
            left.astype(BF16), right.astype(BF16), NT, preferred_element_type=F32
        )

    edge_rows = weight_high * last[:modes]
    ends = product(
        jnp.concatenate([weight_low * first[:modes], edge_rows], axis=1),
        jnp.concatenate([first[:modes], last[:modes]], axis=1),
    )
    square = partial[:modes, :] + 0.5 * (cross + ends)
    out[:modes, :modes] = square + square.T
    out[:modes, modes:] = -product(edge_rows, next_first[:modes])
    out[modes:, :modes] = partial[modes:, :]
    out[modes:, modes:] = jnp.zeros((8, modes), F32)


def terms_kernel(
    levels, pair, one_got, two_got, weights, inner_face, outer_face, terms, picked, coef_ref
):
    modes, width = picked.shape[1:]
    rows, layers = inner_face.shape
    side = lax.rem(here_on("pln"), 2)
    odd = lax.rem(here_on("sub"), 2) == 1
    one_other, two_other = one_got[...].astype(F32), two_got[...].astype(F32)
    next_first = jnp.where(odd, two_other, one_other)
    prev_last = jnp.where(odd, one_other, two_other)
    picked[0] = next_first[:modes]
    picked[1] = prev_last[:modes]
    end_labels = lax.dot_general(
        next_first[modes:].astype(BF16), pick_row(layers - 1, layers), TN, preferred_element_type=F32
    ) + lax.dot_general(
        prev_last[modes:].astype(BF16), pick_row(0, layers), TN, preferred_element_type=F32
    )
    coef_ref[...] = coefficients(end_labels, levels).reshape(width // rows, rows, layers)
    row = lax.broadcasted_iota(jnp.int32, (rows, layers), 0)
    lane = lax.broadcasted_iota(jnp.int32, (rows, layers), 1)
    for x, face in enumerate((inner_face, outer_face)):
        c = weights[5 + x]
        end_weight = harmonic(c, coef_ref[1 - side if x == 0 else side])
        up_y, up_z = weights[1 + x], weights[3 + x]
        down_y = jnp.where(row == 0, c, pltpu.roll(up_y, 1, 0))
        down_z = pltpu.roll(up_z, 1, 1)
        total = face[...] + weights[0] + up_y + down_y
        total = total + jnp.where(lane == layers - 1, end_weight, up_z)
        terms[x, 0] = total + jnp.where(lane == 0, end_weight, down_z)
        terms[x, 1] = jnp.where(row == 0, 0.0, down_y)
        terms[x, 2] = jnp.where(row == rows - 1, 0.0, up_y)
        terms[x, 3] = jnp.where(lane == 0, 0.0, down_z)
        terms[x, 4] = jnp.where(lane == layers - 1, 0.0, up_z)
        terms[x, 5] = end_weight


def pair_kernel(own, across, beside, oblique, out):
    modes = own.shape[1] // 2
    encode(own[...] + across[...], modes, out.at[0])
    encode(beside[...] + oblique[...], modes, out.at[1])


def single_kernel(own, out):
    encode(own[...], own.shape[1] // 2, out)


def encode(total, modes, out):
    row = lax.broadcasted_iota(jnp.int32, (modes, 2 * modes), 0)
    lane = lax.broadcasted_iota(jnp.int32, (modes, 2 * modes), 1)
    values = total[:modes]
    high = values.astype(BF16).astype(F32)
    low = values - high
    out[:modes] = jnp.where((lane <= row) | (lane >= modes), high, low).astype(BF16)
    diagonal = lane == row
    right = total[modes:modes + 1]
    parts = []
    for _ in range(3):
        part = right.astype(BF16).astype(F32)
        parts.append(part)
        right = right - part
    for part in (high, low):
        parts.append(jnp.sum(jnp.where(diagonal, part, 0.0), axis=0, keepdims=True))
    rows = lax.broadcasted_iota(jnp.int32, (16, 2 * modes), 0)
    extra = jnp.zeros((16, 2 * modes), F32)
    for index, part in enumerate(parts):
        extra = jnp.where(rows == index, part, extra)
    out[modes:] = extra.astype(BF16)


def widen_kernel(pair, zvec, inner_got, outer_got, own_wide, inner_wide, outer_wide):
    modes, half = outer_wide.shape[:2]
    side = lax.rem(here_on("pln"), 2)

    def some(j, carry):
        at = pl.ds(pl.multiple_of(j * MODES, MODES), MODES)
        own_wide[at, 0] = zvec[at, 1 - side].astype(F32)
        own_wide[at, 1] = zvec[at, side].astype(F32)
        inner_wide[at] = inner_got[at].astype(F32)
        outer_wide[at] = outer_got[at].astype(F32)
        return carry

    lax.fori_loop(0, modes // MODES, some, 0)


def finish_kernel(*refs):
    count = len(refs) - 17
    blocks, refs = refs[:count], refs[count:]
    zvec, inner_got, outer_got, outer_last, picked, terms, middle, inner_face, outer_face, resid = refs[:10]
    solution, deflated, direction_ref, spread, outer_field, staged, sems = refs[10:]
    subs = direction_ref.shape[0]
    modes, planes, rows, layers = zvec.shape
    half = rows // 2
    me = here_on("sub")
    side = lax.rem(here_on("pln"), 2)
    odd = lax.rem(me, 2) == 1
    at_edge = ends_the_line()
    held = (1 - side, side)
    square = (modes, modes)
    eye = lax.broadcasted_iota(jnp.int32, square, 0) == lax.broadcasted_iota(jnp.int32, square, 1)

    def column(row):
        return jnp.sum(jnp.where(eye, row, 0.0), axis=1, keepdims=True)

    def each(body, carry):
        for index, block in enumerate(blocks):
            held_here = block.shape[0]
            if held_here <= 8:
                for entry in range(held_here):
                    s = jnp.bitwise_xor(jnp.bitwise_xor(me, mask_of(index, len(blocks))), entry)
                    carry = body(block.at[entry], s, carry)
            else:
                carry = lax.fori_loop(
                    0, held_here, lambda entry, c, block=block: body(block.at[entry], entry, c), carry
                )
        return carry

    def row_is(s, width):
        return lax.broadcasted_iota(jnp.int32, (subs, width), 0) == s

    def load(block, s, carry):
        extra = block[modes:modes + 16, :].astype(F32)
        right = (extra[0:1] + extra[1:2]) + extra[2:3]
        here = row_is(s, 2 * modes)
        return jnp.where(here, right, carry[0]), jnp.where(here, extra[4:5] - extra[3:4], carry[1])

    empty = jnp.zeros((subs, 2 * modes), F32)
    right_side, fix = each(load, (empty, empty))
    fix = fix[:, :modes]

    def turned(rows_of, by):
        by = by % subs
        return jnp.concatenate([rows_of[by:], rows_of[:by]], axis=0)

    def in_parts(value):
        parts = []
        for _ in range(3):
            part = value.astype(BF16)
            parts.append(part.astype(F32))
            value = value - parts[-1]
        return jnp.concatenate(parts, axis=0).astype(BF16)

    def joined(value):
        return (value[:subs] + value[subs:2 * subs]) + value[2 * subs:]

    def coarse_apply(direction):
        pairs = in_parts(jnp.concatenate([direction, turned(direction, 1)], axis=1))
        single = pairs[:, :modes]

        def one(block, s, carry):
            values = block[:modes, :]
            ahead = lax.dot_general(pairs, values, NT, preferred_element_type=F32)
            image = jnp.dot(single, values, preferred_element_type=F32)
            return (
                jnp.where(row_is(s, modes), joined(ahead), carry[0]),
                jnp.where(row_is(s, 2 * modes), joined(image), carry[1]),
            )

        ahead, image = each(one, (jnp.zeros((subs, modes), F32), empty))
        return ahead + image[:, :modes] + fix * direction + turned(image[:, modes:], -1)

    def inner(left, right):
        return jnp.sum(jnp.sum(left * right, axis=0, keepdims=True), axis=1, keepdims=True)

    remain = right_side[:, :modes]
    direction = remain
    result = jnp.zeros_like(remain)
    norm_now = inner(remain, remain)
    for iteration in range(CITERS):
        image = coarse_apply(direction)
        step_size = norm_now / inner(direction, image)
        result = result + step_size * direction
        if iteration + 1 < CITERS:
            remain = remain - step_size * image
            norm_next = inner(remain, remain)
            direction = remain + (norm_next / norm_now) * direction
            norm_now = norm_next
    direction_ref[...] = result
    own = direction_ref[pl.ds(me, 1), :]
    solution[...] = own
    spread[...] = jnp.broadcast_to(column(own), (modes, layers))
    ahead_column = column(direction_ref[pl.ds(lax.rem(me + 1, subs), 1), :])
    behind_column = column(direction_ref[pl.ds(lax.rem(me + subs - 1, subs), 1), :])
    ahead_row = jnp.sum(ahead_column * picked[0], axis=0, keepdims=True)
    behind_row = jnp.sum(behind_column * picked[1], axis=0, keepdims=True)
    width = planes * rows
    both_rows = jnp.where(
        lax.broadcasted_iota(jnp.int32, (8, width), 0) == 0,
        jnp.broadcast_to(ahead_row, (8, width)),
        jnp.broadcast_to(behind_row, (8, width)),
    )
    columns = both_rows.T
    ends = jnp.where(
        lane_is((width, layers), layers - 1),
        columns[:, 0:1],
        jnp.where(lane_is((width, layers), 0), columns[:, 1:2], 0.0),
    ).reshape(planes, rows, layers)

    def add_mode(j, carry):
        fields, near, last = list(carry[0]), carry[1], carry[2]
        for u in range(MODES):
            k = j * MODES + u
            scale = spread[pl.ds(k, 1), :]
            for x, plane in enumerate((zvec[k, 0], zvec[k, 1], inner_got[k])):
                fields[x] = fields[x] + scale * plane
            near = near + scale * outer_got[k]
            last = last + scale * outer_last[k].astype(F32)
        return tuple(fields), near, last

    zero, short = jnp.zeros((rows, layers), F32), jnp.zeros((half, layers), F32)
    field, near, last = lax.fori_loop(0, modes // MODES, add_mode, ((zero,) * 3, short, short))
    outer_field[pl.ds(pl.multiple_of(side * half, half), half), :] = near
    outer_field[pl.ds(pl.multiple_of((1 - side) * half, half), half), :] = last
    outside = (field[2], jnp.where(at_edge, 0.0, outer_field[...]))
    faces = (inner_face[...], outer_face[...])
    copies = []
    for x in range(2):
        f = field[x]
        end_field = jnp.where(side == x, ends[1], ends[0])
        image = (
            terms[x, 0] * f
            - middle[0] * field[1 - x]
            - faces[x] * outside[x]
            - terms[x, 1] * pltpu.roll(f, 1, 0)
            - terms[x, 2] * pltpu.roll(f, rows - 1, 0)
            - terms[x, 3] * pltpu.roll(f, 1, 1)
            - terms[x, 4] * pltpu.roll(f, layers - 1, 1)
            - terms[x, 5] * end_field
        )
        staged[x] = resid[held[x]] - image
        copy = pltpu.make_async_copy(staged.at[x], deflated.at[held[x]], sems.at[x])
        copy.start()
        copies.append(copy)
    for copy in copies:
        copy.wait()


def swapped(value, axis, first):
    count = lax.axis_size(axis)
    pairs = []
    for i in range(count):
        up = (i - first) % 2 == 0
        pairs.append((i, (i + 1) % count if up else (i - 1) % count))
    return lax.ppermute(value, axis, pairs)


def swapped_all(value):
    subs, count = lax.axis_size("sub"), lax.axis_size("pln")
    pairs = []
    for s in range(subs):
        for i in range(count):
            if 0 < i < count - 1:
                to = (s, i + 1 if i % 2 else i - 1)
            else:
                to = (s ^ 1, i)
            pairs.append((s * count + i, to[0] * count + to[1]))
    return lax.ppermute(value, ("sub", "pln"), pairs)


def exchanged(value, axis, mask):
    return lax.ppermute(value, axis, [(i, i ^ mask) for i in range(lax.axis_size(axis))])


def partner(value, sub_mask, pln_mask):
    subs, count = lax.axis_size("sub"), lax.axis_size("pln")
    pairs = [
        (s * count + p, (s ^ sub_mask) * count + (p ^ pln_mask)) for s in range(subs) for p in range(count)
    ]
    return lax.ppermute(value, ("sub", "pln"), pairs)


FAR = (4, 6)


def mask_of(index, count):
    if count == 1:
        return 0
    swap = far_role(here_on("sub"), here_on("pln")) * (FAR[1] - FAR[0])
    return (0, FAR[0] + swap, 2, FAR[1] - swap)[index]


def far_role(s, p):
    return (p ^ (s >> 2)) & 1


def far_partner(value):
    subs, count = lax.axis_size("sub"), lax.axis_size("pln")
    pairs = [
        (s * count + p, (s ^ FAR[far_role(s, p)]) * count + (p ^ 1)) for s in range(subs) for p in range(count)
    ]
    return lax.ppermute(value, ("sub", "pln"), pairs)


def body(labels, levels, zvec, resid):
    modes, planes, rows, layers = zvec.shape
    half = rows // 2
    subs, parts = lax.axis_size("sub"), lax.axis_size("pln")
    shape = jax.ShapeDtypeStruct
    levels = levels.reshape(1, -1)
    pack = shape((modes + 16, planes * rows), BF16)
    inner_send, outer_near = call(
        stage_kernel,
        [shape((modes + 1, rows, layers), BF16), shape((modes + rows // half, half, layers), BF16)],
        [HBM, HBM],
        [pltpu.VMEM(labels.shape, jnp.int32), pltpu.SemaphoreType.DMA, pltpu.SemaphoreType.DMA((2,))],
        moved=2 << 20,
    )(*(pltpu.with_memory_space_constraint(v, pltpu.HBM) for v in (labels, zvec)))
    outer_got = swapped_all(outer_near)
    inner_got = swapped(inner_send, "pln", 0)
    rest = shape((modes, half, layers), BF16)
    outer_rest, one_pack, two_pack = call(
        prepare_kernel,
        [rest, pack, pack],
        [VMEM, VMEM],
        flops=10_000_000,
        moved=6 << 20,
    )(labels, zvec)
    one_got = swapped(one_pack, "sub", 0)
    two_got = swapped(two_pack, "sub", 1)
    field = (planes, rows, layers)
    plane = (rows, layers)
    partial, weights, here = call(
        block_kernel,
        [
            shape((modes + 8, modes), F32),
            shape((7,) + plane, F32),
            shape((planes, rows, modes, layers), BF16),
        ],
        [VMEM] * 4 + [ANY],
        [pltpu.VMEM(field, F32)] * 3,
        flops=400_000_000,
        moved=3 << 20,
    )(levels, labels, resid, zvec, one_pack)
    turned = pltpu.VMEM((half, modes, layers), BF16)
    partial, inner_face = call(
        inner_kernel,
        [shape((modes + 8, modes), F32), shape(plane, F32)],
        [VMEM] * 5,
        [turned],
        flops=100_000_000,
        moved=1 << 20,
    )(levels, partial, weights, here, inner_got)
    block, outer_face = call(
        outer_kernel,
        [shape((modes + 8, 2 * modes), F32), shape(plane, F32)],
        [VMEM] * 9,
        [turned, pltpu.VMEM(plane, F32)],
        flops=100_000_000,
        moved=1 << 20,
    )(levels, partial, weights, here, outer_got, one_pack, two_pack, one_got, two_got)
    packed = (modes + 16, 2 * modes)
    if parts == 4 and subs == 8:
        block = block + exchanged(block, "pln", 1)
        others = [partner(block, *masks) for masks in ((0, 3), (1, 1), (1, 3))]
        [pair] = call(
            pair_kernel, [shape((2,) + packed, BF16)], [VMEM] * 4, flops=1 << 33
        )(block, *others)
        far = far_partner(pair)
        blocks = [pair, far, partner(pair, 2, 1), exchanged(far, "pln", 1)]
    else:
        [single] = call(single_kernel, [shape(packed, BF16)], [VMEM])(lax.psum(block, "pln"))
        blocks = [lax.all_gather(single, "sub")]
    [outer_rest] = call(release_kernel, [rest], [ANY] * 2, aliases={1: 0})(block, outer_rest)
    outer_last = swapped_all(outer_rest)
    terms, picked = call(
        terms_kernel,
        [shape((planes, 6) + plane, F32), shape((2, modes, planes * rows), F32)],
        [VMEM, ANY] + [VMEM] * 5,
        [pltpu.VMEM(field, F32)],

        flops=1 << 31,
        moved=1 << 20,
    )(levels, blocks[0], one_got, two_got, weights, inner_face, outer_face)
    wide = call(
        widen_kernel,
        [
            shape((modes,) + field, F32),
            shape((modes,) + plane, F32),
            shape((modes, half, layers), F32),
        ],
        [ANY] + [VMEM] * 3,
        flops=1 << 30,
        moved=1 << 20,
    )(blocks[0], zvec, inner_got, outer_got)
    return tuple(
        call(
            finish_kernel,
            [shape((1, modes), F32), shape(field, F32)],
            [VMEM] * (10 + len(blocks)),
            [
                pltpu.VMEM((subs, modes), F32),
                pltpu.VMEM((modes, layers), F32),
                pltpu.VMEM(plane, F32),
                pltpu.VMEM(field, F32),
                pltpu.SemaphoreType.DMA((2,)),
            ],
            far=(1,),
            flops=10_000_000,
            moved=5 << 20,
        )(
            *blocks, *wide, outer_last, picked, terms, weights, inner_face,
            outer_face, resid,
        )
    )


def solution(mesh):
    in_specs = (P("pln", None, "sub"), P(), P(None, "pln", None, "sub"), P("pln", None, "sub"))
    out_specs = (P("sub", None), P("pln", None, "sub"))
    return jax.shard_map(body, mesh=mesh, in_specs=in_specs, out_specs=out_specs, check_vma=False)
```

```python
import jax
import jax.numpy as jnp
from jax import lax
from jax.experimental import pallas as pl
from jax.experimental.pallas import tpu as pltpu
from jax.sharding import PartitionSpec as P

CITERS = 2
STEP = 32
MODES = 16
CHUNK = 16
F32 = jnp.float32
BF16 = jnp.bfloat16
PRECISE = lax.Precision.HIGHEST
NT = (((1,), (1,)), ((), ()))
TN = (((0,), (0,)), ((), ()))
VMEM = pl.BlockSpec(memory_space=pltpu.VMEM)
HBM = pl.BlockSpec(memory_space=pltpu.HBM)
ANY = pl.BlockSpec(memory_space=pl.ANY)


def call(kernel, outs, specs, scratch=(), flops=0, moved=0, limit=32, aliases=None):
    return pl.pallas_call(
        kernel,
        out_shape=outs,
        in_specs=specs,
        out_specs=[ANY if at in (aliases or {}).values() else VMEM for at in range(len(outs))],
        input_output_aliases=aliases or {},
        scratch_shapes=list(scratch),
        cost_estimate=pl.CostEstimate(flops=flops, bytes_accessed=moved, transcendentals=0),
        compiler_params=pltpu.CompilerParams(vmem_limit_bytes=limit << 20),
    )


def here_on(axis):
    return lax.axis_index(axis).astype(jnp.int32)


def ends_the_line():
    p = here_on("pln")
    return (p == 0) | (p == lax.axis_size("pln") - 1)


def harmonic(left_value, right_value):
    return 2.0 * left_value * right_value / (left_value + right_value)


def coefficients(labels, levels_ref):
    weighted = jnp.zeros(labels.shape, F32)
    for level in range(levels_ref.shape[1]):
        weighted = weighted + jnp.where(labels == level, levels_ref[:, level:level + 1], 0.0)
    return weighted


def lane_is(shape, lane):
    return lax.broadcasted_iota(jnp.int32, shape, len(shape) - 1) == lane


def pick_row(lane, width):
    row = lax.broadcasted_iota(jnp.int32, (16, width), 0)
    return ((row == 0) & lane_is((16, width), lane)).astype(BF16)


def stage_kernel(labels_far, zvec, inner_send, outer_near, labels, label_sem, sems):
    modes, planes, rows, layers = zvec.shape
    half = rows // 2
    side = lax.rem(here_on("pln"), 2)
    start = pl.multiple_of((1 - side) * half, half)
    label_copy = pltpu.make_async_copy(labels_far, labels, label_sem)
    copies = [
        pltpu.make_async_copy(
            zvec.at[:, side, pl.ds(start, half), :], outer_near.at[pl.ds(0, modes)], sems.at[0]
        ),
        pltpu.make_async_copy(zvec.at[:, 1 - side], inner_send.at[pl.ds(0, modes)], sems.at[1]),
    ]
    label_copy.start()
    for copy in copies:
        copy.start()
    label_copy.wait()
    outer_near[modes:] = labels[side].astype(F32).astype(BF16).reshape(rows // half, half, layers)
    inner_send[modes] = labels[1 - side].astype(F32).astype(BF16)
    for copy in copies:
        copy.wait()


def release_kernel(after, outer_rest, outer_out):
    pass


def prepare_kernel(labels, held, outer_rest, one_pack, two_pack):
    modes, planes, rows, layers = held.shape
    half = rows // 2
    width = planes * rows
    side = lax.rem(here_on("pln"), 2)
    odd = lax.rem(here_on("sub"), 2) == 1
    one_lane = jnp.where(odd, 0, layers - 1)
    two_lane = jnp.where(odd, layers - 1, 0)
    row = lax.broadcasted_iota(jnp.int32, (16, layers), 0)
    both = ((row == 0) & lane_is((16, layers), one_lane)) | ((row == 1) & lane_is((16, layers), two_lane))
    both = both.astype(BF16)
    flat = labels[...].astype(F32).astype(BF16).reshape(width, layers)
    for out, lane in ((one_pack, one_lane), (two_pack, two_lane)):
        out[modes:] = lax.dot_general(
            pick_row(lane, layers), flat, NT, preferred_element_type=F32
        ).astype(BF16)
    for k in range(0, modes, CHUNK):
        at = slice(k, k + CHUNK)
        ends = lax.dot_general(
            both, held[at].reshape(-1, layers), NT, preferred_element_type=F32
        )
        for out, index in ((one_pack, 0), (two_pack, 1)):
            out[at] = jnp.concatenate(
                [ends[index:index + 1, j * width:(j + 1) * width] for j in range(CHUNK)], axis=0
            ).astype(BF16)
        outer_rest[at] = held[at, side, pl.ds(pl.multiple_of(side * half, half), half), :]


def block_kernel(
    levels, labels, resid, zvec, after, partial, weights, here, half_diag, link_y, link_z,
):
    planes, rows, layers = labels.shape
    modes = here.shape[2]
    side = lax.rem(here_on("pln"), 2)
    at_edge = ends_the_line()
    held = (1 - side, side)

    def turn_rows(start):
        for slot, plane in enumerate(held):
            for k in range(0, modes, CHUNK):
                block = zvec[k:k + CHUNK, plane, pl.ds(start, STEP), :]
                here[slot, pl.ds(start, STEP), k:k + CHUNK, :] = jnp.swapaxes(block, 0, 1)

    turn_rows(0)
    coef = [coefficients(labels[x], levels) for x in held]
    middle = harmonic(coef[0], coef[1])
    weights[0] = middle
    row = lax.broadcasted_iota(jnp.int32, (rows, layers), 0)
    lane = lax.broadcasted_iota(jnp.int32, (rows, layers), 1)
    for x in range(2):
        c = coef[x]
        up_y = harmonic(c, jnp.where(row == rows - 1, c, pltpu.roll(c, rows - 1, 0)))
        up_z = harmonic(c, pltpu.roll(c, layers - 1, 1))
        down_y = jnp.where(row == 0, c, pltpu.roll(up_y, 1, 0))
        weights[1 + x] = up_y
        weights[3 + x] = up_z
        weights[5 + x] = c
        inner_z = jnp.where(lane == layers - 1, 0.0, up_z)
        total = middle + up_y + down_y + inner_z + pltpu.roll(inner_z, 1, 1)
        if x == 1:
            total = total + jnp.where(at_edge, c, 0.0)
        half_diag[x] = 0.5 * total
        link_y[x] = jnp.where(row == rows - 1, 0.0, up_y)
        link_z[x] = inner_z

    def step(j, carry):
        total, wide = carry
        turn_rows(pl.multiple_of(jnp.minimum((j + 1) * STEP, rows - STEP), STEP))
        for u in range(STEP):
            y = j * STEP + u
            at = pl.ds(y, 1)
            ahead = jnp.minimum(y + 1, rows - 1)
            up = [here[x, ahead].astype(F32) for x in range(2)]
            images, parts = [], []
            for x in range(2):
                image = (
                    half_diag[x, at, :] * wide[x]
                    - link_y[x, at, :] * up[x]
                    - link_z[x, at, :] * pltpu.roll(here[x, y], layers - 1, 1).astype(F32)
                )
                if x == 0:
                    image = image - weights[0, at, :] * wide[1]
                images.append(image.astype(BF16))
                value = resid[held[x], at, :]
                high = value.astype(BF16).astype(F32)
                part = jnp.where(part_row == 0, high, jnp.where(part_row == 1, value - high, 0.0))
                parts.append(part.astype(BF16))
            total = total + lax.dot_general(
                jnp.concatenate(
                    [jnp.concatenate(images, axis=1), jnp.concatenate(parts, axis=1)], axis=0
                ),
                jnp.concatenate([here[0, y], here[1, y]], axis=1),
                NT,
                preferred_element_type=F32,
            )
            wide = up
        return total, wide

    part_row = lax.broadcasted_iota(jnp.int32, (16, layers), 0)
    total, _ = lax.fori_loop(
        0,
        rows // STEP,
        step,
        (
            jnp.zeros((modes + 16, modes), F32),
            [here[x, 0].astype(F32) for x in range(2)],
        ),
    )
    partial[:modes, :] = total[:modes]
    partial[modes:, :] = jnp.broadcast_to(total[modes:modes + 1] + total[modes + 1:modes + 2], (8, modes))


def turn(got, start, out):
    half, modes, layers = out.shape
    for k in range(0, modes, CHUNK):
        out[:, k:k + CHUNK, :] = jnp.swapaxes(got[k:k + CHUNK, pl.ds(start, half), :], 0, 1)


def face_product(weight_ref, base, own, other):
    half, modes, layers = other.shape

    def step(j, total):
        left, right = [], []
        for u in range(STEP):
            y = j * STEP + u
            weight = weight_ref[pl.ds(base + y, 1), :]
            image = weight * (own[base + y].astype(F32) - other[y].astype(F32))
            left.append(jnp.concatenate([own[base + y], other[y]], axis=0))
            right.append(image.astype(BF16))
        return total + lax.dot_general(
            jnp.concatenate(left, axis=1), jnp.concatenate(right, axis=1), NT,
            preferred_element_type=F32,
        )

    total = lax.fori_loop(0, half // STEP, step, jnp.zeros((2 * modes, modes), F32))
    return total[:modes] - total[modes:]


def inner_kernel(levels, partial, weights, here, inner_got, out, face, turned):
    planes, rows, modes, layers = here.shape
    half = rows // 2
    side = lax.rem(here_on("pln"), 2)
    base = pl.multiple_of(side * half, half)
    turn(inner_got, base, turned)
    face[...] = harmonic(weights[5], coefficients(inner_got[modes].astype(F32), levels))
    out[:modes, :] = partial[:modes, :] + 0.5 * face_product(face, base, here.at[0], turned)
    out[modes:, :] = partial[modes:, :]


def outer_kernel(
    levels, partial, weights, here, outer_got, one_pack, two_pack, one_got, two_got,
    out, face, turned, face_here,
):
    planes, rows, modes, layers = here.shape
    half = rows // 2
    side = lax.rem(here_on("pln"), 2)
    at_edge = ends_the_line()
    base = pl.multiple_of(side * half, half)
    turn(outer_got, 0, turned)
    coef = coefficients(outer_got[modes:].astype(F32).reshape(rows, layers), levels)
    between = harmonic(weights[6], coef)
    face[...] = jnp.where(at_edge, weights[6], between)
    face_here[...] = jnp.where(at_edge, 0.0, between)
    cross = face_product(face_here, base, here.at[1], turned)
    odd = lax.rem(here_on("sub"), 2) == 1

    def coef_row(pack):
        return coefficients(pack[modes:modes + 16].astype(F32)[0:1], levels)

    one, two = one_pack[...].astype(F32), two_pack[...].astype(F32)
    one_other, two_other = one_got[...].astype(F32), two_got[...].astype(F32)
    first, last = jnp.where(odd, one, two), jnp.where(odd, two, one)
    next_first = jnp.where(odd, two_other, one_other)
    prev_last = jnp.where(odd, one_other, two_other)
    weight_low = harmonic(coef_row(first), coef_row(prev_last))
    weight_high = harmonic(coef_row(last), coef_row(next_first))

    def product(left, right):
        return lax.dot_general(
            left.astype(BF16), right.astype(BF16), NT, preferred_element_type=F32
        )

    edge_rows = weight_high * last[:modes]
    ends = product(
        jnp.concatenate([weight_low * first[:modes], edge_rows], axis=1),
        jnp.concatenate([first[:modes], last[:modes]], axis=1),
    )
    square = partial[:modes, :] + 0.5 * (cross + ends)
    out[:modes, :modes] = square + square.T
    out[:modes, modes:] = -product(edge_rows, next_first[:modes])
    out[modes:, :modes] = partial[modes:, :]
    out[modes:, modes:] = jnp.zeros((8, modes), F32)


def terms_kernel(
    levels, pair, one_got, two_got, weights, inner_face, outer_face, terms, picked, coef_ref
):
    modes, width = picked.shape[1:]
    rows, layers = inner_face.shape
    side = lax.rem(here_on("pln"), 2)
    odd = lax.rem(here_on("sub"), 2) == 1
    one_other, two_other = one_got[...].astype(F32), two_got[...].astype(F32)
    next_first = jnp.where(odd, two_other, one_other)
    prev_last = jnp.where(odd, one_other, two_other)
    picked[0] = next_first[:modes]
    picked[1] = prev_last[:modes]
    end_labels = lax.dot_general(
        next_first[modes:].astype(BF16), pick_row(layers - 1, layers), TN, preferred_element_type=F32
    ) + lax.dot_general(
        prev_last[modes:].astype(BF16), pick_row(0, layers), TN, preferred_element_type=F32
    )
    coef_ref[...] = coefficients(end_labels, levels).reshape(width // rows, rows, layers)
    row = lax.broadcasted_iota(jnp.int32, (rows, layers), 0)
    lane = lax.broadcasted_iota(jnp.int32, (rows, layers), 1)
    for x, face in enumerate((inner_face, outer_face)):
        c = weights[5 + x]
        end_weight = harmonic(c, coef_ref[1 - side if x == 0 else side])
        up_y, up_z = weights[1 + x], weights[3 + x]
        down_y = jnp.where(row == 0, c, pltpu.roll(up_y, 1, 0))
        down_z = pltpu.roll(up_z, 1, 1)
        total = face[...] + weights[0] + up_y + down_y
        total = total + jnp.where(lane == layers - 1, end_weight, up_z)
        terms[x, 0] = total + jnp.where(lane == 0, end_weight, down_z)
        terms[x, 1] = jnp.where(row == 0, 0.0, down_y)
        terms[x, 2] = jnp.where(row == rows - 1, 0.0, up_y)
        terms[x, 3] = jnp.where(lane == 0, 0.0, down_z)
        terms[x, 4] = jnp.where(lane == layers - 1, 0.0, up_z)
        terms[x, 5] = end_weight


def pair_kernel(own, across, beside, oblique, out):
    modes = own.shape[1] // 2
    encode(own[...] + across[...], modes, out.at[0])
    encode(beside[...] + oblique[...], modes, out.at[1])


def single_kernel(own, out):
    encode(own[...], own.shape[1] // 2, out)


def encode(total, modes, out):
    row = lax.broadcasted_iota(jnp.int32, (modes, 2 * modes), 0)
    lane = lax.broadcasted_iota(jnp.int32, (modes, 2 * modes), 1)
    values = total[:modes]
    high = values.astype(BF16).astype(F32)
    low = values - high
    out[:modes] = jnp.where((lane <= row) | (lane >= modes), high, low).astype(BF16)
    diagonal = lane == row
    right = total[modes:modes + 1]
    parts = []
    for _ in range(3):
        part = right.astype(BF16).astype(F32)
        parts.append(part)
        right = right - part
    for part in (high, low):
        parts.append(jnp.sum(jnp.where(diagonal, part, 0.0), axis=0, keepdims=True))
    rows = lax.broadcasted_iota(jnp.int32, (16, 2 * modes), 0)
    extra = jnp.zeros((16, 2 * modes), F32)
    for index, part in enumerate(parts):
        extra = jnp.where(rows == index, part, extra)
    out[modes:] = extra.astype(BF16)


def widen_kernel(pair, zvec, inner_got, outer_got, own_wide, inner_wide, outer_wide):
    modes, half = outer_wide.shape[:2]
    side = lax.rem(here_on("pln"), 2)

    def some(j, carry):
        at = pl.ds(pl.multiple_of(j * MODES, MODES), MODES)
        own_wide[at, 0] = zvec[at, 1 - side].astype(F32)
        own_wide[at, 1] = zvec[at, side].astype(F32)
        inner_wide[at] = inner_got[at].astype(F32)
        outer_wide[at] = outer_got[at].astype(F32)
        return carry

    lax.fori_loop(0, modes // MODES, some, 0)


def finish_kernel(*refs):
    count = len(refs) - 15
    blocks, refs = refs[:count], refs[count:]
    zvec, inner_got, outer_got, outer_last, picked, terms, middle, inner_face, outer_face, resid = refs[:10]
    solution, deflated, direction_ref, spread, outer_field = refs[10:]
    subs = direction_ref.shape[0]
    modes, planes, rows, layers = zvec.shape
    half = rows // 2
    me = here_on("sub")
    side = lax.rem(here_on("pln"), 2)
    odd = lax.rem(me, 2) == 1
    at_edge = ends_the_line()
    held = (1 - side, side)
    square = (modes, modes)
    eye = lax.broadcasted_iota(jnp.int32, square, 0) == lax.broadcasted_iota(jnp.int32, square, 1)

    def column(row):
        return jnp.sum(jnp.where(eye, row, 0.0), axis=1, keepdims=True)

    def each(body, carry):
        for index, block in enumerate(blocks):
            held_here = block.shape[0]
            if held_here <= 8:
                for entry in range(held_here):
                    s = jnp.bitwise_xor(jnp.bitwise_xor(me, mask_of(index, len(blocks))), entry)
                    carry = body(block.at[entry], s, carry)
            else:
                carry = lax.fori_loop(
                    0, held_here, lambda entry, c, block=block: body(block.at[entry], entry, c), carry
                )
        return carry

    def row_is(s, width):
        return lax.broadcasted_iota(jnp.int32, (subs, width), 0) == s

    def load(block, s, carry):
        extra = block[modes:modes + 16, :].astype(F32)
        right = (extra[0:1] + extra[1:2]) + extra[2:3]
        here = row_is(s, 2 * modes)
        return jnp.where(here, right, carry[0]), jnp.where(here, extra[4:5] - extra[3:4], carry[1])

    empty = jnp.zeros((subs, 2 * modes), F32)
    right_side, fix = each(load, (empty, empty))
    fix = fix[:, :modes]

    def turned(rows_of, by):
        by = by % subs
        return jnp.concatenate([rows_of[by:], rows_of[:by]], axis=0)

    def in_parts(value):
        parts = []
        for _ in range(2):
            part = value.astype(BF16)
            parts.append(part.astype(F32))
            value = value - parts[-1]
        return jnp.concatenate(parts, axis=0).astype(BF16)

    def joined(value):
        return value[:subs] + value[subs:]

    def coarse_apply(direction):
        pairs = in_parts(jnp.concatenate([direction, turned(direction, 1)], axis=1))
        single = pairs[:, :modes]

        def one(block, s, carry):
            values = block[:modes, :]
            ahead = lax.dot_general(pairs, values, NT, preferred_element_type=F32)
            image = jnp.dot(single, values, preferred_element_type=F32)
            return (
                jnp.where(row_is(s, modes), joined(ahead), carry[0]),
                jnp.where(row_is(s, 2 * modes), joined(image), carry[1]),
            )

        ahead, image = each(one, (jnp.zeros((subs, modes), F32), empty))
        return ahead + image[:, :modes] + fix * direction + turned(image[:, modes:], -1)

    def inner(left, right):
        return jnp.sum(jnp.sum(left * right, axis=0, keepdims=True), axis=1, keepdims=True)

    remain = right_side[:, :modes]
    direction = remain
    result = jnp.zeros_like(remain)
    norm_now = inner(remain, remain)
    for iteration in range(CITERS):
        image = coarse_apply(direction)
        step_size = norm_now / inner(direction, image)
        result = result + step_size * direction
        if iteration + 1 < CITERS:
            remain = remain - step_size * image
            norm_next = inner(remain, remain)
            direction = remain + (norm_next / norm_now) * direction
            norm_now = norm_next
    direction_ref[...] = result
    own = direction_ref[pl.ds(me, 1), :]
    solution[...] = own
    spread[...] = jnp.broadcast_to(column(own), (modes, layers))
    ahead_column = column(direction_ref[pl.ds(lax.rem(me + 1, subs), 1), :])
    behind_column = column(direction_ref[pl.ds(lax.rem(me + subs - 1, subs), 1), :])
    ahead_row = jnp.sum(ahead_column * picked[0], axis=0, keepdims=True)
    behind_row = jnp.sum(behind_column * picked[1], axis=0, keepdims=True)
    width = planes * rows
    both_rows = jnp.where(
        lax.broadcasted_iota(jnp.int32, (8, width), 0) == 0,
        jnp.broadcast_to(ahead_row, (8, width)),
        jnp.broadcast_to(behind_row, (8, width)),
    )
    columns = both_rows.T
    ends = jnp.where(
        lane_is((width, layers), layers - 1),
        columns[:, 0:1],
        jnp.where(lane_is((width, layers), 0), columns[:, 1:2], 0.0),
    ).reshape(planes, rows, layers)

    def add_mode(j, carry):
        fields, near, last = list(carry[0]), carry[1], carry[2]
        for u in range(MODES):
            k = j * MODES + u
            scale = spread[pl.ds(k, 1), :]
            for x, plane in enumerate((zvec[k, 0], zvec[k, 1], inner_got[k])):
                fields[x] = fields[x] + scale * plane
            near = near + scale * outer_got[k]
            last = last + scale * outer_last[k].astype(F32)
        return tuple(fields), near, last

    zero, short = jnp.zeros((rows, layers), F32), jnp.zeros((half, layers), F32)
    field, near, last = lax.fori_loop(0, modes // MODES, add_mode, ((zero,) * 3, short, short))
    outer_field[pl.ds(pl.multiple_of(side * half, half), half), :] = near
    outer_field[pl.ds(pl.multiple_of((1 - side) * half, half), half), :] = last
    outside = (field[2], jnp.where(at_edge, 0.0, outer_field[...]))
    faces = (inner_face[...], outer_face[...])
    for x in range(2):
        f = field[x]
        end_field = jnp.where(side == x, ends[1], ends[0])
        image = (
            terms[x, 0] * f
            - middle[0] * field[1 - x]
            - faces[x] * outside[x]
            - terms[x, 1] * pltpu.roll(f, 1, 0)
            - terms[x, 2] * pltpu.roll(f, rows - 1, 0)
            - terms[x, 3] * pltpu.roll(f, 1, 1)
            - terms[x, 4] * pltpu.roll(f, layers - 1, 1)
            - terms[x, 5] * end_field
        )
        deflated[held[x]] = resid[held[x]] - image


def swapped(value, axis, first):
    count = lax.axis_size(axis)
    pairs = []
    for i in range(count):
        up = (i - first) % 2 == 0
        pairs.append((i, (i + 1) % count if up else (i - 1) % count))
    return lax.ppermute(value, axis, pairs)


def swapped_all(value):
    subs, count = lax.axis_size("sub"), lax.axis_size("pln")
    pairs = []
    for s in range(subs):
        for i in range(count):
            if 0 < i < count - 1:
                to = (s, i + 1 if i % 2 else i - 1)
            else:
                to = (s ^ 1, i)
            pairs.append((s * count + i, to[0] * count + to[1]))
    return lax.ppermute(value, ("sub", "pln"), pairs)


def exchanged(value, axis, mask):
    return lax.ppermute(value, axis, [(i, i ^ mask) for i in range(lax.axis_size(axis))])


def partner(value, sub_mask, pln_mask):
    subs, count = lax.axis_size("sub"), lax.axis_size("pln")
    pairs = [
        (s * count + p, (s ^ sub_mask) * count + (p ^ pln_mask)) for s in range(subs) for p in range(count)
    ]
    return lax.ppermute(value, ("sub", "pln"), pairs)


FAR = (4, 6)


def mask_of(index, count):
    if count == 1:
        return 0
    swap = far_role(here_on("sub"), here_on("pln")) * (FAR[1] - FAR[0])
    return (0, FAR[0] + swap, 2, FAR[1] - swap)[index]


def far_role(s, p):
    return (p ^ (s >> 2)) & 1


def far_partner(value):
    subs, count = lax.axis_size("sub"), lax.axis_size("pln")
    pairs = [
        (s * count + p, (s ^ FAR[far_role(s, p)]) * count + (p ^ 1)) for s in range(subs) for p in range(count)
    ]
    return lax.ppermute(value, ("sub", "pln"), pairs)


def body(labels, levels, zvec, resid):
    modes, planes, rows, layers = zvec.shape
    half = rows // 2
    subs, parts = lax.axis_size("sub"), lax.axis_size("pln")
    shape = jax.ShapeDtypeStruct
    levels = levels.reshape(1, -1)
    pack = shape((modes + 16, planes * rows), BF16)
    inner_send, outer_near = call(
        stage_kernel,
        [shape((modes + 1, rows, layers), BF16), shape((modes + rows // half, half, layers), BF16)],
        [HBM, HBM],
        [pltpu.VMEM(labels.shape, jnp.int32), pltpu.SemaphoreType.DMA, pltpu.SemaphoreType.DMA((2,))],
        moved=2 << 20,
    )(*(pltpu.with_memory_space_constraint(v, pltpu.HBM) for v in (labels, zvec)))
    outer_got = swapped_all(outer_near)
    inner_got = swapped(inner_send, "pln", 0)
    rest = shape((modes, half, layers), BF16)
    outer_rest, one_pack, two_pack = call(
        prepare_kernel,
        [rest, pack, pack],
        [VMEM, VMEM],
        flops=10_000_000,
        moved=6 << 20,
    )(labels, zvec)
    one_got = swapped(one_pack, "sub", 0)
    two_got = swapped(two_pack, "sub", 1)
    field = (planes, rows, layers)
    plane = (rows, layers)
    partial, weights, here = call(
        block_kernel,
        [
            shape((modes + 8, modes), F32),
            shape((7,) + plane, F32),
            shape((planes, rows, modes, layers), BF16),
        ],
        [VMEM] * 4 + [ANY],
        [pltpu.VMEM(field, F32)] * 3,
        flops=400_000_000,
        moved=3 << 20,
    )(levels, labels, resid, zvec, one_pack)
    turned = pltpu.VMEM((half, modes, layers), BF16)
    partial, inner_face = call(
        inner_kernel,
        [shape((modes + 8, modes), F32), shape(plane, F32)],
        [VMEM] * 5,
        [turned],
        flops=100_000_000,
        moved=1 << 20,
    )(levels, partial, weights, here, inner_got)
    block, outer_face = call(
        outer_kernel,
        [shape((modes + 8, 2 * modes), F32), shape(plane, F32)],
        [VMEM] * 9,
        [turned, pltpu.VMEM(plane, F32)],
        flops=100_000_000,
        moved=1 << 20,
    )(levels, partial, weights, here, outer_got, one_pack, two_pack, one_got, two_got)
    packed = (modes + 16, 2 * modes)
    if parts == 4 and subs == 8:
        block = block + exchanged(block, "pln", 1)
        others = [partner(block, *masks) for masks in ((0, 3), (1, 1), (1, 3))]
        [pair] = call(
            pair_kernel, [shape((2,) + packed, BF16)], [VMEM] * 4, flops=1 << 33
        )(block, *others)
        far = far_partner(pair)
        blocks = [pair, far, partner(pair, 2, 1), exchanged(far, "pln", 1)]
    else:
        [single] = call(single_kernel, [shape(packed, BF16)], [VMEM])(lax.psum(block, "pln"))
        blocks = [lax.all_gather(single, "sub")]
    [outer_rest] = call(release_kernel, [rest], [ANY] * 2, aliases={1: 0})(block, outer_rest)
    outer_last = swapped_all(outer_rest)
    terms, picked = call(
        terms_kernel,
        [shape((planes, 6) + plane, F32), shape((2, modes, planes * rows), F32)],
        [VMEM, ANY] + [VMEM] * 5,
        [pltpu.VMEM(field, F32)],

        flops=1 << 31,
        moved=1 << 20,
    )(levels, blocks[0], one_got, two_got, weights, inner_face, outer_face)
    wide = call(
        widen_kernel,
        [
            shape((modes,) + field, F32),
            shape((modes,) + plane, F32),
            shape((modes, half, layers), F32),
        ],
        [ANY] + [VMEM] * 3,
        flops=1 << 30,
        moved=1 << 20,
    )(blocks[0], zvec, inner_got, outer_got)
    return tuple(
        call(
            finish_kernel,
            [shape((1, modes), F32), shape(field, F32)],
            [VMEM] * (10 + len(blocks)),
            [
                pltpu.VMEM((subs, modes), F32),
                pltpu.VMEM((modes, layers), F32),
                pltpu.VMEM(plane, F32),
            ],
            flops=10_000_000,
            moved=5 << 20,
        )(
            *blocks, *wide, outer_last, picked, terms, weights, inner_face,
            outer_face, resid,
        )
    )


def solution(mesh):
    in_specs = (P("pln", None, "sub"), P(), P(None, "pln", None, "sub"), P("pln", None, "sub"))
    out_specs = (P("sub", None), P("pln", None, "sub"))
    return jax.shard_map(body, mesh=mesh, in_specs=in_specs, out_specs=out_specs, check_vma=False)
```
